32 devices in a mesh: dp: 8 (over z, y), expert: 4 (over x, core).
Axes of the slice: x: 2, y: 2, z: 4, core: 2. Of those that a mesh axis runs over, the one named last changes fastest.
Arguments:
- hidden: bfloat16 [2, 4, 1024, 768], P(None, 'expert', 'dp'), may hold values from -6 to 6
- routes: int32 [2, 4, 1024, 2], P(None, 'expert', 'dp'), may hold values from 0 to 3, all different within a row
- prefix: int32 [2, 4], P(None, 'expert'), may hold values from 102 to 512, as said below
- cotangent: bfloat16 [2, 4, 1024, 768], P(None, 'expert', 'dp'), may hold values from -6 to 6
- attn_gain: bfloat16 [768], P(('dp', 'expert')), may hold values from 0.5 to 1.5
- w_query: bfloat16 [768, 768], P(('dp', 'expert')), may hold values from -0.21875 to 0.21875
- w_key: bfloat16 [768, 768], P(('dp', 'expert')), may hold values from -0.21875 to 0.21875
- w_value: bfloat16 [768, 768], P(('dp', 'expert')), may hold values from -0.21875 to 0.21875
- w_output: bfloat16 [768, 768], P(('dp', 'expert')), may hold values from -1.25 to 1.25
- ffn_gain: bfloat16 [768], P(('dp', 'expert')), may hold values from 0.5 to 1.5
- router: bfloat16 [768, 4], P(('dp', 'expert')), may hold values from -0.15625 to 0.15625
- shared_gate: bfloat16 [768, 2048], P(('dp', 'expert')), may hold values from -0.21875 to 0.21875
- shared_up: bfloat16 [768, 2048], P(('dp', 'expert')), may hold values from -0.21875 to 0.21875
- shared_down: bfloat16 [2048, 768], P(('dp', 'expert')), may hold values from -0.125 to 0.125
- expert_gate: bfloat16 [4, 768, 2048], P('expert', 'dp'), may hold values from -0.21875 to 0.21875
- expert_up: bfloat16 [4, 768, 2048], P('expert', 'dp'), may hold values from -0.21875 to 0.21875
- expert_down: bfloat16 [4, 2048, 768], P('expert', 'dp'), may hold values from -0.125 to 0.125
Outputs:
- block_out: bfloat16 [2, 4, 1024, 768], P(None, 'expert', 'dp')
- grad_hidden: bfloat16 [2, 4, 1024, 768], P(None, 'expert', 'dp')
- grad_attn_gain: float32 [768], P(('dp', 'expert'))
- grad_w_query: float32 [768, 768], P(('dp', 'expert'))
- grad_w_key: float32 [768, 768], P(('dp', 'expert'))
- grad_w_value: float32 [768, 768], P(('dp', 'expert'))
- grad_w_output: float32 [768, 768], P(('dp', 'expert'))
- grad_ffn_gain: float32 [768], P(('dp', 'expert'))
- grad_router: float32 [768, 4], P(('dp', 'expert'))
- grad_shared_gate: float32 [768, 2048], P(('dp', 'expert'))
- grad_shared_up: float32 [768, 2048], P(('dp', 'expert'))
- grad_shared_down: float32 [2048, 768], P(('dp', 'expert'))
- grad_expert_gate: float32 [4, 768, 2048], P('expert', 'dp')
- grad_expert_up: float32 [4, 768, 2048], P('expert', 'dp')
- grad_expert_down: float32 [4, 2048, 768], P('expert', 'dp')
The draws below stay inside these ranges and needn't reach their ends.
Inputs may be any that keep to these rules, and one draw needn't show every extreme that they name: `routes`: each token names 2 different experts; every expert is named by some token. Each sequence's prefix length is drawn evenly from 102 to 512; in every draw one sequence has exactly 102 and another exactly 512.
All inputs are finite; a program needn't handle non-finite values.
Results may differ from the reference program's by a relative error of at most 0.024.
Values may be sent and summed in bfloat16 or wider, within the bound.
A program may use at most 320 MiB of HBM per device.

```python
import math
import jax
import jax.numpy as jnp
from jax import lax

WIDTH = 768
HEADS = 12
HEAD_DIM = 64
EXPERT_FF = 2048
SHARED_FF = 2048
TOP_K = 2
TOK_DEV = 128
MICRO_BATCHES = 2
EXPERTS = 4
SEQ_LEN = 1024
SEQUENCES = 4
CAPACITY = 80
N_DP = 8


def draw_prefix(key, part):
    key = jax.random.fold_in(key, 7)
    value_key, place_key = jax.random.split(key)
    lowest = SEQ_LEN // 10
    highest_len = SEQ_LEN // 2
    count_all = MICRO_BATCHES * SEQUENCES
    lengths = jax.random.randint(value_key, (count_all,), lowest, highest_len + 1, dtype=jnp.int32)
    order = jax.random.permutation(place_key, count_all)
    lengths = lengths.at[order[0]].set(lowest).at[order[1]].set(highest_len)
    return lengths.reshape(MICRO_BATCHES, SEQUENCES)


def block_scale(key, dims, cuts, low, top_value):
    loudness = 1.0
    for position, blocks in cuts:
        heights = jax.random.uniform(jax.random.fold_in(jax.random.fold_in(key, 6), position), (blocks,), jnp.float32, low / len(cuts), top_value / len(cuts))
        loudness = loudness * jnp.repeat(jnp.exp(heights), dims[position] // blocks).reshape((-1,) + (1,) * (len(dims) - 1 - position))
    return loudness


def different_ones(key, rows, number_of, top, lift):
    sequence = jax.random.permutation(jax.random.fold_in(key, 1), number_of)
    boost = sequence
    for power in range(3):
        boost = boost * boost // number_of
    boost = boost * lift // number_of
    tickets = jax.random.randint(jax.random.fold_in(key, 2), (rows, number_of), 0, 4096) + boost
    sure = jax.random.permutation(jax.random.fold_in(key, 3), rows)[jnp.arange(number_of) % rows]
    tickets = jnp.where(jnp.arange(rows)[:, None] == sure[None, :], 1 << 14, tickets)
    score = tickets * number_of + jnp.arange(number_of)
    return lax.top_k(score.astype(jnp.int32), top)[1].astype(jnp.int32)


def normal_values(key, shape, deviation, most, cuts=(), kind=jnp.bfloat16):
    drawn = jax.random.normal(key, shape, jnp.float32) * deviation
    if len(cuts) > 0:
        drawn = block_scale(key, shape, cuts, -0.22, 0.18) * drawn
    return jnp.clip(drawn, min=-most, max=most).astype(kind)


def setup_inputs(seed: int = 0) -> dict:
    splits = jax.random.split(jax.random.key(seed), 18)
    hidden = normal_values(splits[0], (MICRO_BATCHES, SEQUENCES, SEQ_LEN, WIDTH), 1.0, 6.0, ((1, 4), (2, 8)))
    routes = different_ones(splits[1], MICRO_BATCHES * SEQUENCES * SEQ_LEN, EXPERTS, TOP_K, 4096).reshape((MICRO_BATCHES, SEQUENCES, SEQ_LEN, TOP_K))
    prefix = draw_prefix(jax.random.fold_in(splits[17], 71), 0)
    cotangent = normal_values(splits[3], (MICRO_BATCHES, SEQUENCES, SEQ_LEN, WIDTH), 1.0, 6.0, ((1, 4), (2, 8)))
    attn_gain = jnp.clip(1.0 + 0.1 * jax.random.normal(splits[4], (WIDTH,), jnp.float32), 0.5, 1.5).astype(jnp.bfloat16)
    w_query = normal_values(splits[5], (WIDTH, WIDTH), WIDTH ** -0.5, 0.21875, ((0, 32),))
    w_key = normal_values(splits[6], (WIDTH, WIDTH), WIDTH ** -0.5, 0.21875, ((0, 32),))
    w_value = normal_values(splits[7], (WIDTH, WIDTH), WIDTH ** -0.5, 0.21875, ((0, 32),))
    w_output = normal_values(splits[8], (WIDTH, WIDTH), (WIDTH // 32) ** -0.5, 1.25, ((0, 32),))
    ffn_gain = jnp.clip(1.0 + 0.1 * jax.random.normal(splits[9], (WIDTH,), jnp.float32), 0.5, 1.5).astype(jnp.bfloat16)
    router = normal_values(splits[10], (WIDTH, EXPERTS), (2 * WIDTH) ** -0.5, 0.15625, ((0, 32),))
    shared_gate = normal_values(splits[11], (WIDTH, SHARED_FF), WIDTH ** -0.5, 0.21875, ((0, 32),))
    shared_up = normal_values(splits[12], (WIDTH, SHARED_FF), WIDTH ** -0.5, 0.21875, ((0, 32),))
    shared_down = normal_values(splits[13], (SHARED_FF, WIDTH), SHARED_FF ** -0.5, 0.125, ((0, 32),))
    expert_gate = normal_values(splits[14], (EXPERTS, WIDTH, EXPERT_FF), WIDTH ** -0.5, 0.21875, ((0, 4), (1, 8)))
    expert_up = normal_values(splits[15], (EXPERTS, WIDTH, EXPERT_FF), WIDTH ** -0.5, 0.21875, ((0, 4), (1, 8)))
    expert_down = normal_values(splits[16], (EXPERTS, EXPERT_FF, WIDTH), EXPERT_FF ** -0.5, 0.125, ((0, 4), (1, 8)))
    return dict(hidden=hidden, routes=routes, prefix=prefix, cotangent=cotangent, attn_gain=attn_gain, w_query=w_query, w_key=w_key, w_value=w_value, w_output=w_output, ffn_gain=ffn_gain, router=router, shared_gate=shared_gate, shared_up=shared_up, shared_down=shared_down, expert_gate=expert_gate, expert_up=expert_up, expert_down=expert_down)


eps = 1e-06
highest = lax.Precision.HIGHEST
neg_fill = -1e+30

@jax.custom_vjp
def low(v):
    return lax.optimization_barrier(v.astype(jnp.bfloat16)).astype(jnp.float32)

@jax.custom_vjp
def low_back(v):
    return v

def low_keep(v):
    return (low(v), None)

def low_pass(kept, grad):
    return (grad,)

def back_keep(v):
    return (v, None)

def back_low(kept, grad):
    return (low(grad),)
low.defvjp(low_keep, low_pass)
low_back.defvjp(back_keep, back_low)

def rms_scale(values):
    return lax.rsqrt(lax.optimization_barrier(jnp.mean(values * values, axis=-1, keepdims=True)) + eps)

def rotary_tables(positions, head_size):
    halfway = head_size // 2
    frequency = jnp.exp(jnp.arange(halfway, dtype=jnp.float32) * (-math.log(10000.0) * 2.0 / head_size))
    angles = positions.astype(jnp.float32)[:, None] * frequency[None, :]
    return (jnp.cos(angles)[:, None, :], jnp.sin(angles)[:, None, :])

def rotate(values, cosine, sine_tab):
    halfway = values.shape[-1] // 2
    first_part = values[..., :halfway]
    second_part = values[..., halfway:]
    return jnp.concatenate([first_part * cosine - second_part * sine_tab, second_part * cosine + first_part * sine_tab], axis=-1)

def visible(query_pos, key_pos, prefix_len):
    return (key_pos[None, :] <= query_pos[:, None]) | (query_pos[:, None] < prefix_len) & (key_pos[None, :] < prefix_len)

def attend_block(block_queries, block_start, key_rows, value_rows, prefix_len):
    row_count = block_queries.shape[0]
    query_pos = block_start + jnp.arange(row_count, dtype=jnp.int32)
    key_pos = jnp.arange(key_rows.shape[0], dtype=jnp.int32)
    allowed = visible(query_pos, key_pos, prefix_len)[None]
    scores = low_back(jnp.einsum('qhd,khd->hqk', block_queries, key_rows, precision=highest) * (1.0 / math.sqrt(HEAD_DIM)))
    scores = jnp.where(allowed, scores, neg_fill)
    row_max = lax.optimization_barrier(jnp.max(scores, axis=-1, keepdims=True))
    log_total = row_max + jnp.log(lax.optimization_barrier(jnp.sum(jnp.exp(scores - row_max), axis=-1, keepdims=True)))
    weights = jnp.exp(scores - log_total)
    return jnp.einsum('hqk,khd->qhd', low(weights), value_rows, precision=highest)

def full_layer(params, seq_hidden, seq_routes, prefix_len):
    attn_gain, w_query, w_key, w_value, w_output, ffn_gain, router, shared_gate, shared_up, shared_down, expert_gate, expert_up, expert_down = params
    length = seq_hidden.shape[0]
    positions = jnp.arange(length, dtype=jnp.int32)
    cosine, sine_tab = rotary_tables(positions, HEAD_DIM)
    attn_norm = seq_hidden * rms_scale(seq_hidden)
    normed = low(attn_norm * attn_gain)

    def heads_of(matrix):
        return jnp.dot(normed, matrix, precision=highest).reshape(length, HEADS, HEAD_DIM)
    queries = low(rotate(low_back(heads_of(w_query)), cosine, sine_tab))
    key_rows = low(rotate(low_back(heads_of(w_key)), cosine, sine_tab))
    value_rows = low(low_back(heads_of(w_value)))
    block_rows = TOK_DEV * math.gcd(N_DP, max(1, 512 // TOK_DEV))
    block_count = length // block_rows
    starts = jnp.arange(block_count, dtype=jnp.int32) * block_rows
    checked = jax.checkpoint(attend_block)

    def one_block(packed):
        return checked(packed[0], packed[1], key_rows, value_rows, prefix_len)
    context = lax.map(one_block, (queries.reshape(block_count, block_rows, HEADS, HEAD_DIM), starts))
    context = low(low_back(context.reshape(length, WIDTH)))
    attended = seq_hidden + low_back(jnp.dot(context, w_output, precision=highest))
    ffn_norm = attended * rms_scale(attended)
    mixed = low(ffn_norm * ffn_gain)
    logits = jnp.dot(mixed, router, precision=highest)
    expert_ids = jnp.arange(EXPERTS, dtype=jnp.int32)
    route_hot = (seq_routes[..., None] == expert_ids).astype(jnp.float32)
    gate_probs = jax.nn.softmax(lax.optimization_barrier(jnp.sum(route_hot * logits[:, None, :], axis=-1)), axis=-1)
    groups = length // TOK_DEV
    hot_int = (seq_routes[..., None] == expert_ids).astype(jnp.int32).reshape(groups, TOK_DEV * TOP_K, EXPERTS)
    earlier = jnp.cumsum(hot_int, axis=1) - hot_int
    pair_rank = lax.optimization_barrier(jnp.sum(earlier * hot_int, axis=-1)).reshape(groups, TOK_DEV, TOP_K)
    group_routes = seq_routes.reshape(groups, TOK_DEV, TOP_K)
    slot_index = jnp.where(pair_rank < CAPACITY, group_routes * CAPACITY + pair_rank, EXPERTS * CAPACITY)
    slot_hot = (slot_index[..., None] == jnp.arange(EXPERTS * CAPACITY, dtype=jnp.int32)).astype(jnp.float32)
    grouped = mixed.reshape(groups, TOK_DEV, WIDTH)
    dispatched = low_back(jnp.einsum('gtks,gtd->gsd', slot_hot, grouped, precision=highest)).reshape(groups, EXPERTS, CAPACITY, WIDTH)
    gate_activation = low_back(jnp.einsum('gecd,edf->gecf', dispatched, expert_gate, precision=highest))
    up_activation = low_back(jnp.einsum('gecd,edf->gecf', dispatched, expert_up, precision=highest))
    expert_hidden = low(jax.nn.silu(gate_activation) * up_activation)
    returned = low(low_back(jnp.einsum('gecf,efd->gecd', expert_hidden, expert_down, precision=highest)))
    weighted = slot_hot * gate_probs.reshape(groups, TOK_DEV, TOP_K)[..., None]
    expert_sum = jnp.einsum('gtks,gsd->gtd', weighted, returned.reshape(groups, EXPERTS * CAPACITY, WIDTH), precision=highest).reshape(length, WIDTH)
    shared_in = low_back(jnp.dot(mixed, shared_gate, precision=highest))
    shared_lift = low_back(jnp.dot(mixed, shared_up, precision=highest))
    shared_hidden = low(jax.nn.silu(shared_in) * shared_lift)
    shared_out = jnp.dot(shared_hidden, shared_down, precision=highest)
    return attended + shared_out + expert_sum

def reference(hidden, routes, prefix, cotangent, attn_gain, w_query, w_key, w_value, w_output, ffn_gain, router, shared_gate, shared_up, shared_down, expert_gate, expert_up, expert_down):
    params = (attn_gain.astype(jnp.float32), w_query.astype(jnp.float32), w_key.astype(jnp.float32), w_value.astype(jnp.float32), w_output.astype(jnp.float32), ffn_gain.astype(jnp.float32), router.astype(jnp.float32), shared_gate.astype(jnp.float32), shared_up.astype(jnp.float32), shared_down.astype(jnp.float32), expert_gate.astype(jnp.float32), expert_up.astype(jnp.float32), expert_down.astype(jnp.float32))
    seq_total = MICRO_BATCHES * SEQUENCES
    flat_hidden = hidden.reshape(seq_total, SEQ_LEN, WIDTH).astype(jnp.float32)
    flat_cot = cotangent.reshape(seq_total, SEQ_LEN, WIDTH).astype(jnp.float32)
    flat_routes = routes.reshape(seq_total, SEQ_LEN, TOP_K)
    flat_prefix = prefix.reshape(seq_total)

    def one_sequence(totals, packed):
        seq_hidden, seq_cot, seq_routes, prefix_len = packed

        def forward(weights, inputs):
            return full_layer(weights, inputs, seq_routes, prefix_len)
        result, pullback = jax.vjp(forward, params, seq_hidden)
        weight_grads, input_grad = pullback(seq_cot)
        totals = jax.tree.map(jnp.add, totals, weight_grads)
        return (totals, (result.astype(jnp.bfloat16), input_grad.astype(jnp.bfloat16)))
    empty_totals = jax.tree.map(jnp.zeros_like, params)
    totals, (outputs, input_grads) = lax.scan(one_sequence, empty_totals, (flat_hidden, flat_cot, flat_routes, flat_prefix))
    shape_out = hidden.shape
    return (outputs.reshape(shape_out), input_grads.reshape(shape_out), totals[0], totals[1], totals[2], totals[3], totals[4], totals[5], totals[6], totals[7], totals[8], totals[9], totals[10], totals[11], totals[12])
```

```python
import math

import jax
import jax.numpy as jnp
from jax import lax
from jax.sharding import Mesh
from jax.sharding import PartitionSpec as P

HEAD_DIM = 64
TOP_K = 2
MISC = 128

eps = 1e-06
highest = lax.Precision.HIGHEST
neg_fill = -1e30
f32 = jnp.float32
bf16 = jnp.bfloat16

ALL = ("z", "y", "x", "c")
PLANE = ("y", "x", "c")
DP = ("z", "y")
EXPERT = ("x", "c")


def rms_scale(values):
    return lax.rsqrt(jnp.mean(values * values, axis=-1, keepdims=True) + eps)


def silu_grad(values):
    sig = jax.nn.sigmoid(values)
    return sig * (1.0 + values * (1.0 - sig))


def dot(a, b, dims, batch=((), ())):
    return lax.dot_general(a, b, (dims, batch), preferred_element_type=f32)


def rotary_tables(positions):
    half = HEAD_DIM // 2
    frequency = jnp.exp(jnp.arange(half, dtype=f32) * (-math.log(10000.0) * 2.0 / HEAD_DIM))
    angles = frequency[:, None] * positions.astype(f32)[None, :]
    return jnp.cos(angles), jnp.sin(angles)


def rotate_t(values, cosine, sine, sign):
    rows = values.shape[-1]
    halves = values.reshape(-1, 2, HEAD_DIM // 2, rows)
    first, second = halves[:, 0], halves[:, 1]
    turned = jnp.stack([first * cosine - sign * second * sine, second * cosine + sign * first * sine], axis=1)
    return turned.reshape(values.shape)


def gather_all(shard):
    return lax.all_gather(shard, ALL, axis=0, tiled=True)


def gather_weights(egu, sgu, ed, sd):
    nz, ny, ne = lax.axis_size("z"), lax.axis_size("y"), lax.axis_size(EXPERT)

    def spread(blocks):
        mine = lax.all_to_all(blocks, "z", 0, 0, tiled=True)
        return lax.all_gather(mine, PLANE, axis=0).reshape(ny, ne, nz, *blocks.shape[1:])

    egu_all = jnp.transpose(spread(egu), (1, 2, 0, 3, 4)).reshape(ne, -1, egu.shape[-1])
    sgu_all = jnp.transpose(spread(sgu), (2, 0, 1, 3, 4)).reshape(-1, sgu.shape[-1])
    ed_all = lax.all_gather(ed, PLANE, axis=0).reshape(ny, ne, *ed.shape)
    ed_all = jnp.transpose(ed_all, (1, 0, 2, 3)).reshape(ne, -1, ed.shape[-1])
    sd_all = lax.all_gather(sd, PLANE, axis=0, tiled=True)
    return egu_all, sgu_all, ed_all, sd_all


def gather_line(rows):
    return lax.all_gather(rows, "z", axis=0, tiled=True)


def sum_line(rows):
    return lax.psum_scatter(rows, "z", scatter_dimension=0, tiled=True)


def sum_weights(egu, sgu, ed, sd):
    nz, ny, ne = lax.axis_size("z"), lax.axis_size("y"), lax.axis_size(EXPERT)

    def collect(parts):
        mine = lax.psum_scatter(parts, PLANE, scatter_dimension=0, tiled=True)
        return lax.all_to_all(mine.reshape(nz, *mine.shape[1:]), "z", 0, 0, tiled=True)

    wide = egu.shape[-1]
    egu = jnp.transpose(egu.reshape(ne, nz, ny, -1, wide), (2, 0, 1, 3, 4))
    sgu = jnp.transpose(sgu.reshape(nz, ny, ne, -1, wide), (1, 2, 0, 3, 4))
    egu = collect(egu.reshape(ny * ne * nz, -1, wide))
    sgu = collect(sgu.reshape(ny * ne * nz, -1, wide))
    ed = jnp.transpose(ed.reshape(ne, ny, -1, ed.shape[-1]), (1, 0, 2, 3)).reshape(ny * ne, -1, ed.shape[-1])
    ed = lax.psum_scatter(ed, PLANE, scatter_dimension=0, tiled=True)[0]
    sd = lax.psum_scatter(sd, PLANE, scatter_dimension=0, tiled=True)
    return egu, sgu, ed, sd


def sum_all(parts):
    return lax.psum_scatter(parts, ALL, scatter_dimension=0, tiled=True)


def units_here(batches, heads):
    return -(-batches * heads // lax.axis_size(DP))


def to_units(tensor):
    kinds, batches, width, rows = tensor.shape
    n_dp = lax.axis_size(DP)
    heads = width // HEAD_DIM
    here = units_here(batches, heads)
    units = tensor.reshape(kinds, batches * heads, HEAD_DIM, rows)
    units = jnp.pad(units, ((0, 0), (0, here * n_dp - batches * heads), (0, 0), (0, 0)))
    units = jnp.transpose(units.reshape(kinds, n_dp, here, HEAD_DIM, rows), (1, 2, 0, 3, 4))
    units = lax.all_to_all(units, DP, 0, 0, tiled=True)
    return jnp.transpose(units, (1, 2, 3, 0, 4)).reshape(here, kinds, HEAD_DIM, n_dp * rows)


def from_units(units, batches, heads):
    here, kinds, _, length = units.shape
    n_dp = lax.axis_size(DP)
    rows = length // n_dp
    parts = jnp.transpose(units.reshape(here, kinds, HEAD_DIM, n_dp, rows), (3, 0, 1, 2, 4))
    parts = lax.all_to_all(parts, DP, 0, 0, tiled=True)
    parts = parts.reshape(n_dp * here, kinds, HEAD_DIM, rows)[: batches * heads]
    return jnp.transpose(parts, (1, 0, 2, 3)).reshape(kinds, batches, heads * HEAD_DIM, rows)


def visible_units(prefix, heads, here, length):
    unit = lax.axis_index(DP) * here + jnp.arange(here)
    lengths = prefix[jnp.minimum(unit // heads, prefix.shape[0] - 1), 0]
    pos = jnp.arange(length, dtype=jnp.int32)
    low = pos[None, :] < lengths[:, None]
    return (pos[None, None, :] <= pos[None, :, None]) | (low[:, :, None] & low[:, None, :])


def attention_forward(qkv, batches, heads, prefix):
    units = to_units(qkv)
    q, k, v = units[:, 0], units[:, 1], units[:, 2]
    allowed = visible_units(prefix, heads, q.shape[0], q.shape[-1])
    scores = dot(q, k, ((1,), (1,)), ((0,), (0,))) * (1.0 / math.sqrt(HEAD_DIM))
    scores = jnp.where(allowed, scores, neg_fill)
    top = jnp.max(scores, axis=-1, keepdims=True)
    weights = jnp.exp(scores - top)
    total = jnp.sum(weights, axis=-1, keepdims=True)
    lse = top + jnp.log(total)
    probs = (weights / total).astype(bf16)
    context = dot(v, probs, ((2,), (2,)), ((0,), (0,))).astype(bf16)
    return from_units(context[:, None], batches, heads)[0], (q, k, v, lse)


def attention_backward(context_grad, saved, batches, heads, prefix):
    q, k, v, lse = saved
    grad = to_units(context_grad[None])[:, 0]
    allowed = visible_units(prefix, heads, q.shape[0], q.shape[-1])
    inv = 1.0 / math.sqrt(HEAD_DIM)
    scores = dot(q, k, ((1,), (1,)), ((0,), (0,))) * inv
    probs = jnp.where(allowed, jnp.exp(scores - lse), 0.0)
    prob_grad = dot(grad, v, ((1,), (1,)), ((0,), (0,)))
    delta = jnp.sum(probs * prob_grad, axis=-1, keepdims=True)
    score_grad = (probs * (prob_grad - delta)).astype(bf16)
    dq = dot(k, score_grad, ((2,), (2,)), ((0,), (0,))) * inv
    dk = dot(q, score_grad, ((2,), (1,)), ((0,), (0,))) * inv
    dv = dot(grad, probs.astype(bf16), ((2,), (1,)), ((0,), (0,)))
    return from_units(jnp.stack([dq, dk, dv], axis=1).astype(bf16), batches, heads)


def shards(
    hidden,
    routes,
    prefix,
    cotangent,
    attn_gain,
    w_query,
    w_key,
    w_value,
    w_output,
    ffn_gain,
    router,
    shared_gate,
    shared_up,
    shared_down,
    expert_gate,
    expert_up,
    expert_down,
):
    nz = lax.axis_size("z")
    batches, _, rows, width = hidden.shape
    count = batches * rows
    heads = width // HEAD_DIM
    experts = router.shape[1]
    own = router.shape[0]
    capacity = (5 * rows * TOP_K + 4 * experts - 1) // (4 * experts)
    slice_ff = shared_gate.shape[1] // nz

    misc = jnp.concatenate(
        [router, attn_gain[:, None], ffn_gain[:, None], jnp.zeros((own, MISC - experts - 2), bf16)], axis=1
    )
    attn_shard = jnp.concatenate([w_query, w_key, w_value, w_output, misc], axis=1)

    def slices(gate, up):
        both = jnp.stack([gate.reshape(-1, nz, slice_ff), up.reshape(-1, nz, slice_ff)], axis=2)
        return jnp.transpose(both.reshape(-1, nz, 2 * slice_ff), (1, 0, 2))

    cot = cotangent.reshape(count, width)
    pair_ids = routes.reshape(count, TOP_K)
    cot_routes = jnp.concatenate(
        [cot, pair_ids.astype(bf16), jnp.zeros((count, MISC - TOP_K), bf16)], axis=1
    )
    attn_full = gather_all(attn_shard)
    egu, sgu, ed, sd = gather_weights(
        slices(expert_gate[0], expert_up[0]), slices(shared_gate, shared_up), expert_down[0], shared_down
    )
    cot_line = gather_line(cot_routes)

    w_qkv = attn_full[:, : 3 * width]
    w_out = attn_full[:, 3 * width : 4 * width]
    misc_full = attn_full[:, 4 * width :]
    router_w = misc_full[:, :experts]
    gain_attn = misc_full[:, experts].astype(f32)
    gain_ffn = misc_full[:, experts + 1].astype(f32)

    x_in = hidden.reshape(count, width).astype(f32)
    attn_scale = rms_scale(x_in)
    attn_norm = x_in * attn_scale
    normed = (attn_norm * gain_attn).astype(bf16)
    positions = lax.axis_index(DP) * rows + jnp.arange(rows, dtype=jnp.int32)
    cosine, sine = rotary_tables(jnp.tile(positions, batches))
    projected = dot(w_qkv, normed, ((0,), (1,)))
    turned = rotate_t(projected[: 2 * width], cosine, sine, 1.0)
    qkv = jnp.concatenate([turned, projected[2 * width :]], axis=0).astype(bf16)
    qkv = jnp.transpose(qkv.reshape(3, width, batches, rows), (0, 2, 1, 3))
    context, saved = attention_forward(qkv, batches, heads, prefix)
    context = jnp.transpose(context, (1, 0, 2)).reshape(width, count)
    attended = x_in + dot(context, w_out, ((0,), (0,)))
    ffn_scale = rms_scale(attended)
    ffn_norm = attended * ffn_scale
    mixed = (ffn_norm * gain_ffn).astype(bf16)

    mixed_line = gather_line(mixed)
    cot_rows = cot_line[:, :width]
    ids = cot_line[:, width : width + TOP_K].astype(jnp.int32)
    lines = mixed_line.shape[0]
    groups = lines // rows

    def gates(mixed_rows, pair_ids):
        hot = (pair_ids[..., None] == jnp.arange(experts, dtype=jnp.int32)).astype(f32)
        logits = dot(mixed_rows, router_w, ((1,), (0,)))
        return hot, jax.nn.softmax(jnp.sum(hot * logits[:, None, :], axis=-1), axis=-1)

    hot, probs = gates(mixed_line, ids)
    hot_int = hot.astype(jnp.int32).reshape(groups, rows * TOP_K, experts)
    earlier = jnp.cumsum(hot_int, axis=1) - hot_int
    rank = jnp.sum(earlier * hot_int, axis=-1).reshape(groups, rows, TOP_K)
    group_ids = ids.reshape(groups, rows, TOP_K)
    slot = jnp.where(rank < capacity, group_ids * capacity + rank, experts * capacity)
    slot_hot = (slot[..., None] == jnp.arange(experts * capacity, dtype=jnp.int32)).astype(bf16)
    token_hot = jnp.sum(slot_hot, axis=2)
    slot_probs = jnp.sum(slot_hot.astype(f32) * probs.reshape(groups, rows, TOP_K, 1), axis=(1, 2))

    def dispatch(values):
        per_group = dot(token_hot, values.reshape(groups, rows, width), ((1,), (1,)), ((0,), (0,)))
        per_group = per_group.reshape(groups, experts, capacity, width)
        return jnp.transpose(per_group, (1, 0, 2, 3)).reshape(experts, groups * capacity, width)

    def per_slot(values):
        return jnp.transpose(values.reshape(groups, experts, capacity), (1, 0, 2)).reshape(experts, -1, 1)

    def combine(slots):
        per_group = jnp.transpose(slots.reshape(experts, groups, capacity, width), (1, 0, 2, 3))
        per_group = per_group.reshape(groups, experts * capacity, width)
        return dot(token_hot, per_group, ((2,), (1,)), ((0,), (0,))).reshape(lines, width)

    slot_p = per_slot(slot_probs)
    arrived = dispatch(mixed_line).astype(bf16)
    cot_slots = dispatch(cot_rows)
    pair_grad = (cot_slots * slot_p).astype(bf16)
    batch = ((0,), (0,))
    act = dot(arrived, egu, ((2,), (1,)), batch)
    gate_act, up_act = act[..., :slice_ff], act[..., slice_ff:]
    sig = jax.nn.sigmoid(gate_act)
    silu_act = gate_act * sig
    expert_hidden = (silu_act * up_act).astype(bf16)
    expert_out = dot(expert_hidden, ed, ((2,), (1,)), batch)
    hidden_grad = dot(pair_grad, ed, ((2,), (2,)), batch)
    gate_up_grad = jnp.concatenate(
        [hidden_grad * up_act * sig * (1.0 + gate_act * (1.0 - sig)), hidden_grad * silu_act], axis=-1
    ).astype(bf16)
    grad_egu = dot(arrived, gate_up_grad, ((1,), (1,)), batch).astype(bf16)
    grad_ed = dot(expert_hidden, pair_grad, ((1,), (1,)), batch).astype(bf16)
    slot_grad = dot(gate_up_grad, egu, ((2,), (2,)), batch).astype(bf16)
    gate_dot = jnp.sum(cot_slots * expert_out, axis=-1)
    gate_dot = jnp.transpose(gate_dot.reshape(experts, groups, capacity), (1, 0, 2)).reshape(groups, 1, 1, -1)
    pair_dot = jnp.sum(slot_hot.astype(f32) * gate_dot, axis=-1).reshape(lines, TOP_K)
    expert_sum = combine((expert_out * slot_p).astype(bf16))

    s_act = dot(mixed_line, sgu, ((1,), (0,)))
    s_in, s_lift = s_act[:, :slice_ff], s_act[:, slice_ff:]
    s_sig = jax.nn.sigmoid(s_in)
    s_silu = s_in * s_sig
    s_hidden = (s_silu * s_lift).astype(bf16)
    s_hidden_grad = dot(cot_rows, sd, ((1,), (1,)))
    s_grad = jnp.concatenate(
        [s_hidden_grad * s_lift * s_sig * (1.0 + s_in * (1.0 - s_sig)), s_hidden_grad * s_silu], axis=-1
    ).astype(bf16)
    grad_sgu = dot(mixed_line, s_grad, ((0,), (0,))).astype(bf16)
    grad_sd = dot(s_hidden, cot_rows, ((0,), (0,))).astype(bf16)
    out_part = (dot(s_hidden, sd, ((1,), (0,))) + expert_sum).astype(bf16)
    mixed_part = combine(slot_grad) + dot(s_grad, sgu, ((1,), (1,)))
    mixed_part = jnp.concatenate(
        [mixed_part.astype(bf16), pair_dot.astype(bf16), jnp.zeros((lines, MISC - TOP_K), bf16)], axis=1
    )
    mixed_sum = sum_line(mixed_part).astype(f32)
    out_sum = sum_line(out_part).astype(f32)
    block_rows = (attended + out_sum).astype(bf16)

    hot, probs = gates(mixed, pair_ids)
    gate_grads = mixed_sum[:, width : width + TOP_K]
    picked = probs * (gate_grads - jnp.sum(probs * gate_grads, axis=-1, keepdims=True))
    logit_grad = jnp.sum(hot * picked[..., None], axis=1)
    grad_router = jnp.dot(mixed.astype(f32).T, logit_grad, precision=highest)
    mixed_grad = mixed_sum[:, :width] + jnp.dot(logit_grad, router_w.astype(f32).T, precision=highest)
    cot_wide = cot.astype(f32)
    inner = mixed_grad * gain_ffn
    grad_gffn = jnp.sum(mixed_grad * ffn_norm, axis=0)
    attended_grad = cot_wide + ffn_scale * (inner - ffn_norm * jnp.mean(inner * ffn_norm, axis=-1, keepdims=True))
    out_grad = attended_grad.astype(bf16)
    grad_wout = dot(context, out_grad, ((1,), (0,)))
    context_grad = dot(w_out, out_grad, ((1,), (1,))).astype(bf16)
    context_grad = jnp.transpose(context_grad.reshape(width, batches, rows), (1, 0, 2))

    rot_grad = attention_backward(context_grad, saved, batches, heads, prefix)
    rot_grad = jnp.transpose(rot_grad, (0, 2, 1, 3)).reshape(3 * width, count).astype(f32)
    turned = rotate_t(rot_grad[: 2 * width], cosine, sine, -1.0)
    qkv_grad = jnp.concatenate([turned, rot_grad[2 * width :]], axis=0).astype(bf16)
    grad_wqkv = dot(normed, qkv_grad, ((0,), (1,)))
    normed_grad = dot(qkv_grad, w_qkv, ((0,), (1,)))
    grad_gattn = jnp.sum(normed_grad * attn_norm, axis=0)
    inner = normed_grad * gain_attn
    input_grad = (
        attended_grad + attn_scale * (inner - attn_norm * jnp.mean(inner * attn_norm, axis=-1, keepdims=True))
    ).astype(bf16)

    grad_misc = jnp.concatenate(
        [grad_router, grad_gattn[:, None], grad_gffn[:, None], jnp.zeros((width, MISC - experts - 2), f32)], axis=1
    )
    attn_parts = jnp.concatenate([grad_wqkv, grad_wout, grad_misc], axis=1).astype(bf16)
    attn_sums = sum_all(attn_parts).astype(f32)
    egu_sum, sgu_sum, ed_sum, sd_sum = sum_weights(grad_egu, grad_sgu, grad_ed, grad_sd)

    def joined(blocks):
        both = jnp.transpose(blocks.reshape(nz, -1, 2, slice_ff), (2, 1, 0, 3)).astype(f32)
        return both.reshape(2, -1, nz * slice_ff)

    egu_sum, sgu_sum = joined(egu_sum), joined(sgu_sum)
    return (
        block_rows.reshape(batches, 1, rows, width),
        input_grad.reshape(batches, 1, rows, width),
        attn_sums[:, 4 * width + experts],
        attn_sums[:, :width],
        attn_sums[:, width : 2 * width],
        attn_sums[:, 2 * width : 3 * width],
        attn_sums[:, 3 * width : 4 * width],
        attn_sums[:, 4 * width + experts + 1],
        attn_sums[:, 4 * width : 4 * width + experts],
        sgu_sum[0],
        sgu_sum[1],
        sd_sum.astype(f32),
        egu_sum[0][None],
        egu_sum[1][None],
        ed_sum.astype(f32)[None],
    )


def solution(mesh):
    n_dp, n_expert = mesh.shape["dp"], mesh.shape["expert"]
    nz = 4 if n_dp % 4 == 0 else 1
    grid = Mesh(mesh.devices.reshape(nz, n_dp // nz, n_expert // 2, 2), ALL)
    rows = P(None, EXPERT, DP, None)
    line = P(ALL)
    dense = P(ALL, None)
    expert = P(EXPERT, DP, None)
    return jax.shard_map(
        shards,
        mesh=grid,
        in_specs=(rows, rows, P(None, EXPERT), rows, line)
        + (dense,) * 4
        + (line,)
        + (dense,) * 4
        + (expert,) * 3,
        out_specs=(rows, rows, line) + (dense,) * 4 + (line,) + (dense,) * 4 + (expert,) * 3,
        check_vma=False,
    )
```

```python
import functools
import math

import jax
import jax.numpy as jnp
from jax import lax
from jax.experimental import pallas as pl
from jax.experimental.pallas import tpu as pltpu
from jax.sharding import Mesh
from jax.sharding import PartitionSpec as P

HEAD_DIM = 64
TOP_K = 2
MISC = 128

eps = 1e-06
highest = lax.Precision.HIGHEST
neg_fill = -1e30
f32 = jnp.float32
bf16 = jnp.bfloat16

ALL = ("z", "y", "x", "c")
PLANE = ("y", "x", "c")
DP = ("z", "y")
EXPERT = ("x", "c")


def rms_scale(values):
    return lax.rsqrt(jnp.mean(values * values, axis=-1, keepdims=True) + eps)


def silu_grad(values):
    sig = jax.nn.sigmoid(values)
    return sig * (1.0 + values * (1.0 - sig))


def dot(a, b, dims, batch=((), ())):
    return lax.dot_general(a, b, (dims, batch), preferred_element_type=f32)


def rotary_tables(positions):
    half = HEAD_DIM // 2
    frequency = jnp.exp(jnp.arange(half, dtype=f32) * (-math.log(10000.0) * 2.0 / HEAD_DIM))
    angles = frequency[:, None] * positions.astype(f32)[None, :]
    return jnp.cos(angles), jnp.sin(angles)


def rotate_t(values, cosine, sine, sign):
    rows = values.shape[-1]
    halves = values.reshape(-1, 2, HEAD_DIM // 2, rows)
    first, second = halves[:, 0], halves[:, 1]
    turned = jnp.stack([first * cosine - sign * second * sine, second * cosine + sign * first * sine], axis=1)
    return turned.reshape(values.shape)


def gather_all(shard):
    return lax.all_gather(shard, ALL, axis=0, tiled=True)


def gather_weights(egu, sgu, ed, sd):
    nz, ny, ne = lax.axis_size("z"), lax.axis_size("y"), lax.axis_size(EXPERT)

    def spread(blocks):
        mine = lax.all_to_all(blocks, "z", 0, 0, tiled=True)
        return lax.all_gather(mine, PLANE, axis=0).reshape(ny, ne, nz, *blocks.shape[1:])

    egu_all = jnp.transpose(spread(egu), (1, 2, 0, 3, 4)).reshape(ne, -1, egu.shape[-1])
    sgu_all = jnp.transpose(spread(sgu), (2, 0, 1, 3, 4)).reshape(-1, sgu.shape[-1])
    ed_all = lax.all_gather(ed, PLANE, axis=0).reshape(ny, ne, *ed.shape)
    ed_all = jnp.transpose(ed_all, (1, 0, 2, 3)).reshape(ne, -1, ed.shape[-1])
    sd_all = lax.all_gather(sd, PLANE, axis=0, tiled=True)
    return egu_all, sgu_all, ed_all, sd_all


def gather_line(rows):
    return lax.all_gather(rows, "z", axis=0, tiled=True)


def gather_inputs_plain(attn, egu, sgu, ed, sd, cot):
    return (gather_all(attn), *gather_weights(egu, sgu, ed, sd), gather_line(cot))


def paired():
    return tuple(lax.axis_size(name) for name in PLANE) == (2, 2, 2)


def sum_line(rows):
    return lax.psum_scatter(rows, "z", scatter_dimension=0, tiled=True)


def sum_weights(egu, sgu, ed, sd):
    nz, ny, ne = lax.axis_size("z"), lax.axis_size("y"), lax.axis_size(EXPERT)

    def collect(parts):
        mine = lax.psum_scatter(parts, PLANE, scatter_dimension=0, tiled=True)
        return lax.all_to_all(mine.reshape(nz, *mine.shape[1:]), "z", 0, 0, tiled=True)

    wide = egu.shape[-1]
    egu = jnp.transpose(egu.reshape(ne, nz, ny, -1, wide), (2, 0, 1, 3, 4))
    sgu = jnp.transpose(sgu.reshape(nz, ny, ne, -1, wide), (1, 2, 0, 3, 4))
    egu = collect(egu.reshape(ny * ne * nz, -1, wide))
    sgu = collect(sgu.reshape(ny * ne * nz, -1, wide))
    ed = jnp.transpose(ed.reshape(ne, ny, -1, ed.shape[-1]), (1, 0, 2, 3)).reshape(ny * ne, -1, ed.shape[-1])
    ed = lax.psum_scatter(ed, PLANE, scatter_dimension=0, tiled=True)[0]
    sd = lax.psum_scatter(sd, PLANE, scatter_dimension=0, tiled=True)
    return egu, sgu, ed, sd


def sum_all(parts):
    return lax.psum_scatter(parts, ALL, scatter_dimension=0, tiled=True)


def sum_everything_plain(attn, egu, sgu, ed, sd, out):
    return (sum_all(attn), *sum_weights(egu, sgu, ed, sd), sum_line(out))


def units_here(batches, heads):
    return -(-batches * heads // lax.axis_size(DP))


def to_units(tensor):
    kinds, batches, width, rows = tensor.shape
    n_dp = lax.axis_size(DP)
    heads = width // HEAD_DIM
    here = units_here(batches, heads)
    units = tensor.reshape(kinds, batches * heads, HEAD_DIM, rows)
    units = jnp.pad(units, ((0, 0), (0, here * n_dp - batches * heads), (0, 0), (0, 0)))
    units = jnp.transpose(units.reshape(kinds, n_dp, here, HEAD_DIM, rows), (1, 2, 0, 3, 4))
    units = lax.all_to_all(units, DP, 0, 0, tiled=True)
    return jnp.transpose(units, (1, 2, 3, 0, 4)).reshape(here, kinds, HEAD_DIM, n_dp * rows)


def from_units(units, batches, heads):
    here, kinds, _, length = units.shape
    n_dp = lax.axis_size(DP)
    rows = length // n_dp
    parts = jnp.transpose(units.reshape(here, kinds, HEAD_DIM, n_dp, rows), (3, 0, 1, 2, 4))
    parts = lax.all_to_all(parts, DP, 0, 0, tiled=True)
    parts = parts.reshape(n_dp * here, kinds, HEAD_DIM, rows)[: batches * heads]
    return jnp.transpose(parts, (1, 0, 2, 3)).reshape(kinds, batches, heads * HEAD_DIM, rows)


MESH = pl.DeviceIdType.MESH


def position():
    return tuple(lax.axis_index(name) for name in ALL)


def remote(src, dst, send, recv, device):
    return pltpu.make_async_remote_copy(
        src_ref=src, dst_ref=dst, send_sem=send, recv_sem=recv, device_id=device, device_id_type=MESH
    )


def greet(partners):
    barrier = pltpu.get_barrier_semaphore()
    for device in partners:
        pl.semaphore_signal(barrier, inc=1, device_id=device, device_id_type=MESH)
    pl.semaphore_wait(barrier, len(partners))


def any_specs(count):
    return [pl.BlockSpec(memory_space=pl.ANY)] * count


def params(collective_id, vmem=16 << 20):
    return pltpu.CompilerParams(collective_id=collective_id, has_side_effects=True, vmem_limit_bytes=vmem)


class PlaneItem:
    def __init__(self, here, index, place, own, x_first):
        self.here, self.index, self.place, self.own, self.x_first = here, index, place, own, x_first

    def moved(self, along_first, along_second, along_core):
        z, y, x, c = self.here
        move_x, move_y = (along_first, along_second) if self.x_first else (along_second, along_first)
        return (z, 1 - y if move_y else y, 1 - x if move_x else x, 1 - c if along_core else c)

    def ref(self, *moves):
        return self.place(*self.moved(*moves)[1:])

    COPIES = (
        ((0, 0, 0), (1, 0, 0)),
        ((0, 0, 0), (0, 1, 0)),
        ((1, 0, 0), (0, 1, 0)),
        ((0, 0, 0), (0, 0, 1)),
        ((1, 0, 0), (0, 0, 1)),
        ((0, 1, 0), (0, 0, 1)),
        ((1, 1, 0), (0, 0, 1)),
    )

    def copy(self, number, send, recv):
        source, to = self.COPIES[number]
        src = self.own if source == (0, 0, 0) else self.ref(*source)
        return remote(
            src, self.ref(*source), send.at[self.index, number], recv.at[self.index, number], self.moved(*to)
        )

    def arrival(self, number, send, recv):
        source, to = self.COPIES[number]
        ref = self.ref(*[a ^ b for a, b in zip(source, to)])
        return remote(ref, ref, send.at[self.index, number], recv.at[self.index, number], self.moved(*to))


def gather_kernel(nz, *refs):
    inputs, outputs = refs[:6], refs[6:12]
    local, zsend, zrecv, psend, precv = refs[12:]
    attn_in, egu_in, sgu_in, ed_in, sd_in, cot_in = inputs
    attn, egu, sgu, ed, sd, cot = outputs
    here = position()
    z, y, x, c = here
    line = [lax.rem(z + d, nz) for d in range(nz)]
    others = [(line[d], y, x, c) for d in range(1, nz)]
    greet(others + [(z, 1 - y, x, c), (z, y, 1 - x, c), (z, y, x, 1 - c)])

    def flat(zs, py, px, pc):
        return ((zs * 2 + py) * 2 + px) * 2 + pc

    half = ed_in.shape[0] // 2
    places = {
        "attn": lambda zs: lambda py, px, pc: attn.at[flat(zs, py, px, pc)],
        "egu": lambda zs: lambda py, px, pc: egu.at[px * 2 + pc, zs * 2 + py],
        "sgu": lambda zs: lambda py, px, pc: sgu.at[flat(zs, py, px, pc)],
    }
    firsts = {"attn": lambda zs: attn_in, "egu": lambda zs: egu_in.at[zs], "sgu": lambda zs: sgu_in.at[zs]}
    kinds = ("attn", "egu", "sgu")

    def line_copy(kind, d):
        number = kinds.index(kind)
        to, frm = line[d], line[(nz - d) % nz]
        mine = places[kind](z)(y, x, c)
        src = firsts[kind](to)
        theirs = places[kind](frm)(y, x, c)
        sends = remote(src, mine, zsend.at[number, d], zrecv.at[number, d], (to, y, x, c))
        gets = remote(theirs, theirs, zsend.at[number, d], zrecv.at[number, d], (to, y, x, c))
        return sends, gets

    def cot_copy(d):
        to, frm = line[d], line[(nz - d) % nz]
        sends = remote(cot_in, cot.at[z], zsend.at[3, d], zrecv.at[3, d], (to, y, x, c))
        gets = remote(cot.at[frm], cot.at[frm], zsend.at[3, d], zrecv.at[3, d], (to, y, x, c))
        return sends, gets

    items, sums = {}, 0
    for kind in kinds:
        for d in range(nz):
            frm = line[(nz - d) % nz]
            place = places[kind](frm)
            own = firsts[kind](z) if d == 0 else place(y, x, c)
            items[kind, d] = PlaneItem(here, sums, place, own, d % 2 == 1)
            sums += 1
    for h in range(2):
        rows = pl.ds(h * half, half)
        place = lambda py, px, pc, rows=rows: ed.at[px * 2 + pc, py, rows]
        items["ed", h] = PlaneItem(here, sums, place, ed_in.at[rows], h == 1)
        sums += 1
    items["sd", 0] = PlaneItem(here, sums, lambda py, px, pc: sd.at[(py * 2 + px) * 2 + pc], sd_in, False)

    owns = [
        (attn_in, attn.at[flat(z, y, x, c)]),
        (egu_in.at[z], egu.at[x * 2 + c, z * 2 + y]),
        (sgu_in.at[z], sgu.at[flat(z, y, x, c)]),
        (ed_in, ed.at[x * 2 + c, y]),
        (sd_in, sd.at[(y * 2 + x) * 2 + c]),
        (cot_in, cot.at[z]),
    ]
    keeps = [pltpu.make_async_copy(src, dst, local.at[i]) for i, (src, dst) in enumerate(owns)]

    def have_own(item):
        for number in (0, 1, 3):
            item.copy(number, psend, precv).start()

    def have_first(item):
        item.arrival(0, psend, precv).wait_recv()
        item.copy(2, psend, precv).start()
        item.copy(4, psend, precv).start()

    def have_second(item):
        item.arrival(1, psend, precv).wait_recv()
        item.copy(5, psend, precv).start()
        item.arrival(2, psend, precv).wait_recv()
        item.copy(6, psend, precv).start()

    for d in range(1, nz):
        line_copy("attn", d)[0].start()
    have_own(items["attn", 0])
    for kind in ("egu", "sgu"):
        for d in range(1, nz):
            line_copy(kind, d)[0].start()
    for d in range(1, nz):
        cot_copy(d)[0].start()
    rest = [items["ed", 0], items["ed", 1], items["sd", 0], items["egu", 0], items["sgu", 0]]
    for item in rest:
        have_own(item)
    for copy in keeps:
        copy.start()
    for d in range(1, nz):
        line_copy("attn", d)[1].wait_recv()
        have_own(items["attn", d])
    for d in range(nz):
        have_first(items["attn", d])
    for item in rest:
        have_first(item)
    for d in range(1, nz):
        for kind in ("egu", "sgu"):
            line_copy(kind, d)[1].wait_recv()
            have_own(items[kind, d])
    for d in range(nz):
        have_second(items["attn", d])
    late = [items[kind, d] for d in range(1, nz) for kind in ("egu", "sgu")]
    for item in late:
        have_first(item)
    for item in rest + late:
        have_second(item)
    for d in range(1, nz):
        cot_copy(d)[1].wait_recv()
    for item in items.values():
        for number in range(3, 7):
            item.arrival(number, psend, precv).wait_recv()
    for item in items.values():
        for number in range(7):
            item.copy(number, psend, precv).wait_send()
    for d in range(1, nz):
        for kind in kinds:
            line_copy(kind, d)[0].wait_send()
        cot_copy(d)[0].wait_send()
    for copy in keeps:
        copy.wait()


def gather_inputs_fast(attn, egu, sgu, ed, sd, cot):
    nz = lax.axis_size("z")
    all_devices, plane = nz * 8, 8
    items = 3 * nz + 3
    shapes = [
        (all_devices, *attn.shape),
        (4, nz * 2, *egu.shape[1:]),
        (all_devices, *sgu.shape[1:]),
        (4, 2, *ed.shape),
        (plane, *sd.shape),
        (nz, *cot.shape),
    ]
    attn, egu, sgu, ed, sd, cot = pl.pallas_call(
        functools.partial(gather_kernel, nz),
        out_shape=[jax.ShapeDtypeStruct(shape, bf16) for shape in shapes],
        in_specs=any_specs(6),
        out_specs=any_specs(6),
        scratch_shapes=[
            pltpu.SemaphoreType.DMA((6,)),
            pltpu.SemaphoreType.DMA((4, nz)),
            pltpu.SemaphoreType.DMA((4, nz)),
            pltpu.SemaphoreType.DMA((items, 7)),
            pltpu.SemaphoreType.DMA((items, 7)),
        ],
        compiler_params=params(0),
        name="gather_inputs",
    )(attn, egu, sgu, ed, sd, cot)
    return (
        attn.reshape(-1, attn.shape[-1]),
        egu.reshape(4, -1, egu.shape[-1]),
        sgu.reshape(-1, sgu.shape[-1]),
        ed.reshape(4, -1, ed.shape[-1]),
        sd.reshape(-1, sd.shape[-1]),
        cot.reshape(-1, cot.shape[-1]),
    )


def line_gather_steps(z, nz, own, out, sends, gets, neighbour, pieces):
    rows = out.shape[1] // pieces

    def copy(way, source, piece, src=None):
        part = pl.ds(piece * rows, rows)
        dst = out.at[source, part]
        src = dst if src is None else src.at[part]
        return remote(src, dst, sends.at[way, source, piece], gets.at[way, source, piece], neighbour(1 - 2 * way))

    def may_send(way):
        return z < nz - 1 if way == 0 else z > 0

    def start():
        for piece in range(pieces):
            for way in range(2):
                pl.when(may_send(way))(lambda: copy(way, z, piece, own).start())

    def step(distance, piece):
        for way in range(2):
            source = z - distance if way == 0 else z + distance

            @pl.when((source >= 0) & (source < nz))
            def _():
                copy(way, source, piece).wait_recv()
                pl.when(may_send(way))(lambda: copy(way, source, piece).start())

    def end():
        for distance in range(nz):
            for piece in range(pieces):
                for way in range(2):
                    source = z - distance if way == 0 else z + distance

                    @pl.when((source >= 0) & (source < nz) & may_send(way))
                    def _():
                        copy(way, source, piece).wait_send()

    steps = [functools.partial(step, distance, piece) for distance in range(1, nz) for piece in range(pieces)]
    return start, steps, end


def line_partners(here, nz):
    z, y, x, c = here
    return lambda way: (jnp.clip(z + way, 0, nz - 1), y, x, c)


def greet_line(here, nz):
    z = here[0]
    neighbour = line_partners(here, nz)
    barrier = pltpu.get_barrier_semaphore()

    @pl.when(z > 0)
    def _():
        pl.semaphore_signal(barrier, inc=1, device_id=neighbour(-1), device_id_type=MESH)

    @pl.when(z < nz - 1)
    def _():
        pl.semaphore_signal(barrier, inc=1, device_id=neighbour(1), device_id_type=MESH)

    pl.semaphore_wait(barrier, jnp.where(z > 0, 1, 0) + jnp.where(z < nz - 1, 1, 0))


LINE_PIECES = 2


def line_gather_kernel(nz, own, out, local, sends, gets):
    here = position()
    z = here[0]
    greet_line(here, nz)
    start, steps, end = line_gather_steps(z, nz, own, out, sends, gets, line_partners(here, nz), LINE_PIECES)
    start()
    keep = pltpu.make_async_copy(own, out.at[z], local)
    keep.start()
    for step in steps:
        step()
    end()
    keep.wait()


def gather_line_fast(rows):
    nz = lax.axis_size("z")
    sems = pltpu.SemaphoreType.DMA((2, nz, LINE_PIECES))
    out = pl.pallas_call(
        functools.partial(line_gather_kernel, nz),
        out_shape=jax.ShapeDtypeStruct((nz, *rows.shape), bf16),
        in_specs=any_specs(1),
        out_specs=pl.BlockSpec(memory_space=pl.ANY),
        scratch_shapes=[pltpu.SemaphoreType.DMA, sems, sems],
        compiler_params=params(1),
        name="gather_line",
    )(rows)
    return out.reshape(-1, rows.shape[-1])


def line_sum_steps(z, nz, parts, total, up, down, sends, gets, neighbour, pieces):
    rows = parts.shape[1] // pieces
    arrived = (up, down)

    def copy(way, target, piece, src):
        part = pl.ds(piece * rows, rows)
        dst = arrived[way].at[target, part]
        return remote(src, dst, sends.at[way, target, piece], gets.at[way, target, piece], neighbour(1 - 2 * way))

    def part_of(ref, target, piece):
        return ref.at[target, pl.ds(piece * rows, rows)]

    def step(distance, piece):
        for way in range(2):
            target = nz - distance if way == 0 else distance - 1
            ahead = z < target if way == 0 else z > target
            first = z == 0 if way == 0 else z == nz - 1
            mine, theirs = part_of(parts, target, piece), part_of(arrived[way], target, piece)

            @pl.when(ahead & first)
            def _():
                copy(way, target, piece, mine).start()

            @pl.when(ahead & jnp.logical_not(first))
            def _():
                copy(way, target, piece, theirs).wait_recv()
                mine[...] = (mine[...].astype(f32) + theirs[...].astype(f32)).astype(bf16)
                copy(way, target, piece, mine).start()

    def end():
        for piece in range(pieces):
            part = pl.ds(piece * rows, rows)
            total[part, :] = parts[z, part, :].astype(f32)
            for way in range(2):
                theirs = part_of(arrived[way], z, piece)

                @pl.when(z > 0 if way == 0 else z < nz - 1)
                def _():
                    copy(way, z, piece, theirs).wait_recv()
                    total[part, :] += theirs[...].astype(f32)

        for distance in range(1, nz):
            for piece in range(pieces):
                for way in range(2):
                    target = nz - distance if way == 0 else distance - 1

                    @pl.when(z < target if way == 0 else z > target)
                    def _():
                        copy(way, target, piece, part_of(parts, target, piece)).wait_send()

    steps = [functools.partial(step, distance, piece) for distance in range(1, nz) for piece in range(pieces)]
    return steps, end


def line_sum_kernel(nz, parts_in, total, parts, up, down, local, sends, gets):
    here = position()
    z = here[0]
    load = pltpu.make_async_copy(parts_in, parts, local)
    load.start()
    greet_line(here, nz)
    steps, end = line_sum_steps(z, nz, parts, total, up, down, sends, gets, line_partners(here, nz), LINE_PIECES)
    load.wait()
    for step in steps:
        step()
    end()


def sum_line_fast(parts):
    nz = lax.axis_size("z")
    parts = parts.reshape(nz, -1, parts.shape[-1])
    sems = pltpu.SemaphoreType.DMA((2, nz, LINE_PIECES))
    return pl.pallas_call(
        functools.partial(line_sum_kernel, nz),
        out_shape=jax.ShapeDtypeStruct(parts.shape[1:], f32),
        in_specs=any_specs(1),
        out_specs=pl.BlockSpec(memory_space=pltpu.VMEM),
        scratch_shapes=[pltpu.VMEM(parts.shape, bf16)] * 3 + [pltpu.SemaphoreType.DMA, sems, sems],
        compiler_params=params(2, 32 << 20),
        name="sum_line",
    )(parts)


class SumItem:
    def __init__(self, here, index, place, buffers, x_first):
        self.here, self.index, self.place, self.x_first = here, index, place, x_first
        self.own, self.sib, self.second, self.first = buffers

    moved = PlaneItem.moved

    def slot(self, a, b):
        return 2 * a + b

    def begin(self, load, send, recv):
        for a in range(2):
            for b in range(2):
                n = self.slot(a, b)
                self.sib_copy(a, b, send, recv).start()
                pltpu.make_async_copy(self.place(*self.moved(a, b, 0)[1:]), self.own.at[n], load.at[self.index, n]).start()

    def sib_copy(self, a, b, send, recv):
        n = self.slot(a, b)
        src = self.place(*self.moved(a, b, 1)[1:])
        return remote(src, self.sib.at[n], send.at[self.index, n], recv.at[self.index, n], self.moved(0, 0, 1))

    def second_copy(self, a, send, recv):
        n = 4 + a
        src = self.sib.at[self.slot(a, 1)]
        return remote(src, self.second.at[a], send.at[self.index, n], recv.at[self.index, n], self.moved(0, 1, 0))

    def first_copy(self, send, recv):
        src = self.second.at[1]
        return remote(src, self.first, send.at[self.index, 6], recv.at[self.index, 6], self.moved(1, 0, 0))

    def after_core(self, load, send, recv):
        for b in (1, 0):
            for a in range(2):
                n = self.slot(a, b)
                pltpu.make_async_copy(self.own.at[n], self.own.at[n], load.at[self.index, n]).wait()
                self.sib_copy(a, b, send, recv).wait_recv()
                add_to(self.sib.at[n], self.own.at[n])
                if b == 1:
                    self.second_copy(a, send, recv).start()

    def after_second(self, send, recv):
        for a in (1, 0):
            self.second_copy(a, send, recv).wait_recv()
            add_to(self.second.at[a], self.sib.at[self.slot(a, 0)])
            if a == 1:
                self.first_copy(send, recv).start()

    def after_first(self, send, recv):
        self.first_copy(send, recv).wait_recv()
        add_to(self.first, self.second.at[0])

    def end(self, send, recv):
        for a in range(2):
            for b in range(2):
                self.sib_copy(a, b, send, recv).wait_send()
            self.second_copy(a, send, recv).wait_send()
        self.first_copy(send, recv).wait_send()


def add_to(total, term):
    rows, columns = total.shape
    if rows % 16 == 0:

        @pl.loop(0, rows // 16)
        def _(i):
            part = pl.ds(pl.multiple_of(i * 16, 16), 16)
            total[part, :] = (total[part, :].astype(f32) + term[part, :].astype(f32)).astype(bf16)
    else:
        wide = max(w for w in (128, 256, 384, 512, 640) if columns % w == 0)

        @pl.loop(0, columns // wide)
        def _(i):
            part = pl.ds(pl.multiple_of(i * wide, 128), wide)
            total[:, part] = (total[:, part].astype(f32) + term[:, part].astype(f32)).astype(bf16)


SUM_LAG = 2


def sum_kernel(nz, kinds, extra, *refs):
    refs = list(refs)
    take = lambda n: [refs.pop(0) for _ in range(n)]
    inputs = dict(zip(kinds, take(len(kinds))))
    out_parts_in = take(1)[0] if extra else None
    outputs = dict(zip(kinds, take(len(kinds))))
    out_total = take(1)[0] if extra else None
    buffers = {kind: take(4) for kind in kinds}
    zbuf = take(1)[0] if "attn" in kinds else None
    load, send, recv, zsend, zrecv, store = take(6)
    if extra:
        out_parts, up, down, line_load, line_send, line_recv = take(6)
    here = position()
    z, y, x, c = here
    line = [lax.rem(z + d, nz) for d in range(nz)]
    if extra:
        out_load = pltpu.make_async_copy(out_parts_in, out_parts, line_load)
        out_load.start()
    greet([(line[d], y, x, c) for d in range(1, nz)] + [(z, 1 - y, x, c), (z, y, 1 - x, c), (z, y, x, 1 - c)])

    def flat(zs, py, px, pc):
        return ((zs * 2 + py) * 2 + px) * 2 + pc

    places = {
        "attn": lambda zs: lambda py, px, pc: inputs["attn"].at[flat(zs, py, px, pc)],
        "egu": lambda zs: lambda py, px, pc: inputs["egu"].at[px * 2 + pc, zs * 2 + py],
        "sgu": lambda zs: lambda py, px, pc: inputs["sgu"].at[flat(zs, py, px, pc)],
        "ed": lambda h: lambda py, px, pc: inputs["ed"].at[px * 2 + pc, py, pl.ds(h * half, half)],
        "sd": lambda h: lambda py, px, pc: inputs["sd"].at[(py * 2 + px) * 2 + pc],
    }
    if "ed" in kinds:
        half = inputs["ed"].shape[2] // 2
    items, finals = [], []

    def line_copy(number, d, src, dst):
        return remote(src, dst, zsend.at[number, d], zrecv.at[number, d], (line[d], y, x, c))

    def add_item(kind, k):
        own, sib, second, first = buffers[kind]
        row = k
        zs = line[k] if kind in ("attn", "egu", "sgu") else k
        item = SumItem(
            here,
            len(items),
            places[kind](zs),
            (own.at[row], sib.at[row], second.at[row], first.at[row]),
            (k % 2 == 1),
        )
        items.append(item)
        number = ("egu", "sgu", "attn").index(kind) if kind in ("egu", "sgu", "attn") else None

        def finish(wait):
            result = first.at[row]
            if kind in ("ed", "sd"):
                out = outputs[kind]
                dst = out.at[pl.ds(k * half, half)] if kind == "ed" else out
                copy = pltpu.make_async_copy(result, dst, store.at[item.index])
                copy.wait() if wait else copy.start()
                return
            dst = zbuf.at[z] if kind == "attn" else outputs[kind].at[z]
            if k == 0:
                copy = pltpu.make_async_copy(result, dst, store.at[item.index])
                copy.wait() if wait else copy.start()
                return
            copy = line_copy(number, k, result, dst)
            if not wait:
                copy.start()
                return
            copy.wait_send()
            frm = line[(nz - k) % nz]
            dst = zbuf.at[frm] if kind == "attn" else outputs[kind].at[frm]
            line_copy(number, k, dst, dst).wait_recv()

        finals.append(finish)

    order = {"ed": range(2), "sd": range(1)}
    for kind in kinds:
        steps_of = order.get(kind, [d for d in range(nz - 1, -1, -1)])
        for k in steps_of:
            add_item(kind, k)

    line_steps = []
    if extra:
        line_steps, line_end = line_sum_steps(
            z, nz, out_parts, out_total, up, down, line_send, line_recv, line_partners(here, nz), LINE_PIECES
        )
        out_load.wait()
    for item in items:
        item.begin(load, send, recv)
    count = len(items)
    for t in range(count + 2 * SUM_LAG):
        if t < count:
            items[t].after_core(load, send, recv)
        if line_steps:
            line_steps.pop(0)()
        if 0 <= t - SUM_LAG < count:
            items[t - SUM_LAG].after_second(send, recv)
        if 0 <= t - 2 * SUM_LAG < count:
            items[t - 2 * SUM_LAG].after_first(send, recv)
            finals[t - 2 * SUM_LAG](False)
    for step in line_steps:
        step()
    if extra:
        line_end()
    for finish in finals:
        finish(True)
    if "attn" in kinds:
        total = outputs["attn"]
        columns = total.shape[1] // 5

        @pl.loop(0, 5)
        def _(i):
            part = pl.ds(pl.multiple_of(i * columns, 128), columns)
            total[:, part] = sum(zbuf[k, :, part].astype(f32) for k in range(nz))

    for item in items:
        item.end(send, recv)


def sum_fast(arrays, out_parts, collective_id):
    nz = lax.axis_size("z")
    kinds = tuple(arrays)
    shape = {kind: arrays[kind].shape[-2:] for kind in kinds}
    rows = {kind: nz for kind in kinds} | {"ed": 2, "sd": 1}
    if "ed" in kinds:
        shape["ed"] = (shape["ed"][0] // 2, shape["ed"][1])
    results, specs = [], []
    for kind in kinds:
        if kind == "attn":
            results.append(jax.ShapeDtypeStruct(shape[kind], f32))
            specs.append(pl.BlockSpec(memory_space=pltpu.VMEM))
        else:
            whole = {"ed": arrays[kind].shape[-2:], "sd": arrays[kind].shape[-2:]}.get(kind, (nz, *shape[kind]))
            results.append(jax.ShapeDtypeStruct(whole, bf16))
            specs.append(pl.BlockSpec(memory_space=pl.ANY))
    operands = list(arrays.values())
    scratch, items = [], 0
    for kind in kinds:
        n, block = rows[kind], shape[kind]
        items += n
        scratch += [pltpu.VMEM((n, 4, *block), bf16), pltpu.VMEM((n, 4, *block), bf16)]
        scratch += [pltpu.VMEM((n, 2, *block), bf16), pltpu.VMEM((n, *block), bf16)]
    if "attn" in kinds:
        scratch.append(pltpu.VMEM((nz, *shape["attn"]), bf16))
    dma = pltpu.SemaphoreType.DMA
    scratch += [dma((items, 4)), dma((items, 7)), dma((items, 7)), dma((3, nz)), dma((3, nz)), dma((items,))]
    extra = out_parts is not None
    if extra:
        out_parts = out_parts.reshape(nz, -1, out_parts.shape[-1])
        operands.append(out_parts)
        results.append(jax.ShapeDtypeStruct(out_parts.shape[1:], f32))
        specs.append(pl.BlockSpec(memory_space=pltpu.VMEM))
        sems = dma((2, nz, LINE_PIECES))
        scratch += [pltpu.VMEM(out_parts.shape, bf16)] * 3 + [dma, sems, sems]
    return pl.pallas_call(
        functools.partial(sum_kernel, nz, kinds, extra),
        out_shape=results,
        in_specs=any_specs(len(operands)),
        out_specs=specs,
        scratch_shapes=scratch,
        compiler_params=params(collective_id, 58 << 20),
        name="sum_" + "_".join(kinds),
    )(*operands)


def sum_everything_fast(attn, egu, sgu, ed, sd, out_parts):
    nz = lax.axis_size("z")
    wide = egu.shape[-1]
    arrays = {
        "ed": ed.reshape(4, 2, -1, ed.shape[-1]),
        "egu": egu.reshape(4, nz * 2, -1, wide),
        "sd": sd.reshape(8, -1, sd.shape[-1]),
        "sgu": sgu.reshape(nz * 8, -1, wide),
        "attn": attn.reshape(nz * 8, -1, attn.shape[-1]),
    }
    ed, egu, sd, sgu, attn, out = sum_fast(arrays, out_parts, 3)
    return attn, egu, sgu, ed, sd, out


def visible_units(prefix, heads, here, length):
    unit = lax.axis_index(DP) * here + jnp.arange(here)
    lengths = prefix[jnp.minimum(unit // heads, prefix.shape[0] - 1), 0]
    pos = jnp.arange(length, dtype=jnp.int32)
    low = pos[None, :] < lengths[:, None]
    return (pos[None, None, :] <= pos[None, :, None]) | (low[:, :, None] & low[:, None, :])


def attention_forward(qkv, batches, heads, prefix):
    units = to_units(qkv)
    q, k, v = units[:, 0], units[:, 1], units[:, 2]
    allowed = visible_units(prefix, heads, q.shape[0], q.shape[-1])
    scores = dot(q, k, ((1,), (1,)), ((0,), (0,))) * (1.0 / math.sqrt(HEAD_DIM))
    scores = jnp.where(allowed, scores, neg_fill)
    top = jnp.max(scores, axis=-1, keepdims=True)
    weights = jnp.exp(scores - top)
    total = jnp.sum(weights, axis=-1, keepdims=True)
    lse = top + jnp.log(total)
    probs = (weights / total).astype(bf16)
    context = dot(v, probs, ((2,), (2,)), ((0,), (0,))).astype(bf16)
    return from_units(context[:, None], batches, heads)[0], (q, k, v, lse)


def attention_backward(context_grad, saved, batches, heads, prefix):
    q, k, v, lse = saved
    grad = to_units(context_grad[None])[:, 0]
    allowed = visible_units(prefix, heads, q.shape[0], q.shape[-1])
    inv = 1.0 / math.sqrt(HEAD_DIM)
    scores = dot(q, k, ((1,), (1,)), ((0,), (0,))) * inv
    probs = jnp.where(allowed, jnp.exp(scores - lse), 0.0)
    prob_grad = dot(grad, v, ((1,), (1,)), ((0,), (0,)))
    delta = jnp.sum(probs * prob_grad, axis=-1, keepdims=True)
    score_grad = (probs * (prob_grad - delta)).astype(bf16)
    dq = dot(k, score_grad, ((2,), (2,)), ((0,), (0,))) * inv
    dk = dot(q, score_grad, ((2,), (1,)), ((0,), (0,))) * inv
    dv = dot(grad, probs.astype(bf16), ((2,), (1,)), ((0,), (0,)))
    return from_units(jnp.stack([dq, dk, dv], axis=1).astype(bf16), batches, heads)


def shards(
    hidden,
    routes,
    prefix,
    cotangent,
    attn_gain,
    w_query,
    w_key,
    w_value,
    w_output,
    ffn_gain,
    router,
    shared_gate,
    shared_up,
    shared_down,
    expert_gate,
    expert_up,
    expert_down,
):
    nz = lax.axis_size("z")
    batches, _, rows, width = hidden.shape
    count = batches * rows
    heads = width // HEAD_DIM
    experts = router.shape[1]
    own = router.shape[0]
    capacity = (5 * rows * TOP_K + 4 * experts - 1) // (4 * experts)
    slice_ff = shared_gate.shape[1] // nz

    misc = jnp.concatenate(
        [router, attn_gain[:, None], ffn_gain[:, None], jnp.zeros((own, MISC - experts - 2), bf16)], axis=1
    )
    attn_shard = jnp.concatenate([w_query, w_key, w_value, w_output, misc], axis=1)

    def slices(gate, up):
        both = jnp.stack([gate.reshape(-1, nz, slice_ff), up.reshape(-1, nz, slice_ff)], axis=2)
        return jnp.transpose(both.reshape(-1, nz, 2 * slice_ff), (1, 0, 2))

    cot = cotangent.reshape(count, width)
    pair_ids = routes.reshape(count, TOP_K)
    cot_routes = jnp.concatenate(
        [cot, pair_ids.astype(bf16), jnp.zeros((count, MISC - TOP_K), bf16)], axis=1
    )
    gather_inputs = gather_inputs_fast if paired() else gather_inputs_plain
    attn_full, egu, sgu, ed, sd, cot_line = gather_inputs(
        attn_shard,
        slices(expert_gate[0], expert_up[0]),
        slices(shared_gate, shared_up),
        expert_down[0],
        shared_down,
        cot_routes,
    )

    w_qkv = attn_full[:, : 3 * width]
    w_out = attn_full[:, 3 * width : 4 * width]
    misc_full = attn_full[:, 4 * width :]
    router_w = misc_full[:, :experts]
    gain_attn = misc_full[:, experts].astype(f32)
    gain_ffn = misc_full[:, experts + 1].astype(f32)

    x_in = hidden.reshape(count, width).astype(f32)
    attn_scale = rms_scale(x_in)
    attn_norm = x_in * attn_scale
    normed = (attn_norm * gain_attn).astype(bf16)
    positions = lax.axis_index(DP) * rows + jnp.arange(rows, dtype=jnp.int32)
    cosine, sine = rotary_tables(jnp.tile(positions, batches))
    projected = dot(w_qkv, normed, ((0,), (1,)))
    turned = rotate_t(projected[: 2 * width], cosine, sine, 1.0)
    qkv = jnp.concatenate([turned, projected[2 * width :]], axis=0).astype(bf16)
    qkv = jnp.transpose(qkv.reshape(3, width, batches, rows), (0, 2, 1, 3))
    context, saved = attention_forward(qkv, batches, heads, prefix)
    context = jnp.transpose(context, (1, 0, 2)).reshape(width, count)
    attended = x_in + dot(context, w_out, ((0,), (0,)))
    ffn_scale = rms_scale(attended)
    ffn_norm = attended * ffn_scale
    mixed = (ffn_norm * gain_ffn).astype(bf16)

    mixed_line = (gather_line_fast if paired() else gather_line)(mixed)
    cot_rows = cot_line[:, :width]
    ids = cot_line[:, width : width + TOP_K].astype(jnp.int32)
    lines = mixed_line.shape[0]
    groups = lines // rows

    def gates(mixed_rows, pair_ids):
        hot = (pair_ids[..., None] == jnp.arange(experts, dtype=jnp.int32)).astype(f32)
        logits = dot(mixed_rows, router_w, ((1,), (0,)))
        return hot, jax.nn.softmax(jnp.sum(hot * logits[:, None, :], axis=-1), axis=-1)

    hot, probs = gates(mixed_line, ids)
    hot_int = hot.astype(jnp.int32).reshape(groups, rows * TOP_K, experts)
    earlier = jnp.cumsum(hot_int, axis=1) - hot_int
    rank = jnp.sum(earlier * hot_int, axis=-1).reshape(groups, rows, TOP_K)
    group_ids = ids.reshape(groups, rows, TOP_K)
    slot = jnp.where(rank < capacity, group_ids * capacity + rank, experts * capacity)
    slot_hot = (slot[..., None] == jnp.arange(experts * capacity, dtype=jnp.int32)).astype(bf16)
    token_hot = jnp.sum(slot_hot, axis=2)
    slot_probs = jnp.sum(slot_hot.astype(f32) * probs.reshape(groups, rows, TOP_K, 1), axis=(1, 2))

    def dispatch(values):
        per_group = dot(token_hot, values.reshape(groups, rows, width), ((1,), (1,)), ((0,), (0,)))
        per_group = per_group.reshape(groups, experts, capacity, width)
        return jnp.transpose(per_group, (1, 0, 2, 3)).reshape(experts, groups * capacity, width)

    def per_slot(values):
        return jnp.transpose(values.reshape(groups, experts, capacity), (1, 0, 2)).reshape(experts, -1, 1)

    def combine(slots):
        per_group = jnp.transpose(slots.reshape(experts, groups, capacity, width), (1, 0, 2, 3))
        per_group = per_group.reshape(groups, experts * capacity, width)
        return dot(token_hot, per_group, ((2,), (1,)), ((0,), (0,))).reshape(lines, width)

    slot_p = per_slot(slot_probs)
    arrived = dispatch(mixed_line).astype(bf16)
    cot_slots = dispatch(cot_rows)
    pair_grad = (cot_slots * slot_p).astype(bf16)
    batch = ((0,), (0,))
    act = dot(arrived, egu, ((2,), (1,)), batch)
    gate_act, up_act = act[..., :slice_ff], act[..., slice_ff:]
    sig = jax.nn.sigmoid(gate_act)
    silu_act = gate_act * sig
    expert_hidden = (silu_act * up_act).astype(bf16)
    expert_out = dot(expert_hidden, ed, ((2,), (1,)), batch)
    hidden_grad = dot(pair_grad, ed, ((2,), (2,)), batch)
    gate_up_grad = jnp.concatenate(
        [hidden_grad * up_act * sig * (1.0 + gate_act * (1.0 - sig)), hidden_grad * silu_act], axis=-1
    ).astype(bf16)
    grad_egu = dot(arrived, gate_up_grad, ((1,), (1,)), batch).astype(bf16)
    grad_ed = dot(expert_hidden, pair_grad, ((1,), (1,)), batch).astype(bf16)
    slot_grad = dot(gate_up_grad, egu, ((2,), (2,)), batch).astype(bf16)
    gate_dot = jnp.sum(cot_slots * expert_out, axis=-1)
    gate_dot = jnp.transpose(gate_dot.reshape(experts, groups, capacity), (1, 0, 2)).reshape(groups, 1, 1, -1)
    pair_dot = jnp.sum(slot_hot.astype(f32) * gate_dot, axis=-1).reshape(lines, TOP_K)
    expert_sum = combine((expert_out * slot_p).astype(bf16))

    s_act = dot(mixed_line, sgu, ((1,), (0,)))
    s_in, s_lift = s_act[:, :slice_ff], s_act[:, slice_ff:]
    s_sig = jax.nn.sigmoid(s_in)
    s_silu = s_in * s_sig
    s_hidden = (s_silu * s_lift).astype(bf16)
    s_hidden_grad = dot(cot_rows, sd, ((1,), (1,)))
    s_grad = jnp.concatenate(
        [s_hidden_grad * s_lift * s_sig * (1.0 + s_in * (1.0 - s_sig)), s_hidden_grad * s_silu], axis=-1
    ).astype(bf16)
    grad_sgu = dot(mixed_line, s_grad, ((0,), (0,))).astype(bf16)
    grad_sd = dot(s_hidden, cot_rows, ((0,), (0,))).astype(bf16)
    out_part = (dot(s_hidden, sd, ((1,), (0,))) + expert_sum).astype(bf16)
    mixed_part = combine(slot_grad) + dot(s_grad, sgu, ((1,), (1,)))
    mixed_part = jnp.concatenate(
        [mixed_part.astype(bf16), pair_dot.astype(bf16), jnp.zeros((lines, MISC - TOP_K), bf16)], axis=1
    )
    mixed_sum = (sum_line_fast if paired() else sum_line)(mixed_part).astype(f32)

    hot, probs = gates(mixed, pair_ids)
    gate_grads = mixed_sum[:, width : width + TOP_K]
    picked = probs * (gate_grads - jnp.sum(probs * gate_grads, axis=-1, keepdims=True))
    logit_grad = jnp.sum(hot * picked[..., None], axis=1)
    grad_router = jnp.dot(mixed.astype(f32).T, logit_grad, precision=highest)
    mixed_grad = mixed_sum[:, :width] + jnp.dot(logit_grad, router_w.astype(f32).T, precision=highest)
    cot_wide = cot.astype(f32)
    inner = mixed_grad * gain_ffn
    grad_gffn = jnp.sum(mixed_grad * ffn_norm, axis=0)
    attended_grad = cot_wide + ffn_scale * (inner - ffn_norm * jnp.mean(inner * ffn_norm, axis=-1, keepdims=True))
    out_grad = attended_grad.astype(bf16)
    grad_wout = dot(context, out_grad, ((1,), (0,)))
    context_grad = dot(w_out, out_grad, ((1,), (1,))).astype(bf16)
    context_grad = jnp.transpose(context_grad.reshape(width, batches, rows), (1, 0, 2))

    rot_grad = attention_backward(context_grad, saved, batches, heads, prefix)
    rot_grad = jnp.transpose(rot_grad, (0, 2, 1, 3)).reshape(3 * width, count).astype(f32)
    turned = rotate_t(rot_grad[: 2 * width], cosine, sine, -1.0)
    qkv_grad = jnp.concatenate([turned, rot_grad[2 * width :]], axis=0).astype(bf16)
    grad_wqkv = dot(normed, qkv_grad, ((0,), (1,)))
    normed_grad = dot(qkv_grad, w_qkv, ((0,), (1,)))
    grad_gattn = jnp.sum(normed_grad * attn_norm, axis=0)
    inner = normed_grad * gain_attn
    input_grad = (
        attended_grad + attn_scale * (inner - attn_norm * jnp.mean(inner * attn_norm, axis=-1, keepdims=True))
    ).astype(bf16)

    grad_misc = jnp.concatenate(
        [grad_router, grad_gattn[:, None], grad_gffn[:, None], jnp.zeros((width, MISC - experts - 2), f32)], axis=1
    )
    attn_parts = jnp.concatenate([grad_wqkv, grad_wout, grad_misc], axis=1).astype(bf16)
    sum_everything = sum_everything_fast if paired() else sum_everything_plain
    attn_sums, egu_sum, sgu_sum, ed_sum, sd_sum, out_sum = sum_everything(
        attn_parts, grad_egu, grad_sgu, grad_ed, grad_sd, out_part
    )
    attn_sums = attn_sums.astype(f32)
    block_rows = (attended + out_sum.astype(f32)).astype(bf16)

    def joined(blocks):
        both = jnp.transpose(blocks.reshape(nz, -1, 2, slice_ff), (2, 1, 0, 3)).astype(f32)
        return both.reshape(2, -1, nz * slice_ff)

    egu_sum, sgu_sum = joined(egu_sum), joined(sgu_sum)
    return (
        block_rows.reshape(batches, 1, rows, width),
        input_grad.reshape(batches, 1, rows, width),
        attn_sums[:, 4 * width + experts],
        attn_sums[:, :width],
        attn_sums[:, width : 2 * width],
        attn_sums[:, 2 * width : 3 * width],
        attn_sums[:, 3 * width : 4 * width],
        attn_sums[:, 4 * width + experts + 1],
        attn_sums[:, 4 * width : 4 * width + experts],
        sgu_sum[0],
        sgu_sum[1],
        sd_sum.astype(f32),
        egu_sum[0][None],
        egu_sum[1][None],
        ed_sum.astype(f32)[None],
    )


def solution(mesh):
    n_dp, n_expert = mesh.shape["dp"], mesh.shape["expert"]
    nz = 4 if n_dp % 4 == 0 else 1
    grid = Mesh(mesh.devices.reshape(nz, n_dp // nz, n_expert // 2, 2), ALL)
    rows = P(None, EXPERT, DP, None)
    line = P(ALL)
    dense = P(ALL, None)
    expert = P(EXPERT, DP, None)
    return jax.shard_map(
        shards,
        mesh=grid,
        in_specs=(rows, rows, P(None, EXPERT), rows, line)
        + (dense,) * 4
        + (line,)
        + (dense,) * 4
        + (expert,) * 3,
        out_specs=(rows, rows, line) + (dense,) * 4 + (line,) + (dense,) * 4 + (expert,) * 3,
        check_vma=False,
    )
```

```python
import functools
import math

import jax
import jax.numpy as jnp
from jax import lax
from jax.experimental import pallas as pl
from jax.experimental.pallas import tpu as pltpu
from jax.sharding import Mesh
from jax.sharding import PartitionSpec as P

HEAD_DIM = 64
TOP_K = 2
MISC = 128

eps = 1e-06
highest = lax.Precision.HIGHEST
neg_fill = -1e30
f32 = jnp.float32
bf16 = jnp.bfloat16

ALL = ("z", "y", "x", "c")
PLANE = ("y", "x", "c")
DP = ("z", "y")
EXPERT = ("x", "c")


def rms_scale(values):
    return lax.rsqrt(jnp.mean(values * values, axis=-1, keepdims=True) + eps)


def silu_grad(values):
    sig = jax.nn.sigmoid(values)
    return sig * (1.0 + values * (1.0 - sig))


def dot(a, b, dims, batch=((), ())):
    return lax.dot_general(a, b, (dims, batch), preferred_element_type=f32)


def rotary_tables(positions):
    half = HEAD_DIM // 2
    frequency = jnp.exp(jnp.arange(half, dtype=f32) * (-math.log(10000.0) * 2.0 / HEAD_DIM))
    angles = frequency[:, None] * positions.astype(f32)[None, :]
    return jnp.cos(angles), jnp.sin(angles)


def rotate_t(values, cosine, sine, sign):
    rows = values.shape[-1]
    halves = values.reshape(-1, 2, HEAD_DIM // 2, rows)
    first, second = halves[:, 0], halves[:, 1]
    turned = jnp.stack([first * cosine - sign * second * sine, second * cosine + sign * first * sine], axis=1)
    return turned.reshape(values.shape)


def gather_all(shard):
    return lax.all_gather(shard, ALL, axis=0, tiled=True)


def gather_weights(egu, sgu, ed, sd):
    nz, ny, ne = lax.axis_size("z"), lax.axis_size("y"), lax.axis_size(EXPERT)

    def spread(blocks):
        mine = lax.all_to_all(blocks, "z", 0, 0, tiled=True)
        return lax.all_gather(mine, PLANE, axis=0).reshape(ny, ne, nz, *blocks.shape[1:])

    egu_all = jnp.transpose(spread(egu), (1, 2, 0, 3, 4)).reshape(ne, -1, egu.shape[-1])
    sgu_all = jnp.transpose(spread(sgu), (2, 0, 1, 3, 4)).reshape(-1, sgu.shape[-1])
    ed_all = lax.all_gather(ed, PLANE, axis=0).reshape(ny, ne, *ed.shape)
    ed_all = jnp.transpose(ed_all, (1, 0, 2, 3)).reshape(ne, -1, ed.shape[-1])
    sd_all = lax.all_gather(sd, PLANE, axis=0, tiled=True)
    return egu_all, sgu_all, ed_all, sd_all


def gather_line(rows):
    return lax.all_gather(rows, "z", axis=0, tiled=True)


def paired(batches, heads):
    n_dp = lax.axis_size(DP)
    here = batches * heads // n_dp
    even = here * n_dp == batches * heads and heads % max(1, here) == 0
    return even and tuple(lax.axis_size(name) for name in PLANE) == (2, 2, 2)


def sum_line(rows):
    return lax.psum_scatter(rows, "z", scatter_dimension=0, tiled=True)


def sum_weights(egu, sgu, ed, sd):
    nz, ny, ne = lax.axis_size("z"), lax.axis_size("y"), lax.axis_size(EXPERT)

    def collect(parts):
        mine = lax.psum_scatter(parts, PLANE, scatter_dimension=0, tiled=True)
        return lax.all_to_all(mine.reshape(nz, *mine.shape[1:]), "z", 0, 0, tiled=True)

    wide = egu.shape[-1]
    egu = jnp.transpose(egu.reshape(ne, nz, ny, -1, wide), (2, 0, 1, 3, 4))
    sgu = jnp.transpose(sgu.reshape(nz, ny, ne, -1, wide), (1, 2, 0, 3, 4))
    egu = collect(egu.reshape(ny * ne * nz, -1, wide))
    sgu = collect(sgu.reshape(ny * ne * nz, -1, wide))
    ed = jnp.transpose(ed.reshape(ne, ny, -1, ed.shape[-1]), (1, 0, 2, 3)).reshape(ny * ne, -1, ed.shape[-1])
    ed = lax.psum_scatter(ed, PLANE, scatter_dimension=0, tiled=True)[0]
    sd = lax.psum_scatter(sd, PLANE, scatter_dimension=0, tiled=True)
    return egu, sgu, ed, sd


def sum_all(parts):
    return lax.psum_scatter(parts, ALL, scatter_dimension=0, tiled=True)


def units_here(batches, heads):
    return -(-batches * heads // lax.axis_size(DP))


def to_units(tensor):
    kinds, batches, width, rows = tensor.shape
    n_dp = lax.axis_size(DP)
    heads = width // HEAD_DIM
    here = units_here(batches, heads)
    units = tensor.reshape(kinds, batches * heads, HEAD_DIM, rows)
    units = jnp.pad(units, ((0, 0), (0, here * n_dp - batches * heads), (0, 0), (0, 0)))
    units = jnp.transpose(units.reshape(kinds, n_dp, here, HEAD_DIM, rows), (1, 2, 0, 3, 4))
    units = lax.all_to_all(units, DP, 0, 0, tiled=True)
    return jnp.transpose(units, (1, 2, 3, 0, 4)).reshape(here, kinds, HEAD_DIM, n_dp * rows)


def from_units(units, batches, heads):
    here, kinds, _, length = units.shape
    n_dp = lax.axis_size(DP)
    rows = length // n_dp
    parts = jnp.transpose(units.reshape(here, kinds, HEAD_DIM, n_dp, rows), (3, 0, 1, 2, 4))
    parts = lax.all_to_all(parts, DP, 0, 0, tiled=True)
    parts = parts.reshape(n_dp * here, kinds, HEAD_DIM, rows)[: batches * heads]
    return jnp.transpose(parts, (1, 0, 2, 3)).reshape(kinds, batches, heads * HEAD_DIM, rows)


MESH = pl.DeviceIdType.MESH


def position():
    return tuple(lax.axis_index(name) for name in ALL)


def remote(src, dst, send, recv, device):
    return pltpu.make_async_remote_copy(
        src_ref=src, dst_ref=dst, send_sem=send, recv_sem=recv, device_id=device, device_id_type=MESH
    )


def greet(partners):
    barrier = pltpu.get_barrier_semaphore()
    for device in partners:
        pl.semaphore_signal(barrier, inc=1, device_id=device, device_id_type=MESH)
    pl.semaphore_wait(barrier, len(partners))


def any_specs(count):
    return [pl.BlockSpec(memory_space=pl.ANY)] * count


def params(collective_id, vmem=16 << 20):
    return pltpu.CompilerParams(collective_id=collective_id, has_side_effects=True, vmem_limit_bytes=vmem)


class PlaneItem:
    def __init__(self, here, index, place, own, x_first):
        self.here, self.index, self.place, self.own, self.x_first = here, index, place, own, x_first

    def moved(self, along_first, along_second, along_core):
        z, y, x, c = self.here
        move_x, move_y = (along_first, along_second) if self.x_first else (along_second, along_first)
        return (z, 1 - y if move_y else y, 1 - x if move_x else x, 1 - c if along_core else c)

    def ref(self, *moves):
        return self.place(*self.moved(*moves)[1:])

    COPIES = (
        ((0, 0, 0), (1, 0, 0)),
        ((0, 0, 0), (0, 1, 0)),
        ((1, 0, 0), (0, 1, 0)),
        ((0, 0, 0), (0, 0, 1)),
        ((1, 0, 0), (0, 0, 1)),
        ((0, 1, 0), (0, 0, 1)),
        ((1, 1, 0), (0, 0, 1)),
    )

    def copy(self, number, send, recv):
        source, to = self.COPIES[number]
        src = self.own if source == (0, 0, 0) else self.ref(*source)
        return remote(
            src, self.ref(*source), send.at[self.index, number], recv.at[self.index, number], self.moved(*to)
        )

    def arrival(self, number, send, recv):
        source, to = self.COPIES[number]
        ref = self.ref(*[a ^ b for a, b in zip(source, to)])
        return remote(ref, ref, send.at[self.index, number], recv.at[self.index, number], self.moved(*to))


def line_gather_steps(z, nz, own, out, sends, gets, neighbour, pieces):
    rows = out.shape[1] // pieces

    def copy(way, source, piece, src=None):
        part = pl.ds(piece * rows, rows)
        dst = out.at[source, part]
        src = dst if src is None else src.at[part]
        return remote(src, dst, sends.at[way, source, piece], gets.at[way, source, piece], neighbour(1 - 2 * way))

    def may_send(way):
        return z < nz - 1 if way == 0 else z > 0

    def start():
        for piece in range(pieces):
            for way in range(2):
                pl.when(may_send(way))(lambda: copy(way, z, piece, own).start())

    def step(distance, piece):
        for way in range(2):
            source = z - distance if way == 0 else z + distance

            @pl.when((source >= 0) & (source < nz))
            def _():
                copy(way, source, piece).wait_recv()
                pl.when(may_send(way))(lambda: copy(way, source, piece).start())

    def end():
        for distance in range(nz):
            for piece in range(pieces):
                for way in range(2):
                    source = z - distance if way == 0 else z + distance

                    @pl.when((source >= 0) & (source < nz) & may_send(way))
                    def _():
                        copy(way, source, piece).wait_send()

    steps = [functools.partial(step, distance, piece) for distance in range(1, nz) for piece in range(pieces)]
    return start, steps, end


def line_partners(here, nz):
    z, y, x, c = here
    return lambda way: (jnp.clip(z + way, 0, nz - 1), y, x, c)


def greet_line(here, nz):
    z = here[0]
    neighbour = line_partners(here, nz)
    barrier = pltpu.get_barrier_semaphore()

    @pl.when(z > 0)
    def _():
        pl.semaphore_signal(barrier, inc=1, device_id=neighbour(-1), device_id_type=MESH)

    @pl.when(z < nz - 1)
    def _():
        pl.semaphore_signal(barrier, inc=1, device_id=neighbour(1), device_id_type=MESH)

    pl.semaphore_wait(barrier, jnp.where(z > 0, 1, 0) + jnp.where(z < nz - 1, 1, 0))


LINE_PIECES = 2


def line_gather_kernel(nz, own, out, local, sends, gets):
    here = position()
    z = here[0]
    greet_line(here, nz)
    start, steps, end = line_gather_steps(z, nz, own, out, sends, gets, line_partners(here, nz), LINE_PIECES)
    start()
    keep = pltpu.make_async_copy(own, out.at[z], local)
    keep.start()
    for step in steps:
        step()
    end()
    keep.wait()


def gather_line_fast(rows):
    nz = lax.axis_size("z")
    sems = pltpu.SemaphoreType.DMA((2, nz, LINE_PIECES))
    out = pl.pallas_call(
        functools.partial(line_gather_kernel, nz),
        out_shape=jax.ShapeDtypeStruct((nz, *rows.shape), bf16),
        in_specs=any_specs(1),
        out_specs=pl.BlockSpec(memory_space=pl.ANY),
        scratch_shapes=[pltpu.SemaphoreType.DMA, sems, sems],
        compiler_params=params(1),
        name="gather_line",
    )(rows)
    return out.reshape(-1, rows.shape[-1])


def line_sum_steps(z, nz, parts, total, up, down, sends, gets, neighbour, pieces):
    rows = parts.shape[1] // pieces
    arrived = (up, down)

    def copy(way, target, piece, src):
        part = pl.ds(piece * rows, rows)
        dst = arrived[way].at[target, part]
        return remote(src, dst, sends.at[way, target, piece], gets.at[way, target, piece], neighbour(1 - 2 * way))

    def part_of(ref, target, piece):
        return ref.at[target, pl.ds(piece * rows, rows)]

    def step(distance, piece):
        for way in range(2):
            target = nz - distance if way == 0 else distance - 1
            ahead = z < target if way == 0 else z > target
            first = z == 0 if way == 0 else z == nz - 1
            mine, theirs = part_of(parts, target, piece), part_of(arrived[way], target, piece)

            @pl.when(ahead & first)
            def _():
                copy(way, target, piece, mine).start()

            @pl.when(ahead & jnp.logical_not(first))
            def _():
                copy(way, target, piece, theirs).wait_recv()
                mine[...] = (mine[...].astype(f32) + theirs[...].astype(f32)).astype(bf16)
                copy(way, target, piece, mine).start()

    def end():
        for piece in range(pieces):
            part = pl.ds(piece * rows, rows)
            total[part, :] = parts[z, part, :].astype(f32)
            for way in range(2):
                theirs = part_of(arrived[way], z, piece)

                @pl.when(z > 0 if way == 0 else z < nz - 1)
                def _():
                    copy(way, z, piece, theirs).wait_recv()
                    total[part, :] += theirs[...].astype(f32)

        for distance in range(1, nz):
            for piece in range(pieces):
                for way in range(2):
                    target = nz - distance if way == 0 else distance - 1

                    @pl.when(z < target if way == 0 else z > target)
                    def _():
                        copy(way, target, piece, part_of(parts, target, piece)).wait_send()

    steps = [functools.partial(step, distance, piece) for distance in range(1, nz) for piece in range(pieces)]
    return steps, end


def line_sum_kernel(nz, parts_in, total, parts, up, down, local, sends, gets):
    here = position()
    z = here[0]
    load = pltpu.make_async_copy(parts_in, parts, local)
    load.start()
    greet_line(here, nz)
    steps, end = line_sum_steps(z, nz, parts, total, up, down, sends, gets, line_partners(here, nz), LINE_PIECES)
    load.wait()
    for step in steps:
        step()
    end()


def sum_line_fast(parts):
    nz = lax.axis_size("z")
    parts = parts.reshape(nz, -1, parts.shape[-1])
    sems = pltpu.SemaphoreType.DMA((2, nz, LINE_PIECES))
    return pl.pallas_call(
        functools.partial(line_sum_kernel, nz),
        out_shape=jax.ShapeDtypeStruct(parts.shape[1:], f32),
        in_specs=any_specs(1),
        out_specs=pl.BlockSpec(memory_space=pltpu.VMEM),
        scratch_shapes=[pltpu.VMEM(parts.shape, bf16)] * 3 + [pltpu.SemaphoreType.DMA, sems, sems],
        compiler_params=params(2, 32 << 20),
        name="sum_line",
    )(parts)


class SumItem:
    def __init__(self, here, index, place, buffers, x_first):
        self.here, self.index, self.place, self.x_first = here, index, place, x_first
        self.own, self.sib, self.second, self.first = buffers

    moved = PlaneItem.moved

    def slot(self, a, b):
        return 2 * a + b

    def begin(self, load, send, recv):
        for a in range(2):
            for b in range(2):
                n = self.slot(a, b)
                self.sib_copy(a, b, send, recv).start()
                pltpu.make_async_copy(self.place(*self.moved(a, b, 0)[1:]), self.own.at[n], load.at[self.index, n]).start()

    def sib_copy(self, a, b, send, recv):
        n = self.slot(a, b)
        src = self.place(*self.moved(a, b, 1)[1:])
        return remote(src, self.sib.at[n], send.at[self.index, n], recv.at[self.index, n], self.moved(0, 0, 1))

    def second_copy(self, a, send, recv):
        n = 4 + a
        src = self.sib.at[self.slot(a, 1)]
        return remote(src, self.second.at[a], send.at[self.index, n], recv.at[self.index, n], self.moved(0, 1, 0))

    def first_copy(self, send, recv):
        src = self.second.at[1]
        return remote(src, self.first, send.at[self.index, 6], recv.at[self.index, 6], self.moved(1, 0, 0))

    def after_core(self, load, send, recv):
        for b in (1, 0):
            for a in range(2):
                n = self.slot(a, b)
                pltpu.make_async_copy(self.own.at[n], self.own.at[n], load.at[self.index, n]).wait()
                self.sib_copy(a, b, send, recv).wait_recv()
                add_to(self.sib.at[n], self.own.at[n])
                if b == 1:
                    self.second_copy(a, send, recv).start()

    def after_second(self, send, recv):
        for a in (1, 0):
            self.second_copy(a, send, recv).wait_recv()
            add_to(self.second.at[a], self.sib.at[self.slot(a, 0)])
            if a == 1:
                self.first_copy(send, recv).start()

    def after_first(self, send, recv):
        self.first_copy(send, recv).wait_recv()
        add_to(self.first, self.second.at[0])

    def end(self, send, recv):
        for a in range(2):
            for b in range(2):
                self.sib_copy(a, b, send, recv).wait_send()
            self.second_copy(a, send, recv).wait_send()
        self.first_copy(send, recv).wait_send()


def add_to(total, term):
    rows, columns = total.shape
    if rows % 16 == 0:

        @pl.loop(0, rows // 16)
        def _(i):
            part = pl.ds(pl.multiple_of(i * 16, 16), 16)
            total[part, :] = (total[part, :].astype(f32) + term[part, :].astype(f32)).astype(bf16)
    else:
        wide = max(w for w in (128, 256, 384, 512, 640) if columns % w == 0)

        @pl.loop(0, columns // wide)
        def _(i):
            part = pl.ds(pl.multiple_of(i * wide, 128), wide)
            total[:, part] = (total[:, part].astype(f32) + term[:, part].astype(f32)).astype(bf16)


SUM_LAG = 2


def unit_owner(number, batches, heads, here_units):
    per_batch = heads // here_units
    return number // per_batch, lax.rem(number, per_batch) * here_units


def exchange(me, n_dp, copy):
    ny = 2

    def device(number):
        return (number // ny, lax.rem(number, ny))

    far = [lax.rem(me + d, n_dp) for d in range(1, n_dp)]
    near = [lax.rem(me + n_dp - d, n_dp) for d in range(1, n_dp)]

    def start():
        for number in far:
            copy(number, me, device(number)).start()

    def arrive():
        for number in near:
            copy(me, number, device(number)).wait_recv()

    def end():
        for number in far:
            copy(number, me, device(number)).wait_send()

    return start, arrive, end


def tile_spans(length):
    tile = 256 if length % 512 == 0 else length // 2
    for start in range(0, length, tile):
        if start < length // 2:
            yield start, tile, 0, length // 2
        else:
            yield start, tile, start, start + tile


def masked(values, start, tile, mask_from, keys, length, fill):
    key = mask_from + lax.broadcasted_iota(jnp.int32, (keys - mask_from, tile), 0)
    query = start + lax.broadcasted_iota(jnp.int32, (keys - mask_from, tile), 1)
    allowed = (key <= query) | ((key < length) & (query < length))
    tail = jnp.where(allowed, values[mask_from:], fill)
    return tail if mask_from == 0 else jnp.concatenate([values[:mask_from], tail], axis=0)


def plane_items(here, arrays, outs):
    egu_in, sgu_in, ed_in, sd_in = arrays
    egu, sgu, ed, sd = outs
    half = ed_in.shape[0] // 2
    items = []

    def add(place, own, x_first):
        items.append(PlaneItem(here, len(items), place, own, x_first))

    for h in range(2):
        rows = pl.ds(h * half, half)
        add(lambda py, px, pc, rows=rows: ed.at[px * 2 + pc, py, rows], ed_in.at[rows], h == 1)
    for zs in range(egu_in.shape[0]):
        add(lambda py, px, pc, zs=zs: egu.at[px * 2 + pc, zs * 2 + py], egu_in.at[zs], zs % 2 == 1)
    for zs in range(sgu_in.shape[0]):
        add(lambda py, px, pc, zs=zs: sgu.at[((zs * 2 + py) * 2 + px) * 2 + pc], sgu_in.at[zs], zs % 2 == 1)
    add(lambda py, px, pc: sd.at[(py * 2 + px) * 2 + pc], sd_in, False)
    return items


def attend_kernel(nz, *refs):
    prefix, qkv, egu_in, sgu_in, ed_in, sd_in, cot_in = refs[:7]
    context, units, lse, egu, sgu, ed, sd, cot = refs[7:15]
    result, local, send, recv, csend, crecv, psend, precv, lsend, lrecv = refs[15:]
    here = position()
    z, y, x, c = here
    n_dp = nz * 2
    me = z * 2 + y
    kinds, batches, width, rows = qkv.shape
    heads = width // HEAD_DIM
    count = units.shape[1] // HEAD_DIM
    span = count * HEAD_DIM
    length = units.shape[2]
    greet(
        [(lax.rem(me + d, n_dp) // 2, lax.rem(me + d, 2), x, c) for d in range(1, n_dp)]
        + [(z, y, 1 - x, c), (z, y, x, 1 - c)]
    )

    def columns(number):
        return pl.ds(pl.multiple_of(number * rows, rows), rows)

    def qkv_block(number):
        batch, head = unit_owner(number, batches, heads, count)
        return qkv.at[:, batch, pl.ds(pl.multiple_of(head * HEAD_DIM, HEAD_DIM), span), :]

    def qkv_copy(number, source, device):
        return remote(
            qkv_block(number), units.at[:, :, columns(source)], send.at[number], recv.at[source], (*device, x, c)
        )

    start, arrive, end = exchange(me, n_dp, qkv_copy)
    start()
    keep = pltpu.make_async_copy(qkv_block(me), units.at[:, :, columns(me)], local.at[0])
    keep.start()
    items = plane_items(here, (egu_in, sgu_in, ed_in, sd_in), (egu, sgu, ed, sd))
    for item in items:
        for number in (0, 1, 3):
            item.copy(number, psend, precv).start()
    owns = [(cot_in, cot.at[z]), (ed_in, ed.at[x * 2 + c, y]), (sd_in, sd.at[(y * 2 + x) * 2 + c])]
    owns += [(egu_in.at[zs], egu.at[x * 2 + c, zs * 2 + y]) for zs in range(nz)]
    owns += [(sgu_in.at[zs], sgu.at[((zs * 2 + y) * 2 + x) * 2 + c]) for zs in range(nz)]
    keeps = [pltpu.make_async_copy(src, dst, local.at[1 + i]) for i, (src, dst) in enumerate(owns)]
    for copy in keeps:
        copy.start()

    def have_first(item):
        item.arrival(0, psend, precv).wait_recv()
        item.copy(2, psend, precv).start()
        item.copy(4, psend, precv).start()

    def have_second(item):
        item.arrival(1, psend, precv).wait_recv()
        item.copy(5, psend, precv).start()
        item.arrival(2, psend, precv).wait_recv()
        item.copy(6, psend, precv).start()

    early = len(items) // 2
    for item in items[:early]:
        have_first(item)
    arrive()
    keep.wait()
    line_start, line_steps, line_end = line_gather_steps(
        z, nz, cot_in, cot, lsend, lrecv, line_partners(here, nz), LINE_PIECES
    )
    line_start()

    my_batch, my_head = unit_owner(me, batches, heads, count)
    limit = prefix[my_batch, 0]

    def context_copy(head):
        def copy(number, source, device):
            _, first_head = unit_owner(source, batches, heads, count)
            batch, _ = unit_owner(source, batches, heads, count)
            part = pl.ds(pl.multiple_of((first_head + head) * HEAD_DIM, HEAD_DIM), HEAD_DIM)
            return remote(
                result.at[pl.ds(head * HEAD_DIM, HEAD_DIM), columns(number)],
                context.at[batch, part, :],
                csend.at[head, number],
                crecv.at[head, source],
                (*device, x, c),
            )

        return copy

    def attend(head):
        part = pl.ds(head * HEAD_DIM, HEAD_DIM)
        for first, tile, mask_from, keys in tile_spans(length):
            queries = units[0, part, pl.ds(first, tile)] * bf16(1.0 / math.sqrt(HEAD_DIM))
            scores = dot(units[1, part, pl.ds(0, keys)], queries, ((0,), (0,)))
            scores = masked(scores, first, tile, mask_from, keys, limit, neg_fill)
            top = jnp.max(scores, axis=0, keepdims=True)
            weights = jnp.exp(scores - top)
            total = jnp.sum(weights, axis=0, keepdims=True)
            lse[head, :, pl.ds(first, tile)] = top + jnp.log(total)
            mean = dot(units[2, part, pl.ds(0, keys)], weights.astype(bf16), ((1,), (0,))) / total
            result[part, pl.ds(first, tile)] = mean.astype(bf16)

    exchanges = [exchange(me, n_dp, context_copy(head)) for head in range(count)]
    own_part = [pl.ds(pl.multiple_of((my_head + head) * HEAD_DIM, HEAD_DIM), HEAD_DIM) for head in range(count)]
    own_copies = [
        pltpu.make_async_copy(
            result.at[pl.ds(head * HEAD_DIM, HEAD_DIM), columns(me)],
            context.at[my_batch, own_part[head], :],
            local.at[1 + len(owns) + head],
        )
        for head in range(count)
    ]
    later = [functools.partial(have_first, item) for item in items[early:]]
    later += [functools.partial(have_second, item) for item in items]
    line_steps = list(line_steps)
    for head in range(count):
        attend(head)
        exchanges[head][0]()
        own_copies[head].start()
        if head == 0:
            for step in later[: len(items) - early]:
                step()
            later = later[len(items) - early :]
            for step in line_steps[:LINE_PIECES]:
                step()
            line_steps = line_steps[LINE_PIECES:]
    share = -(-len(later) // max(1, len(line_steps)))
    while later or line_steps:
        for step in later[:share]:
            step()
        later = later[share:]
        if line_steps:
            line_steps.pop(0)()
    for item in items:
        for number in range(3, 7):
            item.arrival(number, psend, precv).wait_recv()
    for head in range(count):
        exchanges[head][1]()
        own_copies[head].wait()
    for item in items:
        for number in range(7):
            item.copy(number, psend, precv).wait_send()
    end()
    line_end()
    for head in range(count):
        exchanges[head][2]()
    for copy in keeps:
        copy.wait()


def attend_fast(prefix, qkv, egu, sgu, ed, sd, cot):
    nz = lax.axis_size("z")
    n_dp = nz * 2
    kinds, batches, width, rows = qkv.shape
    heads = width // HEAD_DIM
    count = batches * heads // n_dp
    length = n_dp * rows
    any_space, vmem = pl.BlockSpec(memory_space=pl.ANY), pl.BlockSpec(memory_space=pltpu.VMEM)
    shapes = [
        ((batches, width, rows), bf16),
        ((kinds, count * HEAD_DIM, length), bf16),
        ((count, 1, length), f32),
        ((4, nz * 2, *egu.shape[1:]), bf16),
        ((nz * 8, *sgu.shape[1:]), bf16),
        ((4, 2, *ed.shape), bf16),
        ((8, *sd.shape), bf16),
        ((nz, *cot.shape), bf16),
    ]
    dma = pltpu.SemaphoreType.DMA
    items = 2 * nz + 3
    line = dma((2, nz, LINE_PIECES))
    context, units, lse, egu, sgu, ed, sd, cot = pl.pallas_call(
        functools.partial(attend_kernel, nz),
        out_shape=[jax.ShapeDtypeStruct(*shape) for shape in shapes],
        in_specs=[pl.BlockSpec(memory_space=pltpu.SMEM)] + [any_space] * 6,
        out_specs=[any_space, vmem, vmem] + [any_space] * 5,
        scratch_shapes=[
            pltpu.VMEM((count * HEAD_DIM, length), bf16),
            dma((4 + 2 * nz + count,)),
            dma((n_dp,)),
            dma((n_dp,)),
            dma((count, n_dp)),
            dma((count, n_dp)),
            dma((items, 7)),
            dma((items, 7)),
            line,
            line,
        ],
        compiler_params=params(4, 40 << 20),
        name="attend",
    )(prefix, qkv, egu, sgu, ed, sd, cot)
    weights = (
        egu.reshape(4, -1, egu.shape[-1]),
        sgu.reshape(-1, sgu.shape[-1]),
        ed.reshape(4, -1, ed.shape[-1]),
        sd.reshape(-1, sd.shape[-1]),
    )
    return context, (units, lse), weights, cot.reshape(-1, cot.shape[-1])


def first_kernel(nz, *refs):
    attn_in, egu_in, sgu_in, attn, egu, sgu, local, zsend, zrecv, psend, precv = refs
    here = position()
    z, y, x, c = here
    line = [lax.rem(z + d, nz) for d in range(nz)]
    greet([(line[d], y, x, c) for d in range(1, nz)] + [(z, 1 - y, x, c), (z, y, 1 - x, c), (z, y, x, 1 - c)])

    def flat(zs, py, px, pc):
        return ((zs * 2 + py) * 2 + px) * 2 + pc

    def line_copy(kind, d, arriving=False):
        to, frm = line[d], line[(nz - d) % nz]
        at = frm if arriving else z
        dst = (attn.at[flat(at, y, x, c)], egu.at[at], sgu.at[at])[kind]
        src = dst if arriving else (attn_in, egu_in.at[to], sgu_in.at[to])[kind]
        return remote(src, dst, zsend.at[kind, d], zrecv.at[kind, d], (to, y, x, c))

    for d in (2, 1, 3) if nz == 4 else range(1, nz):
        line_copy(0, d).start()
    items = []
    for d in range(nz):
        frm = line[(nz - d) % nz]
        place = lambda py, px, pc, frm=frm: attn.at[flat(frm, py, px, pc)]
        items.append(PlaneItem(here, d, place, attn_in if d == 0 else place(y, x, c), d % 2 == 1))

    def have_own(item):
        for number in (0, 1, 3):
            item.copy(number, psend, precv).start()

    have_own(items[0])
    for kind in (1, 2):
        for d in range(1, nz):
            line_copy(kind, d).start()
    owns = [(attn_in, attn.at[flat(z, y, x, c)]), (egu_in.at[z], egu.at[z]), (sgu_in.at[z], sgu.at[z])]
    keeps = [pltpu.make_async_copy(src, dst, local.at[i]) for i, (src, dst) in enumerate(owns)]
    for copy in keeps:
        copy.start()
    for d in range(1, nz):
        line_copy(0, d, True).wait_recv()
        have_own(items[d])
    for item in items:
        item.arrival(0, psend, precv).wait_recv()
        item.copy(2, psend, precv).start()
        item.copy(4, psend, precv).start()
    for item in items:
        item.arrival(1, psend, precv).wait_recv()
        item.copy(5, psend, precv).start()
    for item in items:
        item.arrival(2, psend, precv).wait_recv()
        item.copy(6, psend, precv).start()
    for item in items:
        for number in range(3, 7):
            item.arrival(number, psend, precv).wait_recv()
    for kind in (1, 2):
        for d in range(1, nz):
            line_copy(kind, d, True).wait_recv()
    for item in items:
        for number in range(7):
            item.copy(number, psend, precv).wait_send()
    for kind in range(3):
        for d in range(1, nz):
            line_copy(kind, d).wait_send()
    for copy in keeps:
        copy.wait()


def first_fast(attn, egu, sgu):
    nz = lax.axis_size("z")
    dma = pltpu.SemaphoreType.DMA
    shapes = [(nz * 8, *attn.shape), egu.shape, sgu.shape]
    attn, egu, sgu = pl.pallas_call(
        functools.partial(first_kernel, nz),
        out_shape=[jax.ShapeDtypeStruct(shape, bf16) for shape in shapes],
        in_specs=any_specs(3),
        out_specs=any_specs(3),
        scratch_shapes=[dma((3,)), dma((3, nz)), dma((3, nz)), dma((nz, 7)), dma((nz, 7))],
        compiler_params=params(0),
        name="first",
    )(attn, egu, sgu)
    return attn.reshape(-1, attn.shape[-1]), egu, sgu


def backward_kernel(nz, kinds, *refs):
    refs = list(refs)
    take = lambda n: [refs.pop(0) for _ in range(n)]
    prefix, grad_in, units, lse = take(4)
    inputs = dict(zip(kinds, take(len(kinds))))
    (rows_in,) = take(1)
    (grads,) = take(1)
    outputs = dict(zip(kinds, take(len(kinds))))
    (rows_total,) = take(1)
    grad, dkey, dvalue, result = take(4)
    buffers = {kind: take(4) for kind in kinds}
    local, send, recv, csend, crecv, load, psend, precv, store = take(9)
    rows_parts, up, down, lload, lsend, lrecv = take(6)
    here = position()
    z, y, x, c = here
    n_dp = nz * 2
    me = z * 2 + y
    batches, width, rows = grad_in.shape
    heads = width // HEAD_DIM
    span, length = grad.shape
    count = span // HEAD_DIM
    row_load = pltpu.make_async_copy(rows_in, rows_parts, lload)
    row_load.start()
    greet(
        [(lax.rem(me + d, n_dp) // 2, lax.rem(me + d, 2), x, c) for d in range(1, n_dp)]
        + [(z, y, 1 - x, c), (z, y, x, 1 - c)]
    )

    def columns(number):
        return pl.ds(pl.multiple_of(number * rows, rows), rows)

    def grad_block(number):
        batch, head = unit_owner(number, batches, heads, count)
        return grad_in.at[batch, pl.ds(pl.multiple_of(head * HEAD_DIM, HEAD_DIM), span), :]

    def grad_copy(number, source, device):
        return remote(
            grad_block(number), grad.at[:, columns(source)], send.at[number], recv.at[source], (*device, x, c)
        )

    start, arrive, end = exchange(me, n_dp, grad_copy)
    start()
    keep = pltpu.make_async_copy(grad_block(me), grad.at[:, columns(me)], local.at[0])
    keep.start()

    half = inputs["ed"].shape[2] // 2
    places = {
        "egu": lambda zs: lambda py, px, pc: inputs["egu"].at[px * 2 + pc, zs * 2 + py],
        "sgu": lambda zs: lambda py, px, pc: inputs["sgu"].at[((zs * 2 + py) * 2 + px) * 2 + pc],
        "ed": lambda h: lambda py, px, pc: inputs["ed"].at[px * 2 + pc, py, pl.ds(h * half, half)],
        "sd": lambda h: lambda py, px, pc: inputs["sd"].at[(py * 2 + px) * 2 + pc],
    }
    targets = {
        "egu": lambda k: outputs["egu"].at[k],
        "sgu": lambda k: outputs["sgu"].at[k],
        "ed": lambda k: outputs["ed"].at[pl.ds(k * half, half)],
        "sd": lambda k: outputs["sd"],
    }
    number_of = {"egu": nz, "sgu": nz, "ed": 2, "sd": 1}
    items, finals = [], []
    for kind in kinds:
        for k in range(number_of[kind]):
            parts = tuple(buffer.at[k] for buffer in buffers[kind])
            item = SumItem(here, len(items), places[kind](k), parts, k % 2 == 1)
            finals.append(pltpu.make_async_copy(item.first, targets[kind](k), store.at[item.index]))
            items.append(item)
    for item in items:
        item.begin(load, psend, precv)
    row_load.wait()
    row_steps, row_end = line_sum_steps(
        z, nz, rows_parts, rows_total, up, down, lsend, lrecv, line_partners(here, nz), LINE_PIECES
    )

    def stage(t):
        if t < len(items):
            items[t].after_core(load, psend, precv)
        if 0 <= t - SUM_LAG < len(items):
            items[t - SUM_LAG].after_second(psend, precv)
        if 0 <= t - 2 * SUM_LAG < len(items):
            items[t - 2 * SUM_LAG].after_first(psend, precv)
            finals[t - 2 * SUM_LAG].start()

    steps = [functools.partial(stage, t) for t in range(len(items) + 2 * SUM_LAG)]
    for step in steps[:2]:
        step()
    steps = steps[2:]
    arrive()
    keep.wait()

    my_batch, my_head = unit_owner(me, batches, heads, count)
    limit = prefix[my_batch, 0]
    inv = 1.0 / math.sqrt(HEAD_DIM)

    def head_rows(source, head):
        _, first_head = unit_owner(source, batches, heads, count)
        return pl.ds(pl.multiple_of((first_head + head) * HEAD_DIM, HEAD_DIM), HEAD_DIM)

    def grads_copy(head):
        def copy(number, source, device):
            batch, _ = unit_owner(source, batches, heads, count)
            return remote(
                result.at[:, pl.ds(head * HEAD_DIM, HEAD_DIM), columns(number)],
                grads.at[:, batch, head_rows(source, head), :],
                csend.at[head, number],
                crecv.at[head, source],
                (*device, x, c),
            )

        return copy

    def attend(head):
        part = pl.ds(head * HEAD_DIM, HEAD_DIM)
        dkey[...] = jnp.zeros_like(dkey)
        dvalue[...] = jnp.zeros_like(dvalue)
        for first, tile, mask_from, keys in tile_spans(length):
            here_q, upto = pl.ds(first, tile), pl.ds(0, keys)
            queries = units[0, part, here_q] * bf16(inv)
            key, value, out_grad = units[1, part, upto], units[2, part, upto], grad[part, here_q]
            scores = dot(key, queries, ((0,), (0,)))
            probs = jnp.exp(scores - lse[head, :, here_q])
            probs = masked(probs, first, tile, mask_from, keys, limit, 0.0)
            prob_grad = dot(value, out_grad, ((0,), (0,)))
            delta = jnp.sum(probs * prob_grad, axis=0, keepdims=True)
            score_grad = (probs * (prob_grad - delta)).astype(bf16)
            result[0, part, here_q] = (dot(key, score_grad, ((1,), (0,))) * inv).astype(bf16)
            dkey[:, upto] += dot(queries, score_grad, ((1,), (1,)))
            dvalue[:, upto] += dot(out_grad, probs.astype(bf16), ((1,), (1,)))
        result[1, part, :] = dkey[...].astype(bf16)
        result[2, part, :] = dvalue[...].astype(bf16)

    exchanges = [exchange(me, n_dp, grads_copy(head)) for head in range(count)]
    own_copies = [
        pltpu.make_async_copy(
            result.at[:, pl.ds(head * HEAD_DIM, HEAD_DIM), columns(me)],
            grads.at[:, my_batch, head_rows(me, head), :],
            local.at[1 + head],
        )
        for head in range(count)
    ]
    for head in range(count):
        attend(head)
        exchanges[head][0]()
        own_copies[head].start()
        for step in steps[:3]:
            step()
        steps = steps[3:]
        for step in row_steps[:LINE_PIECES]:
            step()
        row_steps = row_steps[LINE_PIECES:]
    for step in steps + row_steps:
        step()
    row_end()
    for head in range(count):
        exchanges[head][1]()
        own_copies[head].wait()
    for item in items:
        item.end(psend, precv)
    for final in finals:
        final.wait()
    end()
    for head in range(count):
        exchanges[head][2]()


def backward_fast(prefix, grad, saved, egu, sgu, ed, sd, rows):
    nz = lax.axis_size("z")
    n_dp = nz * 2
    units, lse = saved
    batches, width, count_rows = grad.shape
    span, length = units.shape[1:]
    count = span // HEAD_DIM
    wide = egu.shape[-1]
    arrays = {
        "ed": ed.reshape(4, 2, -1, ed.shape[-1]),
        "egu": egu.reshape(4, nz * 2, -1, wide),
        "sgu": sgu.reshape(nz * 8, -1, wide),
        "sd": sd.reshape(8, -1, sd.shape[-1]),
    }
    kinds = tuple(arrays)
    rows = rows.reshape(nz, -1, rows.shape[-1])
    any_space, vmem = pl.BlockSpec(memory_space=pl.ANY), pl.BlockSpec(memory_space=pltpu.VMEM)
    block = {kind: arrays[kind].shape[-2:] for kind in kinds}
    number_of = {"egu": nz, "sgu": nz, "ed": 2, "sd": 1}
    wholes = {"ed": block["ed"], "sd": block["sd"], "egu": (nz, *block["egu"]), "sgu": (nz, *block["sgu"])}
    block["ed"] = (block["ed"][0] // 2, block["ed"][1])
    results = [((3, batches, width, count_rows), bf16)] + [(wholes[kind], bf16) for kind in kinds]
    results += [(rows.shape[1:], f32)]
    scratch = [
        pltpu.VMEM((span, length), bf16),
        pltpu.VMEM((HEAD_DIM, length), f32),
        pltpu.VMEM((HEAD_DIM, length), f32),
        pltpu.VMEM((3, span, length), bf16),
    ]
    items = sum(number_of.values())
    for kind in kinds:
        n = number_of[kind]
        scratch += [pltpu.VMEM((n, 4, *block[kind]), bf16), pltpu.VMEM((n, 4, *block[kind]), bf16)]
        scratch += [pltpu.VMEM((n, 2, *block[kind]), bf16), pltpu.VMEM((n, *block[kind]), bf16)]
    dma = pltpu.SemaphoreType.DMA
    scratch += [dma((1 + count,)), dma((n_dp,)), dma((n_dp,)), dma((count, n_dp)), dma((count, n_dp))]
    scratch += [dma((items, 4)), dma((items, 7)), dma((items, 7)), dma((items,))]
    line = dma((2, nz, LINE_PIECES))
    scratch += [pltpu.VMEM(rows.shape, bf16)] * 3 + [dma, line, line]
    outs = pl.pallas_call(
        functools.partial(backward_kernel, nz, kinds),
        out_shape=[jax.ShapeDtypeStruct(*result) for result in results],
        in_specs=[pl.BlockSpec(memory_space=pltpu.SMEM), any_space, vmem, vmem] + [any_space] * 5,
        out_specs=[any_space] * 5 + [vmem],
        scratch_shapes=scratch,
        compiler_params=params(5, 56 << 20),
        name="attend_backward",
    )(prefix, grad, units, lse, *arrays.values(), rows)
    grads, ed, egu, sgu, sd, total = outs
    return grads, (egu, sgu, ed, sd), total


def last_kernel(nz, *refs):
    attn_in, egu_in, sgu_in, attn, egu, sgu, own, sib, second, first, zbuf = refs[:11]
    local, load, zsend, zrecv, psend, precv, store = refs[11:]
    here = position()
    z, y, x, c = here
    line = [lax.rem(z + d, nz) for d in range(nz)]
    greet([(line[d], y, x, c) for d in range(1, nz)] + [(z, 1 - y, x, c), (z, y, 1 - x, c), (z, y, x, 1 - c)])
    items = []
    for d in (3, 2, 1, 0) if nz == 4 else range(nz - 1, -1, -1):
        place = lambda py, px, pc, zs=line[d]: attn_in.at[((zs * 2 + py) * 2 + px) * 2 + pc]
        items.append((d, SumItem(here, d, place, (own.at[d], sib.at[d], second.at[d], first.at[d]), d % 2 == 1)))
    for _, item in items:
        item.begin(load, psend, precv)

    def line_copy(kind, d, arriving=False):
        to, frm = line[d], line[(nz - d) % nz]
        at = frm if arriving else z
        dst = (zbuf, egu, sgu)[kind].at[at]
        src = dst if arriving else (first.at[d], egu_in.at[to], sgu_in.at[to])[kind]
        return remote(src, dst, zsend.at[kind, d], zrecv.at[kind, d], (to, y, x, c))

    for kind in (1, 2):
        for d in range(1, nz):
            line_copy(kind, d).start()
    keeps = [pltpu.make_async_copy(src.at[z], dst.at[z], local.at[i]) for i, (src, dst) in enumerate(((egu_in, egu), (sgu_in, sgu)))]
    for copy in keeps:
        copy.start()
    mine = pltpu.make_async_copy(first.at[0], zbuf.at[z], store)
    for _, item in items:
        item.after_core(load, psend, precv)
    for _, item in items:
        item.after_second(psend, precv)
    for d, item in items:
        item.after_first(psend, precv)
        if d == 0:
            mine.start()
        else:
            line_copy(0, d).start()
    mine.wait()
    for kind in range(3):
        for d in range(1, nz):
            line_copy(kind, d, True).wait_recv()
    columns = attn.shape[1] // 5

    @pl.loop(0, 5)
    def _(i):
        part = pl.ds(pl.multiple_of(i * columns, 128), columns)
        attn[:, part] = sum(zbuf[k, :, part].astype(f32) for k in range(nz))

    for _, item in items:
        item.end(psend, precv)
    for kind in range(3):
        for d in range(1, nz):
            line_copy(kind, d).wait_send()
    for copy in keeps:
        copy.wait()


def last_fast(attn, egu, sgu):
    nz = lax.axis_size("z")
    dma = pltpu.SemaphoreType.DMA
    attn = attn.reshape(nz * 8, -1, attn.shape[-1])
    block = attn.shape[1:]
    any_space = pl.BlockSpec(memory_space=pl.ANY)
    return pl.pallas_call(
        functools.partial(last_kernel, nz),
        out_shape=[
            jax.ShapeDtypeStruct(block, f32),
            jax.ShapeDtypeStruct(egu.shape, bf16),
            jax.ShapeDtypeStruct(sgu.shape, bf16),
        ],
        in_specs=any_specs(3),
        out_specs=[pl.BlockSpec(memory_space=pltpu.VMEM), any_space, any_space],
        scratch_shapes=[
            pltpu.VMEM((nz, 4, *block), bf16),
            pltpu.VMEM((nz, 4, *block), bf16),
            pltpu.VMEM((nz, 2, *block), bf16),
            pltpu.VMEM((nz, *block), bf16),
            pltpu.VMEM((nz, *block), bf16),
            dma((2,)),
            dma((nz, 4)),
            dma((3, nz)),
            dma((3, nz)),
            dma((nz, 7)),
            dma((nz, 7)),
            dma,
        ],
        compiler_params=params(3, 32 << 20),
        name="last",
    )(attn, egu, sgu)


def visible_units(prefix, heads, here, length):
    unit = lax.axis_index(DP) * here + jnp.arange(here)
    lengths = prefix[jnp.minimum(unit // heads, prefix.shape[0] - 1), 0]
    pos = jnp.arange(length, dtype=jnp.int32)
    low = pos[None, :] < lengths[:, None]
    return (pos[None, None, :] <= pos[None, :, None]) | (low[:, :, None] & low[:, None, :])


def attention_forward(qkv, batches, heads, prefix):
    units = to_units(qkv)
    q, k, v = units[:, 0], units[:, 1], units[:, 2]
    allowed = visible_units(prefix, heads, q.shape[0], q.shape[-1])
    scores = dot(q, k, ((1,), (1,)), ((0,), (0,))) * (1.0 / math.sqrt(HEAD_DIM))
    scores = jnp.where(allowed, scores, neg_fill)
    top = jnp.max(scores, axis=-1, keepdims=True)
    weights = jnp.exp(scores - top)
    total = jnp.sum(weights, axis=-1, keepdims=True)
    lse = top + jnp.log(total)
    probs = (weights / total).astype(bf16)
    context = dot(v, probs, ((2,), (2,)), ((0,), (0,))).astype(bf16)
    return from_units(context[:, None], batches, heads)[0], (q, k, v, lse)


def attention_backward(context_grad, saved, batches, heads, prefix):
    q, k, v, lse = saved
    grad = to_units(context_grad[None])[:, 0]
    allowed = visible_units(prefix, heads, q.shape[0], q.shape[-1])
    inv = 1.0 / math.sqrt(HEAD_DIM)
    scores = dot(q, k, ((1,), (1,)), ((0,), (0,))) * inv
    probs = jnp.where(allowed, jnp.exp(scores - lse), 0.0)
    prob_grad = dot(grad, v, ((1,), (1,)), ((0,), (0,)))
    delta = jnp.sum(probs * prob_grad, axis=-1, keepdims=True)
    score_grad = (probs * (prob_grad - delta)).astype(bf16)
    dq = dot(k, score_grad, ((2,), (2,)), ((0,), (0,))) * inv
    dk = dot(q, score_grad, ((2,), (1,)), ((0,), (0,))) * inv
    dv = dot(grad, probs.astype(bf16), ((2,), (1,)), ((0,), (0,)))
    return from_units(jnp.stack([dq, dk, dv], axis=1).astype(bf16), batches, heads)


def shards(
    hidden,
    routes,
    prefix,
    cotangent,
    attn_gain,
    w_query,
    w_key,
    w_value,
    w_output,
    ffn_gain,
    router,
    shared_gate,
    shared_up,
    shared_down,
    expert_gate,
    expert_up,
    expert_down,
):
    nz = lax.axis_size("z")
    batches, _, rows, width = hidden.shape
    count = batches * rows
    heads = width // HEAD_DIM
    experts = router.shape[1]
    own = router.shape[0]
    capacity = (5 * rows * TOP_K + 4 * experts - 1) // (4 * experts)
    slice_ff = shared_gate.shape[1] // nz

    misc = jnp.concatenate(
        [router, attn_gain[:, None], ffn_gain[:, None], jnp.zeros((own, MISC - experts - 2), bf16)], axis=1
    )
    attn_shard = jnp.concatenate([w_query, w_key, w_value, w_output, misc], axis=1)

    def slices(gate, up):
        both = jnp.stack([gate.reshape(-1, nz, slice_ff), up.reshape(-1, nz, slice_ff)], axis=2)
        return jnp.transpose(both.reshape(-1, nz, 2 * slice_ff), (1, 0, 2))

    cot = cotangent.reshape(count, width)
    pair_ids = routes.reshape(count, TOP_K)
    cot_routes = jnp.concatenate(
        [cot, pair_ids.astype(bf16), jnp.zeros((count, MISC - TOP_K), bf16)], axis=1
    )
    parts = (slices(expert_gate[0], expert_up[0]), slices(shared_gate, shared_up), expert_down[0], shared_down)
    fast = paired(batches, heads)
    if fast:
        attn_full, *lined = first_fast(attn_shard, *parts[:2])
    else:
        attn_full = gather_all(attn_shard)

    w_qkv = attn_full[:, : 3 * width]
    w_out = attn_full[:, 3 * width : 4 * width]
    misc_full = attn_full[:, 4 * width :]
    router_w = misc_full[:, :experts]
    gain_attn = misc_full[:, experts].astype(f32)
    gain_ffn = misc_full[:, experts + 1].astype(f32)

    x_in = hidden.reshape(count, width).astype(f32)
    attn_scale = rms_scale(x_in)
    attn_norm = x_in * attn_scale
    normed = (attn_norm * gain_attn).astype(bf16)
    positions = lax.axis_index(DP) * rows + jnp.arange(rows, dtype=jnp.int32)
    cosine, sine = rotary_tables(jnp.tile(positions, batches))
    projected = dot(w_qkv, normed, ((0,), (1,)))
    turned = rotate_t(projected[: 2 * width], cosine, sine, 1.0)
    qkv = jnp.concatenate([turned, projected[2 * width :]], axis=0).astype(bf16)
    qkv = jnp.transpose(qkv.reshape(3, width, batches, rows), (0, 2, 1, 3))
    if fast:
        context, saved, ffn, cot_line = attend_fast(prefix, qkv, *lined, *parts[2:], cot_routes)
    else:
        context, saved = attention_forward(qkv, batches, heads, prefix)
        ffn, cot_line = gather_weights(*parts), gather_line(cot_routes)
    egu, sgu, ed, sd = ffn
    context = jnp.transpose(context, (1, 0, 2)).reshape(width, count)
    attended = x_in + dot(context, w_out, ((0,), (0,)))
    ffn_scale = rms_scale(attended)
    ffn_norm = attended * ffn_scale
    mixed = (ffn_norm * gain_ffn).astype(bf16)

    mixed_line = (gather_line_fast if fast else gather_line)(mixed)
    cot_rows = cot_line[:, :width]
    ids = cot_line[:, width : width + TOP_K].astype(jnp.int32)
    lines = mixed_line.shape[0]
    groups = lines // rows

    def gates(mixed_rows, pair_ids):
        hot = (pair_ids[..., None] == jnp.arange(experts, dtype=jnp.int32)).astype(f32)
        logits = dot(mixed_rows, router_w, ((1,), (0,)))
        return hot, jax.nn.softmax(jnp.sum(hot * logits[:, None, :], axis=-1), axis=-1)

    hot, probs = gates(mixed_line, ids)
    hot_int = hot.astype(jnp.int32).reshape(groups, rows * TOP_K, experts)
    earlier = jnp.cumsum(hot_int, axis=1) - hot_int
    rank = jnp.sum(earlier * hot_int, axis=-1).reshape(groups, rows, TOP_K)
    group_ids = ids.reshape(groups, rows, TOP_K)
    slot = jnp.where(rank < capacity, group_ids * capacity + rank, experts * capacity)
    slot_hot = (slot[..., None] == jnp.arange(experts * capacity, dtype=jnp.int32)).astype(bf16)
    token_hot = jnp.sum(slot_hot, axis=2)
    slot_probs = jnp.sum(slot_hot.astype(f32) * probs.reshape(groups, rows, TOP_K, 1), axis=(1, 2))

    def dispatch(values):
        per_group = dot(token_hot, values.reshape(groups, rows, width), ((1,), (1,)), ((0,), (0,)))
        per_group = per_group.reshape(groups, experts, capacity, width)
        return jnp.transpose(per_group, (1, 0, 2, 3)).reshape(experts, groups * capacity, width)

    def per_slot(values):
        return jnp.transpose(values.reshape(groups, experts, capacity), (1, 0, 2)).reshape(experts, -1, 1)

    def combine(slots):
        per_group = jnp.transpose(slots.reshape(experts, groups, capacity, width), (1, 0, 2, 3))
        per_group = per_group.reshape(groups, experts * capacity, width)
        return dot(token_hot, per_group, ((2,), (1,)), ((0,), (0,))).reshape(lines, width)

    slot_p = per_slot(slot_probs)
    arrived = dispatch(mixed_line).astype(bf16)
    cot_slots = dispatch(cot_rows)
    pair_grad = (cot_slots * slot_p).astype(bf16)
    batch = ((0,), (0,))
    act = dot(arrived, egu, ((2,), (1,)), batch)
    gate_act, up_act = act[..., :slice_ff], act[..., slice_ff:]
    sig = jax.nn.sigmoid(gate_act)
    silu_act = gate_act * sig
    expert_hidden = (silu_act * up_act).astype(bf16)
    expert_out = dot(expert_hidden, ed, ((2,), (1,)), batch)
    hidden_grad = dot(pair_grad, ed, ((2,), (2,)), batch)
    gate_up_grad = jnp.concatenate(
        [hidden_grad * up_act * sig * (1.0 + gate_act * (1.0 - sig)), hidden_grad * silu_act], axis=-1
    ).astype(bf16)
    grad_egu = dot(arrived, gate_up_grad, ((1,), (1,)), batch).astype(bf16)
    grad_ed = dot(expert_hidden, pair_grad, ((1,), (1,)), batch).astype(bf16)
    slot_grad = dot(gate_up_grad, egu, ((2,), (2,)), batch).astype(bf16)
    gate_dot = jnp.sum(cot_slots * expert_out, axis=-1)
    gate_dot = jnp.transpose(gate_dot.reshape(experts, groups, capacity), (1, 0, 2)).reshape(groups, 1, 1, -1)
    pair_dot = jnp.sum(slot_hot.astype(f32) * gate_dot, axis=-1).reshape(lines, TOP_K)
    expert_sum = combine((expert_out * slot_p).astype(bf16))

    s_act = dot(mixed_line, sgu, ((1,), (0,)))
    s_in, s_lift = s_act[:, :slice_ff], s_act[:, slice_ff:]
    s_sig = jax.nn.sigmoid(s_in)
    s_silu = s_in * s_sig
    s_hidden = (s_silu * s_lift).astype(bf16)
    s_hidden_grad = dot(cot_rows, sd, ((1,), (1,)))
    s_grad = jnp.concatenate(
        [s_hidden_grad * s_lift * s_sig * (1.0 + s_in * (1.0 - s_sig)), s_hidden_grad * s_silu], axis=-1
    ).astype(bf16)
    grad_sgu = dot(mixed_line, s_grad, ((0,), (0,))).astype(bf16)
    grad_sd = dot(s_hidden, cot_rows, ((0,), (0,))).astype(bf16)
    out_part = (dot(s_hidden, sd, ((1,), (0,))) + expert_sum).astype(bf16)
    mixed_part = combine(slot_grad) + dot(s_grad, sgu, ((1,), (1,)))
    mixed_part = jnp.concatenate(
        [mixed_part.astype(bf16), pair_dot.astype(bf16), jnp.zeros((lines, MISC - TOP_K), bf16)], axis=1
    )
    mixed_sum = (sum_line_fast if fast else sum_line)(mixed_part).astype(f32)

    hot, probs = gates(mixed, pair_ids)
    gate_grads = mixed_sum[:, width : width + TOP_K]
    picked = probs * (gate_grads - jnp.sum(probs * gate_grads, axis=-1, keepdims=True))
    logit_grad = jnp.sum(hot * picked[..., None], axis=1)
    grad_router = jnp.dot(mixed.astype(f32).T, logit_grad, precision=highest)
    mixed_grad = mixed_sum[:, :width] + jnp.dot(logit_grad, router_w.astype(f32).T, precision=highest)
    cot_wide = cot.astype(f32)
    inner = mixed_grad * gain_ffn
    grad_gffn = jnp.sum(mixed_grad * ffn_norm, axis=0)
    attended_grad = cot_wide + ffn_scale * (inner - ffn_norm * jnp.mean(inner * ffn_norm, axis=-1, keepdims=True))
    out_grad = attended_grad.astype(bf16)
    grad_wout = dot(context, out_grad, ((1,), (0,)))
    context_grad = dot(w_out, out_grad, ((1,), (1,))).astype(bf16)
    context_grad = jnp.transpose(context_grad.reshape(width, batches, rows), (1, 0, 2))

    ffn_grads = (grad_egu, grad_sgu, grad_ed, grad_sd)
    if fast:
        rot_grad, (*lined, ed_sum, sd_sum), out_sum = backward_fast(prefix, context_grad, saved, *ffn_grads, out_part)
    else:
        rot_grad = attention_backward(context_grad, saved, batches, heads, prefix)
        egu_sum, sgu_sum, ed_sum, sd_sum = sum_weights(*ffn_grads)
        out_sum = sum_line(out_part)
    rot_grad = jnp.transpose(rot_grad, (0, 2, 1, 3)).reshape(3 * width, count).astype(f32)
    turned = rotate_t(rot_grad[: 2 * width], cosine, sine, -1.0)
    qkv_grad = jnp.concatenate([turned, rot_grad[2 * width :]], axis=0).astype(bf16)
    grad_wqkv = dot(normed, qkv_grad, ((0,), (1,)))
    normed_grad = dot(qkv_grad, w_qkv, ((0,), (1,)))
    grad_gattn = jnp.sum(normed_grad * attn_norm, axis=0)
    inner = normed_grad * gain_attn
    input_grad = (
        attended_grad + attn_scale * (inner - attn_norm * jnp.mean(inner * attn_norm, axis=-1, keepdims=True))
    ).astype(bf16)

    grad_misc = jnp.concatenate(
        [grad_router, grad_gattn[:, None], grad_gffn[:, None], jnp.zeros((width, MISC - experts - 2), f32)], axis=1
    )
    attn_parts = jnp.concatenate([grad_wqkv, grad_wout, grad_misc], axis=1).astype(bf16)
    if fast:
        attn_sums, egu_sum, sgu_sum = last_fast(attn_parts, *lined)
    else:
        attn_sums = sum_all(attn_parts)
    attn_sums = attn_sums.astype(f32)
    block_rows = (attended + out_sum.astype(f32)).astype(bf16)

    def joined(blocks):
        both = jnp.transpose(blocks.reshape(nz, -1, 2, slice_ff), (2, 1, 0, 3)).astype(f32)
        return both.reshape(2, -1, nz * slice_ff)

    egu_sum, sgu_sum = joined(egu_sum), joined(sgu_sum)
    return (
        block_rows.reshape(batches, 1, rows, width),
        input_grad.reshape(batches, 1, rows, width),
        attn_sums[:, 4 * width + experts],
        attn_sums[:, :width],
        attn_sums[:, width : 2 * width],
        attn_sums[:, 2 * width : 3 * width],
        attn_sums[:, 3 * width : 4 * width],
        attn_sums[:, 4 * width + experts + 1],
        attn_sums[:, 4 * width : 4 * width + experts],
        sgu_sum[0],
        sgu_sum[1],
        sd_sum.astype(f32),
        egu_sum[0][None],
        egu_sum[1][None],
        ed_sum.astype(f32)[None],
    )


def solution(mesh):
    n_dp, n_expert = mesh.shape["dp"], mesh.shape["expert"]
    nz = 4 if n_dp % 4 == 0 else 1
    grid = Mesh(mesh.devices.reshape(nz, n_dp // nz, n_expert // 2, 2), ALL)
    rows = P(None, EXPERT, DP, None)
    line = P(ALL)
    dense = P(ALL, None)
    expert = P(EXPERT, DP, None)
    return jax.shard_map(
        shards,
        mesh=grid,
        in_specs=(rows, rows, P(None, EXPERT), rows, line)
        + (dense,) * 4
        + (line,)
        + (dense,) * 4
        + (expert,) * 3,
        out_specs=(rows, rows, line) + (dense,) * 4 + (line,) + (dense,) * 4 + (expert,) * 3,
        check_vma=False,
    )
```

```python
import functools
import math

import jax
import jax.numpy as jnp
from jax import lax
from jax.experimental import pallas as pl
from jax.experimental.pallas import tpu as pltpu
from jax.sharding import Mesh
from jax.sharding import PartitionSpec as P

HEAD_DIM = 64
TOP_K = 2
MISC = 128

eps = 1e-06
highest = lax.Precision.HIGHEST
neg_fill = -1e30
f32 = jnp.float32
bf16 = jnp.bfloat16

ALL = ("z", "y", "x", "c")
PLANE = ("y", "x", "c")
DP = ("z", "y")
EXPERT = ("x", "c")


def rms_scale(values):
    return lax.rsqrt(jnp.mean(values * values, axis=-1, keepdims=True) + eps)


def silu_grad(values):
    sig = jax.nn.sigmoid(values)
    return sig * (1.0 + values * (1.0 - sig))


def dot(a, b, dims, batch=((), ())):
    return lax.dot_general(a, b, (dims, batch), preferred_element_type=f32)


def rotary_tables(positions):
    half = HEAD_DIM // 2
    frequency = jnp.exp(jnp.arange(half, dtype=f32) * (-math.log(10000.0) * 2.0 / HEAD_DIM))
    angles = frequency[:, None] * positions.astype(f32)[None, :]
    return jnp.cos(angles), jnp.sin(angles)


def rotate_t(values, cosine, sine, sign):
    rows = values.shape[-1]
    halves = values.reshape(-1, 2, HEAD_DIM // 2, rows)
    first, second = halves[:, 0], halves[:, 1]
    turned = jnp.stack([first * cosine - sign * second * sine, second * cosine + sign * first * sine], axis=1)
    return turned.reshape(values.shape)


def gather_all(shard):
    return lax.all_gather(shard, ALL, axis=0, tiled=True)


def gather_weights(egu, sgu, ed, sd):
    nz, ny, ne = lax.axis_size("z"), lax.axis_size("y"), lax.axis_size(EXPERT)

    def spread(blocks):
        mine = lax.all_to_all(blocks, "z", 0, 0, tiled=True)
        return lax.all_gather(mine, PLANE, axis=0).reshape(ny, ne, nz, *blocks.shape[1:])

    egu_all = jnp.transpose(spread(egu), (1, 2, 0, 3, 4)).reshape(ne, -1, egu.shape[-1])
    sgu_all = jnp.transpose(spread(sgu), (2, 0, 1, 3, 4)).reshape(-1, sgu.shape[-1])
    ed_all = lax.all_gather(ed, PLANE, axis=0).reshape(ny, ne, *ed.shape)
    ed_all = jnp.transpose(ed_all, (1, 0, 2, 3)).reshape(ne, -1, ed.shape[-1])
    sd_all = lax.all_gather(sd, PLANE, axis=0, tiled=True)
    return egu_all, sgu_all, ed_all, sd_all


def gather_line(rows):
    return lax.all_gather(rows, "z", axis=0, tiled=True)


def paired(batches, heads):
    n_dp = lax.axis_size(DP)
    here = batches * heads // n_dp
    even = here * n_dp == batches * heads and heads % max(1, here) == 0
    return even and tuple(lax.axis_size(name) for name in ALL) == (4, 2, 2, 2)


def sum_line(rows):
    return lax.psum_scatter(rows, "z", scatter_dimension=0, tiled=True)


def sum_weights(egu, sgu, ed, sd):
    nz, ny, ne = lax.axis_size("z"), lax.axis_size("y"), lax.axis_size(EXPERT)

    def collect(parts):
        mine = lax.psum_scatter(parts, PLANE, scatter_dimension=0, tiled=True)
        return lax.all_to_all(mine.reshape(nz, *mine.shape[1:]), "z", 0, 0, tiled=True)

    wide = egu.shape[-1]
    egu = jnp.transpose(egu.reshape(ne, nz, ny, -1, wide), (2, 0, 1, 3, 4))
    sgu = jnp.transpose(sgu.reshape(nz, ny, ne, -1, wide), (1, 2, 0, 3, 4))
    egu = collect(egu.reshape(ny * ne * nz, -1, wide))
    sgu = collect(sgu.reshape(ny * ne * nz, -1, wide))
    ed = jnp.transpose(ed.reshape(ne, ny, -1, ed.shape[-1]), (1, 0, 2, 3)).reshape(ny * ne, -1, ed.shape[-1])
    ed = lax.psum_scatter(ed, PLANE, scatter_dimension=0, tiled=True)[0]
    sd = lax.psum_scatter(sd, PLANE, scatter_dimension=0, tiled=True)
    return egu, sgu, ed, sd


def sum_all(parts):
    return lax.psum_scatter(parts, ALL, scatter_dimension=0, tiled=True)


def units_here(batches, heads):
    return -(-batches * heads // lax.axis_size(DP))


def to_units(tensor):
    kinds, batches, width, rows = tensor.shape
    n_dp = lax.axis_size(DP)
    heads = width // HEAD_DIM
    here = units_here(batches, heads)
    units = tensor.reshape(kinds, batches * heads, HEAD_DIM, rows)
    units = jnp.pad(units, ((0, 0), (0, here * n_dp - batches * heads), (0, 0), (0, 0)))
    units = jnp.transpose(units.reshape(kinds, n_dp, here, HEAD_DIM, rows), (1, 2, 0, 3, 4))
    units = lax.all_to_all(units, DP, 0, 0, tiled=True)
    return jnp.transpose(units, (1, 2, 3, 0, 4)).reshape(here, kinds, HEAD_DIM, n_dp * rows)


def from_units(units, batches, heads):
    here, kinds, _, length = units.shape
    n_dp = lax.axis_size(DP)
    rows = length // n_dp
    parts = jnp.transpose(units.reshape(here, kinds, HEAD_DIM, n_dp, rows), (3, 0, 1, 2, 4))
    parts = lax.all_to_all(parts, DP, 0, 0, tiled=True)
    parts = parts.reshape(n_dp * here, kinds, HEAD_DIM, rows)[: batches * heads]
    return jnp.transpose(parts, (1, 0, 2, 3)).reshape(kinds, batches, heads * HEAD_DIM, rows)


MESH = pl.DeviceIdType.MESH


def position():
    return tuple(lax.axis_index(name) for name in ALL)


def remote(src, dst, send, recv, device):
    return pltpu.make_async_remote_copy(
        src_ref=src, dst_ref=dst, send_sem=send, recv_sem=recv, device_id=device, device_id_type=MESH
    )


def greet(partners):
    barrier = pltpu.get_barrier_semaphore()
    for device in partners:
        pl.semaphore_signal(barrier, inc=1, device_id=device, device_id_type=MESH)
    pl.semaphore_wait(barrier, len(partners))


def any_specs(count):
    return [pl.BlockSpec(memory_space=pl.ANY)] * count


def params(collective_id, vmem=16 << 20):
    return pltpu.CompilerParams(collective_id=collective_id, has_side_effects=True, vmem_limit_bytes=vmem)


class PlaneItem:
    def __init__(self, here, index, place, own, x_first):
        self.here, self.index, self.place, self.own, self.x_first = here, index, place, own, x_first

    def moved(self, along_first, along_second, along_core):
        z, y, x, c = self.here
        move_x, move_y = (along_first, along_second) if self.x_first else (along_second, along_first)
        return (z, 1 - y if move_y else y, 1 - x if move_x else x, 1 - c if along_core else c)

    def ref(self, *moves):
        return self.place(*self.moved(*moves)[1:])

    COPIES = (
        ((0, 0, 0), (1, 0, 0)),
        ((0, 0, 0), (0, 1, 0)),
        ((1, 0, 0), (0, 1, 0)),
        ((0, 0, 0), (0, 0, 1)),
        ((1, 0, 0), (0, 0, 1)),
        ((0, 1, 0), (0, 0, 1)),
        ((1, 1, 0), (0, 0, 1)),
    )

    def copy(self, number, send, recv):
        source, to = self.COPIES[number]
        src = self.own if source == (0, 0, 0) else self.ref(*source)
        return remote(
            src, self.ref(*source), send.at[self.index, number], recv.at[self.index, number], self.moved(*to)
        )

    def arrival(self, number, send, recv):
        source, to = self.COPIES[number]
        ref = self.ref(*[a ^ b for a, b in zip(source, to)])
        return remote(ref, ref, send.at[self.index, number], recv.at[self.index, number], self.moved(*to))


def line_gather_steps(z, nz, own, out, sends, gets, neighbour, pieces):
    rows = out.shape[1] // pieces

    def copy(way, source, piece, src=None):
        part = pl.ds(piece * rows, rows)
        dst = out.at[source, part]
        src = dst if src is None else src.at[part]
        return remote(src, dst, sends.at[way, source, piece], gets.at[way, source, piece], neighbour(1 - 2 * way))

    def may_send(way):
        return z < nz - 1 if way == 0 else z > 0

    def start():
        for piece in range(pieces):
            for way in range(2):
                pl.when(may_send(way))(lambda: copy(way, z, piece, own).start())

    def step(distance, piece):
        for way in range(2):
            source = z - distance if way == 0 else z + distance

            @pl.when((source >= 0) & (source < nz))
            def _():
                copy(way, source, piece).wait_recv()
                pl.when(may_send(way))(lambda: copy(way, source, piece).start())

    def end():
        for distance in range(nz):
            for piece in range(pieces):
                for way in range(2):
                    source = z - distance if way == 0 else z + distance

                    @pl.when((source >= 0) & (source < nz) & may_send(way))
                    def _():
                        copy(way, source, piece).wait_send()

    steps = [functools.partial(step, distance, piece) for distance in range(1, nz) for piece in range(pieces)]
    return start, steps, end


def line_partners(here, nz):
    z, y, x, c = here
    return lambda way: (jnp.clip(z + way, 0, nz - 1), y, x, c)


def greet_line(here, nz):
    z = here[0]
    neighbour = line_partners(here, nz)
    barrier = pltpu.get_barrier_semaphore()

    @pl.when(z > 0)
    def _():
        pl.semaphore_signal(barrier, inc=1, device_id=neighbour(-1), device_id_type=MESH)

    @pl.when(z < nz - 1)
    def _():
        pl.semaphore_signal(barrier, inc=1, device_id=neighbour(1), device_id_type=MESH)

    pl.semaphore_wait(barrier, jnp.where(z > 0, 1, 0) + jnp.where(z < nz - 1, 1, 0))


LINE_PIECES = 2


def line_sum_steps(z, nz, parts, total, up, down, sends, gets, neighbour, pieces):
    rows = parts.shape[1] // pieces
    arrived = (up, down)

    def copy(way, target, piece, src):
        part = pl.ds(piece * rows, rows)
        dst = arrived[way].at[target, part]
        return remote(src, dst, sends.at[way, target, piece], gets.at[way, target, piece], neighbour(1 - 2 * way))

    def part_of(ref, target, piece):
        return ref.at[target, pl.ds(piece * rows, rows)]

    def step(distance, piece):
        for way in range(2):
            target = nz - distance if way == 0 else distance - 1
            ahead = z < target if way == 0 else z > target
            first = z == 0 if way == 0 else z == nz - 1
            mine, theirs = part_of(parts, target, piece), part_of(arrived[way], target, piece)

            @pl.when(ahead & first)
            def _():
                copy(way, target, piece, mine).start()

            @pl.when(ahead & jnp.logical_not(first))
            def _():
                copy(way, target, piece, theirs).wait_recv()
                mine[...] = (mine[...].astype(f32) + theirs[...].astype(f32)).astype(bf16)
                copy(way, target, piece, mine).start()

    def end():
        for piece in range(pieces):
            part = pl.ds(piece * rows, rows)
            total[part, :] = parts[z, part, :].astype(f32)
            for way in range(2):
                theirs = part_of(arrived[way], z, piece)

                @pl.when(z > 0 if way == 0 else z < nz - 1)
                def _():
                    copy(way, z, piece, theirs).wait_recv()
                    total[part, :] += theirs[...].astype(f32)

        for distance in range(1, nz):
            for piece in range(pieces):
                for way in range(2):
                    target = nz - distance if way == 0 else distance - 1

                    @pl.when(z < target if way == 0 else z > target)
                    def _():
                        copy(way, target, piece, part_of(parts, target, piece)).wait_send()

    steps = [functools.partial(step, distance, piece) for distance in range(1, nz) for piece in range(pieces)]
    return steps, end


class SumItem:
    def __init__(self, here, index, place, buffers, x_first):
        self.here, self.index, self.place, self.x_first = here, index, place, x_first
        self.own, self.sib, self.second, self.first = buffers

    moved = PlaneItem.moved

    def slot(self, a, b):
        return 2 * a + b

    def begin(self, load, send, recv):
        for a in range(2):
            for b in range(2):
                n = self.slot(a, b)
                self.sib_copy(a, b, send, recv).start()
                pltpu.make_async_copy(self.place(*self.moved(a, b, 0)[1:]), self.own.at[n], load.at[self.index, n]).start()

    def sib_copy(self, a, b, send, recv):
        n = self.slot(a, b)
        src = self.place(*self.moved(a, b, 1)[1:])
        return remote(src, self.sib.at[n], send.at[self.index, n], recv.at[self.index, n], self.moved(0, 0, 1))

    def second_copy(self, a, send, recv):
        n = 4 + a
        src = self.sib.at[self.slot(a, 1)]
        return remote(src, self.second.at[a], send.at[self.index, n], recv.at[self.index, n], self.moved(0, 1, 0))

    def first_copy(self, send, recv):
        src = self.second.at[1]
        return remote(src, self.first, send.at[self.index, 6], recv.at[self.index, 6], self.moved(1, 0, 0))

    def after_core(self, load, send, recv):
        for b in (1, 0):
            for a in range(2):
                n = self.slot(a, b)
                pltpu.make_async_copy(self.own.at[n], self.own.at[n], load.at[self.index, n]).wait()
                self.sib_copy(a, b, send, recv).wait_recv()
                add_to(self.sib.at[n], self.own.at[n])
                if b == 1:
                    self.second_copy(a, send, recv).start()

    def after_second(self, send, recv):
        for a in (1, 0):
            self.second_copy(a, send, recv).wait_recv()
            add_to(self.second.at[a], self.sib.at[self.slot(a, 0)])
            if a == 1:
                self.first_copy(send, recv).start()

    def after_first(self, send, recv):
        self.first_copy(send, recv).wait_recv()
        add_to(self.first, self.second.at[0])

    def end(self, send, recv):
        for a in range(2):
            for b in range(2):
                self.sib_copy(a, b, send, recv).wait_send()
            self.second_copy(a, send, recv).wait_send()
        self.first_copy(send, recv).wait_send()


def add_to(total, term):
    rows, columns = total.shape
    if rows % 16 == 0:

        @pl.loop(0, rows // 16)
        def _(i):
            part = pl.ds(pl.multiple_of(i * 16, 16), 16)
            total[part, :] = (total[part, :].astype(f32) + term[part, :].astype(f32)).astype(bf16)
    else:
        wide = max(w for w in (128, 256, 384, 512, 640) if columns % w == 0)

        @pl.loop(0, columns // wide)
        def _(i):
            part = pl.ds(pl.multiple_of(i * wide, 128), wide)
            total[:, part] = (total[:, part].astype(f32) + term[:, part].astype(f32)).astype(bf16)


SUM_LAG = 2


def unit_owner(number, batches, heads, here_units):
    per_batch = heads // here_units
    return number // per_batch, lax.rem(number, per_batch) * here_units


def exchange(me, n_dp, copy):
    ny = 2

    def device(number):
        return (number // ny, lax.rem(number, ny))

    far = [lax.rem(me + d, n_dp) for d in range(1, n_dp)]
    near = [lax.rem(me + n_dp - d, n_dp) for d in range(1, n_dp)]

    def start():
        for number in far:
            copy(number, me, device(number)).start()

    def arrive():
        for number in near:
            copy(me, number, device(number)).wait_recv()

    def end():
        for number in far:
            copy(number, me, device(number)).wait_send()

    return start, arrive, end


def tile_spans(length):
    tile = 256 if length % 512 == 0 else length // 2
    for start in range(0, length, tile):
        if start < length // 2:
            yield start, tile, 0, length // 2
        else:
            yield start, tile, start, start + tile


def masked(values, start, tile, mask_from, keys, length, fill):
    key = mask_from + lax.broadcasted_iota(jnp.int32, (keys - mask_from, tile), 0)
    query = start + lax.broadcasted_iota(jnp.int32, (keys - mask_from, tile), 1)
    allowed = (key <= query) | ((key < length) & (query < length))
    tail = jnp.where(allowed, values[mask_from:], fill)
    return tail if mask_from == 0 else jnp.concatenate([values[:mask_from], tail], axis=0)


def plane_items(here, arrays, outs):
    egu_in, sgu_in, ed_in, sd_in = arrays
    egu, sgu, ed, sd = outs
    half = ed_in.shape[0] // 2
    items = []

    def add(place, own, x_first):
        items.append(PlaneItem(here, len(items), place, own, x_first))

    for h in range(2):
        rows = pl.ds(h * half, half)
        add(lambda py, px, pc, rows=rows: ed.at[px * 2 + pc, py, rows], ed_in.at[rows], h == 1)
    for zs in range(egu_in.shape[0]):
        add(lambda py, px, pc, zs=zs: egu.at[px * 2 + pc, zs * 2 + py], egu_in.at[zs], zs % 2 == 1)
    for zs in range(sgu_in.shape[0]):
        add(lambda py, px, pc, zs=zs: sgu.at[((zs * 2 + py) * 2 + px) * 2 + pc], sgu_in.at[zs], zs % 2 == 1)
    add(lambda py, px, pc: sd.at[(py * 2 + px) * 2 + pc], sd_in, False)
    return items


def attend_kernel(nz, *refs):
    prefix, qkv, egu_in, sgu_in, ed_in, sd_in, cot_in = refs[:7]
    context, units, lse, egu, sgu, ed, sd, cot = refs[7:15]
    result, local, send, recv, csend, crecv, psend, precv, lsend, lrecv = refs[15:]
    here = position()
    z, y, x, c = here
    n_dp = nz * 2
    me = z * 2 + y
    kinds, batches, width, rows = qkv.shape
    heads = width // HEAD_DIM
    count = units.shape[1] // HEAD_DIM
    span = count * HEAD_DIM
    length = units.shape[2]
    greet(
        [(lax.rem(me + d, n_dp) // 2, lax.rem(me + d, 2), x, c) for d in range(1, n_dp)]
        + [(z, y, 1 - x, c), (z, y, x, 1 - c)]
    )

    def columns(number):
        return pl.ds(pl.multiple_of(number * rows, rows), rows)

    def qkv_block(number):
        batch, head = unit_owner(number, batches, heads, count)
        return qkv.at[:, batch, pl.ds(pl.multiple_of(head * HEAD_DIM, HEAD_DIM), span), :]

    def qkv_copy(number, source, device):
        return remote(
            qkv_block(number), units.at[:, :, columns(source)], send.at[number], recv.at[source], (*device, x, c)
        )

    start, arrive, end = exchange(me, n_dp, qkv_copy)
    start()
    keep = pltpu.make_async_copy(qkv_block(me), units.at[:, :, columns(me)], local.at[0])
    keep.start()
    items = plane_items(here, (egu_in, sgu_in, ed_in, sd_in), (egu, sgu, ed, sd))
    for item in items:
        for number in (0, 1, 3):
            item.copy(number, psend, precv).start()
    owns = [(cot_in, cot.at[z]), (ed_in, ed.at[x * 2 + c, y]), (sd_in, sd.at[(y * 2 + x) * 2 + c])]
    owns += [(egu_in.at[zs], egu.at[x * 2 + c, zs * 2 + y]) for zs in range(nz)]
    owns += [(sgu_in.at[zs], sgu.at[((zs * 2 + y) * 2 + x) * 2 + c]) for zs in range(nz)]
    keeps = [pltpu.make_async_copy(src, dst, local.at[1 + i]) for i, (src, dst) in enumerate(owns)]
    for copy in keeps:
        copy.start()

    def have_first(item):
        item.arrival(0, psend, precv).wait_recv()
        item.copy(2, psend, precv).start()
        item.copy(4, psend, precv).start()

    def have_second(item):
        item.arrival(1, psend, precv).wait_recv()
        item.copy(5, psend, precv).start()
        item.arrival(2, psend, precv).wait_recv()
        item.copy(6, psend, precv).start()

    early = len(items) // 2
    for item in items[:early]:
        have_first(item)
    arrive()
    keep.wait()
    line_start, line_steps, line_end = line_gather_steps(
        z, nz, cot_in, cot, lsend, lrecv, line_partners(here, nz), LINE_PIECES
    )
    line_start()

    my_batch, my_head = unit_owner(me, batches, heads, count)
    limit = prefix[my_batch, 0]

    def context_copy(head):
        def copy(number, source, device):
            _, first_head = unit_owner(source, batches, heads, count)
            batch, _ = unit_owner(source, batches, heads, count)
            part = pl.ds(pl.multiple_of((first_head + head) * HEAD_DIM, HEAD_DIM), HEAD_DIM)
            return remote(
                result.at[pl.ds(head * HEAD_DIM, HEAD_DIM), columns(number)],
                context.at[batch, part, :],
                csend.at[head, number],
                crecv.at[head, source],
                (*device, x, c),
            )

        return copy

    def attend(head):
        part = pl.ds(head * HEAD_DIM, HEAD_DIM)
        for first, tile, mask_from, keys in tile_spans(length):
            queries = units[0, part, pl.ds(first, tile)] * bf16(1.0 / math.sqrt(HEAD_DIM))
            scores = dot(units[1, part, pl.ds(0, keys)], queries, ((0,), (0,)))
            scores = masked(scores, first, tile, mask_from, keys, limit, neg_fill)
            top = jnp.max(scores, axis=0, keepdims=True)
            weights = jnp.exp(scores - top)
            total = jnp.sum(weights, axis=0, keepdims=True)
            lse[head, :, pl.ds(first, tile)] = top + jnp.log(total)
            mean = dot(units[2, part, pl.ds(0, keys)], weights.astype(bf16), ((1,), (0,))) / total
            result[part, pl.ds(first, tile)] = mean.astype(bf16)

    exchanges = [exchange(me, n_dp, context_copy(head)) for head in range(count)]
    own_part = [pl.ds(pl.multiple_of((my_head + head) * HEAD_DIM, HEAD_DIM), HEAD_DIM) for head in range(count)]
    own_copies = [
        pltpu.make_async_copy(
            result.at[pl.ds(head * HEAD_DIM, HEAD_DIM), columns(me)],
            context.at[my_batch, own_part[head], :],
            local.at[1 + len(owns) + head],
        )
        for head in range(count)
    ]
    later = [functools.partial(have_first, item) for item in items[early:]]
    later += [functools.partial(have_second, item) for item in items]
    line_steps = list(line_steps)
    for head in range(count):
        attend(head)
        exchanges[head][0]()
        own_copies[head].start()
        if head == 0:
            for step in later[: len(items) - early]:
                step()
            later = later[len(items) - early :]
            for step in line_steps[:LINE_PIECES]:
                step()
            line_steps = line_steps[LINE_PIECES:]
    share = -(-len(later) // max(1, len(line_steps)))
    while later or line_steps:
        for step in later[:share]:
            step()
        later = later[share:]
        if line_steps:
            line_steps.pop(0)()
    for item in items:
        for number in range(3, 7):
            item.arrival(number, psend, precv).wait_recv()
    for head in range(count):
        exchanges[head][1]()
        own_copies[head].wait()
    for item in items:
        for number in range(7):
            item.copy(number, psend, precv).wait_send()
    end()
    line_end()
    for head in range(count):
        exchanges[head][2]()
    for copy in keeps:
        copy.wait()


def attend_fast(prefix, qkv, egu, sgu, ed, sd, cot):
    nz = lax.axis_size("z")
    n_dp = nz * 2
    kinds, batches, width, rows = qkv.shape
    heads = width // HEAD_DIM
    count = batches * heads // n_dp
    length = n_dp * rows
    any_space, vmem = pl.BlockSpec(memory_space=pl.ANY), pl.BlockSpec(memory_space=pltpu.VMEM)
    shapes = [
        ((batches, width, rows), bf16),
        ((kinds, count * HEAD_DIM, length), bf16),
        ((count, 1, length), f32),
        ((4, nz * 2, *egu.shape[1:]), bf16),
        ((nz * 8, *sgu.shape[1:]), bf16),
        ((4, 2, *ed.shape), bf16),
        ((8, *sd.shape), bf16),
        ((nz, *cot.shape), bf16),
    ]
    dma = pltpu.SemaphoreType.DMA
    items = 2 * nz + 3
    line = dma((2, nz, LINE_PIECES))
    context, units, lse, egu, sgu, ed, sd, cot = pl.pallas_call(
        functools.partial(attend_kernel, nz),
        out_shape=[jax.ShapeDtypeStruct(*shape) for shape in shapes],
        in_specs=[pl.BlockSpec(memory_space=pltpu.SMEM)] + [any_space] * 6,
        out_specs=[any_space, vmem, vmem] + [any_space] * 5,
        scratch_shapes=[
            pltpu.VMEM((count * HEAD_DIM, length), bf16),
            dma((4 + 2 * nz + count,)),
            dma((n_dp,)),
            dma((n_dp,)),
            dma((count, n_dp)),
            dma((count, n_dp)),
            dma((items, 7)),
            dma((items, 7)),
            line,
            line,
        ],
        compiler_params=params(4, 40 << 20),
        name="attend",
    )(prefix, qkv, egu, sgu, ed, sd, cot)
    weights = (
        egu.reshape(4, -1, egu.shape[-1]),
        sgu.reshape(-1, sgu.shape[-1]),
        ed.reshape(4, -1, ed.shape[-1]),
        sd.reshape(-1, sd.shape[-1]),
    )
    return context, (units, lse), weights, cot.reshape(-1, cot.shape[-1])


def first_kernel(nz, *refs):
    attn_in, egu_in, sgu_in, attn, egu, sgu, local, zsend, zrecv, psend, precv = refs
    here = position()
    z, y, x, c = here
    line = [lax.rem(z + d, nz) for d in range(nz)]
    greet([(line[d], y, x, c) for d in range(1, nz)] + [(z, 1 - y, x, c), (z, y, 1 - x, c), (z, y, x, 1 - c)])

    def flat(zs, py, px, pc):
        return ((zs * 2 + py) * 2 + px) * 2 + pc

    def line_copy(kind, d, arriving=False):
        to, frm = line[d], line[(nz - d) % nz]
        at = frm if arriving else z
        dst = (attn.at[flat(at, y, x, c)], egu.at[at], sgu.at[at])[kind]
        src = dst if arriving else (attn_in, egu_in.at[to], sgu_in.at[to])[kind]
        return remote(src, dst, zsend.at[kind, d], zrecv.at[kind, d], (to, y, x, c))

    for d in (2, 1, 3) if nz == 4 else range(1, nz):
        line_copy(0, d).start()
    items = []
    for d in range(nz):
        frm = line[(nz - d) % nz]
        place = lambda py, px, pc, frm=frm: attn.at[flat(frm, py, px, pc)]
        items.append(PlaneItem(here, d, place, attn_in if d == 0 else place(y, x, c), d % 2 == 1))

    def have_own(item):
        for number in (0, 1, 3):
            item.copy(number, psend, precv).start()

    have_own(items[0])
    for kind in (1, 2):
        for d in range(1, nz):
            line_copy(kind, d).start()
    owns = [(attn_in, attn.at[flat(z, y, x, c)]), (egu_in.at[z], egu.at[z]), (sgu_in.at[z], sgu.at[z])]
    keeps = [pltpu.make_async_copy(src, dst, local.at[i]) for i, (src, dst) in enumerate(owns)]
    for copy in keeps:
        copy.start()
    for d in range(1, nz):
        line_copy(0, d, True).wait_recv()
        have_own(items[d])
    for item in items:
        item.arrival(0, psend, precv).wait_recv()
        item.copy(2, psend, precv).start()
        item.copy(4, psend, precv).start()
    for item in items:
        item.arrival(1, psend, precv).wait_recv()
        item.copy(5, psend, precv).start()
    for item in items:
        item.arrival(2, psend, precv).wait_recv()
        item.copy(6, psend, precv).start()
    for item in items:
        for number in range(3, 7):
            item.arrival(number, psend, precv).wait_recv()
    for kind in (1, 2):
        for d in range(1, nz):
            line_copy(kind, d, True).wait_recv()
    for item in items:
        for number in range(7):
            item.copy(number, psend, precv).wait_send()
    for kind in range(3):
        for d in range(1, nz):
            line_copy(kind, d).wait_send()
    for copy in keeps:
        copy.wait()


def first_fast(attn, egu, sgu):
    nz = lax.axis_size("z")
    dma = pltpu.SemaphoreType.DMA
    shapes = [(nz * 8, *attn.shape), egu.shape, sgu.shape]
    attn, egu, sgu = pl.pallas_call(
        functools.partial(first_kernel, nz),
        out_shape=[jax.ShapeDtypeStruct(shape, bf16) for shape in shapes],
        in_specs=any_specs(3),
        out_specs=any_specs(3),
        scratch_shapes=[dma((3,)), dma((3, nz)), dma((3, nz)), dma((nz, 7)), dma((nz, 7))],
        compiler_params=params(0),
        name="first",
    )(attn, egu, sgu)
    return attn.reshape(-1, attn.shape[-1]), egu, sgu


def backward_kernel(nz, kinds, *refs):
    refs = list(refs)
    take = lambda n: [refs.pop(0) for _ in range(n)]
    prefix, grad_in, units, lse = take(4)
    inputs = dict(zip(kinds, take(len(kinds))))
    (rows_in,) = take(1)
    (grads,) = take(1)
    outputs = dict(zip(kinds, take(len(kinds))))
    (rows_total,) = take(1)
    grad, dkey, dvalue, result = take(4)
    buffers = {kind: take(4) for kind in kinds}
    local, send, recv, csend, crecv, load, psend, precv, store = take(9)
    rows_parts, up, down, lload, lsend, lrecv = take(6)
    here = position()
    z, y, x, c = here
    n_dp = nz * 2
    me = z * 2 + y
    batches, width, rows = grad_in.shape
    heads = width // HEAD_DIM
    span, length = grad.shape
    count = span // HEAD_DIM
    row_load = pltpu.make_async_copy(rows_in, rows_parts, lload)
    row_load.start()
    greet(
        [(lax.rem(me + d, n_dp) // 2, lax.rem(me + d, 2), x, c) for d in range(1, n_dp)]
        + [(z, y, 1 - x, c), (z, y, x, 1 - c)]
    )

    def columns(number):
        return pl.ds(pl.multiple_of(number * rows, rows), rows)

    def grad_block(number):
        batch, head = unit_owner(number, batches, heads, count)
        return grad_in.at[batch, pl.ds(pl.multiple_of(head * HEAD_DIM, HEAD_DIM), span), :]

    def grad_copy(number, source, device):
        return remote(
            grad_block(number), grad.at[:, columns(source)], send.at[number], recv.at[source], (*device, x, c)
        )

    start, arrive, end = exchange(me, n_dp, grad_copy)
    start()
    keep = pltpu.make_async_copy(grad_block(me), grad.at[:, columns(me)], local.at[0])
    keep.start()

    half = inputs["ed"].shape[2] // 2
    places = {
        "egu": lambda zs: lambda py, px, pc: inputs["egu"].at[px * 2 + pc, zs * 2 + py],
        "sgu": lambda zs: lambda py, px, pc: inputs["sgu"].at[((zs * 2 + py) * 2 + px) * 2 + pc],
        "ed": lambda h: lambda py, px, pc: inputs["ed"].at[px * 2 + pc, py, pl.ds(h * half, half)],
        "sd": lambda h: lambda py, px, pc: inputs["sd"].at[(py * 2 + px) * 2 + pc],
    }
    targets = {
        "egu": lambda k: outputs["egu"].at[k],
        "sgu": lambda k: outputs["sgu"].at[k],
        "ed": lambda k: outputs["ed"].at[pl.ds(k * half, half)],
        "sd": lambda k: outputs["sd"],
    }
    number_of = {"egu": nz, "sgu": nz, "ed": 2, "sd": 1}
    items, finals = [], []
    for kind in kinds:
        for k in range(number_of[kind]):
            parts = tuple(buffer.at[k] for buffer in buffers[kind])
            item = SumItem(here, len(items), places[kind](k), parts, k % 2 == 1)
            finals.append(pltpu.make_async_copy(item.first, targets[kind](k), store.at[item.index]))
            items.append(item)
    for item in items:
        item.begin(load, psend, precv)
    row_load.wait()
    row_steps, row_end = line_sum_steps(
        z, nz, rows_parts, rows_total, up, down, lsend, lrecv, line_partners(here, nz), LINE_PIECES
    )

    def stage(t):
        if t < len(items):
            items[t].after_core(load, psend, precv)
        if 0 <= t - SUM_LAG < len(items):
            items[t - SUM_LAG].after_second(psend, precv)
        if 0 <= t - 2 * SUM_LAG < len(items):
            items[t - 2 * SUM_LAG].after_first(psend, precv)
            finals[t - 2 * SUM_LAG].start()

    steps = [functools.partial(stage, t) for t in range(len(items) + 2 * SUM_LAG)]
    for step in steps[:2]:
        step()
    steps = steps[2:]
    arrive()
    keep.wait()

    my_batch, my_head = unit_owner(me, batches, heads, count)
    limit = prefix[my_batch, 0]
    inv = 1.0 / math.sqrt(HEAD_DIM)

    def head_rows(source, head):
        _, first_head = unit_owner(source, batches, heads, count)
        return pl.ds(pl.multiple_of((first_head + head) * HEAD_DIM, HEAD_DIM), HEAD_DIM)

    def grads_copy(head):
        def copy(number, source, device):
            batch, _ = unit_owner(source, batches, heads, count)
            return remote(
                result.at[:, pl.ds(head * HEAD_DIM, HEAD_DIM), columns(number)],
                grads.at[:, batch, head_rows(source, head), :],
                csend.at[head, number],
                crecv.at[head, source],
                (*device, x, c),
            )

        return copy

    def attend(head):
        part = pl.ds(head * HEAD_DIM, HEAD_DIM)
        dkey[...] = jnp.zeros_like(dkey)
        dvalue[...] = jnp.zeros_like(dvalue)
        for first, tile, mask_from, keys in tile_spans(length):
            here_q, upto = pl.ds(first, tile), pl.ds(0, keys)
            queries = units[0, part, here_q] * bf16(inv)
            key, value, out_grad = units[1, part, upto], units[2, part, upto], grad[part, here_q]
            scores = dot(key, queries, ((0,), (0,)))
            probs = jnp.exp(scores - lse[head, :, here_q])
            probs = masked(probs, first, tile, mask_from, keys, limit, 0.0)
            prob_grad = dot(value, out_grad, ((0,), (0,)))
            delta = jnp.sum(probs * prob_grad, axis=0, keepdims=True)
            score_grad = (probs * (prob_grad - delta)).astype(bf16)
            result[0, part, here_q] = (dot(key, score_grad, ((1,), (0,))) * inv).astype(bf16)
            dkey[:, upto] += dot(queries, score_grad, ((1,), (1,)))
            dvalue[:, upto] += dot(out_grad, probs.astype(bf16), ((1,), (1,)))
        result[1, part, :] = dkey[...].astype(bf16)
        result[2, part, :] = dvalue[...].astype(bf16)

    exchanges = [exchange(me, n_dp, grads_copy(head)) for head in range(count)]
    own_copies = [
        pltpu.make_async_copy(
            result.at[:, pl.ds(head * HEAD_DIM, HEAD_DIM), columns(me)],
            grads.at[:, my_batch, head_rows(me, head), :],
            local.at[1 + head],
        )
        for head in range(count)
    ]
    for head in range(count):
        attend(head)
        exchanges[head][0]()
        own_copies[head].start()
        for step in steps[:3]:
            step()
        steps = steps[3:]
        for step in row_steps[:LINE_PIECES]:
            step()
        row_steps = row_steps[LINE_PIECES:]
    for step in steps + row_steps:
        step()
    row_end()
    for head in range(count):
        exchanges[head][1]()
        own_copies[head].wait()
    for item in items:
        item.end(psend, precv)
    for final in finals:
        final.wait()
    end()
    for head in range(count):
        exchanges[head][2]()


def backward_fast(prefix, grad, saved, egu, sgu, ed, sd, rows):
    nz = lax.axis_size("z")
    n_dp = nz * 2
    units, lse = saved
    batches, width, count_rows = grad.shape
    span, length = units.shape[1:]
    count = span // HEAD_DIM
    wide = egu.shape[-1]
    arrays = {
        "ed": ed.reshape(4, 2, -1, ed.shape[-1]),
        "egu": egu.reshape(4, nz * 2, -1, wide),
        "sgu": sgu.reshape(nz * 8, -1, wide),
        "sd": sd.reshape(8, -1, sd.shape[-1]),
    }
    kinds = tuple(arrays)
    rows = rows.reshape(nz, -1, rows.shape[-1])
    any_space, vmem = pl.BlockSpec(memory_space=pl.ANY), pl.BlockSpec(memory_space=pltpu.VMEM)
    block = {kind: arrays[kind].shape[-2:] for kind in kinds}
    number_of = {"egu": nz, "sgu": nz, "ed": 2, "sd": 1}
    wholes = {"ed": block["ed"], "sd": block["sd"], "egu": (nz, *block["egu"]), "sgu": (nz, *block["sgu"])}
    block["ed"] = (block["ed"][0] // 2, block["ed"][1])
    results = [((3, batches, width, count_rows), bf16)] + [(wholes[kind], bf16) for kind in kinds]
    results += [(rows.shape[1:], f32)]
    scratch = [
        pltpu.VMEM((span, length), bf16),
        pltpu.VMEM((HEAD_DIM, length), f32),
        pltpu.VMEM((HEAD_DIM, length), f32),
        pltpu.VMEM((3, span, length), bf16),
    ]
    items = sum(number_of.values())
    for kind in kinds:
        n = number_of[kind]
        scratch += [pltpu.VMEM((n, 4, *block[kind]), bf16), pltpu.VMEM((n, 4, *block[kind]), bf16)]
        scratch += [pltpu.VMEM((n, 2, *block[kind]), bf16), pltpu.VMEM((n, *block[kind]), bf16)]
    dma = pltpu.SemaphoreType.DMA
    scratch += [dma((1 + count,)), dma((n_dp,)), dma((n_dp,)), dma((count, n_dp)), dma((count, n_dp))]
    scratch += [dma((items, 4)), dma((items, 7)), dma((items, 7)), dma((items,))]
    line = dma((2, nz, LINE_PIECES))
    scratch += [pltpu.VMEM(rows.shape, bf16)] * 3 + [dma, line, line]
    outs = pl.pallas_call(
        functools.partial(backward_kernel, nz, kinds),
        out_shape=[jax.ShapeDtypeStruct(*result) for result in results],
        in_specs=[pl.BlockSpec(memory_space=pltpu.SMEM), any_space, vmem, vmem] + [any_space] * 5,
        out_specs=[any_space] * 5 + [vmem],
        scratch_shapes=scratch,
        compiler_params=params(5, 56 << 20),
        name="attend_backward",
    )(prefix, grad, units, lse, *arrays.values(), rows)
    grads, ed, egu, sgu, sd, total = outs
    return grads, (egu, sgu, ed, sd), total


def last_kernel(nz, *refs):
    attn_in, egu_in, sgu_in, attn, egu, sgu, own, sib, second, first, zbuf = refs[:11]
    local, load, zsend, zrecv, psend, precv, store = refs[11:]
    here = position()
    z, y, x, c = here
    line = [lax.rem(z + d, nz) for d in range(nz)]
    greet([(line[d], y, x, c) for d in range(1, nz)] + [(z, 1 - y, x, c), (z, y, 1 - x, c), (z, y, x, 1 - c)])
    items = []
    for d in (3, 2, 1, 0) if nz == 4 else range(nz - 1, -1, -1):
        place = lambda py, px, pc, zs=line[d]: attn_in.at[((zs * 2 + py) * 2 + px) * 2 + pc]
        items.append((d, SumItem(here, d, place, (own.at[d], sib.at[d], second.at[d], first.at[d]), d % 2 == 1)))
    for _, item in items:
        item.begin(load, psend, precv)

    def line_copy(kind, d, arriving=False):
        to, frm = line[d], line[(nz - d) % nz]
        at = frm if arriving else z
        dst = (zbuf, egu, sgu)[kind].at[at]
        src = dst if arriving else (first.at[d], egu_in.at[to], sgu_in.at[to])[kind]
        return remote(src, dst, zsend.at[kind, d], zrecv.at[kind, d], (to, y, x, c))

    for kind in (1, 2):
        for d in range(1, nz):
            line_copy(kind, d).start()
    keeps = [pltpu.make_async_copy(src.at[z], dst.at[z], local.at[i]) for i, (src, dst) in enumerate(((egu_in, egu), (sgu_in, sgu)))]
    for copy in keeps:
        copy.start()
    mine = pltpu.make_async_copy(first.at[0], zbuf.at[z], store)
    for _, item in items:
        item.after_core(load, psend, precv)
    for _, item in items:
        item.after_second(psend, precv)
    for d, item in items:
        item.after_first(psend, precv)
        if d == 0:
            mine.start()
        else:
            line_copy(0, d).start()
    mine.wait()
    for kind in range(3):
        for d in range(1, nz):
            line_copy(kind, d, True).wait_recv()
    columns = attn.shape[1] // 5

    @pl.loop(0, 5)
    def _(i):
        part = pl.ds(pl.multiple_of(i * columns, 128), columns)
        attn[:, part] = sum(zbuf[k, :, part].astype(f32) for k in range(nz))

    for _, item in items:
        item.end(psend, precv)
    for kind in range(3):
        for d in range(1, nz):
            line_copy(kind, d).wait_send()
    for copy in keeps:
        copy.wait()


def last_fast(attn, egu, sgu):
    nz = lax.axis_size("z")
    dma = pltpu.SemaphoreType.DMA
    attn = attn.reshape(nz * 8, -1, attn.shape[-1])
    block = attn.shape[1:]
    any_space = pl.BlockSpec(memory_space=pl.ANY)
    return pl.pallas_call(
        functools.partial(last_kernel, nz),
        out_shape=[
            jax.ShapeDtypeStruct(block, f32),
            jax.ShapeDtypeStruct(egu.shape, bf16),
            jax.ShapeDtypeStruct(sgu.shape, bf16),
        ],
        in_specs=any_specs(3),
        out_specs=[pl.BlockSpec(memory_space=pltpu.VMEM), any_space, any_space],
        scratch_shapes=[
            pltpu.VMEM((nz, 4, *block), bf16),
            pltpu.VMEM((nz, 4, *block), bf16),
            pltpu.VMEM((nz, 2, *block), bf16),
            pltpu.VMEM((nz, *block), bf16),
            pltpu.VMEM((nz, *block), bf16),
            dma((2,)),
            dma((nz, 4)),
            dma((3, nz)),
            dma((3, nz)),
            dma((nz, 7)),
            dma((nz, 7)),
            dma,
        ],
        compiler_params=params(3, 32 << 20),
        name="last",
    )(attn, egu, sgu)


ORDER = ((0, 1, 2, 3), (1, 0, 2, 3), (2, 3, 1, 0), (3, 2, 1, 0))
EXTRA = 16


def by_distance(z, index):
    code = jnp.int32(0)
    for plane, order in enumerate(ORDER):
        code = jnp.where(z == plane, sum(p * 4**i for i, p in enumerate(order)), code)
    for _ in range(3):
        code = jnp.where(index > 0, code // 4, code)
        index = index - 1
    return lax.rem(code, 4)


def ffn_kernel(capacity, *refs):
    refs = list(refs)
    take = lambda n: [refs.pop(0) for _ in range(n)]
    mixed_in, cot_in, router_in, *weights_in = take(7)
    out_part, total, *grads = take(6)
    weights = take(4)
    egu, sgu, ed, sd = weights
    mixed, cot, router, arrived, pair_grad, expert_hidden, act_grad, s_hidden, s_grad = take(9)
    slot_out, slot_grad, hots, gate_dot, outs, parts, up, down, wide_stage, deep_stage = take(10)
    local, loads, gsend, grecv, ssend, srecv, stores = take(7)
    here = position()
    z, y, x, c = here
    nz = 4
    neighbour = line_partners(here, nz)
    experts = egu.shape[0]
    rows, width = mixed_in.shape
    group = 128
    groups = rows // group
    slots = groups * capacity
    ff = ed.shape[1]

    loading = [pltpu.make_async_copy(router_in, router, local.at[0])]
    loading += [pltpu.make_async_copy(mixed_in, mixed.at[z], local.at[1])]
    loading += [pltpu.make_async_copy(cot_in, cot, local.at[2])]
    shared_loads = [
        pltpu.make_async_copy(weights_in[1], sgu, local.at[3]),
        pltpu.make_async_copy(weights_in[3], sd, local.at[4]),
    ]
    for copy in loading:
        copy.start()

    def expert_loads(e):
        return [
            pltpu.make_async_copy(weights_in[0].at[e], egu.at[e], loads.at[0, e]),
            pltpu.make_async_copy(weights_in[2].at[e], ed.at[e], loads.at[1, e]),
        ]

    for e in range(experts):
        for copy in expert_loads(e):
            copy.start()
    for copy in shared_loads:
        copy.start()
    greet_line(here, nz)

    def may_send(way):
        return z < nz - 1 if way == 0 else z > 0

    def chunk_copy(way, source, src=None):
        dst = mixed.at[source]
        return remote(dst if src is None else src, dst, gsend.at[way, source], grecv.at[way, source], neighbour(1 - 2 * way))

    for way in range(2):
        pl.when(may_send(way))(lambda: chunk_copy(way, z, mixed_in).start())

    def receive(source):
        for way in range(2):

            @pl.when(source < z if way == 0 else source > z)
            def _():
                chunk_copy(way, source).wait_recv()
                pl.when(may_send(way))(lambda: chunk_copy(way, source).start())

    piece_rows = (pl.ds(0, group), pl.ds(group, parts.shape[1] - group))
    came = (up, down)

    def part_copy(way, target, piece):
        part = piece_rows[piece]
        return remote(
            parts.at[target, part],
            came[way].at[target, part],
            ssend.at[way, target, piece],
            srecv.at[way, target, piece],
            neighbour(1 - 2 * way),
        )

    def relay(target, piece):
        part = piece_rows[piece]
        for way in range(2):
            ahead = z < target if way == 0 else z > target
            inner = z > 0 if way == 0 else z < nz - 1

            @pl.when(ahead & inner)
            def _():
                part_copy(way, target, piece).wait_recv()
                mine, theirs = parts.at[target, part], came[way].at[target, part]
                mine[...] = (mine[...].astype(f32) + theirs[...].astype(f32)).astype(bf16)

            pl.when(ahead)(lambda: part_copy(way, target, piece).start())

    for copy in loading:
        copy.wait()

    sub = lax.broadcasted_iota(jnp.int32, (8, group), 0).astype(f32)
    before = lax.broadcasted_iota(jnp.int32, (group, group), 0) < lax.broadcasted_iota(jnp.int32, (group, group), 1)
    before = jnp.where(before, 1.0, 0.0).astype(bf16)
    slot_iota = lax.broadcasted_iota(jnp.int32, (capacity, group), 0).astype(f32)

    def chunk(index, source):
        tokens = mixed.at[source]
        named, ranks, probs = [], [], []
        for g in range(groups):
            lanes = pl.ds(g * group, group)
            ids = cot[source, pl.ds(rows, EXTRA), lanes].astype(f32)
            hot = jnp.where((sub == ids[0:1]) | (sub == ids[1:2]), 1.0, 0.0)
            logits = dot(router[...], mixed[source, lanes, :], ((1,), (1,)))[:8]
            top = jnp.max(jnp.where(hot > 0, logits, neg_fill), axis=0, keepdims=True)
            powers = jnp.where(hot > 0, jnp.exp(logits - top), 0.0)
            probs.append(powers / jnp.sum(powers, axis=0, keepdims=True))
            rank = dot(jnp.concatenate([hot, hot], axis=0).astype(bf16), before, ((1,), (0,)))[:8]
            ranks.append(jnp.where(hot > 0, rank, float(group * TOP_K)))
        gate_dot[...] = jnp.zeros_like(gate_dot)

        def row_of(table, e):
            return jnp.sum(jnp.where(sub == e.astype(f32), table, 0.0), axis=0, keepdims=True)

        @pl.loop(0, experts)
        def _(e):
            @pl.when(index == 0)
            def _():
                for copy in expert_loads(e):
                    copy.wait()

            here_slots = pl.ds(pl.multiple_of(source * slots, 16), slots)
            hot_of, prob_of, cot_of = [], [], []
            for g in range(groups):
                lanes = pl.ds(g * group, group)
                hot = jnp.where(slot_iota == row_of(ranks[g], e), 1.0, 0.0)
                prob_of.append(jnp.sum(hot * row_of(probs[g], e), axis=1, keepdims=True))
                low_hot = hot.astype(bf16)
                hots[g, pl.ds(pl.multiple_of(e * capacity, 16), capacity), :] = low_hot
                hot_of.append(hot)
                mine = pl.ds(pl.multiple_of(source * slots + g * capacity, 16), capacity)
                arrived[e, mine, :] = dot(low_hot, mixed[source, lanes, :], ((1,), (0,))).astype(bf16)
                picked = dot(low_hot, cot[source, lanes, :], ((1,), (0,)))
                cot_of.append(picked)
                pair_grad[e, mine, :] = (picked * prob_of[g]).astype(bf16)
            act = dot(arrived[e, here_slots, :], egu[e], ((1,), (0,)))
            hidden_grad = dot(pair_grad[e, here_slots, :], ed[e], ((1,), (1,)))
            gate_act, up_act = act[:, :ff], act[:, ff:]
            sig = jax.nn.sigmoid(gate_act)
            silu = gate_act * sig
            hidden = (silu * up_act).astype(bf16)
            expert_hidden[e, here_slots, :] = hidden
            gate_grad = (hidden_grad * up_act * (sig * (1.0 + gate_act * (1.0 - sig)))).astype(bf16)
            up_grad = (hidden_grad * silu).astype(bf16)
            act_grad[e, here_slots, pl.ds(0, ff)] = gate_grad
            act_grad[e, here_slots, pl.ds(ff, ff)] = up_grad
            out = dot(hidden, ed[e], ((1,), (0,)))
            back = dot(act_grad[e, here_slots, :], egu[e], ((1,), (1,)))
            for g in range(groups):
                mine, stack = slice(g * capacity, (g + 1) * capacity), pl.ds(pl.multiple_of(e * capacity, 16), capacity)
                lanes = pl.ds(g * group, group)
                slot_out[g, stack, :] = (out[mine] * prob_of[g]).astype(bf16)
                slot_grad[g, stack, :] = back[mine].astype(bf16)
                dots = jnp.sum(out[mine] * cot_of[g], axis=1, keepdims=True)
                dots = jnp.sum(hot_of[g] * dots, axis=0, keepdims=True)
                gate_dot[:, lanes] += jnp.where(sub == e.astype(f32), dots, 0.0)

        @pl.when(index == 0)
        def _():
            for copy in shared_loads:
                copy.wait()

        act = dot(tokens[...], sgu[...], ((1,), (0,)))
        hidden_grad = dot(cot[source, pl.ds(0, rows), :], sd[...], ((1,), (1,)))
        gate_act, up_act = act[:, :ff], act[:, ff:]
        sig = jax.nn.sigmoid(gate_act)
        silu = gate_act * sig
        hidden = (silu * up_act).astype(bf16)
        mine = pl.ds(pl.multiple_of(source * rows, 16), rows)
        s_hidden[mine, :] = hidden
        s_grad[mine, pl.ds(0, ff)] = (hidden_grad * up_act * (sig * (1.0 + gate_act * (1.0 - sig)))).astype(bf16)
        s_grad[mine, pl.ds(ff, ff)] = (hidden_grad * silu).astype(bf16)
        out = dot(hidden, sd[...], ((1,), (0,)))
        back = dot(s_grad[mine, :], sgu[...], ((1,), (1,)))
        for g in range(groups):
            lanes = pl.ds(g * group, group)
            span = slice(g * group, (g + 1) * group)
            outs[source, lanes, :] = (out[span] + dot(hots[g], slot_out[g], ((0,), (0,)))).astype(bf16)
            parts[source, lanes, :] = (back[span] + dot(hots[g], slot_grad[g], ((0,), (0,)))).astype(bf16)
        dots = jnp.concatenate([gate_dot[...], jnp.zeros((EXTRA - 8, rows), f32)], axis=0)
        parts[source, pl.ds(rows, EXTRA), :] = jnp.concatenate(
            [dots, jnp.zeros((EXTRA, width - rows), f32)], axis=1
        ).astype(bf16)

    inner = (z > 0) & (z < nz - 1)

    @pl.loop(0, nz)
    def _(index):
        source = by_distance(z, index)
        pl.when((index == 1) | (index == 3) | ((index == 2) & jnp.logical_not(inner)))(lambda: receive(source))
        pl.when((index == 1) & inner)(lambda: receive(by_distance(z, jnp.int32(2))))
        chunk(index, source)

        @pl.when(jnp.logical_not(inner) & (index > 0))
        def _():
            for piece in range(2):
                relay(source, piece)

        @pl.when(inner & (index == 3))
        def _():
            for piece in range(2):
                relay(by_distance(z, jnp.int32(2)), piece)

    out_copy = pltpu.make_async_copy(outs, out_part, local.at[5])
    out_copy.start()
    far, near = by_distance(z, jnp.int32(3)), by_distance(z, jnp.int32(1))

    def stage_copies(e, slot):
        return [
            pltpu.make_async_copy(wide_stage.at[slot], grads[0].at[e], stores.at[0, slot]),
            pltpu.make_async_copy(deep_stage.at[slot], grads[2].at[e], stores.at[1, slot]),
        ]

    def weight_grads(slot, rows_in, wide, hidden, deep):
        for k in range(0, wide.shape[1], 512):
            span = pl.ds(k, 512)
            wide_stage[slot, :, span] = dot(rows_in[...], wide[:, span], ((0,), (0,))).astype(bf16)
        deep_stage[slot] = dot(hidden[...], deep[...], ((0,), (0,))).astype(bf16)

    @pl.loop(0, experts)
    def _(e):
        slot = lax.rem(e, 2)

        @pl.when(e >= 2)
        def _():
            for copy in stage_copies(e - 2, slot):
                copy.wait()

        weight_grads(slot, arrived.at[e], act_grad.at[e], expert_hidden.at[e], pair_grad.at[e])
        for copy in stage_copies(e, slot):
            copy.start()
        pl.when(inner & (e == 1))(lambda: relay(far, 0))
        pl.when(inner & (e == 2))(lambda: relay(far, 1))
        pl.when(inner & (e == 3))(lambda: relay(near, 0))

    for copy in stage_copies(experts - 2, 0):
        copy.wait()
    tokens = mixed.reshape(nz * rows, width)
    for k in range(0, 2 * ff, 512):
        span = pl.ds(k, 512)
        wide_stage[0, :, span] = dot(tokens[...], s_grad[:, span], ((0,), (0,))).astype(bf16)
    cots = jnp.concatenate([cot[k, pl.ds(0, rows), :] for k in range(nz)], axis=0)
    deep_stage[0] = dot(s_hidden[...], cots, ((0,), (0,))).astype(bf16)
    shared_stores = [
        pltpu.make_async_copy(wide_stage.at[0], grads[1], stores.at[0, 0]),
        pltpu.make_async_copy(deep_stage.at[0], grads[3], stores.at[1, 0]),
    ]
    for copy in shared_stores:
        copy.start()
    pl.when(inner)(lambda: relay(near, 1))
    total[...] = parts[z].astype(f32)
    for way in range(2):

        @pl.when(z > 0 if way == 0 else z < nz - 1)
        def _():
            for piece in range(2):
                part_copy(way, z, piece).wait_recv()
            total[...] += came[way][z].astype(f32)

    for copy in stage_copies(experts - 1, 1) + shared_stores + [out_copy]:
        copy.wait()
    for way in range(2):
        for plane in range(nz):
            sent = (plane <= z if way == 0 else plane >= z) & may_send(way)
            pl.when(sent)(lambda: chunk_copy(way, plane).wait_send())

            @pl.when(z < plane if way == 0 else z > plane)
            def _():
                for piece in range(2):
                    part_copy(way, plane, piece).wait_send()


def ffn_fast(mixed, cot, router, weights, capacity):
    nz = lax.axis_size("z")
    egu, sgu, ed, sd = weights
    rows, width = mixed.shape
    experts, ff = ed.shape[:2]
    cot = cot.reshape(nz, -1, width)
    slots = nz * rows // 128 * capacity
    groups = rows // 128
    vmem, dma = pltpu.VMEM, pltpu.SemaphoreType.DMA
    low = lambda *shape: vmem(shape, bf16)
    scratch = [low(*w.shape) for w in weights]
    scratch += [low(nz, rows, width), low(*cot.shape), low(*router.shape)]
    scratch += [low(experts, slots, width), low(experts, slots, width)]
    scratch += [low(experts, slots, ff), low(experts, slots, 2 * ff), low(nz * rows, ff), low(nz * rows, 2 * ff)]
    stack = experts * capacity
    scratch += [low(groups, stack, width), low(groups, stack, width), low(groups, stack, 128), vmem((8, rows), f32)]
    scratch += [low(nz, rows, width)] + [low(*cot.shape)] * 3
    scratch += [low(2, width, 2 * ff), low(2, ff, width)]
    scratch += [dma((6,)), dma((2, experts)), dma((2, nz)), dma((2, nz)), dma((2, nz, 2)), dma((2, nz, 2)), dma((2, 2))]
    any_space = pl.BlockSpec(memory_space=pl.ANY)
    out_part, total, *grads = pl.pallas_call(
        functools.partial(ffn_kernel, capacity),
        out_shape=[
            jax.ShapeDtypeStruct((nz, rows, width), bf16),
            jax.ShapeDtypeStruct((rows + EXTRA, width), f32),
        ]
        + [jax.ShapeDtypeStruct(w.shape, bf16) for w in weights],
        in_specs=any_specs(7),
        out_specs=[any_space, pl.BlockSpec(memory_space=pltpu.VMEM)] + [any_space] * 4,
        scratch_shapes=scratch,
        compiler_params=params(1, 60 << 20),
        name="feed_forward",
    )(mixed, cot, router, *weights)
    return out_part, total, grads


def visible_units(prefix, heads, here, length):
    unit = lax.axis_index(DP) * here + jnp.arange(here)
    lengths = prefix[jnp.minimum(unit // heads, prefix.shape[0] - 1), 0]
    pos = jnp.arange(length, dtype=jnp.int32)
    low = pos[None, :] < lengths[:, None]
    return (pos[None, None, :] <= pos[None, :, None]) | (low[:, :, None] & low[:, None, :])


def attention_forward(qkv, batches, heads, prefix):
    units = to_units(qkv)
    q, k, v = units[:, 0], units[:, 1], units[:, 2]
    allowed = visible_units(prefix, heads, q.shape[0], q.shape[-1])
    scores = dot(q, k, ((1,), (1,)), ((0,), (0,))) * (1.0 / math.sqrt(HEAD_DIM))
    scores = jnp.where(allowed, scores, neg_fill)
    top = jnp.max(scores, axis=-1, keepdims=True)
    weights = jnp.exp(scores - top)
    total = jnp.sum(weights, axis=-1, keepdims=True)
    lse = top + jnp.log(total)
    probs = (weights / total).astype(bf16)
    context = dot(v, probs, ((2,), (2,)), ((0,), (0,))).astype(bf16)
    return from_units(context[:, None], batches, heads)[0], (q, k, v, lse)


def attention_backward(context_grad, saved, batches, heads, prefix):
    q, k, v, lse = saved
    grad = to_units(context_grad[None])[:, 0]
    allowed = visible_units(prefix, heads, q.shape[0], q.shape[-1])
    inv = 1.0 / math.sqrt(HEAD_DIM)
    scores = dot(q, k, ((1,), (1,)), ((0,), (0,))) * inv
    probs = jnp.where(allowed, jnp.exp(scores - lse), 0.0)
    prob_grad = dot(grad, v, ((1,), (1,)), ((0,), (0,)))
    delta = jnp.sum(probs * prob_grad, axis=-1, keepdims=True)
    score_grad = (probs * (prob_grad - delta)).astype(bf16)
    dq = dot(k, score_grad, ((2,), (2,)), ((0,), (0,))) * inv
    dk = dot(q, score_grad, ((2,), (1,)), ((0,), (0,))) * inv
    dv = dot(grad, probs.astype(bf16), ((2,), (1,)), ((0,), (0,)))
    return from_units(jnp.stack([dq, dk, dv], axis=1).astype(bf16), batches, heads)


def gates(mixed_rows, pair_ids, router_w):
    hot = (pair_ids[..., None] == jnp.arange(router_w.shape[1], dtype=jnp.int32)).astype(f32)
    logits = dot(mixed_rows, router_w, ((1,), (0,)))
    return hot, jax.nn.softmax(jnp.sum(hot * logits[:, None, :], axis=-1), axis=-1)


def ffn_plain(mixed, cot_line, router_w, weights, capacity, rows):
    nz, (count, width), experts = lax.axis_size("z"), mixed.shape, router_w.shape[1]
    egu, sgu, ed, sd = weights
    slice_ff = sd.shape[0]
    cot_line = cot_line.reshape(nz, -1, width)
    mixed_line = gather_line(mixed)
    cot_rows = cot_line[:, :count].reshape(nz * count, width)
    ids = jnp.transpose(cot_line[:, count : count + TOP_K, :count], (0, 2, 1)).reshape(-1, TOP_K).astype(jnp.int32)
    lines = mixed_line.shape[0]
    groups = lines // rows

    hot, probs = gates(mixed_line, ids, router_w)
    hot_int = hot.astype(jnp.int32).reshape(groups, rows * TOP_K, experts)
    earlier = jnp.cumsum(hot_int, axis=1) - hot_int
    rank = jnp.sum(earlier * hot_int, axis=-1).reshape(groups, rows, TOP_K)
    group_ids = ids.reshape(groups, rows, TOP_K)
    slot = jnp.where(rank < capacity, group_ids * capacity + rank, experts * capacity)
    slot_hot = (slot[..., None] == jnp.arange(experts * capacity, dtype=jnp.int32)).astype(bf16)
    token_hot = jnp.sum(slot_hot, axis=2)
    slot_probs = jnp.sum(slot_hot.astype(f32) * probs.reshape(groups, rows, TOP_K, 1), axis=(1, 2))

    def dispatch(values):
        per_group = dot(token_hot, values.reshape(groups, rows, width), ((1,), (1,)), ((0,), (0,)))
        per_group = per_group.reshape(groups, experts, capacity, width)
        return jnp.transpose(per_group, (1, 0, 2, 3)).reshape(experts, groups * capacity, width)

    def per_slot(values):
        return jnp.transpose(values.reshape(groups, experts, capacity), (1, 0, 2)).reshape(experts, -1, 1)

    def combine(slots):
        per_group = jnp.transpose(slots.reshape(experts, groups, capacity, width), (1, 0, 2, 3))
        per_group = per_group.reshape(groups, experts * capacity, width)
        return dot(token_hot, per_group, ((2,), (1,)), ((0,), (0,))).reshape(lines, width)

    slot_p = per_slot(slot_probs)
    arrived = dispatch(mixed_line).astype(bf16)
    cot_slots = dispatch(cot_rows)
    pair_grad = (cot_slots * slot_p).astype(bf16)
    batch = ((0,), (0,))
    act = dot(arrived, egu, ((2,), (1,)), batch)
    gate_act, up_act = act[..., :slice_ff], act[..., slice_ff:]
    sig = jax.nn.sigmoid(gate_act)
    silu_act = gate_act * sig
    expert_hidden = (silu_act * up_act).astype(bf16)
    expert_out = dot(expert_hidden, ed, ((2,), (1,)), batch)
    hidden_grad = dot(pair_grad, ed, ((2,), (2,)), batch)
    gate_up_grad = jnp.concatenate(
        [hidden_grad * up_act * sig * (1.0 + gate_act * (1.0 - sig)), hidden_grad * silu_act], axis=-1
    ).astype(bf16)
    grad_egu = dot(arrived, gate_up_grad, ((1,), (1,)), batch).astype(bf16)
    grad_ed = dot(expert_hidden, pair_grad, ((1,), (1,)), batch).astype(bf16)
    slot_grad = dot(gate_up_grad, egu, ((2,), (2,)), batch).astype(bf16)
    gate_dot = jnp.sum(cot_slots * expert_out, axis=-1)
    gate_dot = jnp.transpose(gate_dot.reshape(experts, groups, capacity), (1, 0, 2)).reshape(groups, 1, 1, -1)
    pair_dot = jnp.sum(slot_hot.astype(f32) * gate_dot, axis=-1).reshape(lines, TOP_K)
    expert_sum = combine((expert_out * slot_p).astype(bf16))

    s_act = dot(mixed_line, sgu, ((1,), (0,)))
    s_in, s_lift = s_act[:, :slice_ff], s_act[:, slice_ff:]
    s_sig = jax.nn.sigmoid(s_in)
    s_silu = s_in * s_sig
    s_hidden = (s_silu * s_lift).astype(bf16)
    s_hidden_grad = dot(cot_rows, sd, ((1,), (1,)))
    s_grad = jnp.concatenate(
        [s_hidden_grad * s_lift * s_sig * (1.0 + s_in * (1.0 - s_sig)), s_hidden_grad * s_silu], axis=-1
    ).astype(bf16)
    grad_sgu = dot(mixed_line, s_grad, ((0,), (0,))).astype(bf16)
    grad_sd = dot(s_hidden, cot_rows, ((0,), (0,))).astype(bf16)
    out_part = (dot(s_hidden, sd, ((1,), (0,))) + expert_sum).astype(bf16)
    mixed_part = combine(slot_grad) + dot(s_grad, sgu, ((1,), (1,)))
    pair_dot = jnp.sum(hot * pair_dot[..., None], axis=1).reshape(nz, count, experts)
    pair_dot = jnp.pad(jnp.transpose(pair_dot, (0, 2, 1)), ((0, 0), (0, EXTRA - experts), (0, width - count)))
    mixed_part = jnp.concatenate([mixed_part.reshape(nz, count, width), pair_dot], axis=1).astype(bf16)
    mixed_sum = sum_line(mixed_part.reshape(-1, width)).astype(f32)
    return out_part, mixed_sum, (grad_egu, grad_sgu, grad_ed, grad_sd)


def shards(
    hidden,
    routes,
    prefix,
    cotangent,
    attn_gain,
    w_query,
    w_key,
    w_value,
    w_output,
    ffn_gain,
    router,
    shared_gate,
    shared_up,
    shared_down,
    expert_gate,
    expert_up,
    expert_down,
):
    nz = lax.axis_size("z")
    batches, _, rows, width = hidden.shape
    count = batches * rows
    heads = width // HEAD_DIM
    experts = router.shape[1]
    own = router.shape[0]
    capacity = (5 * rows * TOP_K + 4 * experts - 1) // (4 * experts)
    slice_ff = shared_gate.shape[1] // nz

    misc = jnp.concatenate(
        [router, attn_gain[:, None], ffn_gain[:, None], jnp.zeros((own, MISC - experts - 2), bf16)], axis=1
    )
    attn_shard = jnp.concatenate([w_query, w_key, w_value, w_output, misc], axis=1)

    def slices(gate, up):
        both = jnp.stack([gate.reshape(-1, nz, slice_ff), up.reshape(-1, nz, slice_ff)], axis=2)
        return jnp.transpose(both.reshape(-1, nz, 2 * slice_ff), (1, 0, 2))

    cot = cotangent.reshape(count, width)
    pair_ids = routes.reshape(count, TOP_K)
    ids_rows = jnp.pad(pair_ids.T.astype(bf16), ((0, EXTRA - TOP_K), (0, width - count)))
    cot_routes = jnp.concatenate([cot, ids_rows], axis=0)
    parts = (slices(expert_gate[0], expert_up[0]), slices(shared_gate, shared_up), expert_down[0], shared_down)
    fast = paired(batches, heads)
    if fast:
        attn_full, *lined = first_fast(attn_shard, *parts[:2])
    else:
        attn_full = gather_all(attn_shard)

    w_qkv = attn_full[:, : 3 * width]
    w_out = attn_full[:, 3 * width : 4 * width]
    misc_full = attn_full[:, 4 * width :]
    router_w = misc_full[:, :experts]
    gain_attn = misc_full[:, experts].astype(f32)
    gain_ffn = misc_full[:, experts + 1].astype(f32)

    x_in = hidden.reshape(count, width).astype(f32)
    attn_scale = rms_scale(x_in)
    attn_norm = x_in * attn_scale
    normed = (attn_norm * gain_attn).astype(bf16)
    positions = lax.axis_index(DP) * rows + jnp.arange(rows, dtype=jnp.int32)
    cosine, sine = rotary_tables(jnp.tile(positions, batches))
    projected = dot(w_qkv, normed, ((0,), (1,)))
    turned = rotate_t(projected[: 2 * width], cosine, sine, 1.0)
    qkv = jnp.concatenate([turned, projected[2 * width :]], axis=0).astype(bf16)
    qkv = jnp.transpose(qkv.reshape(3, width, batches, rows), (0, 2, 1, 3))
    if fast:
        context, saved, ffn, cot_line = attend_fast(prefix, qkv, *lined, *parts[2:], cot_routes)
    else:
        context, saved = attention_forward(qkv, batches, heads, prefix)
        ffn, cot_line = gather_weights(*parts), gather_line(cot_routes)
    context = jnp.transpose(context, (1, 0, 2)).reshape(width, count)
    attended = x_in + dot(context, w_out, ((0,), (0,)))
    ffn_scale = rms_scale(attended)
    ffn_norm = attended * ffn_scale
    mixed = (ffn_norm * gain_ffn).astype(bf16)

    if fast:
        router_rows = jnp.pad(router_w.T, ((0, 16 - experts), (0, 0)))
        out_part, mixed_sum, ffn_grads = ffn_fast(mixed, cot_line, router_rows, ffn, capacity)
    else:
        out_part, mixed_sum, ffn_grads = ffn_plain(mixed, cot_line, router_w, ffn, capacity, rows)

    hot, probs = gates(mixed, pair_ids, router_w)
    gate_grads = jnp.sum(hot * mixed_sum[count : count + experts, :count].T[:, None, :], axis=-1)
    picked = probs * (gate_grads - jnp.sum(probs * gate_grads, axis=-1, keepdims=True))
    logit_grad = jnp.sum(hot * picked[..., None], axis=1)
    grad_router = jnp.dot(mixed.astype(f32).T, logit_grad, precision=highest)
    mixed_grad = mixed_sum[:count] + jnp.dot(logit_grad, router_w.astype(f32).T, precision=highest)
    cot_wide = cot.astype(f32)
    inner = mixed_grad * gain_ffn
    grad_gffn = jnp.sum(mixed_grad * ffn_norm, axis=0)
    attended_grad = cot_wide + ffn_scale * (inner - ffn_norm * jnp.mean(inner * ffn_norm, axis=-1, keepdims=True))
    out_grad = attended_grad.astype(bf16)
    grad_wout = dot(context, out_grad, ((1,), (0,)))
    context_grad = dot(w_out, out_grad, ((1,), (1,))).astype(bf16)
    context_grad = jnp.transpose(context_grad.reshape(width, batches, rows), (1, 0, 2))

    if fast:
        rot_grad, (*lined, ed_sum, sd_sum), out_sum = backward_fast(prefix, context_grad, saved, *ffn_grads, out_part)
    else:
        rot_grad = attention_backward(context_grad, saved, batches, heads, prefix)
        egu_sum, sgu_sum, ed_sum, sd_sum = sum_weights(*ffn_grads)
        out_sum = sum_line(out_part)
    rot_grad = jnp.transpose(rot_grad, (0, 2, 1, 3)).reshape(3 * width, count).astype(f32)
    turned = rotate_t(rot_grad[: 2 * width], cosine, sine, -1.0)
    qkv_grad = jnp.concatenate([turned, rot_grad[2 * width :]], axis=0).astype(bf16)
    grad_wqkv = dot(normed, qkv_grad, ((0,), (1,)))
    normed_grad = dot(qkv_grad, w_qkv, ((0,), (1,)))
    grad_gattn = jnp.sum(normed_grad * attn_norm, axis=0)
    inner = normed_grad * gain_attn
    input_grad = (
        attended_grad + attn_scale * (inner - attn_norm * jnp.mean(inner * attn_norm, axis=-1, keepdims=True))
    ).astype(bf16)

    grad_misc = jnp.concatenate(
        [grad_router, grad_gattn[:, None], grad_gffn[:, None], jnp.zeros((width, MISC - experts - 2), f32)], axis=1
    )
    attn_parts = jnp.concatenate([grad_wqkv, grad_wout, grad_misc], axis=1).astype(bf16)
    if fast:
        attn_sums, egu_sum, sgu_sum = last_fast(attn_parts, *lined)
    else:
        attn_sums = sum_all(attn_parts)
    attn_sums = attn_sums.astype(f32)
    block_rows = (attended + out_sum.astype(f32)).astype(bf16)

    def joined(blocks):
        both = jnp.transpose(blocks.reshape(nz, -1, 2, slice_ff), (2, 1, 0, 3)).astype(f32)
        return both.reshape(2, -1, nz * slice_ff)

    egu_sum, sgu_sum = joined(egu_sum), joined(sgu_sum)
    return (
        block_rows.reshape(batches, 1, rows, width),
        input_grad.reshape(batches, 1, rows, width),
        attn_sums[:, 4 * width + experts],
        attn_sums[:, :width],
        attn_sums[:, width : 2 * width],
        attn_sums[:, 2 * width : 3 * width],
        attn_sums[:, 3 * width : 4 * width],
        attn_sums[:, 4 * width + experts + 1],
        attn_sums[:, 4 * width : 4 * width + experts],
        sgu_sum[0],
        sgu_sum[1],
        sd_sum.astype(f32),
        egu_sum[0][None],
        egu_sum[1][None],
        ed_sum.astype(f32)[None],
    )


def solution(mesh):
    n_dp, n_expert = mesh.shape["dp"], mesh.shape["expert"]
    nz = 4 if n_dp % 4 == 0 else 1
    grid = Mesh(mesh.devices.reshape(nz, n_dp // nz, n_expert // 2, 2), ALL)
    rows = P(None, EXPERT, DP, None)
    line = P(ALL)
    dense = P(ALL, None)
    expert = P(EXPERT, DP, None)
    return jax.shard_map(
        shards,
        mesh=grid,
        in_specs=(rows, rows, P(None, EXPERT), rows, line)
        + (dense,) * 4
        + (line,)
        + (dense,) * 4
        + (expert,) * 3,
        out_specs=(rows, rows, line) + (dense,) * 4 + (line,) + (dense,) * 4 + (expert,) * 3,
        check_vma=False,
    )
```

```python
import functools
import math

import jax
import jax.numpy as jnp
from jax import lax
from jax.experimental import pallas as pl
from jax.experimental.pallas import tpu as pltpu
from jax.sharding import Mesh
from jax.sharding import PartitionSpec as P

HEAD_DIM = 64
TOP_K = 2
MISC = 128

eps = 1e-06
highest = lax.Precision.HIGHEST
neg_fill = -1e30
f32 = jnp.float32
bf16 = jnp.bfloat16

ALL = ("z", "y", "x", "c")
PLANE = ("y", "x", "c")
DP = ("z", "y")
EXPERT = ("x", "c")


def rms_scale(values):
    return lax.rsqrt(jnp.mean(values * values, axis=-1, keepdims=True) + eps)


def silu_grad(values):
    sig = jax.nn.sigmoid(values)
    return sig * (1.0 + values * (1.0 - sig))


def dot(a, b, dims, batch=((), ())):
    return lax.dot_general(a, b, (dims, batch), preferred_element_type=f32)


def rotary_tables(positions):
    half = HEAD_DIM // 2
    frequency = jnp.exp(jnp.arange(half, dtype=f32) * (-math.log(10000.0) * 2.0 / HEAD_DIM))
    angles = frequency[:, None] * positions.astype(f32)[None, :]
    return jnp.cos(angles), jnp.sin(angles)


def rotate_t(values, cosine, sine, sign):
    rows = values.shape[-1]
    halves = values.reshape(-1, 2, HEAD_DIM // 2, rows)
    first, second = halves[:, 0], halves[:, 1]
    turned = jnp.stack([first * cosine - sign * second * sine, second * cosine + sign * first * sine], axis=1)
    return turned.reshape(values.shape)


def gather_all(shard):
    return lax.all_gather(shard, ALL, axis=0, tiled=True)


def gather_weights(egu, sgu, ed, sd):
    nz, ny, ne = lax.axis_size("z"), lax.axis_size("y"), lax.axis_size(EXPERT)

    def spread(blocks):
        mine = lax.all_to_all(blocks, "z", 0, 0, tiled=True)
        return lax.all_gather(mine, PLANE, axis=0).reshape(ny, ne, nz, *blocks.shape[1:])

    egu_all = jnp.transpose(spread(egu), (1, 2, 0, 3, 4)).reshape(ne, -1, egu.shape[-1])
    sgu_all = jnp.transpose(spread(sgu), (2, 0, 1, 3, 4)).reshape(-1, sgu.shape[-1])
    ed_all = lax.all_gather(ed, PLANE, axis=0).reshape(ny, ne, *ed.shape)
    ed_all = jnp.transpose(ed_all, (1, 0, 2, 3)).reshape(ne, -1, ed.shape[-1])
    sd_all = lax.all_gather(sd, PLANE, axis=0, tiled=True)
    return egu_all, sgu_all, ed_all, sd_all


def gather_line(rows):
    return lax.all_gather(rows, "z", axis=0, tiled=True)


def paired(batches, heads):
    n_dp = lax.axis_size(DP)
    here = batches * heads // n_dp
    even = here * n_dp == batches * heads and heads % max(1, here) == 0
    return even and tuple(lax.axis_size(name) for name in ALL) == (4, 2, 2, 2)


def sum_line(rows):
    return lax.psum_scatter(rows, "z", scatter_dimension=0, tiled=True)


def sum_weights(egu, sgu, ed, sd):
    nz, ny, ne = lax.axis_size("z"), lax.axis_size("y"), lax.axis_size(EXPERT)

    def collect(parts):
        mine = lax.psum_scatter(parts, PLANE, scatter_dimension=0, tiled=True)
        return lax.all_to_all(mine.reshape(nz, *mine.shape[1:]), "z", 0, 0, tiled=True)

    wide = egu.shape[-1]
    egu = jnp.transpose(egu.reshape(ne, nz, ny, -1, wide), (2, 0, 1, 3, 4))
    sgu = jnp.transpose(sgu.reshape(nz, ny, ne, -1, wide), (1, 2, 0, 3, 4))
    egu = collect(egu.reshape(ny * ne * nz, -1, wide))
    sgu = collect(sgu.reshape(ny * ne * nz, -1, wide))
    ed = jnp.transpose(ed.reshape(ne, ny, -1, ed.shape[-1]), (1, 0, 2, 3)).reshape(ny * ne, -1, ed.shape[-1])
    ed = lax.psum_scatter(ed, PLANE, scatter_dimension=0, tiled=True)[0]
    sd = lax.psum_scatter(sd, PLANE, scatter_dimension=0, tiled=True)
    return egu, sgu, ed, sd


def sum_all(parts):
    return lax.psum_scatter(parts, ALL, scatter_dimension=0, tiled=True)


def units_here(batches, heads):
    return -(-batches * heads // lax.axis_size(DP))


def to_units(tensor):
    kinds, batches, width, rows = tensor.shape
    n_dp = lax.axis_size(DP)
    heads = width // HEAD_DIM
    here = units_here(batches, heads)
    units = tensor.reshape(kinds, batches * heads, HEAD_DIM, rows)
    units = jnp.pad(units, ((0, 0), (0, here * n_dp - batches * heads), (0, 0), (0, 0)))
    units = jnp.transpose(units.reshape(kinds, n_dp, here, HEAD_DIM, rows), (1, 2, 0, 3, 4))
    units = lax.all_to_all(units, DP, 0, 0, tiled=True)
    return jnp.transpose(units, (1, 2, 3, 0, 4)).reshape(here, kinds, HEAD_DIM, n_dp * rows)


def from_units(units, batches, heads):
    here, kinds, _, length = units.shape
    n_dp = lax.axis_size(DP)
    rows = length // n_dp
    parts = jnp.transpose(units.reshape(here, kinds, HEAD_DIM, n_dp, rows), (3, 0, 1, 2, 4))
    parts = lax.all_to_all(parts, DP, 0, 0, tiled=True)
    parts = parts.reshape(n_dp * here, kinds, HEAD_DIM, rows)[: batches * heads]
    return jnp.transpose(parts, (1, 0, 2, 3)).reshape(kinds, batches, heads * HEAD_DIM, rows)


MESH = pl.DeviceIdType.MESH


def position():
    return tuple(lax.axis_index(name) for name in ALL)


def remote(src, dst, send, recv, device):
    return pltpu.make_async_remote_copy(
        src_ref=src, dst_ref=dst, send_sem=send, recv_sem=recv, device_id=device, device_id_type=MESH
    )


def greet(partners):
    barrier = pltpu.get_barrier_semaphore()
    for device in partners:
        pl.semaphore_signal(barrier, inc=1, device_id=device, device_id_type=MESH)
    pl.semaphore_wait(barrier, len(partners))


def any_specs(count):
    return [pl.BlockSpec(memory_space=pl.ANY)] * count


def params(collective_id, vmem=16 << 20):
    return pltpu.CompilerParams(collective_id=collective_id, has_side_effects=True, vmem_limit_bytes=vmem)


class PlaneItem:
    def __init__(self, here, index, place, own, x_first):
        self.here, self.index, self.place, self.own, self.x_first = here, index, place, own, x_first

    def moved(self, along_first, along_second, along_core):
        z, y, x, c = self.here
        move_x, move_y = (along_first, along_second) if self.x_first else (along_second, along_first)
        return (z, 1 - y if move_y else y, 1 - x if move_x else x, 1 - c if along_core else c)

    def ref(self, *moves):
        return self.place(*self.moved(*moves)[1:])

    COPIES = (
        ((0, 0, 0), (1, 0, 0)),
        ((0, 0, 0), (0, 1, 0)),
        ((1, 0, 0), (0, 1, 0)),
        ((0, 0, 0), (0, 0, 1)),
        ((1, 0, 0), (0, 0, 1)),
        ((0, 1, 0), (0, 0, 1)),
        ((1, 1, 0), (0, 0, 1)),
    )

    def copy(self, number, send, recv):
        source, to = self.COPIES[number]
        src = self.own if source == (0, 0, 0) else self.ref(*source)
        return remote(
            src, self.ref(*source), send.at[self.index, number], recv.at[self.index, number], self.moved(*to)
        )

    def arrival(self, number, send, recv):
        source, to = self.COPIES[number]
        ref = self.ref(*[a ^ b for a, b in zip(source, to)])
        return remote(ref, ref, send.at[self.index, number], recv.at[self.index, number], self.moved(*to))


def line_gather_steps(z, nz, own, out, sends, gets, neighbour, pieces):
    def copy(way, source, piece, src=None):
        part = pieces[piece]
        dst = out.at[source, part]
        src = dst if src is None else src.at[part]
        return remote(src, dst, sends.at[way, source, piece], gets.at[way, source, piece], neighbour(1 - 2 * way))

    def may_send(way):
        return z < nz - 1 if way == 0 else z > 0

    def start():
        for piece in range(len(pieces)):
            for way in range(2):
                pl.when(may_send(way))(lambda: copy(way, z, piece, own).start())

    def step(distance, piece):
        for way in range(2):
            source = z - distance if way == 0 else z + distance

            @pl.when((source >= 0) & (source < nz))
            def _():
                copy(way, source, piece).wait_recv()
                pl.when(may_send(way))(lambda: copy(way, source, piece).start())

    def end():
        for distance in range(nz):
            for piece in range(len(pieces)):
                for way in range(2):
                    source = z - distance if way == 0 else z + distance

                    @pl.when((source >= 0) & (source < nz) & may_send(way))
                    def _():
                        copy(way, source, piece).wait_send()

    steps = [functools.partial(step, distance, piece) for distance in range(1, nz) for piece in range(len(pieces))]
    return start, steps, end


def line_partners(here, nz):
    z, y, x, c = here
    return lambda way: (jnp.clip(z + way, 0, nz - 1), y, x, c)


def greet_line(here, nz):
    z = here[0]
    neighbour = line_partners(here, nz)
    barrier = pltpu.get_barrier_semaphore()

    @pl.when(z > 0)
    def _():
        pl.semaphore_signal(barrier, inc=1, device_id=neighbour(-1), device_id_type=MESH)

    @pl.when(z < nz - 1)
    def _():
        pl.semaphore_signal(barrier, inc=1, device_id=neighbour(1), device_id_type=MESH)

    pl.semaphore_wait(barrier, jnp.where(z > 0, 1, 0) + jnp.where(z < nz - 1, 1, 0))


LINE_PIECES = 2


def row_pieces(rows):
    half = rows // 2 // 16 * 16
    return pl.ds(0, half), pl.ds(half, rows - half)


def line_sum_steps(z, nz, parts, total, up, down, sends, gets, neighbour, pieces):
    arrived = (up, down)

    def copy(way, target, piece, src):
        part = pieces[piece]
        dst = arrived[way].at[target, part]
        return remote(src, dst, sends.at[way, target, piece], gets.at[way, target, piece], neighbour(1 - 2 * way))

    def part_of(ref, target, piece):
        return ref.at[target, pieces[piece]]

    def step(distance, piece):
        for way in range(2):
            target = nz - distance if way == 0 else distance - 1
            ahead = z < target if way == 0 else z > target
            first = z == 0 if way == 0 else z == nz - 1
            mine, theirs = part_of(parts, target, piece), part_of(arrived[way], target, piece)

            @pl.when(ahead & first)
            def _():
                copy(way, target, piece, mine).start()

            @pl.when(ahead & jnp.logical_not(first))
            def _():
                copy(way, target, piece, theirs).wait_recv()
                mine[...] = (mine[...].astype(f32) + theirs[...].astype(f32)).astype(bf16)
                copy(way, target, piece, mine).start()

    def end():
        for piece, part in enumerate(pieces):
            total[part, :] = parts[z, part, :].astype(f32)
            for way in range(2):
                theirs = part_of(arrived[way], z, piece)

                @pl.when(z > 0 if way == 0 else z < nz - 1)
                def _():
                    copy(way, z, piece, theirs).wait_recv()
                    total[part, :] += theirs[...].astype(f32)

        for distance in range(1, nz):
            for piece in range(len(pieces)):
                for way in range(2):
                    target = nz - distance if way == 0 else distance - 1

                    @pl.when(z < target if way == 0 else z > target)
                    def _():
                        copy(way, target, piece, part_of(parts, target, piece)).wait_send()

    steps = [functools.partial(step, distance, piece) for distance in range(1, nz) for piece in range(len(pieces))]
    return steps, end


class SumItem:
    def __init__(self, here, index, place, buffers, x_first):
        self.here, self.index, self.place, self.x_first = here, index, place, x_first
        self.own, self.sib, self.second, self.first = buffers

    moved = PlaneItem.moved

    def slot(self, a, b):
        return 2 * a + b

    def begin(self, load, send, recv):
        for a in range(2):
            for b in range(2):
                n = self.slot(a, b)
                self.sib_copy(a, b, send, recv).start()
                pltpu.make_async_copy(self.place(*self.moved(a, b, 0)[1:]), self.own.at[n], load.at[self.index, n]).start()

    def sib_copy(self, a, b, send, recv):
        n = self.slot(a, b)
        src = self.place(*self.moved(a, b, 1)[1:])
        return remote(src, self.sib.at[n], send.at[self.index, n], recv.at[self.index, n], self.moved(0, 0, 1))

    def second_copy(self, a, send, recv):
        n = 4 + a
        src = self.sib.at[self.slot(a, 1)]
        return remote(src, self.second.at[a], send.at[self.index, n], recv.at[self.index, n], self.moved(0, 1, 0))

    def first_copy(self, send, recv):
        src = self.second.at[1]
        return remote(src, self.first, send.at[self.index, 6], recv.at[self.index, 6], self.moved(1, 0, 0))

    def after_core(self, load, send, recv):
        for b in (1, 0):
            for a in range(2):
                n = self.slot(a, b)
                pltpu.make_async_copy(self.own.at[n], self.own.at[n], load.at[self.index, n]).wait()
                self.sib_copy(a, b, send, recv).wait_recv()
                add_to(self.sib.at[n], self.own.at[n])
                if b == 1:
                    self.second_copy(a, send, recv).start()

    def after_second(self, send, recv):
        for a in (1, 0):
            self.second_copy(a, send, recv).wait_recv()
            add_to(self.second.at[a], self.sib.at[self.slot(a, 0)])
            if a == 1:
                self.first_copy(send, recv).start()

    def after_first(self, send, recv, total=None):
        self.first_copy(send, recv).wait_recv()
        if total is None:
            add_to(self.first, self.second.at[0])
        else:
            total[...] = self.first[...].astype(f32) + self.second[0].astype(f32)

    def end(self, send, recv):
        for a in range(2):
            for b in range(2):
                self.sib_copy(a, b, send, recv).wait_send()
            self.second_copy(a, send, recv).wait_send()
        self.first_copy(send, recv).wait_send()


def add_to(total, term):
    rows, columns = total.shape
    if rows % 16 == 0:

        @pl.loop(0, rows // 16)
        def _(i):
            part = pl.ds(pl.multiple_of(i * 16, 16), 16)
            total[part, :] = (total[part, :].astype(f32) + term[part, :].astype(f32)).astype(bf16)
    else:
        wide = max(w for w in (128, 256, 384, 512, 640) if columns % w == 0)

        @pl.loop(0, columns // wide)
        def _(i):
            part = pl.ds(pl.multiple_of(i * wide, 128), wide)
            total[:, part] = (total[:, part].astype(f32) + term[:, part].astype(f32)).astype(bf16)


SUM_LAG = 3


def unit_owner(number, batches, heads, here_units):
    per_batch = heads // here_units
    return number // per_batch, lax.rem(number, per_batch) * here_units


def exchange(me, n_dp, copy):
    ny = 2

    def device(number):
        return (number // ny, lax.rem(number, ny))

    far = [lax.rem(me + d, n_dp) for d in range(1, n_dp)]
    near = [lax.rem(me + n_dp - d, n_dp) for d in range(1, n_dp)]

    def start():
        for number in far:
            copy(number, me, device(number)).start()

    def arrive():
        for number in near:
            copy(me, number, device(number)).wait_recv()

    def end():
        for number in far:
            copy(number, me, device(number)).wait_send()

    return start, arrive, end


def tile_spans(length):
    tile = 256 if length % 512 == 0 else length // 2
    for start in range(0, length, tile):
        if start < length // 2:
            yield start, tile, 0, length // 2
        else:
            yield start, tile, start, start + tile


def masked(values, start, tile, mask_from, keys, length, fill):
    key = mask_from + lax.broadcasted_iota(jnp.int32, (keys - mask_from, tile), 0)
    query = start + lax.broadcasted_iota(jnp.int32, (keys - mask_from, tile), 1)
    allowed = (key <= query) | ((key < length) & (query < length))
    tail = jnp.where(allowed, values[mask_from:], fill)
    return tail if mask_from == 0 else jnp.concatenate([values[:mask_from], tail], axis=0)


X_FIRST = {
    "egu": lambda k: k == 1,
    "sgu": lambda k: k % 2 == 1,
    "sd": lambda k: False,
    "ed": lambda k: k == 1,
}


def plane_items(here, arrays, outs, start=0):
    items = []

    def add(place, own, x_first):
        items.append(PlaneItem(here, start + len(items), place, own, x_first))

    if "ed" in arrays:
        source, ed = arrays["ed"], outs["ed"]
        half = source.shape[0] // 2
        for h in range(2):
            rows = pl.ds(h * half, half)
            add(lambda py, px, pc, rows=rows: ed.at[px * 2 + pc, py, rows], source.at[rows], X_FIRST["ed"](h))
    if "sd" in arrays:
        sd = outs["sd"]
        add(lambda py, px, pc: sd.at[(py * 2 + px) * 2 + pc], arrays["sd"], X_FIRST["sd"](0))
    if "egu" in arrays:
        source, egu = arrays["egu"], outs["egu"]
        for zs in range(source.shape[0]):
            add(lambda py, px, pc, zs=zs: egu.at[px * 2 + pc, zs * 2 + py], source.at[zs], X_FIRST["egu"](zs))
    if "sgu" in arrays:
        source, sgu = arrays["sgu"], outs["sgu"]
        for zs in range(source.shape[0]):
            place = lambda py, px, pc, zs=zs: sgu.at[((zs * 2 + py) * 2 + px) * 2 + pc]
            add(place, source.at[zs], X_FIRST["sgu"](zs))
    return items


def attend_kernel(nz, batches, *refs):
    prefix, qkv, egu_in, sgu_in, cot_in, ids_in = refs[:6]
    context, units, lse, egu, sgu, cot = refs[6:12]
    result, cot_own, egu_own, sgu_own, local, loads, send, recv = refs[12:20]
    csend, crecv, psend, precv, lsend, lrecv = refs[20:]
    here = position()
    z, y, x, c = here
    n_dp = nz * 2
    me = z * 2 + y
    kinds, width, all_rows = qkv.shape
    rows = all_rows // batches
    heads = width // HEAD_DIM
    count = units.shape[1] // HEAD_DIM
    span = count * HEAD_DIM
    length = units.shape[2]
    greet(
        [(lax.rem(me + d, n_dp) // 2, lax.rem(me + d, 2), x, c) for d in range(1, n_dp)]
        + [(z, y, 1 - x, c), (z, y, x, 1 - c)]
    )

    def columns(number):
        return pl.ds(pl.multiple_of(number * rows, rows), rows)

    def qkv_block(number):
        batch, head = unit_owner(number, batches, heads, count)
        return qkv.at[:, pl.ds(pl.multiple_of(head * HEAD_DIM, HEAD_DIM), span), columns(batch)]

    def qkv_copy(number, source, device):
        return remote(
            qkv_block(number), units.at[:, :, columns(source)], send.at[number], recv.at[source], (*device, x, c)
        )

    start, arrive, end = exchange(me, n_dp, qkv_copy)
    start()
    keep = pltpu.make_async_copy(qkv_block(me), units.at[:, :, columns(me)], local.at[0])
    keep.start()
    items = plane_items(here, {"egu": egu_in, "sgu": sgu_in}, {"egu": egu, "sgu": sgu})
    for item in items:
        for number in (0, 1, 3):
            item.copy(number, psend, precv).start()
    fills = [(cot_in.at[b, 0], cot_own.at[pl.ds(b * rows, rows)]) for b in range(batches)]
    fills += [(ids_in, cot_own.at[pl.ds(all_rows, EXTRA)])]
    fills += [(egu_in, egu_own), (sgu_in, sgu_own)]
    fills = [pltpu.make_async_copy(src, dst, loads.at[i]) for i, (src, dst) in enumerate(fills)]
    for copy in fills:
        copy.start()
    owns = [(cot_own, cot.at[z])]
    owns += [(egu_own.at[zs], egu.at[x * 2 + c, zs * 2 + y]) for zs in range(nz)]
    owns += [(sgu_own.at[zs], sgu.at[((zs * 2 + y) * 2 + x) * 2 + c]) for zs in range(nz)]
    keeps = [pltpu.make_async_copy(src, dst, local.at[1 + i]) for i, (src, dst) in enumerate(owns)]
    for copy in fills:
        copy.wait()
    for copy in keeps:
        copy.start()

    def have_first(item):
        item.arrival(0, psend, precv).wait_recv()
        item.copy(2, psend, precv).start()
        item.copy(4, psend, precv).start()

    def have_second(item):
        item.arrival(1, psend, precv).wait_recv()
        item.copy(5, psend, precv).start()
        item.arrival(2, psend, precv).wait_recv()
        item.copy(6, psend, precv).start()

    early = len(items) // 2
    for item in items[:early]:
        have_first(item)
    arrive()
    keep.wait()
    line_start, line_steps, line_end = line_gather_steps(
        z, nz, cot_own, cot, lsend, lrecv, line_partners(here, nz), row_pieces(cot.shape[1])
    )
    line_start()

    my_batch, my_head = unit_owner(me, batches, heads, count)
    limit = prefix[my_batch, 0]

    def context_copy(head):
        def copy(number, source, device):
            _, first_head = unit_owner(source, batches, heads, count)
            batch, _ = unit_owner(source, batches, heads, count)
            part = pl.ds(pl.multiple_of((first_head + head) * HEAD_DIM, HEAD_DIM), HEAD_DIM)
            return remote(
                result.at[pl.ds(head * HEAD_DIM, HEAD_DIM), columns(number)],
                context.at[part, columns(batch)],
                csend.at[head, number],
                crecv.at[head, source],
                (*device, x, c),
            )

        return copy

    def attend(head):
        part = pl.ds(head * HEAD_DIM, HEAD_DIM)
        for first, tile, mask_from, keys in tile_spans(length):
            queries = units[0, part, pl.ds(first, tile)] * bf16(1.0 / math.sqrt(HEAD_DIM))
            scores = dot(units[1, part, pl.ds(0, keys)], queries, ((0,), (0,)))
            scores = masked(scores, first, tile, mask_from, keys, limit, neg_fill)
            top = jnp.max(scores, axis=0, keepdims=True)
            weights = jnp.exp(scores - top)
            total = jnp.sum(weights, axis=0, keepdims=True)
            lse[head, :, pl.ds(first, tile)] = top + jnp.log(total)
            mean = dot(units[2, part, pl.ds(0, keys)], weights.astype(bf16), ((1,), (0,))) / total
            result[part, pl.ds(first, tile)] = mean.astype(bf16)

    exchanges = [exchange(me, n_dp, context_copy(head)) for head in range(count)]
    own_part = [pl.ds(pl.multiple_of((my_head + head) * HEAD_DIM, HEAD_DIM), HEAD_DIM) for head in range(count)]
    own_copies = [
        pltpu.make_async_copy(
            result.at[pl.ds(head * HEAD_DIM, HEAD_DIM), columns(me)],
            context.at[own_part[head], columns(my_batch)],
            local.at[1 + len(owns) + head],
        )
        for head in range(count)
    ]
    later = [functools.partial(have_first, item) for item in items[early:]]
    later += [functools.partial(have_second, item) for item in items]
    line_steps = list(line_steps)
    for head in range(count):
        attend(head)
        exchanges[head][0]()
        own_copies[head].start()
        if head == 0:
            for step in later[: len(items) - early]:
                step()
            later = later[len(items) - early :]
            for step in line_steps[:LINE_PIECES]:
                step()
            line_steps = line_steps[LINE_PIECES:]
    share = -(-len(later) // max(1, len(line_steps)))
    while later or line_steps:
        for step in later[:share]:
            step()
        later = later[share:]
        if line_steps:
            line_steps.pop(0)()
    for item in items:
        for number in range(3, 7):
            item.arrival(number, psend, precv).wait_recv()
    for head in range(count):
        exchanges[head][1]()
        own_copies[head].wait()
    for item in items:
        for number in range(7):
            item.copy(number, psend, precv).wait_send()
    end()
    line_end()
    for head in range(count):
        exchanges[head][2]()
    for copy in keeps:
        copy.wait()


def attend_fast(prefix, qkv, egu, sgu, cot, ids):
    nz = lax.axis_size("z")
    n_dp = nz * 2
    kinds, width, all_rows = qkv.shape
    batches = cot.shape[0]
    heads = width // HEAD_DIM
    count = batches * heads // n_dp
    length = n_dp * all_rows // batches
    any_space, vmem = pl.BlockSpec(memory_space=pl.ANY), pl.BlockSpec(memory_space=pltpu.VMEM)
    shapes = [
        ((width, all_rows), bf16),
        ((kinds, count * HEAD_DIM, length), bf16),
        ((count, 1, length), f32),
        ((4, nz * 2, *egu.shape[1:]), bf16),
        ((nz * 8, *sgu.shape[1:]), bf16),
        ((nz, all_rows + EXTRA, width), bf16),
    ]
    dma = pltpu.SemaphoreType.DMA
    items = 2 * nz
    line = dma((2, nz, LINE_PIECES))
    context, units, lse, egu, sgu, cot = pl.pallas_call(
        functools.partial(attend_kernel, nz, batches),
        out_shape=[jax.ShapeDtypeStruct(*shape) for shape in shapes],
        in_specs=[pl.BlockSpec(memory_space=pltpu.SMEM)] + [any_space] * 5,
        out_specs=[any_space, vmem, vmem] + [any_space] * 3,
        scratch_shapes=[
            pltpu.VMEM((count * HEAD_DIM, length), bf16),
            pltpu.VMEM((all_rows + EXTRA, width), bf16),
            *[pltpu.VMEM(a.shape, bf16) for a in (egu, sgu)],
            dma((2 + 2 * nz + count,)),
            dma((batches + 3,)),
            dma((n_dp,)),
            dma((n_dp,)),
            dma((count, n_dp)),
            dma((count, n_dp)),
            dma((items, 7)),
            dma((items, 7)),
            line,
            line,
        ],
        compiler_params=params(4, 58 << 20),
        name="attend",
    )(prefix, qkv, egu, sgu, cot, ids)
    return context, (units, lse), egu.reshape(4, -1, egu.shape[-1]), sgu.reshape(-1, sgu.shape[-1]), cot


def first_kernel(nz, *refs):
    attn_in, halves_in, (ed_in, sd_in) = refs[:5], refs[5:9], refs[9:11]
    attn, egu, sgu, ed, sd, attn_own, egu_own, sgu_own, ed_own, sd_own = refs[11:21]
    local, stores, zsend, zrecv, psend, precv = refs[21:]
    here = position()
    z, y, x, c = here
    line = [lax.rem(z + d, nz) for d in range(nz)]
    ff = egu.shape[-1] // 2

    def flat(zs, py, px, pc):
        return ((zs * 2 + py) * 2 + px) * 2 + pc

    mine = flat(z, y, x, c)
    gathered, start = [], 0
    for i, ref in enumerate(attn_in):
        gathered.append(
            pltpu.make_async_copy(ref, attn_own.at[:, pl.ds(start, ref.shape[1])], local.at[i])
        )
        start += ref.shape[1]
    for kind in range(4):
        src = halves_in[kind].at[:, pl.ds(pl.multiple_of(z * ff, ff), ff)]
        dst = (egu_own if kind < 2 else sgu_own).at[:, pl.ds(kind % 2 * ff, ff)]
        gathered.append(pltpu.make_async_copy(src, dst, local.at[5 + kind]))
    gathered.append(pltpu.make_async_copy(ed_in, ed_own, local.at[9]))
    gathered.append(pltpu.make_async_copy(sd_in, sd_own, local.at[10]))
    for copy in gathered:
        copy.start()
    greet([(line[d], y, x, c) for d in range(1, nz)] + [(z, 1 - y, x, c), (z, y, 1 - x, c), (z, y, x, 1 - c)])

    def half_block(kind, to, at):
        src = halves_in[kind].at[:, pl.ds(pl.multiple_of(to * ff, ff), ff)]
        return src, (egu if kind < 2 else sgu).at[at, :, pl.ds(kind % 2 * ff, ff)]

    def half_copy(kind, d, arriving=False):
        to, frm = line[d], line[(nz - d) % nz]
        src, dst = half_block(kind, to, frm if arriving else z)
        return remote(src, dst, zsend.at[1 + kind, d], zrecv.at[1 + kind, d], (to, y, x, c))

    def attn_copy(d, arriving=False):
        to, frm = line[d], line[(nz - d) % nz]
        ref = attn.at[flat(frm if arriving else z, y, x, c)]
        return remote(ref if arriving else attn_own, ref, zsend.at[0, d], zrecv.at[0, d], (to, y, x, c))

    items = []
    for d in range(nz):
        place = lambda py, px, pc, frm=line[(nz - d) % nz]: attn.at[flat(frm, py, px, pc)]
        items.append(PlaneItem(here, d, place, place(y, x, c) if d else attn_own, d % 2 == 1))

    def have_own(item):
        for number in (0, 1, 3):
            item.copy(number, psend, precv).start()

    far_first = sorted(range(1, nz), key=lambda d: abs(d - nz / 2))
    for copy in gathered:
        copy.wait()
    for d in far_first:
        attn_copy(d).start()
    have_own(items[0])
    for d in far_first:
        for kind in range(4):
            half_copy(kind, d).start()
    more = plane_items(here, {"ed": ed_own, "sd": sd_own}, {"ed": ed, "sd": sd}, nz)
    for item in more:
        have_own(item)
    keeps = [(attn_own, attn.at[mine]), (egu_own, egu.at[z]), (sgu_own, sgu.at[z])]
    keeps += [(ed_own, ed.at[x * 2 + c, y]), (sd_own, sd.at[(y * 2 + x) * 2 + c])]
    keeps = [pltpu.make_async_copy(src, dst, stores.at[i]) for i, (src, dst) in enumerate(keeps)]
    for copy in keeps:
        copy.start()
    for d in range(1, nz):
        attn_copy(d, True).wait_recv()
        have_own(items[d])
    items += more
    for item in items:
        item.arrival(0, psend, precv).wait_recv()
        item.copy(2, psend, precv).start()
        item.copy(4, psend, precv).start()
    for item in items:
        item.arrival(1, psend, precv).wait_recv()
        item.copy(5, psend, precv).start()
    for item in items:
        item.arrival(2, psend, precv).wait_recv()
        item.copy(6, psend, precv).start()
    for item in items:
        for number in range(3, 7):
            item.arrival(number, psend, precv).wait_recv()
    for d in range(1, nz):
        for kind in range(4):
            half_copy(kind, d, True).wait_recv()
    for item in items:
        for number in range(7):
            item.copy(number, psend, precv).wait_send()
    for d in range(1, nz):
        attn_copy(d).wait_send()
        for kind in range(4):
            half_copy(kind, d).wait_send()
    for copy in keeps:
        copy.wait()


def first_fast(attn, halves, ed, sd):
    nz = lax.axis_size("z")
    dma = pltpu.SemaphoreType.DMA
    rows = attn[0].shape[0]
    shapes = [(nz * 8, rows, sum(a.shape[1] for a in attn))]
    shapes += [(nz, half.shape[0], 2 * half.shape[1] // nz) for half in halves[::2]]
    own = [pltpu.VMEM(shape[1:], bf16) for shape in shapes] + [pltpu.VMEM(a.shape, bf16) for a in (ed, sd)]
    shapes += [(4, 2, *ed.shape), (8, *sd.shape)]
    attn, egu, sgu, ed, sd = pl.pallas_call(
        functools.partial(first_kernel, nz),
        out_shape=[jax.ShapeDtypeStruct(shape, bf16) for shape in shapes],
        in_specs=any_specs(11),
        out_specs=any_specs(5),
        scratch_shapes=own
        + [dma((11,)), dma((5,)), dma((5, nz)), dma((5, nz)), dma((nz + 3, 7)), dma((nz + 3, 7))],
        compiler_params=params(0, 58 << 20),
        name="first",
    )(*attn, *halves, ed, sd)
    return attn.reshape(-1, attn.shape[-1]), (egu, sgu), ed.reshape(4, -1, ed.shape[-1]), sd.reshape(-1, sd.shape[-1])


def backward_kernel(nz, batches, kinds, *refs):
    refs = list(refs)
    take = lambda n: [refs.pop(0) for _ in range(n)]
    prefix, cosine, sine, grad_in, units, lse = take(6)
    inputs = dict(zip(kinds, take(len(kinds))))
    (rows_in,) = take(1)
    (grads,) = take(1)
    outputs = dict(zip(kinds, take(len(kinds))))
    (rows_total,) = take(1)
    grad, dkey, dvalue, result = take(4)
    buffers = {kind: take(4) for kind in kinds}
    local, send, recv, csend, crecv, load, psend, precv, store = take(9)
    rows_parts, up, down, lload, lsend, lrecv = take(6)
    here = position()
    z, y, x, c = here
    n_dp = nz * 2
    me = z * 2 + y
    width, all_rows = grad_in.shape
    rows = all_rows // batches
    heads = width // HEAD_DIM
    span, length = grad.shape
    count = span // HEAD_DIM
    row_load = pltpu.make_async_copy(rows_in, rows_parts, lload)
    row_load.start()
    greet(
        [(lax.rem(me + d, n_dp) // 2, lax.rem(me + d, 2), x, c) for d in range(1, n_dp)]
        + [(z, y, 1 - x, c), (z, y, x, 1 - c)]
    )

    def columns(number):
        return pl.ds(pl.multiple_of(number * rows, rows), rows)

    def grad_block(number):
        batch, head = unit_owner(number, batches, heads, count)
        return grad_in.at[pl.ds(pl.multiple_of(head * HEAD_DIM, HEAD_DIM), span), columns(batch)]

    def grad_copy(number, source, device):
        return remote(
            grad_block(number), grad.at[:, columns(source)], send.at[number], recv.at[source], (*device, x, c)
        )

    start, arrive, end = exchange(me, n_dp, grad_copy)
    start()
    keep = pltpu.make_async_copy(grad_block(me), grad.at[:, columns(me)], local.at[0])
    keep.start()

    places = {
        "egu": lambda zs: lambda py, px, pc: inputs["egu"].at[px * 2 + pc, zs * 2 + py],
        "sgu": lambda zs: lambda py, px, pc: inputs["sgu"].at[((zs * 2 + py) * 2 + px) * 2 + pc],
    }
    items, finals = [], []
    for kind in kinds:
        for k in range(nz):
            parts = tuple(buffer.at[k] for buffer in buffers[kind])
            item = SumItem(here, len(items), places[kind](k), parts, X_FIRST[kind](k))
            finals.append(pltpu.make_async_copy(item.first, outputs[kind].at[k], store.at[item.index]))
            items.append(item)
    for item in items:
        item.begin(load, psend, precv)
    row_load.wait()
    row_steps, row_end = line_sum_steps(
        z, nz, rows_parts, rows_total, up, down, lsend, lrecv, line_partners(here, nz), row_pieces(rows_parts.shape[1])
    )

    def stage(t):
        if t < len(items):
            items[t].after_core(load, psend, precv)
        if 0 <= t - SUM_LAG < len(items):
            items[t - SUM_LAG].after_second(psend, precv)
        if 0 <= t - 2 * SUM_LAG < len(items):
            items[t - 2 * SUM_LAG].after_first(psend, precv)
            finals[t - 2 * SUM_LAG].start()

    steps = [functools.partial(stage, t) for t in range(len(items) + 2 * SUM_LAG)]
    for step in steps[:2] + row_steps[:2] + steps[2:2]:
        step()
    steps, row_steps = steps[2:], row_steps[2:]
    arrive()
    keep.wait()

    my_batch, my_head = unit_owner(me, batches, heads, count)
    limit = prefix[my_batch, 0]
    inv = 1.0 / math.sqrt(HEAD_DIM)

    def head_rows(source, head):
        _, first_head = unit_owner(source, batches, heads, count)
        return pl.ds(pl.multiple_of((first_head + head) * HEAD_DIM, HEAD_DIM), HEAD_DIM)

    def grads_copy(head):
        def copy(number, source, device):
            batch, _ = unit_owner(source, batches, heads, count)
            return remote(
                result.at[:, pl.ds(head * HEAD_DIM, HEAD_DIM), columns(number)],
                grads.at[:, head_rows(source, head), columns(batch)],
                csend.at[head, number],
                crecv.at[head, source],
                (*device, x, c),
            )

        return copy

    def unrotate(values, place):
        first, second = values[: HEAD_DIM // 2], values[HEAD_DIM // 2 :]
        cos, sin = cosine[:, place], sine[:, place]
        return jnp.concatenate([first * cos + second * sin, second * cos - first * sin], axis=0).astype(bf16)

    def attend(head):
        part = pl.ds(head * HEAD_DIM, HEAD_DIM)
        dkey[...] = jnp.zeros_like(dkey)
        dvalue[...] = jnp.zeros_like(dvalue)
        for first, tile, mask_from, keys in tile_spans(length):
            here_q, upto = pl.ds(first, tile), pl.ds(0, keys)
            queries = units[0, part, here_q] * bf16(inv)
            key, value, out_grad = units[1, part, upto], units[2, part, upto], grad[part, here_q]
            scores = dot(key, queries, ((0,), (0,)))
            probs = jnp.exp(scores - lse[head, :, here_q])
            probs = masked(probs, first, tile, mask_from, keys, limit, 0.0)
            prob_grad = dot(value, out_grad, ((0,), (0,)))
            delta = jnp.sum(probs * prob_grad, axis=0, keepdims=True)
            score_grad = (probs * (prob_grad - delta)).astype(bf16)
            query_grad = dot(key, score_grad, ((1,), (0,))) * inv
            result[0, part, here_q] = unrotate(query_grad, here_q)
            dkey[:, upto] += dot(queries, score_grad, ((1,), (1,)))
            dvalue[:, upto] += dot(out_grad, probs.astype(bf16), ((1,), (1,)))
        result[1, part, :] = unrotate(dkey[...], slice(None))
        result[2, part, :] = dvalue[...].astype(bf16)

    exchanges = [exchange(me, n_dp, grads_copy(head)) for head in range(count)]
    own_copies = [
        pltpu.make_async_copy(
            result.at[:, pl.ds(head * HEAD_DIM, HEAD_DIM), columns(me)],
            grads.at[:, head_rows(me, head), columns(my_batch)],
            local.at[1 + head],
        )
        for head in range(count)
    ]
    for head in range(count):
        attend(head)
        exchanges[head][0]()
        own_copies[head].start()
        for step in steps[:2]:
            step()
        steps = steps[2:]
        for step in row_steps[:LINE_PIECES]:
            step()
        row_steps = row_steps[LINE_PIECES:]
    for step in steps + row_steps:
        step()
    row_end()
    for head in range(count):
        exchanges[head][1]()
        own_copies[head].wait()
    for item in items:
        item.end(psend, precv)
    for final in finals:
        final.wait()
    end()
    for head in range(count):
        exchanges[head][2]()


def backward_fast(prefix, tables, grad, saved, egu, sgu, rows):
    nz = lax.axis_size("z")
    n_dp = nz * 2
    units, lse = saved
    batches = prefix.shape[0]
    span, length = units.shape[1:]
    count = span // HEAD_DIM
    wide = egu.shape[-1]
    arrays = {
        "egu": egu.reshape(4, nz * 2, -1, wide),
        "sgu": sgu.reshape(nz * 8, -1, wide),
    }
    kinds = tuple(arrays)
    rows = rows.reshape(nz, -1, rows.shape[-1])
    any_space, vmem = pl.BlockSpec(memory_space=pl.ANY), pl.BlockSpec(memory_space=pltpu.VMEM)
    block = {kind: arrays[kind].shape[-2:] for kind in kinds}
    results = [((3, *grad.shape), bf16)] + [((nz, *block[kind]), bf16) for kind in kinds]
    results += [(rows.shape[1:], f32)]
    scratch = [
        pltpu.VMEM((span, length), bf16),
        pltpu.VMEM((HEAD_DIM, length), f32),
        pltpu.VMEM((HEAD_DIM, length), f32),
        pltpu.VMEM((3, span, length), bf16),
    ]
    n, items = nz, 2 * nz
    for kind in kinds:
        scratch += [pltpu.VMEM((n, 4, *block[kind]), bf16), pltpu.VMEM((n, 4, *block[kind]), bf16)]
        scratch += [pltpu.VMEM((n, 2, *block[kind]), bf16), pltpu.VMEM((n, *block[kind]), bf16)]
    dma = pltpu.SemaphoreType.DMA
    scratch += [dma((1 + count,)), dma((n_dp,)), dma((n_dp,)), dma((count, n_dp)), dma((count, n_dp))]
    scratch += [dma((items, 4)), dma((items, 7)), dma((items, 7)), dma((items,))]
    line = dma((2, nz, LINE_PIECES))
    scratch += [pltpu.VMEM(rows.shape, bf16)] * 3 + [dma, line, line]
    outs = pl.pallas_call(
        functools.partial(backward_kernel, nz, batches, kinds),
        out_shape=[jax.ShapeDtypeStruct(*result) for result in results],
        in_specs=[pl.BlockSpec(memory_space=pltpu.SMEM), vmem, vmem, any_space, vmem, vmem] + [any_space] * 3,
        out_specs=[any_space] * 3 + [vmem],
        scratch_shapes=scratch,
        compiler_params=params(5, 58 << 20),
        name="attend_backward",
    )(prefix, *tables, grad, units, lse, *arrays.values(), rows)
    grads, egu, sgu, total = outs
    return grads, (egu, sgu), total


class WideSumItem(SumItem):
    def __init__(self, here, index, place, buffers, x_first, starts):
        super().__init__(here, index, place, buffers, x_first)
        self.starts = starts

    def loads(self, a, b, load):
        n = self.slot(a, b)
        for i, (start, src) in enumerate(zip(self.starts, self.place(*self.moved(a, b, 0)[1:]))):
            part = pl.ds(start, src.shape[1])
            yield pltpu.make_async_copy(src, self.own.at[n, :, part], load.at[self.index, n, i])

    def sib_copies(self, a, b, send, recv):
        n = self.slot(a, b)
        for i, (start, src) in enumerate(zip(self.starts, self.place(*self.moved(a, b, 1)[1:]))):
            part = pl.ds(start, src.shape[1])
            sems = send.at[self.index, n, i], recv.at[self.index, n, i]
            yield remote(src, self.sib.at[n, :, part], *sems, self.moved(0, 0, 1))

    def begin(self, load, send, recv):
        for b in (1, 0):
            for a in range(2):
                for copy in (*self.sib_copies(a, b, send, recv), *self.loads(a, b, load)):
                    copy.start()

    def after_core(self, load, wide_send, wide_recv, send, recv):
        for b in (1, 0):
            for a in range(2):
                n = self.slot(a, b)
                for copy in self.loads(a, b, load):
                    copy.wait()
                for copy in self.sib_copies(a, b, wide_send, wide_recv):
                    copy.wait_recv()
                add_to(self.sib.at[n], self.own.at[n])
                if b == 1:
                    self.second_copy(a, send, recv).start()

    def end(self, wide_send, wide_recv, send, recv):
        for a in range(2):
            for b in range(2):
                for copy in self.sib_copies(a, b, wide_send, wide_recv):
                    copy.wait_send()
            self.second_copy(a, send, recv).wait_send()
        self.first_copy(send, recv).wait_send()


def last_kernel(nz, count, *refs):
    refs = list(refs)
    take = lambda n: [refs.pop(0) for _ in range(n)]
    attn_in, (egu_in, sgu_in, ed_in, sd_in) = take(count), take(4)
    attn_out, egu, sgu, ed_out, sd_out = take(5)
    own, sib, second, first, zbuf = take(5)
    ed_parts, sd_parts = take(4), take(4)
    local, load, zsend, zrecv, wsend, wrecv, psend, precv, store, more_load = take(10)
    here = position()
    z, y, x, c = here
    line = [lax.rem(z + d, nz) for d in range(nz)]
    greet([(line[d], y, x, c) for d in range(1, nz)] + [(z, 1 - y, x, c), (z, y, 1 - x, c), (z, y, x, 1 - c)])
    starts, start = [], 0
    for ref in attn_in:
        starts.append(start)
        start += ref.shape[2]
    far_first = sorted(range(nz), key=lambda d: abs(d - nz / 2))
    items = []
    for d in far_first:
        place = lambda py, px, pc, zs=line[d]: [ref.at[((zs * 2 + py) * 2 + px) * 2 + pc] for ref in attn_in]
        parts = (own.at[d], sib.at[d], second.at[d], first.at[d])
        items.append((d, WideSumItem(here, d, place, parts, d % 2 == 1, starts)))
    half = ed_in.shape[2] // 2
    more = []
    for h in range(2):
        rows = pl.ds(h * half, half)
        place = lambda py, px, pc, rows=rows: ed_in.at[px * 2 + pc, py, rows]
        more.append(SumItem(here, nz + h, place, tuple(p.at[h] for p in ed_parts), X_FIRST["ed"](h)))
        more[-1].total = ed_out.at[rows]
    place = lambda py, px, pc: sd_in.at[(py * 2 + px) * 2 + pc]
    more.append(SumItem(here, nz + 2, place, tuple(p.at[0] for p in sd_parts), X_FIRST["sd"](0)))
    more[-1].total = sd_out
    for _, item in items:
        item.begin(load, wsend, wrecv)
    for item in more:
        item.begin(more_load, psend, precv)

    def line_copy(kind, d, arriving=False):
        to, frm = line[d], line[(nz - d) % nz]
        at = frm if arriving else z
        dst = (zbuf, egu, sgu)[kind].at[at]
        src = dst if arriving else (first.at[d], egu_in.at[to], sgu_in.at[to])[kind]
        return remote(src, dst, zsend.at[kind, d], zrecv.at[kind, d], (to, y, x, c))

    for kind in (1, 2):
        for d in far_first[:-1]:
            line_copy(kind, d).start()
    pairs = ((egu_in, egu), (sgu_in, sgu))
    keeps = [pltpu.make_async_copy(src.at[z], dst.at[z], local.at[i]) for i, (src, dst) in enumerate(pairs)]
    for copy in keeps:
        copy.start()
    mine = pltpu.make_async_copy(first.at[0], zbuf.at[z], store)
    both = items + [(None, item) for item in more]
    for t in range(len(both) + 2 * SUM_LAG):
        if t < len(items):
            items[t][1].after_core(load, wsend, wrecv, psend, precv)
        elif t < len(both):
            both[t][1].after_core(more_load, psend, precv)
        if 0 <= t - SUM_LAG < len(both):
            both[t - SUM_LAG][1].after_second(psend, precv)
        if 0 <= t - 2 * SUM_LAG:
            d, item = both[t - 2 * SUM_LAG]
            item.after_first(psend, precv, None if d is not None else item.total)
            if d == 0:
                mine.start()
            elif d is not None:
                line_copy(0, d).start()
    for copy in keeps:
        copy.wait()
    for kind in (1, 2):
        for d in range(1, nz):
            line_copy(kind, d, True).wait_recv()
    mine.wait()
    for d in range(1, nz):
        line_copy(0, d, True).wait_recv()
    attn_out[...] = sum(zbuf[k].astype(f32) for k in range(nz))
    for _, item in items:
        item.end(wsend, wrecv, psend, precv)
    for item in more:
        item.end(psend, precv)
    for kind in range(3):
        for d in range(1, nz):
            line_copy(kind, d).wait_send()


def last_fast(attn, egu, sgu, ed, sd):
    nz = lax.axis_size("z")
    dma = pltpu.SemaphoreType.DMA
    attn = [part.reshape(nz * 8, -1, part.shape[-1]) for part in attn]
    rows, columns = attn[0].shape[1], sum(part.shape[2] for part in attn)
    width = attn[0].shape[0] * rows
    block = (rows, columns)
    vmem = pl.BlockSpec(memory_space=pltpu.VMEM)
    shapes = [block, egu.shape, sgu.shape]
    ed, sd = ed.reshape(4, 2, -1, width), sd.reshape(8, -1, width)
    shapes += [ed.shape[2:], sd.shape[1:]]
    half = (ed.shape[2] // 2, width)
    count = len(attn)
    types = (f32, bf16, bf16, f32, f32)
    return pl.pallas_call(
        functools.partial(last_kernel, nz, count),
        out_shape=[jax.ShapeDtypeStruct(*both) for both in zip(shapes, types)],
        in_specs=any_specs(count + 4),
        out_specs=[vmem] * 5,
        scratch_shapes=[
            pltpu.VMEM((nz, 4, *block), bf16),
            pltpu.VMEM((nz, 4, *block), bf16),
            pltpu.VMEM((nz, 2, *block), bf16),
            pltpu.VMEM((nz, *block), bf16),
            pltpu.VMEM((nz, *block), bf16),
            *[pltpu.VMEM((2, *n, *half), bf16) for n in ((4,), (4,), (2,), ())],
            *[pltpu.VMEM((1, *n, *shapes[-1]), bf16) for n in ((4,), (4,), (2,), ())],
            dma((2,)),
            dma((nz, 4, count)),
            dma((3, nz)),
            dma((3, nz)),
            dma((nz, 4, count)),
            dma((nz, 4, count)),
            dma((nz + 3, 7)),
            dma((nz + 3, 7)),
            dma,
            dma((nz + 3, 4)),
        ],
        compiler_params=params(3, 58 << 20),
        name="last",
    )(*attn, egu, sgu, ed, sd)


def finish_kernel(*refs):
    attn, egu, sgu, ed, sd, attended, out_sum = refs[:7]
    squares, (sgate, sup, sdown, egate, eup, edown, block_out) = refs[7:11], refs[11:]
    width = attended.shape[1]
    for i, ref in enumerate(squares):
        ref[...] = attn[:, pl.ds(i * width, width)]
    for source, outs in ((egu, (egate, eup)), (sgu, (sgate, sup))):
        planes, ff = source.shape[0], source.shape[2] // 2
        for k in range(planes):
            for j in range(2):
                outs[j][:, pl.ds(k * ff, ff)] = source[k, :, pl.ds(j * ff, ff)].astype(f32)
    edown[...] = ed[...]
    sdown[...] = sd[...]
    block_out[...] = (attended[...] + out_sum[...]).astype(bf16)


def finish_fast(sums, attended, out_sum):
    attn, egu, sgu, ed, sd = sums
    width = attended.shape[1]
    shapes = [(attn.shape[0], width)] * 4
    shapes += [(sgu.shape[1], sgu.shape[0] * sgu.shape[2] // 2)] * 2 + [sd.shape]
    shapes += [(egu.shape[1], egu.shape[0] * egu.shape[2] // 2)] * 2 + [ed.shape]
    return pl.pallas_call(
        finish_kernel,
        out_shape=[jax.ShapeDtypeStruct(shape, f32) for shape in shapes]
        + [jax.ShapeDtypeStruct(attended.shape, bf16)],
        compiler_params=pltpu.CompilerParams(vmem_limit_bytes=32 << 20),
        name="finish",
    )(attn, egu, sgu, ed, sd, attended, out_sum)


ORDER = ((0, 1, 2, 3), (1, 0, 2, 3), (2, 3, 1, 0), (3, 2, 1, 0))
EXTRA = 16


def by_distance(z, index):
    code = jnp.int32(0)
    for plane, order in enumerate(ORDER):
        code = jnp.where(z == plane, sum(p * 4**i for i, p in enumerate(order)), code)
    for _ in range(3):
        code = jnp.where(index > 0, code // 4, code)
        index = index - 1
    return lax.rem(code, 4)


def ffn_kernel(capacity, *refs):
    refs = list(refs)
    take = lambda n: [refs.pop(0) for _ in range(n)]
    mixed_in, cot_in, router_in, *weights_in = take(7)
    out_part, total, *grads = take(6)
    weights = take(4)
    egu, sgu, ed, sd = weights
    mixed, cot, router, arrived, pair_grad, expert_hidden, act_grad, s_hidden, s_grad = take(9)
    slot_out, slot_grad, hots, gate_dot, outs, parts, up, down, wide_stage, deep_stage = take(10)
    local, loads, gsend, grecv, ssend, srecv, stores = take(7)
    here = position()
    z, y, x, c = here
    nz = 4
    neighbour = line_partners(here, nz)
    experts = egu.shape[0]
    rows, width = mixed_in.shape
    group = 128
    groups = rows // group
    slots = groups * capacity
    ff = ed.shape[1]

    loading = [pltpu.make_async_copy(router_in, router, local.at[0])]
    loading += [pltpu.make_async_copy(mixed_in, mixed.at[z], local.at[1])]
    loading += [pltpu.make_async_copy(cot_in, cot, local.at[2])]
    shared_loads = [
        pltpu.make_async_copy(weights_in[1], sgu, local.at[3]),
        pltpu.make_async_copy(weights_in[3], sd, local.at[4]),
    ]
    for copy in loading:
        copy.start()

    def expert_loads(e):
        return [
            pltpu.make_async_copy(weights_in[0].at[e], egu.at[e], loads.at[0, e]),
            pltpu.make_async_copy(weights_in[2].at[e], ed.at[e], loads.at[1, e]),
        ]

    for e in range(experts):
        for copy in expert_loads(e):
            copy.start()
    for copy in shared_loads:
        copy.start()
    greet_line(here, nz)

    def may_send(way):
        return z < nz - 1 if way == 0 else z > 0

    def chunk_copy(way, source, src=None):
        dst = mixed.at[source]
        return remote(dst if src is None else src, dst, gsend.at[way, source], grecv.at[way, source], neighbour(1 - 2 * way))

    for way in range(2):
        pl.when(may_send(way))(lambda: chunk_copy(way, z, mixed_in).start())

    def receive(source):
        for way in range(2):

            @pl.when(source < z if way == 0 else source > z)
            def _():
                chunk_copy(way, source).wait_recv()
                pl.when(may_send(way))(lambda: chunk_copy(way, source).start())

    piece_rows = (pl.ds(0, group), pl.ds(group, parts.shape[1] - group))
    came = (up, down)

    def part_copy(way, target, piece):
        part = piece_rows[piece]
        return remote(
            parts.at[target, part],
            came[way].at[target, part],
            ssend.at[way, target, piece],
            srecv.at[way, target, piece],
            neighbour(1 - 2 * way),
        )

    def relay(target, piece):
        part = piece_rows[piece]
        for way in range(2):
            ahead = z < target if way == 0 else z > target
            inner = z > 0 if way == 0 else z < nz - 1

            @pl.when(ahead & inner)
            def _():
                part_copy(way, target, piece).wait_recv()
                mine, theirs = parts.at[target, part], came[way].at[target, part]
                mine[...] = (mine[...].astype(f32) + theirs[...].astype(f32)).astype(bf16)

            pl.when(ahead)(lambda: part_copy(way, target, piece).start())

    for copy in loading:
        copy.wait()

    sub = lax.broadcasted_iota(jnp.int32, (8, group), 0).astype(f32)
    before = lax.broadcasted_iota(jnp.int32, (group, group), 0) < lax.broadcasted_iota(jnp.int32, (group, group), 1)
    before = jnp.where(before, 1.0, 0.0).astype(bf16)
    slot_iota = lax.broadcasted_iota(jnp.int32, (capacity, group), 0).astype(f32)

    def chunk(index, source):
        tokens = mixed.at[source]
        named, ranks, probs = [], [], []
        for g in range(groups):
            lanes = pl.ds(g * group, group)
            ids = cot[source, pl.ds(rows, EXTRA), lanes].astype(f32)
            hot = jnp.where((sub == ids[0:1]) | (sub == ids[1:2]), 1.0, 0.0)
            logits = dot(router[...], mixed[source, lanes, :], ((1,), (1,)))[:8]
            top = jnp.max(jnp.where(hot > 0, logits, neg_fill), axis=0, keepdims=True)
            powers = jnp.where(hot > 0, jnp.exp(logits - top), 0.0)
            probs.append(powers / jnp.sum(powers, axis=0, keepdims=True))
            rank = dot(jnp.concatenate([hot, hot], axis=0).astype(bf16), before, ((1,), (0,)))[:8]
            ranks.append(jnp.where(hot > 0, rank, float(group * TOP_K)))
        gate_dot[...] = jnp.zeros_like(gate_dot)

        def row_of(table, e):
            return jnp.sum(jnp.where(sub == e.astype(f32), table, 0.0), axis=0, keepdims=True)

        @pl.loop(0, experts)
        def _(e):
            @pl.when(index == 0)
            def _():
                for copy in expert_loads(e):
                    copy.wait()

            here_slots = pl.ds(pl.multiple_of(source * slots, 16), slots)
            hot_of, prob_of, cot_of = [], [], []
            for g in range(groups):
                lanes = pl.ds(g * group, group)
                hot = jnp.where(slot_iota == row_of(ranks[g], e), 1.0, 0.0)
                prob_of.append(jnp.sum(hot * row_of(probs[g], e), axis=1, keepdims=True))
                low_hot = hot.astype(bf16)
                hots[g, pl.ds(pl.multiple_of(e * capacity, 16), capacity), :] = low_hot
                hot_of.append(hot)
                mine = pl.ds(pl.multiple_of(source * slots + g * capacity, 16), capacity)
                arrived[e, mine, :] = dot(low_hot, mixed[source, lanes, :], ((1,), (0,))).astype(bf16)
                picked = dot(low_hot, cot[source, lanes, :], ((1,), (0,)))
                cot_of.append(picked)
                pair_grad[e, mine, :] = (picked * prob_of[g]).astype(bf16)
            act = dot(arrived[e, here_slots, :], egu[e], ((1,), (0,)))
            hidden_grad = dot(pair_grad[e, here_slots, :], ed[e], ((1,), (1,)))
            gate_act, up_act = act[:, :ff], act[:, ff:]
            sig = jax.nn.sigmoid(gate_act)
            silu = gate_act * sig
            hidden = (silu * up_act).astype(bf16)
            expert_hidden[e, here_slots, :] = hidden
            gate_grad = (hidden_grad * up_act * (sig * (1.0 + gate_act * (1.0 - sig)))).astype(bf16)
            up_grad = (hidden_grad * silu).astype(bf16)
            act_grad[e, here_slots, pl.ds(0, ff)] = gate_grad
            act_grad[e, here_slots, pl.ds(ff, ff)] = up_grad
            out = dot(hidden, ed[e], ((1,), (0,)))
            back = dot(act_grad[e, here_slots, :], egu[e], ((1,), (1,)))
            for g in range(groups):
                mine, stack = slice(g * capacity, (g + 1) * capacity), pl.ds(pl.multiple_of(e * capacity, 16), capacity)
                lanes = pl.ds(g * group, group)
                slot_out[g, stack, :] = (out[mine] * prob_of[g]).astype(bf16)
                slot_grad[g, stack, :] = back[mine].astype(bf16)
                dots = jnp.sum(out[mine] * cot_of[g], axis=1, keepdims=True)
                dots = jnp.sum(hot_of[g] * dots, axis=0, keepdims=True)
                gate_dot[:, lanes] += jnp.where(sub == e.astype(f32), dots, 0.0)

        @pl.when(index == 0)
        def _():
            for copy in shared_loads:
                copy.wait()

        act = dot(tokens[...], sgu[...], ((1,), (0,)))
        hidden_grad = dot(cot[source, pl.ds(0, rows), :], sd[...], ((1,), (1,)))
        gate_act, up_act = act[:, :ff], act[:, ff:]
        sig = jax.nn.sigmoid(gate_act)
        silu = gate_act * sig
        hidden = (silu * up_act).astype(bf16)
        mine = pl.ds(pl.multiple_of(source * rows, 16), rows)
        s_hidden[mine, :] = hidden
        s_grad[mine, pl.ds(0, ff)] = (hidden_grad * up_act * (sig * (1.0 + gate_act * (1.0 - sig)))).astype(bf16)
        s_grad[mine, pl.ds(ff, ff)] = (hidden_grad * silu).astype(bf16)
        out = dot(hidden, sd[...], ((1,), (0,)))
        back = dot(s_grad[mine, :], sgu[...], ((1,), (1,)))
        for g in range(groups):
            lanes = pl.ds(g * group, group)
            span = slice(g * group, (g + 1) * group)
            outs[source, lanes, :] = (out[span] + dot(hots[g], slot_out[g], ((0,), (0,)))).astype(bf16)
            parts[source, lanes, :] = (back[span] + dot(hots[g], slot_grad[g], ((0,), (0,)))).astype(bf16)
        dots = jnp.concatenate([gate_dot[...], jnp.zeros((EXTRA - 8, rows), f32)], axis=0)
        parts[source, pl.ds(rows, EXTRA), :] = jnp.concatenate(
            [dots, jnp.zeros((EXTRA, width - rows), f32)], axis=1
        ).astype(bf16)

    inner = (z > 0) & (z < nz - 1)

    @pl.loop(0, nz)
    def _(index):
        source = by_distance(z, index)
        pl.when((index == 1) | (index == 3) | ((index == 2) & jnp.logical_not(inner)))(lambda: receive(source))
        pl.when((index == 1) & inner)(lambda: receive(by_distance(z, jnp.int32(2))))
        chunk(index, source)

        @pl.when(jnp.logical_not(inner) & (index > 0))
        def _():
            for piece in range(2):
                relay(source, piece)

        @pl.when(inner & (index == 3))
        def _():
            for piece in range(2):
                relay(by_distance(z, jnp.int32(2)), piece)

    out_copy = pltpu.make_async_copy(outs, out_part, local.at[5])
    out_copy.start()
    far, near = by_distance(z, jnp.int32(3)), by_distance(z, jnp.int32(1))

    def stage_copies(e, slot):
        return [
            pltpu.make_async_copy(wide_stage.at[slot], grads[0].at[e], stores.at[0, slot]),
            pltpu.make_async_copy(deep_stage.at[slot], grads[2].at[e], stores.at[1, slot]),
        ]

    def weight_grads(slot, rows_in, wide, hidden, deep):
        for k in range(0, wide.shape[1], 512):
            span = pl.ds(k, 512)
            wide_stage[slot, :, span] = dot(rows_in[...], wide[:, span], ((0,), (0,))).astype(bf16)
        deep_stage[slot] = dot(hidden[...], deep[...], ((0,), (0,))).astype(bf16)

    @pl.loop(0, experts)
    def _(e):
        slot = lax.rem(e, 2)

        @pl.when(e >= 2)
        def _():
            for copy in stage_copies(e - 2, slot):
                copy.wait()

        weight_grads(slot, arrived.at[e], act_grad.at[e], expert_hidden.at[e], pair_grad.at[e])
        for copy in stage_copies(e, slot):
            copy.start()
        pl.when(inner & (e == 1))(lambda: relay(far, 0))
        pl.when(inner & (e == 2))(lambda: relay(far, 1))
        pl.when(inner & (e == 3))(lambda: relay(near, 0))

    for copy in stage_copies(experts - 2, 0):
        copy.wait()
    tokens = mixed.reshape(nz * rows, width)
    for k in range(0, 2 * ff, 512):
        span = pl.ds(k, 512)
        wide_stage[0, :, span] = dot(tokens[...], s_grad[:, span], ((0,), (0,))).astype(bf16)
    cots = jnp.concatenate([cot[k, pl.ds(0, rows), :] for k in range(nz)], axis=0)
    deep_stage[0] = dot(s_hidden[...], cots, ((0,), (0,))).astype(bf16)
    shared_stores = [
        pltpu.make_async_copy(wide_stage.at[0], grads[1], stores.at[0, 0]),
        pltpu.make_async_copy(deep_stage.at[0], grads[3], stores.at[1, 0]),
    ]
    for copy in shared_stores:
        copy.start()
    pl.when(inner)(lambda: relay(near, 1))
    total[...] = parts[z].astype(f32)
    for way in range(2):

        @pl.when(z > 0 if way == 0 else z < nz - 1)
        def _():
            for piece in range(2):
                part_copy(way, z, piece).wait_recv()
            total[...] += came[way][z].astype(f32)

    for copy in stage_copies(experts - 1, 1) + shared_stores + [out_copy]:
        copy.wait()
    for way in range(2):
        for plane in range(nz):
            sent = (plane <= z if way == 0 else plane >= z) & may_send(way)
            pl.when(sent)(lambda: chunk_copy(way, plane).wait_send())

            @pl.when(z < plane if way == 0 else z > plane)
            def _():
                for piece in range(2):
                    part_copy(way, plane, piece).wait_send()


def ffn_fast(mixed, cot, router, weights, capacity):
    nz = lax.axis_size("z")
    egu, sgu, ed, sd = weights
    rows, width = mixed.shape
    experts, ff = ed.shape[:2]
    cot = cot.reshape(nz, -1, width)
    slots = nz * rows // 128 * capacity
    groups = rows // 128
    vmem, dma = pltpu.VMEM, pltpu.SemaphoreType.DMA
    low = lambda *shape: vmem(shape, bf16)
    scratch = [low(*w.shape) for w in weights]
    scratch += [low(nz, rows, width), low(*cot.shape), low(*router.shape)]
    scratch += [low(experts, slots, width), low(experts, slots, width)]
    scratch += [low(experts, slots, ff), low(experts, slots, 2 * ff), low(nz * rows, ff), low(nz * rows, 2 * ff)]
    stack = experts * capacity
    scratch += [low(groups, stack, width), low(groups, stack, width), low(groups, stack, 128), vmem((8, rows), f32)]
    scratch += [low(nz, rows, width)] + [low(*cot.shape)] * 3
    scratch += [low(2, width, 2 * ff), low(2, ff, width)]
    scratch += [dma((6,)), dma((2, experts)), dma((2, nz)), dma((2, nz)), dma((2, nz, 2)), dma((2, nz, 2)), dma((2, 2))]
    any_space = pl.BlockSpec(memory_space=pl.ANY)
    out_part, total, *grads = pl.pallas_call(
        functools.partial(ffn_kernel, capacity),
        out_shape=[
            jax.ShapeDtypeStruct((nz, rows, width), bf16),
            jax.ShapeDtypeStruct((rows + EXTRA, width), f32),
        ]
        + [jax.ShapeDtypeStruct(w.shape, bf16) for w in weights],
        in_specs=any_specs(7),
        out_specs=[any_space, pl.BlockSpec(memory_space=pltpu.VMEM)] + [any_space] * 4,
        scratch_shapes=scratch,
        compiler_params=params(1, 60 << 20),
        name="feed_forward",
    )(mixed, cot, router, *weights)
    return out_part, total, grads


def visible_units(prefix, heads, here, length):
    unit = lax.axis_index(DP) * here + jnp.arange(here)
    lengths = prefix[jnp.minimum(unit // heads, prefix.shape[0] - 1), 0]
    pos = jnp.arange(length, dtype=jnp.int32)
    low = pos[None, :] < lengths[:, None]
    return (pos[None, None, :] <= pos[None, :, None]) | (low[:, :, None] & low[:, None, :])


def attention_forward(qkv, batches, heads, prefix):
    units = to_units(qkv)
    q, k, v = units[:, 0], units[:, 1], units[:, 2]
    allowed = visible_units(prefix, heads, q.shape[0], q.shape[-1])
    scores = dot(q, k, ((1,), (1,)), ((0,), (0,))) * (1.0 / math.sqrt(HEAD_DIM))
    scores = jnp.where(allowed, scores, neg_fill)
    top = jnp.max(scores, axis=-1, keepdims=True)
    weights = jnp.exp(scores - top)
    total = jnp.sum(weights, axis=-1, keepdims=True)
    lse = top + jnp.log(total)
    probs = (weights / total).astype(bf16)
    context = dot(v, probs, ((2,), (2,)), ((0,), (0,))).astype(bf16)
    return from_units(context[:, None], batches, heads)[0], (q, k, v, lse)


def attention_backward(context_grad, saved, batches, heads, prefix):
    q, k, v, lse = saved
    grad = to_units(context_grad[None])[:, 0]
    allowed = visible_units(prefix, heads, q.shape[0], q.shape[-1])
    inv = 1.0 / math.sqrt(HEAD_DIM)
    scores = dot(q, k, ((1,), (1,)), ((0,), (0,))) * inv
    probs = jnp.where(allowed, jnp.exp(scores - lse), 0.0)
    prob_grad = dot(grad, v, ((1,), (1,)), ((0,), (0,)))
    delta = jnp.sum(probs * prob_grad, axis=-1, keepdims=True)
    score_grad = (probs * (prob_grad - delta)).astype(bf16)
    dq = dot(k, score_grad, ((2,), (2,)), ((0,), (0,))) * inv
    dk = dot(q, score_grad, ((2,), (1,)), ((0,), (0,))) * inv
    dv = dot(grad, probs.astype(bf16), ((2,), (1,)), ((0,), (0,)))
    return from_units(jnp.stack([dq, dk, dv], axis=1).astype(bf16), batches, heads)


def by_batch(tensor, batches):
    kinds, width, count = tensor.shape
    return jnp.transpose(tensor.reshape(kinds, width, batches, count // batches), (0, 2, 1, 3))


def gates(mixed_rows, pair_ids, router_w):
    hot = (pair_ids[..., None] == jnp.arange(router_w.shape[1], dtype=jnp.int32)).astype(f32)
    logits = dot(mixed_rows, router_w, ((1,), (0,)))
    return hot, jax.nn.softmax(jnp.sum(hot * logits[:, None, :], axis=-1), axis=-1)


def ffn_plain(mixed, cot_line, router_w, weights, capacity, rows):
    nz, (count, width), experts = lax.axis_size("z"), mixed.shape, router_w.shape[1]
    egu, sgu, ed, sd = weights
    slice_ff = sd.shape[0]
    cot_line = cot_line.reshape(nz, -1, width)
    mixed_line = gather_line(mixed)
    cot_rows = cot_line[:, :count].reshape(nz * count, width)
    ids = jnp.transpose(cot_line[:, count : count + TOP_K, :count], (0, 2, 1)).reshape(-1, TOP_K).astype(jnp.int32)
    lines = mixed_line.shape[0]
    groups = lines // rows

    hot, probs = gates(mixed_line, ids, router_w)
    hot_int = hot.astype(jnp.int32).reshape(groups, rows * TOP_K, experts)
    earlier = jnp.cumsum(hot_int, axis=1) - hot_int
    rank = jnp.sum(earlier * hot_int, axis=-1).reshape(groups, rows, TOP_K)
    group_ids = ids.reshape(groups, rows, TOP_K)
    slot = jnp.where(rank < capacity, group_ids * capacity + rank, experts * capacity)
    slot_hot = (slot[..., None] == jnp.arange(experts * capacity, dtype=jnp.int32)).astype(bf16)
    token_hot = jnp.sum(slot_hot, axis=2)
    slot_probs = jnp.sum(slot_hot.astype(f32) * probs.reshape(groups, rows, TOP_K, 1), axis=(1, 2))

    def dispatch(values):
        per_group = dot(token_hot, values.reshape(groups, rows, width), ((1,), (1,)), ((0,), (0,)))
        per_group = per_group.reshape(groups, experts, capacity, width)
        return jnp.transpose(per_group, (1, 0, 2, 3)).reshape(experts, groups * capacity, width)

    def per_slot(values):
        return jnp.transpose(values.reshape(groups, experts, capacity), (1, 0, 2)).reshape(experts, -1, 1)

    def combine(slots):
        per_group = jnp.transpose(slots.reshape(experts, groups, capacity, width), (1, 0, 2, 3))
        per_group = per_group.reshape(groups, experts * capacity, width)
        return dot(token_hot, per_group, ((2,), (1,)), ((0,), (0,))).reshape(lines, width)

    slot_p = per_slot(slot_probs)
    arrived = dispatch(mixed_line).astype(bf16)
    cot_slots = dispatch(cot_rows)
    pair_grad = (cot_slots * slot_p).astype(bf16)
    batch = ((0,), (0,))
    act = dot(arrived, egu, ((2,), (1,)), batch)
    gate_act, up_act = act[..., :slice_ff], act[..., slice_ff:]
    sig = jax.nn.sigmoid(gate_act)
    silu_act = gate_act * sig
    expert_hidden = (silu_act * up_act).astype(bf16)
    expert_out = dot(expert_hidden, ed, ((2,), (1,)), batch)
    hidden_grad = dot(pair_grad, ed, ((2,), (2,)), batch)
    gate_up_grad = jnp.concatenate(
        [hidden_grad * up_act * sig * (1.0 + gate_act * (1.0 - sig)), hidden_grad * silu_act], axis=-1
    ).astype(bf16)
    grad_egu = dot(arrived, gate_up_grad, ((1,), (1,)), batch).astype(bf16)
    grad_ed = dot(expert_hidden, pair_grad, ((1,), (1,)), batch).astype(bf16)
    slot_grad = dot(gate_up_grad, egu, ((2,), (2,)), batch).astype(bf16)
    gate_dot = jnp.sum(cot_slots * expert_out, axis=-1)
    gate_dot = jnp.transpose(gate_dot.reshape(experts, groups, capacity), (1, 0, 2)).reshape(groups, 1, 1, -1)
    pair_dot = jnp.sum(slot_hot.astype(f32) * gate_dot, axis=-1).reshape(lines, TOP_K)
    expert_sum = combine((expert_out * slot_p).astype(bf16))

    s_act = dot(mixed_line, sgu, ((1,), (0,)))
    s_in, s_lift = s_act[:, :slice_ff], s_act[:, slice_ff:]
    s_sig = jax.nn.sigmoid(s_in)
    s_silu = s_in * s_sig
    s_hidden = (s_silu * s_lift).astype(bf16)
    s_hidden_grad = dot(cot_rows, sd, ((1,), (1,)))
    s_grad = jnp.concatenate(
        [s_hidden_grad * s_lift * s_sig * (1.0 + s_in * (1.0 - s_sig)), s_hidden_grad * s_silu], axis=-1
    ).astype(bf16)
    grad_sgu = dot(mixed_line, s_grad, ((0,), (0,))).astype(bf16)
    grad_sd = dot(s_hidden, cot_rows, ((0,), (0,))).astype(bf16)
    out_part = (dot(s_hidden, sd, ((1,), (0,))) + expert_sum).astype(bf16)
    mixed_part = combine(slot_grad) + dot(s_grad, sgu, ((1,), (1,)))
    pair_dot = jnp.sum(hot * pair_dot[..., None], axis=1).reshape(nz, count, experts)
    pair_dot = jnp.pad(jnp.transpose(pair_dot, (0, 2, 1)), ((0, 0), (0, EXTRA - experts), (0, width - count)))
    mixed_part = jnp.concatenate([mixed_part.reshape(nz, count, width), pair_dot], axis=1).astype(bf16)
    mixed_sum = sum_line(mixed_part.reshape(-1, width)).astype(f32)
    return out_part, mixed_sum, (grad_egu, grad_sgu, grad_ed, grad_sd)


def shards(
    hidden,
    routes,
    prefix,
    cotangent,
    attn_gain,
    w_query,
    w_key,
    w_value,
    w_output,
    ffn_gain,
    router,
    shared_gate,
    shared_up,
    shared_down,
    expert_gate,
    expert_up,
    expert_down,
):
    nz = lax.axis_size("z")
    batches, _, rows, width = hidden.shape
    count = batches * rows
    heads = width // HEAD_DIM
    experts = router.shape[1]
    own = router.shape[0]
    capacity = (5 * rows * TOP_K + 4 * experts - 1) // (4 * experts)
    slice_ff = shared_gate.shape[1] // nz

    misc = jnp.concatenate(
        [router, attn_gain[:, None], ffn_gain[:, None], jnp.zeros((own, MISC - experts - 2), bf16)], axis=1
    )
    attn_shard = (w_query, w_key, w_value, w_output, misc)
    cot = cotangent.reshape(count, width)
    pair_ids = routes.reshape(count, TOP_K)
    ids_rows = jnp.pad(pair_ids.T.astype(bf16), ((0, EXTRA - TOP_K), (0, width - count)))
    halves = (expert_gate[0], expert_up[0], shared_gate, shared_up)

    def slices(gate, up):
        both = jnp.stack([gate.reshape(-1, nz, slice_ff), up.reshape(-1, nz, slice_ff)], axis=2)
        return jnp.transpose(both.reshape(-1, nz, 2 * slice_ff), (1, 0, 2))

    fast = paired(batches, heads)
    if fast:
        attn_full, lined, ed, sd = first_fast(attn_shard, halves, expert_down[0], shared_down)
    else:
        attn_full = gather_all(jnp.concatenate(attn_shard, axis=1))

    w_qkv = attn_full[:, : 3 * width]
    w_out = attn_full[:, 3 * width : 4 * width]
    misc_full = attn_full[:, 4 * width :]
    router_w = misc_full[:, :experts]
    gain_attn = misc_full[:, experts].astype(f32)
    gain_ffn = misc_full[:, experts + 1].astype(f32)

    x_in = hidden.reshape(count, width).astype(f32)
    attn_scale = rms_scale(x_in)
    attn_norm = x_in * attn_scale
    normed = (attn_norm * gain_attn).astype(bf16)
    positions = lax.axis_index(DP) * rows + jnp.arange(rows, dtype=jnp.int32)
    cosine, sine = rotary_tables(jnp.tile(positions, batches))
    projected = dot(w_qkv, normed, ((0,), (1,)))
    turned = rotate_t(projected[: 2 * width], cosine, sine, 1.0)
    qkv = jnp.concatenate([turned, projected[2 * width :]], axis=0).astype(bf16).reshape(3, width, count)
    if fast:
        context, saved, egu, sgu, cot_line = attend_fast(prefix, qkv, *lined, cotangent, ids_rows)
        ffn = egu, sgu, ed, sd
    else:
        context, saved = attention_forward(by_batch(qkv, batches), batches, heads, prefix)
        context = jnp.transpose(context, (1, 0, 2)).reshape(width, count)
        ffn = gather_weights(slices(*halves[:2]), slices(*halves[2:]), expert_down[0], shared_down)
        cot_line = gather_line(jnp.concatenate([cot, ids_rows], axis=0))
    attended = x_in + dot(context, w_out, ((0,), (0,)))
    ffn_scale = rms_scale(attended)
    ffn_norm = attended * ffn_scale
    mixed = (ffn_norm * gain_ffn).astype(bf16)

    if fast:
        router_rows = jnp.pad(router_w.T, ((0, 16 - experts), (0, 0)))
        out_part, mixed_sum, ffn_grads = ffn_fast(mixed, cot_line, router_rows, ffn, capacity)
    else:
        out_part, mixed_sum, ffn_grads = ffn_plain(mixed, cot_line, router_w, ffn, capacity, rows)

    hot, probs = gates(mixed, pair_ids, router_w)
    gate_grads = jnp.sum(hot * mixed_sum[count : count + experts, :count].T[:, None, :], axis=-1)
    picked = probs * (gate_grads - jnp.sum(probs * gate_grads, axis=-1, keepdims=True))
    logit_grad = jnp.sum(hot * picked[..., None], axis=1)
    grad_router = jnp.dot(mixed.astype(f32).T, logit_grad, precision=highest)
    mixed_grad = mixed_sum[:count] + jnp.dot(logit_grad, router_w.astype(f32).T, precision=highest)
    cot_wide = cot.astype(f32)
    inner = mixed_grad * gain_ffn
    grad_gffn = jnp.sum(mixed_grad * ffn_norm, axis=0)
    attended_grad = cot_wide + ffn_scale * (inner - ffn_norm * jnp.mean(inner * ffn_norm, axis=-1, keepdims=True))
    out_grad = attended_grad.astype(bf16)
    grad_wout = dot(context, out_grad, ((1,), (0,)))
    context_grad = dot(w_out, out_grad, ((1,), (1,))).astype(bf16)

    if fast:
        tables = rotary_tables(jnp.arange(rows * lax.axis_size(DP), dtype=jnp.int32))
        qkv_grad, lined, out_sum = backward_fast(prefix, tables, context_grad, saved, *ffn_grads[:2], out_part)
        qkv_grad = qkv_grad.reshape(3 * width, count)
    else:
        context_grad = by_batch(context_grad[None], batches)[0]
        rot_grad = attention_backward(context_grad, saved, batches, heads, prefix)
        rot_grad = jnp.transpose(rot_grad, (0, 2, 1, 3)).reshape(3 * width, count).astype(f32)
        turned = rotate_t(rot_grad[: 2 * width], cosine, sine, -1.0)
        qkv_grad = jnp.concatenate([turned, rot_grad[2 * width :]], axis=0).astype(bf16)
        egu_sum, sgu_sum, ed_sum, sd_sum = sum_weights(*ffn_grads)
        out_sum = sum_line(out_part)
    grad_wqkv = dot(normed, qkv_grad, ((0,), (1,)))
    normed_grad = dot(qkv_grad, w_qkv, ((0,), (1,)))
    grad_gattn = jnp.sum(normed_grad * attn_norm, axis=0)
    inner = normed_grad * gain_attn
    input_grad = (
        attended_grad + attn_scale * (inner - attn_norm * jnp.mean(inner * attn_norm, axis=-1, keepdims=True))
    ).astype(bf16)

    grad_misc = jnp.concatenate(
        [grad_router, grad_gattn[:, None], grad_gffn[:, None], jnp.zeros((width, MISC - experts - 2), f32)], axis=1
    )
    attn_parts = [part.astype(bf16) for part in (grad_wqkv, grad_wout, grad_misc)]

    def joined(blocks):
        both = jnp.transpose(blocks.reshape(nz, -1, 2, slice_ff), (2, 1, 0, 3)).astype(f32)
        return both.reshape(2, -1, nz * slice_ff)

    if fast:
        sums = last_fast(attn_parts, *lined, *ffn_grads[2:])
        *weight_sums, block_rows = finish_fast(sums, attended, out_sum)
        misc_sums = sums[0][:, 4 * width :]
    else:
        attn_sums = sum_all(jnp.concatenate(attn_parts, axis=1)).astype(f32)
        *attn_sums, misc_sums = jnp.split(attn_sums, [width, 2 * width, 3 * width, 4 * width], axis=1)
        downs = [down.astype(f32) for down in (sd_sum, ed_sum)]
        weight_sums = (*attn_sums, *joined(sgu_sum), downs[0], *joined(egu_sum), downs[1])
        block_rows = (attended + out_sum.astype(f32)).astype(bf16)
    return (
        block_rows.reshape(batches, 1, rows, width),
        input_grad.reshape(batches, 1, rows, width),
        misc_sums[:, experts],
        *weight_sums[:4],
        misc_sums[:, experts + 1],
        misc_sums[:, :experts],
        *weight_sums[4:7],
        *[total[None] for total in weight_sums[7:]],
    )


def solution(mesh):
    n_dp, n_expert = mesh.shape["dp"], mesh.shape["expert"]
    nz = 4 if n_dp % 4 == 0 else 1
    grid = Mesh(mesh.devices.reshape(nz, n_dp // nz, n_expert // 2, 2), ALL)
    rows = P(None, EXPERT, DP, None)
    line = P(ALL)
    dense = P(ALL, None)
    expert = P(EXPERT, DP, None)
    return jax.shard_map(
        shards,
        mesh=grid,
        in_specs=(rows, rows, P(None, EXPERT), rows, line)
        + (dense,) * 4
        + (line,)
        + (dense,) * 4
        + (expert,) * 3,
        out_specs=(rows, rows, line) + (dense,) * 4 + (line,) + (dense,) * 4 + (expert,) * 3,
        check_vma=False,
    )
```

```python
import functools
import math

import jax
import jax.numpy as jnp
from jax import lax
from jax.experimental import pallas as pl
from jax.experimental.pallas import tpu as pltpu
from jax.sharding import Mesh
from jax.sharding import PartitionSpec as P

HEAD_DIM = 64
TOP_K = 2
MISC = 128

eps = 1e-06
highest = lax.Precision.HIGHEST
neg_fill = -1e30
f32 = jnp.float32
bf16 = jnp.bfloat16

ALL = ("z", "y", "x", "c")
PLANE = ("y", "x", "c")
DP = ("z", "y")
EXPERT = ("x", "c")


def rms_scale(values):
    return lax.rsqrt(jnp.mean(values * values, axis=-1, keepdims=True) + eps)


def silu_grad(values):
    sig = jax.nn.sigmoid(values)
    return sig * (1.0 + values * (1.0 - sig))


def dot(a, b, dims, batch=((), ())):
    return lax.dot_general(a, b, (dims, batch), preferred_element_type=f32)


def rotary_tables(positions):
    half = HEAD_DIM // 2
    frequency = jnp.exp(jnp.arange(half, dtype=f32) * (-math.log(10000.0) * 2.0 / HEAD_DIM))
    angles = frequency[:, None] * positions.astype(f32)[None, :]
    return jnp.cos(angles), jnp.sin(angles)


def rotate_t(values, cosine, sine, sign):
    rows = values.shape[-1]
    halves = values.reshape(-1, 2, HEAD_DIM // 2, rows)
    first, second = halves[:, 0], halves[:, 1]
    turned = jnp.stack([first * cosine - sign * second * sine, second * cosine + sign * first * sine], axis=1)
    return turned.reshape(values.shape)


def gather_all(shard):
    return lax.all_gather(shard, ALL, axis=0, tiled=True)


def gather_weights(egu, sgu, ed, sd):
    nz, ny, ne = lax.axis_size("z"), lax.axis_size("y"), lax.axis_size(EXPERT)

    def spread(blocks):
        mine = lax.all_to_all(blocks, "z", 0, 0, tiled=True)
        return lax.all_gather(mine, PLANE, axis=0).reshape(ny, ne, nz, *blocks.shape[1:])

    egu_all = jnp.transpose(spread(egu), (1, 2, 0, 3, 4)).reshape(ne, -1, egu.shape[-1])
    sgu_all = jnp.transpose(spread(sgu), (2, 0, 1, 3, 4)).reshape(-1, sgu.shape[-1])
    ed_all = lax.all_gather(ed, PLANE, axis=0).reshape(ny, ne, *ed.shape)
    ed_all = jnp.transpose(ed_all, (1, 0, 2, 3)).reshape(ne, -1, ed.shape[-1])
    sd_all = lax.all_gather(sd, PLANE, axis=0, tiled=True)
    return egu_all, sgu_all, ed_all, sd_all


def gather_line(rows):
    return lax.all_gather(rows, "z", axis=0, tiled=True)


def paired(batches, heads):
    n_dp = lax.axis_size(DP)
    here = batches * heads // n_dp
    even = here * n_dp == batches * heads and heads % max(1, here) == 0
    return even and tuple(lax.axis_size(name) for name in ALL) == (4, 2, 2, 2)


def sum_line(rows):
    return lax.psum_scatter(rows, "z", scatter_dimension=0, tiled=True)


def sum_weights(egu, sgu, ed, sd):
    nz, ny, ne = lax.axis_size("z"), lax.axis_size("y"), lax.axis_size(EXPERT)

    def collect(parts):
        mine = lax.psum_scatter(parts, PLANE, scatter_dimension=0, tiled=True)
        return lax.all_to_all(mine.reshape(nz, *mine.shape[1:]), "z", 0, 0, tiled=True)

    wide = egu.shape[-1]
    egu = jnp.transpose(egu.reshape(ne, nz, ny, -1, wide), (2, 0, 1, 3, 4))
    sgu = jnp.transpose(sgu.reshape(nz, ny, ne, -1, wide), (1, 2, 0, 3, 4))
    egu = collect(egu.reshape(ny * ne * nz, -1, wide))
    sgu = collect(sgu.reshape(ny * ne * nz, -1, wide))
    ed = jnp.transpose(ed.reshape(ne, ny, -1, ed.shape[-1]), (1, 0, 2, 3)).reshape(ny * ne, -1, ed.shape[-1])
    ed = lax.psum_scatter(ed, PLANE, scatter_dimension=0, tiled=True)[0]
    sd = lax.psum_scatter(sd, PLANE, scatter_dimension=0, tiled=True)
    return egu, sgu, ed, sd


def sum_all(parts):
    return lax.psum_scatter(parts, ALL, scatter_dimension=0, tiled=True)


def units_here(batches, heads):
    return -(-batches * heads // lax.axis_size(DP))


def to_units(tensor):
    kinds, batches, width, rows = tensor.shape
    n_dp = lax.axis_size(DP)
    heads = width // HEAD_DIM
    here = units_here(batches, heads)
    units = tensor.reshape(kinds, batches * heads, HEAD_DIM, rows)
    units = jnp.pad(units, ((0, 0), (0, here * n_dp - batches * heads), (0, 0), (0, 0)))
    units = jnp.transpose(units.reshape(kinds, n_dp, here, HEAD_DIM, rows), (1, 2, 0, 3, 4))
    units = lax.all_to_all(units, DP, 0, 0, tiled=True)
    return jnp.transpose(units, (1, 2, 3, 0, 4)).reshape(here, kinds, HEAD_DIM, n_dp * rows)


def from_units(units, batches, heads):
    here, kinds, _, length = units.shape
    n_dp = lax.axis_size(DP)
    rows = length // n_dp
    parts = jnp.transpose(units.reshape(here, kinds, HEAD_DIM, n_dp, rows), (3, 0, 1, 2, 4))
    parts = lax.all_to_all(parts, DP, 0, 0, tiled=True)
    parts = parts.reshape(n_dp * here, kinds, HEAD_DIM, rows)[: batches * heads]
    return jnp.transpose(parts, (1, 0, 2, 3)).reshape(kinds, batches, heads * HEAD_DIM, rows)


MESH = pl.DeviceIdType.MESH


def position():
    return tuple(lax.axis_index(name) for name in ALL)


def remote(src, dst, send, recv, device):
    return pltpu.make_async_remote_copy(
        src_ref=src, dst_ref=dst, send_sem=send, recv_sem=recv, device_id=device, device_id_type=MESH
    )


def greet(partners):
    barrier = pltpu.get_barrier_semaphore()
    for device in partners:
        pl.semaphore_signal(barrier, inc=1, device_id=device, device_id_type=MESH)
    pl.semaphore_wait(barrier, len(partners))


def any_specs(count):
    return [pl.BlockSpec(memory_space=pl.ANY)] * count


def params(collective_id, vmem=16 << 20):
    return pltpu.CompilerParams(collective_id=collective_id, has_side_effects=True, vmem_limit_bytes=vmem)


class PlaneItem:
    def __init__(self, here, index, place, own, x_first):
        self.here, self.index, self.place, self.own, self.x_first = here, index, place, own, x_first

    def moved(self, along_first, along_second, along_core):
        z, y, x, c = self.here
        move_x, move_y = (along_first, along_second) if self.x_first else (along_second, along_first)
        return (z, 1 - y if move_y else y, 1 - x if move_x else x, 1 - c if along_core else c)

    def ref(self, *moves):
        return self.place(*self.moved(*moves)[1:])

    COPIES = (
        ((0, 0, 0), (1, 0, 0)),
        ((0, 0, 0), (0, 1, 0)),
        ((1, 0, 0), (0, 1, 0)),
        ((0, 0, 0), (0, 0, 1)),
        ((1, 0, 0), (0, 0, 1)),
        ((0, 1, 0), (0, 0, 1)),
        ((1, 1, 0), (0, 0, 1)),
    )

    def copy(self, number, send, recv):
        source, to = self.COPIES[number]
        src = self.own if source == (0, 0, 0) else self.ref(*source)
        return remote(
            src, self.ref(*source), send.at[self.index, number], recv.at[self.index, number], self.moved(*to)
        )

    def arrival(self, number, send, recv):
        source, to = self.COPIES[number]
        ref = self.ref(*[a ^ b for a, b in zip(source, to)])
        return remote(ref, ref, send.at[self.index, number], recv.at[self.index, number], self.moved(*to))


def line_gather_steps(z, nz, own, out, sends, gets, neighbour, pieces):
    def copy(way, source, piece, src=None):
        part = pieces[piece]
        dst = out.at[source, part]
        src = dst if src is None else src.at[part]
        return remote(src, dst, sends.at[way, source, piece], gets.at[way, source, piece], neighbour(1 - 2 * way))

    def may_send(way):
        return z < nz - 1 if way == 0 else z > 0

    def start():
        for piece in range(len(pieces)):
            for way in range(2):
                pl.when(may_send(way))(lambda: copy(way, z, piece, own).start())

    def step(distance, piece):
        for way in range(2):
            source = z - distance if way == 0 else z + distance

            @pl.when((source >= 0) & (source < nz))
            def _():
                copy(way, source, piece).wait_recv()
                pl.when(may_send(way))(lambda: copy(way, source, piece).start())

    def end():
        for distance in range(nz):
            for piece in range(len(pieces)):
                for way in range(2):
                    source = z - distance if way == 0 else z + distance

                    @pl.when((source >= 0) & (source < nz) & may_send(way))
                    def _():
                        copy(way, source, piece).wait_send()

    steps = [functools.partial(step, distance, piece) for distance in range(1, nz) for piece in range(len(pieces))]
    return start, steps, end


def line_partners(here, nz):
    z, y, x, c = here
    return lambda way: (jnp.clip(z + way, 0, nz - 1), y, x, c)


def greet_line(here, nz):
    z = here[0]
    neighbour = line_partners(here, nz)
    barrier = pltpu.get_barrier_semaphore()

    @pl.when(z > 0)
    def _():
        pl.semaphore_signal(barrier, inc=1, device_id=neighbour(-1), device_id_type=MESH)

    @pl.when(z < nz - 1)
    def _():
        pl.semaphore_signal(barrier, inc=1, device_id=neighbour(1), device_id_type=MESH)

    pl.semaphore_wait(barrier, jnp.where(z > 0, 1, 0) + jnp.where(z < nz - 1, 1, 0))


LINE_PIECES = 2


def row_pieces(rows):
    half = rows // 2 // 16 * 16
    return pl.ds(0, half), pl.ds(half, rows - half)


def line_sum_steps(z, nz, parts, total, up, down, sends, gets, neighbour, pieces):
    arrived = (up, down)

    def copy(way, target, piece, src):
        part = pieces[piece]
        dst = arrived[way].at[target, part]
        return remote(src, dst, sends.at[way, target, piece], gets.at[way, target, piece], neighbour(1 - 2 * way))

    def part_of(ref, target, piece):
        return ref.at[target, pieces[piece]]

    def step(distance, piece):
        for way in range(2):
            target = nz - distance if way == 0 else distance - 1
            ahead = z < target if way == 0 else z > target
            first = z == 0 if way == 0 else z == nz - 1
            mine, theirs = part_of(parts, target, piece), part_of(arrived[way], target, piece)

            @pl.when(ahead & first)
            def _():
                copy(way, target, piece, mine).start()

            @pl.when(ahead & jnp.logical_not(first))
            def _():
                copy(way, target, piece, theirs).wait_recv()
                mine[...] = (mine[...].astype(f32) + theirs[...].astype(f32)).astype(bf16)
                copy(way, target, piece, mine).start()

    def end():
        for piece, part in enumerate(pieces):
            total[part, :] = parts[z, part, :].astype(f32)
            for way in range(2):
                theirs = part_of(arrived[way], z, piece)

                @pl.when(z > 0 if way == 0 else z < nz - 1)
                def _():
                    copy(way, z, piece, theirs).wait_recv()
                    total[part, :] += theirs[...].astype(f32)

        for distance in range(1, nz):
            for piece in range(len(pieces)):
                for way in range(2):
                    target = nz - distance if way == 0 else distance - 1

                    @pl.when(z < target if way == 0 else z > target)
                    def _():
                        copy(way, target, piece, part_of(parts, target, piece)).wait_send()

    steps = [functools.partial(step, distance, piece) for distance in range(1, nz) for piece in range(len(pieces))]
    return steps, end


class SumItem:
    def __init__(self, here, index, place, buffers, x_first):
        self.here, self.index, self.place, self.x_first = here, index, place, x_first
        self.own, self.sib, self.second, self.first = buffers

    moved = PlaneItem.moved

    def slot(self, a, b):
        return 2 * a + b

    def begin(self, load, send, recv):
        for a in range(2):
            for b in range(2):
                n = self.slot(a, b)
                self.sib_copy(a, b, send, recv).start()
                pltpu.make_async_copy(self.place(*self.moved(a, b, 0)[1:]), self.own.at[n], load.at[self.index, n]).start()

    def sib_copy(self, a, b, send, recv):
        n = self.slot(a, b)
        src = self.place(*self.moved(a, b, 1)[1:])
        return remote(src, self.sib.at[n], send.at[self.index, n], recv.at[self.index, n], self.moved(0, 0, 1))

    def second_copy(self, a, send, recv):
        n = 4 + a
        src = self.sib.at[self.slot(a, 1)]
        return remote(src, self.second.at[a], send.at[self.index, n], recv.at[self.index, n], self.moved(0, 1, 0))

    def first_copy(self, send, recv):
        src = self.second.at[1]
        return remote(src, self.first, send.at[self.index, 6], recv.at[self.index, 6], self.moved(1, 0, 0))

    def after_core(self, load, send, recv):
        for b in (1, 0):
            for a in range(2):
                n = self.slot(a, b)
                pltpu.make_async_copy(self.own.at[n], self.own.at[n], load.at[self.index, n]).wait()
                self.sib_copy(a, b, send, recv).wait_recv()
                add_to(self.sib.at[n], self.own.at[n])
                if b == 1:
                    self.second_copy(a, send, recv).start()

    def after_second(self, send, recv):
        for a in (1, 0):
            self.second_copy(a, send, recv).wait_recv()
            add_to(self.second.at[a], self.sib.at[self.slot(a, 0)])
            if a == 1:
                self.first_copy(send, recv).start()

    def after_first(self, send, recv, total=None):
        self.first_copy(send, recv).wait_recv()
        if total is None:
            add_to(self.first, self.second.at[0])
        else:
            total[...] = self.first[...].astype(f32) + self.second[0].astype(f32)

    def end(self, send, recv):
        for a in range(2):
            for b in range(2):
                self.sib_copy(a, b, send, recv).wait_send()
            self.second_copy(a, send, recv).wait_send()
        self.first_copy(send, recv).wait_send()


def add_to(total, term):
    rows, columns = total.shape
    if rows % 16 == 0:

        @pl.loop(0, rows // 16)
        def _(i):
            part = pl.ds(pl.multiple_of(i * 16, 16), 16)
            total[part, :] = (total[part, :].astype(f32) + term[part, :].astype(f32)).astype(bf16)
    else:
        wide = max(w for w in (128, 256, 384, 512, 640) if columns % w == 0)

        @pl.loop(0, columns // wide)
        def _(i):
            part = pl.ds(pl.multiple_of(i * wide, 128), wide)
            total[:, part] = (total[:, part].astype(f32) + term[:, part].astype(f32)).astype(bf16)


SUM_LAG = 3


def unit_owner(number, batches, heads, here_units):
    per_batch = heads // here_units
    return number // per_batch, lax.rem(number, per_batch) * here_units


def exchange(me, n_dp, copy):
    ny = 2

    def device(number):
        return (number // ny, lax.rem(number, ny))

    far = [lax.rem(me + d, n_dp) for d in range(1, n_dp)]
    near = [lax.rem(me + n_dp - d, n_dp) for d in range(1, n_dp)]

    def start():
        for number in far:
            copy(number, me, device(number)).start()

    def arrive():
        for number in near:
            copy(me, number, device(number)).wait_recv()

    def end():
        for number in far:
            copy(number, me, device(number)).wait_send()

    return start, arrive, end


def tile_spans(length):
    tile = 256 if length % 512 == 0 else length // 2
    for start in range(0, length, tile):
        if start < length // 2:
            yield start, tile, 0, length // 2
        else:
            yield start, tile, start, start + tile


def masked(values, start, tile, mask_from, keys, length, fill):
    key = mask_from + lax.broadcasted_iota(jnp.int32, (keys - mask_from, tile), 0)
    query = start + lax.broadcasted_iota(jnp.int32, (keys - mask_from, tile), 1)
    allowed = (key <= query) | ((key < length) & (query < length))
    tail = jnp.where(allowed, values[mask_from:], fill)
    return tail if mask_from == 0 else jnp.concatenate([values[:mask_from], tail], axis=0)


X_FIRST = {
    "egu": lambda k: k == 1,
    "sgu": lambda k: k % 2 == 1,
    "sd": lambda k: False,
    "ed": lambda k: k == 1,
}


def plane_items(here, arrays, outs, start=0):
    items = []

    def add(place, own, x_first):
        items.append(PlaneItem(here, start + len(items), place, own, x_first))

    if "ed" in arrays:
        source, ed = arrays["ed"], outs["ed"]
        half = source.shape[0] // 2
        for h in range(2):
            rows = pl.ds(h * half, half)
            add(lambda py, px, pc, rows=rows: ed.at[px * 2 + pc, py, rows], source.at[rows], X_FIRST["ed"](h))
    if "sd" in arrays:
        sd = outs["sd"]
        add(lambda py, px, pc: sd.at[(py * 2 + px) * 2 + pc], arrays["sd"], X_FIRST["sd"](0))
    if "egu" in arrays:
        source, egu = arrays["egu"], outs["egu"]
        for zs in range(source.shape[0]):
            add(lambda py, px, pc, zs=zs: egu.at[px * 2 + pc, zs * 2 + py], source.at[zs], X_FIRST["egu"](zs))
    if "sgu" in arrays:
        source, sgu = arrays["sgu"], outs["sgu"]
        for zs in range(source.shape[0]):
            place = lambda py, px, pc, zs=zs: sgu.at[((zs * 2 + py) * 2 + px) * 2 + pc]
            add(place, source.at[zs], X_FIRST["sgu"](zs))
    return items


def attend_kernel(nz, batches, *refs):
    prefix, qkv, egu_in, sgu_in, cot_in, ids_in = refs[:6]
    context, units, lse, egu, sgu, cot = refs[6:12]
    result, cot_own, egu_own, sgu_own, local, loads, send, recv = refs[12:20]
    csend, crecv, psend, precv, lsend, lrecv = refs[20:]
    here = position()
    z, y, x, c = here
    n_dp = nz * 2
    me = z * 2 + y
    kinds, width, all_rows = qkv.shape
    rows = all_rows // batches
    heads = width // HEAD_DIM
    count = units.shape[1] // HEAD_DIM
    span = count * HEAD_DIM
    length = units.shape[2]
    greet(
        [(lax.rem(me + d, n_dp) // 2, lax.rem(me + d, 2), x, c) for d in range(1, n_dp)]
        + [(z, y, 1 - x, c), (z, y, x, 1 - c)]
    )

    def columns(number):
        return pl.ds(pl.multiple_of(number * rows, rows), rows)

    def qkv_block(number):
        batch, head = unit_owner(number, batches, heads, count)
        return qkv.at[:, pl.ds(pl.multiple_of(head * HEAD_DIM, HEAD_DIM), span), columns(batch)]

    def qkv_copy(number, source, device):
        return remote(
            qkv_block(number), units.at[:, :, columns(source)], send.at[number], recv.at[source], (*device, x, c)
        )

    start, arrive, end = exchange(me, n_dp, qkv_copy)
    start()
    keep = pltpu.make_async_copy(qkv_block(me), units.at[:, :, columns(me)], local.at[0])
    keep.start()
    items = plane_items(here, {"egu": egu_in, "sgu": sgu_in}, {"egu": egu, "sgu": sgu})
    for item in items:
        for number in (0, 1, 3):
            item.copy(number, psend, precv).start()
    fills = [(cot_in.at[b, 0], cot_own.at[pl.ds(b * rows, rows)]) for b in range(batches)]
    fills += [(ids_in, cot_own.at[pl.ds(all_rows, EXTRA)])]
    fills += [(egu_in, egu_own), (sgu_in, sgu_own)]
    fills = [pltpu.make_async_copy(src, dst, loads.at[i]) for i, (src, dst) in enumerate(fills)]
    for copy in fills:
        copy.start()
    owns = [(cot_own, cot.at[z])]
    owns += [(egu_own.at[zs], egu.at[x * 2 + c, zs * 2 + y]) for zs in range(nz)]
    owns += [(sgu_own.at[zs], sgu.at[((zs * 2 + y) * 2 + x) * 2 + c]) for zs in range(nz)]
    keeps = [pltpu.make_async_copy(src, dst, local.at[1 + i]) for i, (src, dst) in enumerate(owns)]
    for copy in fills:
        copy.wait()
    for copy in keeps:
        copy.start()

    def have_first(item):
        item.arrival(0, psend, precv).wait_recv()
        item.copy(2, psend, precv).start()
        item.copy(4, psend, precv).start()

    def have_second(item):
        item.arrival(1, psend, precv).wait_recv()
        item.copy(5, psend, precv).start()
        item.arrival(2, psend, precv).wait_recv()
        item.copy(6, psend, precv).start()

    early = 0
    for item in items[:early]:
        have_first(item)
    line_start, line_steps, line_end = line_gather_steps(
        z, nz, cot_own, cot, lsend, lrecv, line_partners(here, nz), row_pieces(cot.shape[1])
    )
    line_start()
    arrive()
    keep.wait()

    my_batch, my_head = unit_owner(me, batches, heads, count)
    limit = prefix[my_batch, 0]

    def context_copy(head):
        def copy(number, source, device):
            _, first_head = unit_owner(source, batches, heads, count)
            batch, _ = unit_owner(source, batches, heads, count)
            part = pl.ds(pl.multiple_of((first_head + head) * HEAD_DIM, HEAD_DIM), HEAD_DIM)
            return remote(
                result.at[pl.ds(head * HEAD_DIM, HEAD_DIM), columns(number)],
                context.at[part, columns(batch)],
                csend.at[head, number],
                crecv.at[head, source],
                (*device, x, c),
            )

        return copy

    def attend(head):
        part = pl.ds(head * HEAD_DIM, HEAD_DIM)
        for first, tile, mask_from, keys in tile_spans(length):
            queries = units[0, part, pl.ds(first, tile)] * bf16(1.0 / math.sqrt(HEAD_DIM))
            scores = dot(units[1, part, pl.ds(0, keys)], queries, ((0,), (0,)))
            scores = masked(scores, first, tile, mask_from, keys, limit, neg_fill)
            top = jnp.max(scores, axis=0, keepdims=True)
            weights = jnp.exp(scores - top)
            total = jnp.sum(weights, axis=0, keepdims=True)
            lse[head, :, pl.ds(first, tile)] = top + jnp.log(total)
            mean = dot(units[2, part, pl.ds(0, keys)], weights.astype(bf16), ((1,), (0,))) / total
            result[part, pl.ds(first, tile)] = mean.astype(bf16)

    exchanges = [exchange(me, n_dp, context_copy(head)) for head in range(count)]
    own_part = [pl.ds(pl.multiple_of((my_head + head) * HEAD_DIM, HEAD_DIM), HEAD_DIM) for head in range(count)]
    own_copies = [
        pltpu.make_async_copy(
            result.at[pl.ds(head * HEAD_DIM, HEAD_DIM), columns(me)],
            context.at[own_part[head], columns(my_batch)],
            local.at[1 + len(owns) + head],
        )
        for head in range(count)
    ]
    later = [functools.partial(have_first, item) for item in items[early:]]
    later += [functools.partial(have_second, item) for item in items]
    line_steps = list(line_steps)
    for head in range(count):
        attend(head)
        exchanges[head][0]()
        own_copies[head].start()
    share = -(-len(later) // max(1, len(line_steps)))
    while later or line_steps:
        for step in later[:share]:
            step()
        later = later[share:]
        if line_steps:
            line_steps.pop(0)()
    for item in items:
        for number in range(3, 7):
            item.arrival(number, psend, precv).wait_recv()
    for head in range(count):
        exchanges[head][1]()
        own_copies[head].wait()
    for item in items:
        for number in range(7):
            item.copy(number, psend, precv).wait_send()
    end()
    line_end()
    for head in range(count):
        exchanges[head][2]()
    for copy in keeps:
        copy.wait()


def attend_fast(prefix, qkv, egu, sgu, cot, ids):
    nz = lax.axis_size("z")
    n_dp = nz * 2
    kinds, width, all_rows = qkv.shape
    batches = cot.shape[0]
    heads = width // HEAD_DIM
    count = batches * heads // n_dp
    length = n_dp * all_rows // batches
    any_space, vmem = pl.BlockSpec(memory_space=pl.ANY), pl.BlockSpec(memory_space=pltpu.VMEM)
    shapes = [
        ((width, all_rows), bf16),
        ((kinds, count * HEAD_DIM, length), bf16),
        ((count, 1, length), f32),
        ((4, nz * 2, *egu.shape[1:]), bf16),
        ((nz * 8, *sgu.shape[1:]), bf16),
        ((nz, all_rows + EXTRA, width), bf16),
    ]
    dma = pltpu.SemaphoreType.DMA
    items = 2 * nz
    line = dma((2, nz, LINE_PIECES))
    context, units, lse, egu, sgu, cot = pl.pallas_call(
        functools.partial(attend_kernel, nz, batches),
        out_shape=[jax.ShapeDtypeStruct(*shape) for shape in shapes],
        in_specs=[pl.BlockSpec(memory_space=pltpu.SMEM)] + [any_space] * 5,
        out_specs=[any_space, vmem, vmem] + [any_space] * 3,
        scratch_shapes=[
            pltpu.VMEM((count * HEAD_DIM, length), bf16),
            pltpu.VMEM((all_rows + EXTRA, width), bf16),
            *[pltpu.VMEM(a.shape, bf16) for a in (egu, sgu)],
            dma((2 + 2 * nz + count,)),
            dma((batches + 3,)),
            dma((n_dp,)),
            dma((n_dp,)),
            dma((count, n_dp)),
            dma((count, n_dp)),
            dma((items, 7)),
            dma((items, 7)),
            line,
            line,
        ],
        compiler_params=params(4, 58 << 20),
        name="attend",
    )(prefix, qkv, egu, sgu, cot, ids)
    return context, (units, lse), egu.reshape(4, -1, egu.shape[-1]), sgu.reshape(-1, sgu.shape[-1]), cot


def first_kernel(nz, *refs):
    attn_in, halves_in, (ed_in, sd_in) = refs[:5], refs[5:9], refs[9:11]
    attn, egu, sgu, ed, sd, attn_own, egu_own, sgu_own, ed_own, sd_own = refs[11:21]
    local, stores, zsend, zrecv, psend, precv = refs[21:]
    here = position()
    z, y, x, c = here
    line = [lax.rem(z + d, nz) for d in range(nz)]
    ff = egu.shape[-1] // 2

    def flat(zs, py, px, pc):
        return ((zs * 2 + py) * 2 + px) * 2 + pc

    mine = flat(z, y, x, c)
    gathered, start = [], 0
    for i, ref in enumerate(attn_in):
        gathered.append(
            pltpu.make_async_copy(ref, attn_own.at[:, pl.ds(start, ref.shape[1])], local.at[i])
        )
        start += ref.shape[1]
    for kind in range(4):
        src = halves_in[kind].at[:, pl.ds(pl.multiple_of(z * ff, ff), ff)]
        dst = (egu_own if kind < 2 else sgu_own).at[:, pl.ds(kind % 2 * ff, ff)]
        gathered.append(pltpu.make_async_copy(src, dst, local.at[5 + kind]))
    gathered.append(pltpu.make_async_copy(ed_in, ed_own, local.at[9]))
    gathered.append(pltpu.make_async_copy(sd_in, sd_own, local.at[10]))
    for copy in gathered:
        copy.start()
    greet([(line[d], y, x, c) for d in range(1, nz)] + [(z, 1 - y, x, c), (z, y, 1 - x, c), (z, y, x, 1 - c)])

    def half_block(kind, to, at):
        src = halves_in[kind].at[:, pl.ds(pl.multiple_of(to * ff, ff), ff)]
        return src, (egu if kind < 2 else sgu).at[at, :, pl.ds(kind % 2 * ff, ff)]

    def half_copy(kind, d, arriving=False):
        to, frm = line[d], line[(nz - d) % nz]
        src, dst = half_block(kind, to, frm if arriving else z)
        return remote(src, dst, zsend.at[1 + kind, d], zrecv.at[1 + kind, d], (to, y, x, c))

    def attn_copy(d, arriving=False):
        to, frm = line[d], line[(nz - d) % nz]
        ref = attn.at[flat(frm if arriving else z, y, x, c)]
        return remote(ref if arriving else attn_own, ref, zsend.at[0, d], zrecv.at[0, d], (to, y, x, c))

    items = []
    for d in range(nz):
        place = lambda py, px, pc, frm=line[(nz - d) % nz]: attn.at[flat(frm, py, px, pc)]
        items.append(PlaneItem(here, d, place, place(y, x, c) if d else attn_own, d % 2 == 1))

    def have_own(item):
        for number in (0, 1, 3):
            item.copy(number, psend, precv).start()

    far_first = sorted(range(1, nz), key=lambda d: abs(d - nz / 2))
    for copy in gathered:
        copy.wait()
    for d in far_first:
        attn_copy(d).start()
    have_own(items[0])
    for d in far_first:
        for kind in range(4):
            half_copy(kind, d).start()
    more = plane_items(here, {"ed": ed_own, "sd": sd_own}, {"ed": ed, "sd": sd}, nz)
    for item in more:
        have_own(item)
    keeps = [(attn_own, attn.at[mine]), (egu_own, egu.at[z]), (sgu_own, sgu.at[z])]
    keeps += [(ed_own, ed.at[x * 2 + c, y]), (sd_own, sd.at[(y * 2 + x) * 2 + c])]
    keeps = [pltpu.make_async_copy(src, dst, stores.at[i]) for i, (src, dst) in enumerate(keeps)]
    for copy in keeps:
        copy.start()
    for d in range(1, nz):
        attn_copy(d, True).wait_recv()
        have_own(items[d])
    items += more
    for item in items:
        item.arrival(0, psend, precv).wait_recv()
        item.copy(2, psend, precv).start()
        item.copy(4, psend, precv).start()
    for item in items:
        item.arrival(1, psend, precv).wait_recv()
        item.copy(5, psend, precv).start()
    for item in items:
        item.arrival(2, psend, precv).wait_recv()
        item.copy(6, psend, precv).start()
    for item in items:
        for number in range(3, 7):
            item.arrival(number, psend, precv).wait_recv()
    for d in range(1, nz):
        for kind in range(4):
            half_copy(kind, d, True).wait_recv()
    for item in items:
        for number in range(7):
            item.copy(number, psend, precv).wait_send()
    for d in range(1, nz):
        attn_copy(d).wait_send()
        for kind in range(4):
            half_copy(kind, d).wait_send()
    for copy in keeps:
        copy.wait()


def first_fast(attn, halves, ed, sd):
    nz = lax.axis_size("z")
    dma = pltpu.SemaphoreType.DMA
    rows = attn[0].shape[0]
    shapes = [(nz * 8, rows, sum(a.shape[1] for a in attn))]
    shapes += [(nz, half.shape[0], 2 * half.shape[1] // nz) for half in halves[::2]]
    own = [pltpu.VMEM(shape[1:], bf16) for shape in shapes] + [pltpu.VMEM(a.shape, bf16) for a in (ed, sd)]
    shapes += [(4, 2, *ed.shape), (8, *sd.shape)]
    attn, egu, sgu, ed, sd = pl.pallas_call(
        functools.partial(first_kernel, nz),
        out_shape=[jax.ShapeDtypeStruct(shape, bf16) for shape in shapes],
        in_specs=any_specs(11),
        out_specs=any_specs(5),
        scratch_shapes=own
        + [dma((11,)), dma((5,)), dma((5, nz)), dma((5, nz)), dma((nz + 3, 7)), dma((nz + 3, 7))],
        compiler_params=params(0, 58 << 20),
        name="first",
    )(*attn, *halves, ed, sd)
    return attn.reshape(-1, attn.shape[-1]), (egu, sgu), ed.reshape(4, -1, ed.shape[-1]), sd.reshape(-1, sd.shape[-1])


def backward_kernel(nz, batches, kinds, *refs):
    refs = list(refs)
    take = lambda n: [refs.pop(0) for _ in range(n)]
    prefix, cosine, sine, grad_in, units, lse = take(6)
    inputs = dict(zip(kinds, take(len(kinds))))
    (rows_in,) = take(1)
    (grads,) = take(1)
    outputs = dict(zip(kinds, take(len(kinds))))
    (rows_total,) = take(1)
    grad, dkey, dvalue, result = take(4)
    buffers = {kind: take(4) for kind in kinds}
    local, send, recv, csend, crecv, load, psend, precv, store = take(9)
    rows_parts, up, down, lload, lsend, lrecv = take(6)
    here = position()
    z, y, x, c = here
    n_dp = nz * 2
    me = z * 2 + y
    width, all_rows = grad_in.shape
    rows = all_rows // batches
    heads = width // HEAD_DIM
    span, length = grad.shape
    count = span // HEAD_DIM
    row_load = pltpu.make_async_copy(rows_in, rows_parts, lload)
    row_load.start()
    greet(
        [(lax.rem(me + d, n_dp) // 2, lax.rem(me + d, 2), x, c) for d in range(1, n_dp)]
        + [(z, y, 1 - x, c), (z, y, x, 1 - c)]
    )

    def columns(number):
        return pl.ds(pl.multiple_of(number * rows, rows), rows)

    def grad_block(number):
        batch, head = unit_owner(number, batches, heads, count)
        return grad_in.at[pl.ds(pl.multiple_of(head * HEAD_DIM, HEAD_DIM), span), columns(batch)]

    def grad_copy(number, source, device):
        return remote(
            grad_block(number), grad.at[:, columns(source)], send.at[number], recv.at[source], (*device, x, c)
        )

    start, arrive, end = exchange(me, n_dp, grad_copy)
    start()
    keep = pltpu.make_async_copy(grad_block(me), grad.at[:, columns(me)], local.at[0])
    keep.start()

    places = {
        "egu": lambda zs: lambda py, px, pc: inputs["egu"].at[px * 2 + pc, zs * 2 + py],
        "sgu": lambda zs: lambda py, px, pc: inputs["sgu"].at[((zs * 2 + py) * 2 + px) * 2 + pc],
    }
    items, finals = [], []
    for kind in kinds:
        for k in range(nz):
            parts = tuple(buffer.at[k] for buffer in buffers[kind])
            item = SumItem(here, len(items), places[kind](k), parts, X_FIRST[kind](k))
            finals.append(pltpu.make_async_copy(item.first, outputs[kind].at[k], store.at[item.index]))
            items.append(item)
    for item in items:
        item.begin(load, psend, precv)
    row_load.wait()
    row_steps, row_end = line_sum_steps(
        z, nz, rows_parts, rows_total, up, down, lsend, lrecv, line_partners(here, nz), row_pieces(rows_parts.shape[1])
    )

    def stage(t):
        if t < len(items):
            items[t].after_core(load, psend, precv)
        if 0 <= t - SUM_LAG < len(items):
            items[t - SUM_LAG].after_second(psend, precv)
        if 0 <= t - 2 * SUM_LAG < len(items):
            items[t - 2 * SUM_LAG].after_first(psend, precv)
            finals[t - 2 * SUM_LAG].start()

    steps = [functools.partial(stage, t) for t in range(len(items) + 2 * SUM_LAG)]
    for step in steps[:2] + row_steps[:2] + steps[2:2]:
        step()
    steps, row_steps = steps[2:], row_steps[2:]
    arrive()
    keep.wait()

    my_batch, my_head = unit_owner(me, batches, heads, count)
    limit = prefix[my_batch, 0]
    inv = 1.0 / math.sqrt(HEAD_DIM)

    def head_rows(source, head):
        _, first_head = unit_owner(source, batches, heads, count)
        return pl.ds(pl.multiple_of((first_head + head) * HEAD_DIM, HEAD_DIM), HEAD_DIM)

    def grads_copy(head):
        def copy(number, source, device):
            batch, _ = unit_owner(source, batches, heads, count)
            return remote(
                result.at[:, pl.ds(head * HEAD_DIM, HEAD_DIM), columns(number)],
                grads.at[:, head_rows(source, head), columns(batch)],
                csend.at[head, number],
                crecv.at[head, source],
                (*device, x, c),
            )

        return copy

    def unrotate(values, place):
        first, second = values[: HEAD_DIM // 2], values[HEAD_DIM // 2 :]
        cos, sin = cosine[:, place], sine[:, place]
        return jnp.concatenate([first * cos + second * sin, second * cos - first * sin], axis=0).astype(bf16)

    def attend(head):
        part = pl.ds(head * HEAD_DIM, HEAD_DIM)
        dkey[...] = jnp.zeros_like(dkey)
        dvalue[...] = jnp.zeros_like(dvalue)
        for first, tile, mask_from, keys in tile_spans(length):
            here_q, upto = pl.ds(first, tile), pl.ds(0, keys)
            queries = units[0, part, here_q] * bf16(inv)
            key, value, out_grad = units[1, part, upto], units[2, part, upto], grad[part, here_q]
            scores = dot(key, queries, ((0,), (0,)))
            probs = jnp.exp(scores - lse[head, :, here_q])
            probs = masked(probs, first, tile, mask_from, keys, limit, 0.0)
            prob_grad = dot(value, out_grad, ((0,), (0,)))
            delta = jnp.sum(probs * prob_grad, axis=0, keepdims=True)
            score_grad = (probs * (prob_grad - delta)).astype(bf16)
            query_grad = dot(key, score_grad, ((1,), (0,))) * inv
            result[0, part, here_q] = unrotate(query_grad, here_q)
            dkey[:, upto] += dot(queries, score_grad, ((1,), (1,)))
            dvalue[:, upto] += dot(out_grad, probs.astype(bf16), ((1,), (1,)))
        result[1, part, :] = unrotate(dkey[...], slice(None))
        result[2, part, :] = dvalue[...].astype(bf16)

    exchanges = [exchange(me, n_dp, grads_copy(head)) for head in range(count)]
    own_copies = [
        pltpu.make_async_copy(
            result.at[:, pl.ds(head * HEAD_DIM, HEAD_DIM), columns(me)],
            grads.at[:, head_rows(me, head), columns(my_batch)],
            local.at[1 + head],
        )
        for head in range(count)
    ]
    for head in range(count):
        attend(head)
        exchanges[head][0]()
        own_copies[head].start()
        for step in steps[:2]:
            step()
        steps = steps[2:]
        for step in row_steps[:LINE_PIECES]:
            step()
        row_steps = row_steps[LINE_PIECES:]
    for step in steps + row_steps:
        step()
    row_end()
    for head in range(count):
        exchanges[head][1]()
        own_copies[head].wait()
    for item in items:
        item.end(psend, precv)
    for final in finals:
        final.wait()
    end()
    for head in range(count):
        exchanges[head][2]()


def backward_fast(prefix, tables, grad, saved, egu, sgu, rows):
    nz = lax.axis_size("z")
    n_dp = nz * 2
    units, lse = saved
    batches = prefix.shape[0]
    span, length = units.shape[1:]
    count = span // HEAD_DIM
    wide = egu.shape[-1]
    arrays = {
        "egu": egu.reshape(4, nz * 2, -1, wide),
        "sgu": sgu.reshape(nz * 8, -1, wide),
    }
    kinds = tuple(arrays)
    rows = rows.reshape(nz, -1, rows.shape[-1])
    any_space, vmem = pl.BlockSpec(memory_space=pl.ANY), pl.BlockSpec(memory_space=pltpu.VMEM)
    block = {kind: arrays[kind].shape[-2:] for kind in kinds}
    results = [((3, *grad.shape), bf16)] + [((nz, *block[kind]), bf16) for kind in kinds]
    results += [(rows.shape[1:], f32)]
    scratch = [
        pltpu.VMEM((span, length), bf16),
        pltpu.VMEM((HEAD_DIM, length), f32),
        pltpu.VMEM((HEAD_DIM, length), f32),
        pltpu.VMEM((3, span, length), bf16),
    ]
    n, items = nz, 2 * nz
    for kind in kinds:
        scratch += [pltpu.VMEM((n, 4, *block[kind]), bf16), pltpu.VMEM((n, 4, *block[kind]), bf16)]
        scratch += [pltpu.VMEM((n, 2, *block[kind]), bf16), pltpu.VMEM((n, *block[kind]), bf16)]
    dma = pltpu.SemaphoreType.DMA
    scratch += [dma((1 + count,)), dma((n_dp,)), dma((n_dp,)), dma((count, n_dp)), dma((count, n_dp))]
    scratch += [dma((items, 4)), dma((items, 7)), dma((items, 7)), dma((items,))]
    line = dma((2, nz, LINE_PIECES))
    scratch += [pltpu.VMEM(rows.shape, bf16)] * 3 + [dma, line, line]
    outs = pl.pallas_call(
        functools.partial(backward_kernel, nz, batches, kinds),
        out_shape=[jax.ShapeDtypeStruct(*result) for result in results],
        in_specs=[pl.BlockSpec(memory_space=pltpu.SMEM), vmem, vmem, any_space, vmem, vmem] + [any_space] * 3,
        out_specs=[any_space] * 3 + [vmem],
        scratch_shapes=scratch,
        compiler_params=params(5, 58 << 20),
        name="attend_backward",
    )(prefix, *tables, grad, units, lse, *arrays.values(), rows)
    grads, egu, sgu, total = outs
    return grads, (egu, sgu), total


class WideSumItem(SumItem):
    def __init__(self, here, index, place, buffers, x_first, starts):
        super().__init__(here, index, place, buffers, x_first)
        self.starts = starts

    def loads(self, a, b, load):
        n = self.slot(a, b)
        for i, (start, src) in enumerate(zip(self.starts, self.place(*self.moved(a, b, 0)[1:]))):
            part = pl.ds(start, src.shape[1])
            yield pltpu.make_async_copy(src, self.own.at[n, :, part], load.at[self.index, n, i])

    def sib_copies(self, a, b, send, recv):
        n = self.slot(a, b)
        for i, (start, src) in enumerate(zip(self.starts, self.place(*self.moved(a, b, 1)[1:]))):
            part = pl.ds(start, src.shape[1])
            sems = send.at[self.index, n, i], recv.at[self.index, n, i]
            yield remote(src, self.sib.at[n, :, part], *sems, self.moved(0, 0, 1))

    def begin(self, load, send, recv):
        for b in (1, 0):
            for a in range(2):
                for copy in (*self.sib_copies(a, b, send, recv), *self.loads(a, b, load)):
                    copy.start()

    def after_core(self, load, wide_send, wide_recv, send, recv):
        for b in (1, 0):
            for a in range(2):
                n = self.slot(a, b)
                for copy in self.loads(a, b, load):
                    copy.wait()
                for copy in self.sib_copies(a, b, wide_send, wide_recv):
                    copy.wait_recv()
                add_to(self.sib.at[n], self.own.at[n])
                if b == 1:
                    self.second_copy(a, send, recv).start()

    def end(self, wide_send, wide_recv, send, recv):
        for a in range(2):
            for b in range(2):
                for copy in self.sib_copies(a, b, wide_send, wide_recv):
                    copy.wait_send()
            self.second_copy(a, send, recv).wait_send()
        self.first_copy(send, recv).wait_send()


def last_kernel(nz, count, *refs):
    refs = list(refs)
    take = lambda n: [refs.pop(0) for _ in range(n)]
    attn_in, (egu_in, sgu_in, ed_in, sd_in) = take(count), take(4)
    attn_out, egu, sgu, ed_out, sd_out = take(5)
    own, sib, second, first, zbuf = take(5)
    ed_parts, sd_parts = take(4), take(4)
    local, load, zsend, zrecv, wsend, wrecv, psend, precv, store, more_load = take(10)
    here = position()
    z, y, x, c = here
    line = [lax.rem(z + d, nz) for d in range(nz)]
    greet([(line[d], y, x, c) for d in range(1, nz)] + [(z, 1 - y, x, c), (z, y, 1 - x, c), (z, y, x, 1 - c)])
    starts, start = [], 0
    for ref in attn_in:
        starts.append(start)
        start += ref.shape[2]
    far_first = sorted(range(nz), key=lambda d: abs(d - nz / 2))
    items = []
    for d in far_first:
        place = lambda py, px, pc, zs=line[d]: [ref.at[((zs * 2 + py) * 2 + px) * 2 + pc] for ref in attn_in]
        parts = (own.at[d], sib.at[d], second.at[d], first.at[d])
        items.append((d, WideSumItem(here, d, place, parts, d % 2 == 1, starts)))
    half = ed_in.shape[2] // 2
    more = []
    for h in range(2):
        rows = pl.ds(h * half, half)
        place = lambda py, px, pc, rows=rows: ed_in.at[px * 2 + pc, py, rows]
        more.append(SumItem(here, nz + h, place, tuple(p.at[h] for p in ed_parts), X_FIRST["ed"](h)))
        more[-1].total = ed_out.at[rows]
    place = lambda py, px, pc: sd_in.at[(py * 2 + px) * 2 + pc]
    more.append(SumItem(here, nz + 2, place, tuple(p.at[0] for p in sd_parts), X_FIRST["sd"](0)))
    more[-1].total = sd_out
    for _, item in items:
        item.begin(load, wsend, wrecv)
    for item in more:
        item.begin(more_load, psend, precv)

    def line_copy(kind, d, arriving=False):
        to, frm = line[d], line[(nz - d) % nz]
        at = frm if arriving else z
        dst = (zbuf, egu, sgu)[kind].at[at]
        src = dst if arriving else (first.at[d], egu_in.at[to], sgu_in.at[to])[kind]
        return remote(src, dst, zsend.at[kind, d], zrecv.at[kind, d], (to, y, x, c))

    for kind in (1, 2):
        for d in far_first[:-1]:
            line_copy(kind, d).start()
    pairs = ((egu_in, egu), (sgu_in, sgu))
    keeps = [pltpu.make_async_copy(src.at[z], dst.at[z], local.at[i]) for i, (src, dst) in enumerate(pairs)]
    for copy in keeps:
        copy.start()
    mine = pltpu.make_async_copy(first.at[0], zbuf.at[z], store)
    both = items + [(None, item) for item in more]
    for t in range(len(both) + 2 * SUM_LAG):
        if t < len(items):
            items[t][1].after_core(load, wsend, wrecv, psend, precv)
        elif t < len(both):
            both[t][1].after_core(more_load, psend, precv)
        if 0 <= t - SUM_LAG < len(both):
            both[t - SUM_LAG][1].after_second(psend, precv)
        if 0 <= t - 2 * SUM_LAG:
            d, item = both[t - 2 * SUM_LAG]
            item.after_first(psend, precv, None if d is not None else item.total)
            if d == 0:
                mine.start()
            elif d is not None:
                line_copy(0, d).start()
    for copy in keeps:
        copy.wait()
    for kind in (1, 2):
        for d in range(1, nz):
            line_copy(kind, d, True).wait_recv()
    mine.wait()
    for d in range(1, nz):
        line_copy(0, d, True).wait_recv()
    attn_out[...] = sum(zbuf[k].astype(f32) for k in range(nz))
    for _, item in items:
        item.end(wsend, wrecv, psend, precv)
    for item in more:
        item.end(psend, precv)
    for kind in range(3):
        for d in range(1, nz):
            line_copy(kind, d).wait_send()


def last_fast(attn, egu, sgu, ed, sd):
    nz = lax.axis_size("z")
    dma = pltpu.SemaphoreType.DMA
    attn = [part.reshape(nz * 8, -1, part.shape[-1]) for part in attn]
    rows, columns = attn[0].shape[1], sum(part.shape[2] for part in attn)
    width = attn[0].shape[0] * rows
    block = (rows, columns)
    vmem = pl.BlockSpec(memory_space=pltpu.VMEM)
    shapes = [block, egu.shape, sgu.shape]
    ed, sd = ed.reshape(4, 2, -1, width), sd.reshape(8, -1, width)
    shapes += [ed.shape[2:], sd.shape[1:]]
    half = (ed.shape[2] // 2, width)
    count = len(attn)
    types = (f32, bf16, bf16, f32, f32)
    return pl.pallas_call(
        functools.partial(last_kernel, nz, count),
        out_shape=[jax.ShapeDtypeStruct(*both) for both in zip(shapes, types)],
        in_specs=any_specs(count + 4),
        out_specs=[vmem] * 5,
        scratch_shapes=[
            pltpu.VMEM((nz, 4, *block), bf16),
            pltpu.VMEM((nz, 4, *block), bf16),
            pltpu.VMEM((nz, 2, *block), bf16),
            pltpu.VMEM((nz, *block), bf16),
            pltpu.VMEM((nz, *block), bf16),
            *[pltpu.VMEM((2, *n, *half), bf16) for n in ((4,), (4,), (2,), ())],
            *[pltpu.VMEM((1, *n, *shapes[-1]), bf16) for n in ((4,), (4,), (2,), ())],
            dma((2,)),
            dma((nz, 4, count)),
            dma((3, nz)),
            dma((3, nz)),
            dma((nz, 4, count)),
            dma((nz, 4, count)),
            dma((nz + 3, 7)),
            dma((nz + 3, 7)),
            dma,
            dma((nz + 3, 4)),
        ],
        compiler_params=params(3, 58 << 20),
        name="last",
    )(*attn, egu, sgu, ed, sd)


def finish_kernel(*refs):
    attn, egu, sgu, ed, sd, attended, out_sum = refs[:7]
    squares, (sgate, sup, sdown, egate, eup, edown, block_out) = refs[7:11], refs[11:]
    width = attended.shape[1]
    for i, ref in enumerate(squares):
        ref[...] = attn[:, pl.ds(i * width, width)]
    for source, outs in ((egu, (egate, eup)), (sgu, (sgate, sup))):
        planes, ff = source.shape[0], source.shape[2] // 2
        for k in range(planes):
            for j in range(2):
                outs[j][:, pl.ds(k * ff, ff)] = source[k, :, pl.ds(j * ff, ff)].astype(f32)
    edown[...] = ed[...]
    sdown[...] = sd[...]
    block_out[...] = (attended[...] + out_sum[...]).astype(bf16)


def finish_fast(sums, attended, out_sum):
    attn, egu, sgu, ed, sd = sums
    width = attended.shape[1]
    shapes = [(attn.shape[0], width)] * 4
    shapes += [(sgu.shape[1], sgu.shape[0] * sgu.shape[2] // 2)] * 2 + [sd.shape]
    shapes += [(egu.shape[1], egu.shape[0] * egu.shape[2] // 2)] * 2 + [ed.shape]
    return pl.pallas_call(
        finish_kernel,
        out_shape=[jax.ShapeDtypeStruct(shape, f32) for shape in shapes]
        + [jax.ShapeDtypeStruct(attended.shape, bf16)],
        compiler_params=pltpu.CompilerParams(vmem_limit_bytes=32 << 20),
        name="finish",
    )(attn, egu, sgu, ed, sd, attended, out_sum)


ORDER = ((0, 1, 2, 3), (1, 0, 2, 3), (2, 3, 1, 0), (3, 2, 1, 0))
EXTRA = 16


def by_distance(z, index):
    code = jnp.int32(0)
    for plane, order in enumerate(ORDER):
        code = jnp.where(z == plane, sum(p * 4**i for i, p in enumerate(order)), code)
    for _ in range(3):
        code = jnp.where(index > 0, code // 4, code)
        index = index - 1
    return lax.rem(code, 4)


def ffn_kernel(capacity, *refs):
    refs = list(refs)
    take = lambda n: [refs.pop(0) for _ in range(n)]
    mixed_in, cot_in, router_in, *weights_in = take(7)
    out_part, total, *grads = take(6)
    weights = take(4)
    egu, sgu, ed, sd = weights
    mixed, cot, router, arrived, pair_grad, expert_hidden, act_grad, s_hidden, s_grad = take(9)
    slot_out, slot_grad, hots, gate_dot, outs, parts, up, down, wide_stage, deep_stage = take(10)
    local, loads, gsend, grecv, ssend, srecv, stores = take(7)
    here = position()
    z, y, x, c = here
    nz = 4
    neighbour = line_partners(here, nz)
    experts = egu.shape[0]
    rows, width = mixed_in.shape
    group = 128
    groups = rows // group
    slots = groups * capacity
    ff = ed.shape[1]

    loading = [pltpu.make_async_copy(router_in, router, local.at[0])]
    loading += [pltpu.make_async_copy(mixed_in, mixed.at[z], local.at[1])]
    loading += [pltpu.make_async_copy(cot_in, cot, local.at[2])]
    shared_loads = [
        pltpu.make_async_copy(weights_in[1], sgu, local.at[3]),
        pltpu.make_async_copy(weights_in[3], sd, local.at[4]),
    ]
    for copy in loading:
        copy.start()

    def expert_loads(e):
        return [
            pltpu.make_async_copy(weights_in[0].at[e], egu.at[e], loads.at[0, e]),
            pltpu.make_async_copy(weights_in[2].at[e], ed.at[e], loads.at[1, e]),
        ]

    for e in range(experts):
        for copy in expert_loads(e):
            copy.start()
    for copy in shared_loads:
        copy.start()
    greet_line(here, nz)

    def may_send(way):
        return z < nz - 1 if way == 0 else z > 0

    def chunk_copy(way, source, src=None):
        dst = mixed.at[source]
        return remote(dst if src is None else src, dst, gsend.at[way, source], grecv.at[way, source], neighbour(1 - 2 * way))

    for way in range(2):
        pl.when(may_send(way))(lambda: chunk_copy(way, z, mixed_in).start())

    def receive(source):
        for way in range(2):

            @pl.when(source < z if way == 0 else source > z)
            def _():
                chunk_copy(way, source).wait_recv()
                pl.when(may_send(way))(lambda: chunk_copy(way, source).start())

    piece_rows = (pl.ds(0, group), pl.ds(group, parts.shape[1] - group))
    came = (up, down)

    def part_copy(way, target, piece):
        part = piece_rows[piece]
        return remote(
            parts.at[target, part],
            came[way].at[target, part],
            ssend.at[way, target, piece],
            srecv.at[way, target, piece],
            neighbour(1 - 2 * way),
        )

    def relay(target, piece):
        part = piece_rows[piece]
        for way in range(2):
            ahead = z < target if way == 0 else z > target
            inner = z > 0 if way == 0 else z < nz - 1

            @pl.when(ahead & inner)
            def _():
                part_copy(way, target, piece).wait_recv()
                mine, theirs = parts.at[target, part], came[way].at[target, part]
                mine[...] = (mine[...].astype(f32) + theirs[...].astype(f32)).astype(bf16)

            pl.when(ahead)(lambda: part_copy(way, target, piece).start())

    for copy in loading:
        copy.wait()

    sub = lax.broadcasted_iota(jnp.int32, (8, group), 0).astype(f32)
    before = lax.broadcasted_iota(jnp.int32, (group, group), 0) < lax.broadcasted_iota(jnp.int32, (group, group), 1)
    before = jnp.where(before, 1.0, 0.0).astype(bf16)
    slot_iota = lax.broadcasted_iota(jnp.int32, (capacity, group), 0).astype(f32)

    def chunk(index, source):
        tokens = mixed.at[source]
        named, ranks, probs = [], [], []
        for g in range(groups):
            lanes = pl.ds(g * group, group)
            ids = cot[source, pl.ds(rows, EXTRA), lanes].astype(f32)
            hot = jnp.where((sub == ids[0:1]) | (sub == ids[1:2]), 1.0, 0.0)
            logits = dot(router[...], mixed[source, lanes, :], ((1,), (1,)))[:8]
            top = jnp.max(jnp.where(hot > 0, logits, neg_fill), axis=0, keepdims=True)
            powers = jnp.where(hot > 0, jnp.exp(logits - top), 0.0)
            probs.append(powers / jnp.sum(powers, axis=0, keepdims=True))
            rank = dot(jnp.concatenate([hot, hot], axis=0).astype(bf16), before, ((1,), (0,)))[:8]
            ranks.append(jnp.where(hot > 0, rank, float(group * TOP_K)))
        gate_dot[...] = jnp.zeros_like(gate_dot)

        def row_of(table, e):
            return jnp.sum(jnp.where(sub == e.astype(f32), table, 0.0), axis=0, keepdims=True)

        @pl.loop(0, experts)
        def _(e):
            @pl.when(index == 0)
            def _():
                for copy in expert_loads(e):
                    copy.wait()

            here_slots = pl.ds(pl.multiple_of(source * slots, 16), slots)
            hot_of, prob_of, cot_of = [], [], []
            for g in range(groups):
                lanes = pl.ds(g * group, group)
                hot = jnp.where(slot_iota == row_of(ranks[g], e), 1.0, 0.0)
                prob_of.append(jnp.sum(hot * row_of(probs[g], e), axis=1, keepdims=True))
                low_hot = hot.astype(bf16)
                hots[g, pl.ds(pl.multiple_of(e * capacity, 16), capacity), :] = low_hot
                hot_of.append(hot)
                mine = pl.ds(pl.multiple_of(source * slots + g * capacity, 16), capacity)
                arrived[e, mine, :] = dot(low_hot, mixed[source, lanes, :], ((1,), (0,))).astype(bf16)
                picked = dot(low_hot, cot[source, lanes, :], ((1,), (0,)))
                cot_of.append(picked)
                pair_grad[e, mine, :] = (picked * prob_of[g]).astype(bf16)
            act = dot(arrived[e, here_slots, :], egu[e], ((1,), (0,)))
            hidden_grad = dot(pair_grad[e, here_slots, :], ed[e], ((1,), (1,)))
            gate_act, up_act = act[:, :ff], act[:, ff:]
            sig = jax.nn.sigmoid(gate_act)
            silu = gate_act * sig
            hidden = (silu * up_act).astype(bf16)
            expert_hidden[e, here_slots, :] = hidden
            gate_grad = (hidden_grad * up_act * (sig * (1.0 + gate_act * (1.0 - sig)))).astype(bf16)
            up_grad = (hidden_grad * silu).astype(bf16)
            act_grad[e, here_slots, pl.ds(0, ff)] = gate_grad
            act_grad[e, here_slots, pl.ds(ff, ff)] = up_grad
            out = dot(hidden, ed[e], ((1,), (0,)))
            back = dot(act_grad[e, here_slots, :], egu[e], ((1,), (1,)))
            for g in range(groups):
                mine, stack = slice(g * capacity, (g + 1) * capacity), pl.ds(pl.multiple_of(e * capacity, 16), capacity)
                lanes = pl.ds(g * group, group)
                slot_out[g, stack, :] = (out[mine] * prob_of[g]).astype(bf16)
                slot_grad[g, stack, :] = back[mine].astype(bf16)
                dots = jnp.sum(out[mine] * cot_of[g], axis=1, keepdims=True)
                dots = jnp.sum(hot_of[g] * dots, axis=0, keepdims=True)
                gate_dot[:, lanes] += jnp.where(sub == e.astype(f32), dots, 0.0)

        @pl.when(index == 0)
        def _():
            for copy in shared_loads:
                copy.wait()

        act = dot(tokens[...], sgu[...], ((1,), (0,)))
        hidden_grad = dot(cot[source, pl.ds(0, rows), :], sd[...], ((1,), (1,)))
        gate_act, up_act = act[:, :ff], act[:, ff:]
        sig = jax.nn.sigmoid(gate_act)
        silu = gate_act * sig
        hidden = (silu * up_act).astype(bf16)
        mine = pl.ds(pl.multiple_of(source * rows, 16), rows)
        s_hidden[mine, :] = hidden
        s_grad[mine, pl.ds(0, ff)] = (hidden_grad * up_act * (sig * (1.0 + gate_act * (1.0 - sig)))).astype(bf16)
        s_grad[mine, pl.ds(ff, ff)] = (hidden_grad * silu).astype(bf16)
        out = dot(hidden, sd[...], ((1,), (0,)))
        back = dot(s_grad[mine, :], sgu[...], ((1,), (1,)))
        for g in range(groups):
            lanes = pl.ds(g * group, group)
            span = slice(g * group, (g + 1) * group)
            outs[source, lanes, :] = (out[span] + dot(hots[g], slot_out[g], ((0,), (0,)))).astype(bf16)
            parts[source, lanes, :] = (back[span] + dot(hots[g], slot_grad[g], ((0,), (0,)))).astype(bf16)
        dots = jnp.concatenate([gate_dot[...], jnp.zeros((EXTRA - 8, rows), f32)], axis=0)
        parts[source, pl.ds(rows, EXTRA), :] = jnp.concatenate(
            [dots, jnp.zeros((EXTRA, width - rows), f32)], axis=1
        ).astype(bf16)

    inner = (z > 0) & (z < nz - 1)

    @pl.loop(0, nz)
    def _(index):
        source = by_distance(z, index)
        pl.when((index == 1) | (index == 3) | ((index == 2) & jnp.logical_not(inner)))(lambda: receive(source))
        pl.when((index == 1) & inner)(lambda: receive(by_distance(z, jnp.int32(2))))
        chunk(index, source)

        @pl.when(jnp.logical_not(inner) & (index > 0))
        def _():
            for piece in range(2):
                relay(source, piece)

        @pl.when(inner & (index == 3))
        def _():
            for piece in range(2):
                relay(by_distance(z, jnp.int32(2)), piece)

    out_copy = pltpu.make_async_copy(outs, out_part, local.at[5])
    out_copy.start()
    far, near = by_distance(z, jnp.int32(3)), by_distance(z, jnp.int32(1))

    def stage_copies(e, slot):
        return [
            pltpu.make_async_copy(wide_stage.at[slot], grads[0].at[e], stores.at[0, slot]),
            pltpu.make_async_copy(deep_stage.at[slot], grads[2].at[e], stores.at[1, slot]),
        ]

    def weight_grads(slot, rows_in, wide, hidden, deep):
        for k in range(0, wide.shape[1], 512):
            span = pl.ds(k, 512)
            wide_stage[slot, :, span] = dot(rows_in[...], wide[:, span], ((0,), (0,))).astype(bf16)
        deep_stage[slot] = dot(hidden[...], deep[...], ((0,), (0,))).astype(bf16)

    @pl.loop(0, experts)
    def _(e):
        slot = lax.rem(e, 2)

        @pl.when(e >= 2)
        def _():
            for copy in stage_copies(e - 2, slot):
                copy.wait()

        weight_grads(slot, arrived.at[e], act_grad.at[e], expert_hidden.at[e], pair_grad.at[e])
        for copy in stage_copies(e, slot):
            copy.start()
        pl.when(inner & (e == 1))(lambda: relay(far, 0))
        pl.when(inner & (e == 2))(lambda: relay(far, 1))
        pl.when(inner & (e == 3))(lambda: relay(near, 0))

    for copy in stage_copies(experts - 2, 0):
        copy.wait()
    tokens = mixed.reshape(nz * rows, width)
    for k in range(0, 2 * ff, 512):
        span = pl.ds(k, 512)
        wide_stage[0, :, span] = dot(tokens[...], s_grad[:, span], ((0,), (0,))).astype(bf16)
    cots = jnp.concatenate([cot[k, pl.ds(0, rows), :] for k in range(nz)], axis=0)
    deep_stage[0] = dot(s_hidden[...], cots, ((0,), (0,))).astype(bf16)
    shared_stores = [
        pltpu.make_async_copy(wide_stage.at[0], grads[1], stores.at[0, 0]),
        pltpu.make_async_copy(deep_stage.at[0], grads[3], stores.at[1, 0]),
    ]
    for copy in shared_stores:
        copy.start()
    pl.when(inner)(lambda: relay(near, 1))
    total[...] = parts[z].astype(f32)
    for way in range(2):

        @pl.when(z > 0 if way == 0 else z < nz - 1)
        def _():
            for piece in range(2):
                part_copy(way, z, piece).wait_recv()
            total[...] += came[way][z].astype(f32)

    for copy in stage_copies(experts - 1, 1) + shared_stores + [out_copy]:
        copy.wait()
    for way in range(2):
        for plane in range(nz):
            sent = (plane <= z if way == 0 else plane >= z) & may_send(way)
            pl.when(sent)(lambda: chunk_copy(way, plane).wait_send())

            @pl.when(z < plane if way == 0 else z > plane)
            def _():
                for piece in range(2):
                    part_copy(way, plane, piece).wait_send()


def ffn_fast(mixed, cot, router, weights, capacity):
    nz = lax.axis_size("z")
    egu, sgu, ed, sd = weights
    rows, width = mixed.shape
    experts, ff = ed.shape[:2]
    cot = cot.reshape(nz, -1, width)
    slots = nz * rows // 128 * capacity
    groups = rows // 128
    vmem, dma = pltpu.VMEM, pltpu.SemaphoreType.DMA
    low = lambda *shape: vmem(shape, bf16)
    scratch = [low(*w.shape) for w in weights]
    scratch += [low(nz, rows, width), low(*cot.shape), low(*router.shape)]
    scratch += [low(experts, slots, width), low(experts, slots, width)]
    scratch += [low(experts, slots, ff), low(experts, slots, 2 * ff), low(nz * rows, ff), low(nz * rows, 2 * ff)]
    stack = experts * capacity
    scratch += [low(groups, stack, width), low(groups, stack, width), low(groups, stack, 128), vmem((8, rows), f32)]
    scratch += [low(nz, rows, width)] + [low(*cot.shape)] * 3
    scratch += [low(2, width, 2 * ff), low(2, ff, width)]
    scratch += [dma((6,)), dma((2, experts)), dma((2, nz)), dma((2, nz)), dma((2, nz, 2)), dma((2, nz, 2)), dma((2, 2))]
    any_space = pl.BlockSpec(memory_space=pl.ANY)
    out_part, total, *grads = pl.pallas_call(
        functools.partial(ffn_kernel, capacity),
        out_shape=[
            jax.ShapeDtypeStruct((nz, rows, width), bf16),
            jax.ShapeDtypeStruct((rows + EXTRA, width), f32),
        ]
        + [jax.ShapeDtypeStruct(w.shape, bf16) for w in weights],
        in_specs=any_specs(7),
        out_specs=[any_space, pl.BlockSpec(memory_space=pltpu.VMEM)] + [any_space] * 4,
        scratch_shapes=scratch,
        compiler_params=params(1, 60 << 20),
        name="feed_forward",
    )(mixed, cot, router, *weights)
    return out_part, total, grads


def visible_units(prefix, heads, here, length):
    unit = lax.axis_index(DP) * here + jnp.arange(here)
    lengths = prefix[jnp.minimum(unit // heads, prefix.shape[0] - 1), 0]
    pos = jnp.arange(length, dtype=jnp.int32)
    low = pos[None, :] < lengths[:, None]
    return (pos[None, None, :] <= pos[None, :, None]) | (low[:, :, None] & low[:, None, :])


def attention_forward(qkv, batches, heads, prefix):
    units = to_units(qkv)
    q, k, v = units[:, 0], units[:, 1], units[:, 2]
    allowed = visible_units(prefix, heads, q.shape[0], q.shape[-1])
    scores = dot(q, k, ((1,), (1,)), ((0,), (0,))) * (1.0 / math.sqrt(HEAD_DIM))
    scores = jnp.where(allowed, scores, neg_fill)
    top = jnp.max(scores, axis=-1, keepdims=True)
    weights = jnp.exp(scores - top)
    total = jnp.sum(weights, axis=-1, keepdims=True)
    lse = top + jnp.log(total)
    probs = (weights / total).astype(bf16)
    context = dot(v, probs, ((2,), (2,)), ((0,), (0,))).astype(bf16)
    return from_units(context[:, None], batches, heads)[0], (q, k, v, lse)


def attention_backward(context_grad, saved, batches, heads, prefix):
    q, k, v, lse = saved
    grad = to_units(context_grad[None])[:, 0]
    allowed = visible_units(prefix, heads, q.shape[0], q.shape[-1])
    inv = 1.0 / math.sqrt(HEAD_DIM)
    scores = dot(q, k, ((1,), (1,)), ((0,), (0,))) * inv
    probs = jnp.where(allowed, jnp.exp(scores - lse), 0.0)
    prob_grad = dot(grad, v, ((1,), (1,)), ((0,), (0,)))
    delta = jnp.sum(probs * prob_grad, axis=-1, keepdims=True)
    score_grad = (probs * (prob_grad - delta)).astype(bf16)
    dq = dot(k, score_grad, ((2,), (2,)), ((0,), (0,))) * inv
    dk = dot(q, score_grad, ((2,), (1,)), ((0,), (0,))) * inv
    dv = dot(grad, probs.astype(bf16), ((2,), (1,)), ((0,), (0,)))
    return from_units(jnp.stack([dq, dk, dv], axis=1).astype(bf16), batches, heads)


def by_batch(tensor, batches):
    kinds, width, count = tensor.shape
    return jnp.transpose(tensor.reshape(kinds, width, batches, count // batches), (0, 2, 1, 3))


def gates(mixed_rows, pair_ids, router_w):
    hot = (pair_ids[..., None] == jnp.arange(router_w.shape[1], dtype=jnp.int32)).astype(f32)
    logits = dot(mixed_rows, router_w, ((1,), (0,)))
    return hot, jax.nn.softmax(jnp.sum(hot * logits[:, None, :], axis=-1), axis=-1)


def ffn_plain(mixed, cot_line, router_w, weights, capacity, rows):
    nz, (count, width), experts = lax.axis_size("z"), mixed.shape, router_w.shape[1]
    egu, sgu, ed, sd = weights
    slice_ff = sd.shape[0]
    cot_line = cot_line.reshape(nz, -1, width)
    mixed_line = gather_line(mixed)
    cot_rows = cot_line[:, :count].reshape(nz * count, width)
    ids = jnp.transpose(cot_line[:, count : count + TOP_K, :count], (0, 2, 1)).reshape(-1, TOP_K).astype(jnp.int32)
    lines = mixed_line.shape[0]
    groups = lines // rows

    hot, probs = gates(mixed_line, ids, router_w)
    hot_int = hot.astype(jnp.int32).reshape(groups, rows * TOP_K, experts)
    earlier = jnp.cumsum(hot_int, axis=1) - hot_int
    rank = jnp.sum(earlier * hot_int, axis=-1).reshape(groups, rows, TOP_K)
    group_ids = ids.reshape(groups, rows, TOP_K)
    slot = jnp.where(rank < capacity, group_ids * capacity + rank, experts * capacity)
    slot_hot = (slot[..., None] == jnp.arange(experts * capacity, dtype=jnp.int32)).astype(bf16)
    token_hot = jnp.sum(slot_hot, axis=2)
    slot_probs = jnp.sum(slot_hot.astype(f32) * probs.reshape(groups, rows, TOP_K, 1), axis=(1, 2))

    def dispatch(values):
        per_group = dot(token_hot, values.reshape(groups, rows, width), ((1,), (1,)), ((0,), (0,)))
        per_group = per_group.reshape(groups, experts, capacity, width)
        return jnp.transpose(per_group, (1, 0, 2, 3)).reshape(experts, groups * capacity, width)

    def per_slot(values):
        return jnp.transpose(values.reshape(groups, experts, capacity), (1, 0, 2)).reshape(experts, -1, 1)

    def combine(slots):
        per_group = jnp.transpose(slots.reshape(experts, groups, capacity, width), (1, 0, 2, 3))
        per_group = per_group.reshape(groups, experts * capacity, width)
        return dot(token_hot, per_group, ((2,), (1,)), ((0,), (0,))).reshape(lines, width)

    slot_p = per_slot(slot_probs)
    arrived = dispatch(mixed_line).astype(bf16)
    cot_slots = dispatch(cot_rows)
    pair_grad = (cot_slots * slot_p).astype(bf16)
    batch = ((0,), (0,))
    act = dot(arrived, egu, ((2,), (1,)), batch)
    gate_act, up_act = act[..., :slice_ff], act[..., slice_ff:]
    sig = jax.nn.sigmoid(gate_act)
    silu_act = gate_act * sig
    expert_hidden = (silu_act * up_act).astype(bf16)
    expert_out = dot(expert_hidden, ed, ((2,), (1,)), batch)
    hidden_grad = dot(pair_grad, ed, ((2,), (2,)), batch)
    gate_up_grad = jnp.concatenate(
        [hidden_grad * up_act * sig * (1.0 + gate_act * (1.0 - sig)), hidden_grad * silu_act], axis=-1
    ).astype(bf16)
    grad_egu = dot(arrived, gate_up_grad, ((1,), (1,)), batch).astype(bf16)
    grad_ed = dot(expert_hidden, pair_grad, ((1,), (1,)), batch).astype(bf16)
    slot_grad = dot(gate_up_grad, egu, ((2,), (2,)), batch).astype(bf16)
    gate_dot = jnp.sum(cot_slots * expert_out, axis=-1)
    gate_dot = jnp.transpose(gate_dot.reshape(experts, groups, capacity), (1, 0, 2)).reshape(groups, 1, 1, -1)
    pair_dot = jnp.sum(slot_hot.astype(f32) * gate_dot, axis=-1).reshape(lines, TOP_K)
    expert_sum = combine((expert_out * slot_p).astype(bf16))

    s_act = dot(mixed_line, sgu, ((1,), (0,)))
    s_in, s_lift = s_act[:, :slice_ff], s_act[:, slice_ff:]
    s_sig = jax.nn.sigmoid(s_in)
    s_silu = s_in * s_sig
    s_hidden = (s_silu * s_lift).astype(bf16)
    s_hidden_grad = dot(cot_rows, sd, ((1,), (1,)))
    s_grad = jnp.concatenate(
        [s_hidden_grad * s_lift * s_sig * (1.0 + s_in * (1.0 - s_sig)), s_hidden_grad * s_silu], axis=-1
    ).astype(bf16)
    grad_sgu = dot(mixed_line, s_grad, ((0,), (0,))).astype(bf16)
    grad_sd = dot(s_hidden, cot_rows, ((0,), (0,))).astype(bf16)
    out_part = (dot(s_hidden, sd, ((1,), (0,))) + expert_sum).astype(bf16)
    mixed_part = combine(slot_grad) + dot(s_grad, sgu, ((1,), (1,)))
    pair_dot = jnp.sum(hot * pair_dot[..., None], axis=1).reshape(nz, count, experts)
    pair_dot = jnp.pad(jnp.transpose(pair_dot, (0, 2, 1)), ((0, 0), (0, EXTRA - experts), (0, width - count)))
    mixed_part = jnp.concatenate([mixed_part.reshape(nz, count, width), pair_dot], axis=1).astype(bf16)
    mixed_sum = sum_line(mixed_part.reshape(-1, width)).astype(f32)
    return out_part, mixed_sum, (grad_egu, grad_sgu, grad_ed, grad_sd)


def shards(
    hidden,
    routes,
    prefix,
    cotangent,
    attn_gain,
    w_query,
    w_key,
    w_value,
    w_output,
    ffn_gain,
    router,
    shared_gate,
    shared_up,
    shared_down,
    expert_gate,
    expert_up,
    expert_down,
):
    nz = lax.axis_size("z")
    batches, _, rows, width = hidden.shape
    count = batches * rows
    heads = width // HEAD_DIM
    experts = router.shape[1]
    own = router.shape[0]
    capacity = (5 * rows * TOP_K + 4 * experts - 1) // (4 * experts)
    slice_ff = shared_gate.shape[1] // nz

    misc = jnp.concatenate(
        [router, attn_gain[:, None], ffn_gain[:, None], jnp.zeros((own, MISC - experts - 2), bf16)], axis=1
    )
    attn_shard = (w_query, w_key, w_value, w_output, misc)
    cot = cotangent.reshape(count, width)
    pair_ids = routes.reshape(count, TOP_K)
    ids_rows = jnp.pad(pair_ids.T.astype(bf16), ((0, EXTRA - TOP_K), (0, width - count)))
    halves = (expert_gate[0], expert_up[0], shared_gate, shared_up)

    def slices(gate, up):
        both = jnp.stack([gate.reshape(-1, nz, slice_ff), up.reshape(-1, nz, slice_ff)], axis=2)
        return jnp.transpose(both.reshape(-1, nz, 2 * slice_ff), (1, 0, 2))

    fast = paired(batches, heads)
    if fast:
        attn_full, lined, ed, sd = first_fast(attn_shard, halves, expert_down[0], shared_down)
    else:
        attn_full = gather_all(jnp.concatenate(attn_shard, axis=1))

    w_qkv = attn_full[:, : 3 * width]
    w_out = attn_full[:, 3 * width : 4 * width]
    misc_full = attn_full[:, 4 * width :]
    router_w = misc_full[:, :experts]
    gain_attn = misc_full[:, experts].astype(f32)
    gain_ffn = misc_full[:, experts + 1].astype(f32)

    x_in = hidden.reshape(count, width).astype(f32)
    attn_scale = rms_scale(x_in)
    attn_norm = x_in * attn_scale
    normed = (attn_norm * gain_attn).astype(bf16)
    positions = lax.axis_index(DP) * rows + jnp.arange(rows, dtype=jnp.int32)
    cosine, sine = rotary_tables(jnp.tile(positions, batches))
    projected = dot(w_qkv, normed, ((0,), (1,)))
    turned = rotate_t(projected[: 2 * width], cosine, sine, 1.0)
    qkv = jnp.concatenate([turned, projected[2 * width :]], axis=0).astype(bf16).reshape(3, width, count)
    if fast:
        context, saved, egu, sgu, cot_line = attend_fast(prefix, qkv, *lined, cotangent, ids_rows)
        ffn = egu, sgu, ed, sd
    else:
        context, saved = attention_forward(by_batch(qkv, batches), batches, heads, prefix)
        context = jnp.transpose(context, (1, 0, 2)).reshape(width, count)
        ffn = gather_weights(slices(*halves[:2]), slices(*halves[2:]), expert_down[0], shared_down)
        cot_line = gather_line(jnp.concatenate([cot, ids_rows], axis=0))
    attended = x_in + dot(context, w_out, ((0,), (0,)))
    ffn_scale = rms_scale(attended)
    ffn_norm = attended * ffn_scale
    mixed = (ffn_norm * gain_ffn).astype(bf16)

    if fast:
        router_rows = jnp.pad(router_w.T, ((0, 16 - experts), (0, 0)))
        out_part, mixed_sum, ffn_grads = ffn_fast(mixed, cot_line, router_rows, ffn, capacity)
    else:
        out_part, mixed_sum, ffn_grads = ffn_plain(mixed, cot_line, router_w, ffn, capacity, rows)

    hot, probs = gates(mixed, pair_ids, router_w)
    gate_grads = jnp.sum(hot * mixed_sum[count : count + experts, :count].T[:, None, :], axis=-1)
    picked = probs * (gate_grads - jnp.sum(probs * gate_grads, axis=-1, keepdims=True))
    logit_grad = jnp.sum(hot * picked[..., None], axis=1)
    grad_router = jnp.dot(mixed.astype(f32).T, logit_grad, precision=highest)
    mixed_grad = mixed_sum[:count] + jnp.dot(logit_grad, router_w.astype(f32).T, precision=highest)
    cot_wide = cot.astype(f32)
    inner = mixed_grad * gain_ffn
    grad_gffn = jnp.sum(mixed_grad * ffn_norm, axis=0)
    attended_grad = cot_wide + ffn_scale * (inner - ffn_norm * jnp.mean(inner * ffn_norm, axis=-1, keepdims=True))
    out_grad = attended_grad.astype(bf16)
    grad_wout = dot(context, out_grad, ((1,), (0,)))
    context_grad = dot(w_out, out_grad, ((1,), (1,))).astype(bf16)

    if fast:
        tables = rotary_tables(jnp.arange(rows * lax.axis_size(DP), dtype=jnp.int32))
        qkv_grad, lined, out_sum = backward_fast(prefix, tables, context_grad, saved, *ffn_grads[:2], out_part)
        qkv_grad = qkv_grad.reshape(3 * width, count)
    else:
        context_grad = by_batch(context_grad[None], batches)[0]
        rot_grad = attention_backward(context_grad, saved, batches, heads, prefix)
        rot_grad = jnp.transpose(rot_grad, (0, 2, 1, 3)).reshape(3 * width, count).astype(f32)
        turned = rotate_t(rot_grad[: 2 * width], cosine, sine, -1.0)
        qkv_grad = jnp.concatenate([turned, rot_grad[2 * width :]], axis=0).astype(bf16)
        egu_sum, sgu_sum, ed_sum, sd_sum = sum_weights(*ffn_grads)
        out_sum = sum_line(out_part)
    grad_wqkv = dot(normed, qkv_grad, ((0,), (1,)))
    normed_grad = dot(qkv_grad, w_qkv, ((0,), (1,)))
    grad_gattn = jnp.sum(normed_grad * attn_norm, axis=0)
    inner = normed_grad * gain_attn
    input_grad = (
        attended_grad + attn_scale * (inner - attn_norm * jnp.mean(inner * attn_norm, axis=-1, keepdims=True))
    ).astype(bf16)

    grad_misc = jnp.concatenate(
        [grad_router, grad_gattn[:, None], grad_gffn[:, None], jnp.zeros((width, MISC - experts - 2), f32)], axis=1
    )
    attn_parts = [part.astype(bf16) for part in (grad_wqkv, grad_wout, grad_misc)]

    def joined(blocks):
        both = jnp.transpose(blocks.reshape(nz, -1, 2, slice_ff), (2, 1, 0, 3)).astype(f32)
        return both.reshape(2, -1, nz * slice_ff)

    if fast:
        sums = last_fast(attn_parts, *lined, *ffn_grads[2:])
        *weight_sums, block_rows = finish_fast(sums, attended, out_sum)
        misc_sums = sums[0][:, 4 * width :]
    else:
        attn_sums = sum_all(jnp.concatenate(attn_parts, axis=1)).astype(f32)
        *attn_sums, misc_sums = jnp.split(attn_sums, [width, 2 * width, 3 * width, 4 * width], axis=1)
        downs = [down.astype(f32) for down in (sd_sum, ed_sum)]
        weight_sums = (*attn_sums, *joined(sgu_sum), downs[0], *joined(egu_sum), downs[1])
        block_rows = (attended + out_sum.astype(f32)).astype(bf16)
    return (
        block_rows.reshape(batches, 1, rows, width),
        input_grad.reshape(batches, 1, rows, width),
        misc_sums[:, experts],
        *weight_sums[:4],
        misc_sums[:, experts + 1],
        misc_sums[:, :experts],
        *weight_sums[4:7],
        *[total[None] for total in weight_sums[7:]],
    )


def solution(mesh):
    n_dp, n_expert = mesh.shape["dp"], mesh.shape["expert"]
    nz = 4 if n_dp % 4 == 0 else 1
    grid = Mesh(mesh.devices.reshape(nz, n_dp // nz, n_expert // 2, 2), ALL)
    rows = P(None, EXPERT, DP, None)
    line = P(ALL)
    dense = P(ALL, None)
    expert = P(EXPERT, DP, None)
    return jax.shard_map(
        shards,
        mesh=grid,
        in_specs=(rows, rows, P(None, EXPERT), rows, line)
        + (dense,) * 4
        + (line,)
        + (dense,) * 4
        + (expert,) * 3,
        out_specs=(rows, rows, line) + (dense,) * 4 + (line,) + (dense,) * 4 + (expert,) * 3,
        check_vma=False,
    )
```

```python
import functools
import math

import jax
import jax.numpy as jnp
from jax import lax
from jax.experimental import pallas as pl
from jax.experimental.pallas import tpu as pltpu
from jax.sharding import Mesh
from jax.sharding import PartitionSpec as P

HEAD_DIM = 64
TOP_K = 2
MISC = 128

eps = 1e-06
highest = lax.Precision.HIGHEST
neg_fill = -1e30
f32 = jnp.float32
bf16 = jnp.bfloat16

ALL = ("z", "y", "x", "c")
PLANE = ("y", "x", "c")
DP = ("z", "y")
EXPERT = ("x", "c")


def rms_scale(values):
    return lax.rsqrt(jnp.mean(values * values, axis=-1, keepdims=True) + eps)


def silu_grad(values):
    sig = jax.nn.sigmoid(values)
    return sig * (1.0 + values * (1.0 - sig))


def dot(a, b, dims, batch=((), ())):
    return lax.dot_general(a, b, (dims, batch), preferred_element_type=f32)


def rotary_tables(positions):
    half = HEAD_DIM // 2
    frequency = jnp.exp(jnp.arange(half, dtype=f32) * (-math.log(10000.0) * 2.0 / HEAD_DIM))
    angles = frequency[:, None] * positions.astype(f32)[None, :]
    return jnp.cos(angles), jnp.sin(angles)


def rotate_t(values, cosine, sine, sign):
    rows = values.shape[-1]
    halves = values.reshape(-1, 2, HEAD_DIM // 2, rows)
    first, second = halves[:, 0], halves[:, 1]
    turned = jnp.stack([first * cosine - sign * second * sine, second * cosine + sign * first * sine], axis=1)
    return turned.reshape(values.shape)


def gather_all(shard):
    return lax.all_gather(shard, ALL, axis=0, tiled=True)


def gather_weights(egu, sgu, ed, sd):
    nz, ny, ne = lax.axis_size("z"), lax.axis_size("y"), lax.axis_size(EXPERT)

    def spread(blocks):
        mine = lax.all_to_all(blocks, "z", 0, 0, tiled=True)
        return lax.all_gather(mine, PLANE, axis=0).reshape(ny, ne, nz, *blocks.shape[1:])

    egu_all = jnp.transpose(spread(egu), (1, 2, 0, 3, 4)).reshape(ne, -1, egu.shape[-1])
    sgu_all = jnp.transpose(spread(sgu), (2, 0, 1, 3, 4)).reshape(-1, sgu.shape[-1])
    ed_all = lax.all_gather(ed, PLANE, axis=0).reshape(ny, ne, *ed.shape)
    ed_all = jnp.transpose(ed_all, (1, 0, 2, 3)).reshape(ne, -1, ed.shape[-1])
    sd_all = lax.all_gather(sd, PLANE, axis=0, tiled=True)
    return egu_all, sgu_all, ed_all, sd_all


def gather_line(rows):
    return lax.all_gather(rows, "z", axis=0, tiled=True)


def paired(batches, heads):
    n_dp = lax.axis_size(DP)
    here = batches * heads // n_dp
    even = here * n_dp == batches * heads and heads % max(1, here) == 0
    return even and tuple(lax.axis_size(name) for name in ALL) == (4, 2, 2, 2)


def sum_line(rows):
    return lax.psum_scatter(rows, "z", scatter_dimension=0, tiled=True)


def sum_weights(egu, sgu, ed, sd):
    nz, ny, ne = lax.axis_size("z"), lax.axis_size("y"), lax.axis_size(EXPERT)

    def collect(parts):
        mine = lax.psum_scatter(parts, PLANE, scatter_dimension=0, tiled=True)
        return lax.all_to_all(mine.reshape(nz, *mine.shape[1:]), "z", 0, 0, tiled=True)

    wide = egu.shape[-1]
    egu = jnp.transpose(egu.reshape(ne, nz, ny, -1, wide), (2, 0, 1, 3, 4))
    sgu = jnp.transpose(sgu.reshape(nz, ny, ne, -1, wide), (1, 2, 0, 3, 4))
    egu = collect(egu.reshape(ny * ne * nz, -1, wide))
    sgu = collect(sgu.reshape(ny * ne * nz, -1, wide))
    ed = jnp.transpose(ed.reshape(ne, ny, -1, ed.shape[-1]), (1, 0, 2, 3)).reshape(ny * ne, -1, ed.shape[-1])
    ed = lax.psum_scatter(ed, PLANE, scatter_dimension=0, tiled=True)[0]
    sd = lax.psum_scatter(sd, PLANE, scatter_dimension=0, tiled=True)
    return egu, sgu, ed, sd


def sum_all(parts):
    return lax.psum_scatter(parts, ALL, scatter_dimension=0, tiled=True)


def units_here(batches, heads):
    return -(-batches * heads // lax.axis_size(DP))


def to_units(tensor):
    kinds, batches, width, rows = tensor.shape
    n_dp = lax.axis_size(DP)
    heads = width // HEAD_DIM
    here = units_here(batches, heads)
    units = tensor.reshape(kinds, batches * heads, HEAD_DIM, rows)
    units = jnp.pad(units, ((0, 0), (0, here * n_dp - batches * heads), (0, 0), (0, 0)))
    units = jnp.transpose(units.reshape(kinds, n_dp, here, HEAD_DIM, rows), (1, 2, 0, 3, 4))
    units = lax.all_to_all(units, DP, 0, 0, tiled=True)
    return jnp.transpose(units, (1, 2, 3, 0, 4)).reshape(here, kinds, HEAD_DIM, n_dp * rows)


def from_units(units, batches, heads):
    here, kinds, _, length = units.shape
    n_dp = lax.axis_size(DP)
    rows = length // n_dp
    parts = jnp.transpose(units.reshape(here, kinds, HEAD_DIM, n_dp, rows), (3, 0, 1, 2, 4))
    parts = lax.all_to_all(parts, DP, 0, 0, tiled=True)
    parts = parts.reshape(n_dp * here, kinds, HEAD_DIM, rows)[: batches * heads]
    return jnp.transpose(parts, (1, 0, 2, 3)).reshape(kinds, batches, heads * HEAD_DIM, rows)


MESH = pl.DeviceIdType.MESH


def position():
    return tuple(lax.axis_index(name) for name in ALL)


def remote(src, dst, send, recv, device):
    return pltpu.make_async_remote_copy(
        src_ref=src, dst_ref=dst, send_sem=send, recv_sem=recv, device_id=device, device_id_type=MESH
    )


def greet(partners):
    barrier = pltpu.get_barrier_semaphore()
    for device in partners:
        pl.semaphore_signal(barrier, inc=1, device_id=device, device_id_type=MESH)
    pl.semaphore_wait(barrier, len(partners))


def any_specs(count):
    return [pl.BlockSpec(memory_space=pl.ANY)] * count


def params(collective_id, vmem=16 << 20):
    return pltpu.CompilerParams(collective_id=collective_id, has_side_effects=True, vmem_limit_bytes=vmem)


class PlaneItem:
    def __init__(self, here, index, place, own, x_first):
        self.here, self.index, self.place, self.own, self.x_first = here, index, place, own, x_first

    def moved(self, along_first, along_second, along_core):
        z, y, x, c = self.here
        move_x, move_y = (along_first, along_second) if self.x_first else (along_second, along_first)
        return (z, 1 - y if move_y else y, 1 - x if move_x else x, 1 - c if along_core else c)

    def ref(self, *moves):
        return self.place(*self.moved(*moves)[1:])

    COPIES = (
        ((0, 0, 0), (1, 0, 0)),
        ((0, 0, 0), (0, 1, 0)),
        ((1, 0, 0), (0, 1, 0)),
        ((0, 0, 0), (0, 0, 1)),
        ((1, 0, 0), (0, 0, 1)),
        ((0, 1, 0), (0, 0, 1)),
        ((1, 1, 0), (0, 0, 1)),
    )

    def copy(self, number, send, recv):
        source, to = self.COPIES[number]
        src = self.own if source == (0, 0, 0) else self.ref(*source)
        return remote(
            src, self.ref(*source), send.at[self.index, number], recv.at[self.index, number], self.moved(*to)
        )

    def arrival(self, number, send, recv):
        source, to = self.COPIES[number]
        ref = self.ref(*[a ^ b for a, b in zip(source, to)])
        return remote(ref, ref, send.at[self.index, number], recv.at[self.index, number], self.moved(*to))


def line_gather_steps(z, nz, own, out, sends, gets, neighbour, pieces):
    def copy(way, source, piece, src=None):
        part = pieces[piece]
        dst = out.at[source, part]
        src = dst if src is None else src.at[part]
        return remote(src, dst, sends.at[way, source, piece], gets.at[way, source, piece], neighbour(1 - 2 * way))

    def may_send(way):
        return z < nz - 1 if way == 0 else z > 0

    def start():
        for piece in range(len(pieces)):
            for way in range(2):
                pl.when(may_send(way))(lambda: copy(way, z, piece, own).start())

    def step(distance, piece):
        for way in range(2):
            source = z - distance if way == 0 else z + distance

            @pl.when((source >= 0) & (source < nz))
            def _():
                copy(way, source, piece).wait_recv()
                pl.when(may_send(way))(lambda: copy(way, source, piece).start())

    def end():
        for distance in range(nz):
            for piece in range(len(pieces)):
                for way in range(2):
                    source = z - distance if way == 0 else z + distance

                    @pl.when((source >= 0) & (source < nz) & may_send(way))
                    def _():
                        copy(way, source, piece).wait_send()

    steps = [functools.partial(step, distance, piece) for distance in range(1, nz) for piece in range(len(pieces))]
    return start, steps, end


def line_partners(here, nz):
    z, y, x, c = here
    return lambda way: (jnp.clip(z + way, 0, nz - 1), y, x, c)


def greet_line(here, nz):
    z = here[0]
    neighbour = line_partners(here, nz)
    barrier = pltpu.get_barrier_semaphore()

    @pl.when(z > 0)
    def _():
        pl.semaphore_signal(barrier, inc=1, device_id=neighbour(-1), device_id_type=MESH)

    @pl.when(z < nz - 1)
    def _():
        pl.semaphore_signal(barrier, inc=1, device_id=neighbour(1), device_id_type=MESH)

    pl.semaphore_wait(barrier, jnp.where(z > 0, 1, 0) + jnp.where(z < nz - 1, 1, 0))


LINE_PIECES = 2


def row_pieces(rows):
    half = rows // 2 // 16 * 16
    return pl.ds(0, half), pl.ds(half, rows - half)


def line_sum_steps(z, nz, parts, total, up, down, sends, gets, neighbour, pieces):
    arrived = (up, down)

    def copy(way, target, piece, src):
        part = pieces[piece]
        dst = arrived[way].at[target, part]
        return remote(src, dst, sends.at[way, target, piece], gets.at[way, target, piece], neighbour(1 - 2 * way))

    def part_of(ref, target, piece):
        return ref.at[target, pieces[piece]]

    def step(distance, piece):
        for way in range(2):
            target = nz - distance if way == 0 else distance - 1
            ahead = z < target if way == 0 else z > target
            first = z == 0 if way == 0 else z == nz - 1
            mine, theirs = part_of(parts, target, piece), part_of(arrived[way], target, piece)

            @pl.when(ahead & first)
            def _():
                copy(way, target, piece, mine).start()

            @pl.when(ahead & jnp.logical_not(first))
            def _():
                copy(way, target, piece, theirs).wait_recv()
                mine[...] = (mine[...].astype(f32) + theirs[...].astype(f32)).astype(bf16)
                copy(way, target, piece, mine).start()

    def end():
        for piece, part in enumerate(pieces):
            total[part, :] = parts[z, part, :].astype(f32)
            for way in range(2):
                theirs = part_of(arrived[way], z, piece)

                @pl.when(z > 0 if way == 0 else z < nz - 1)
                def _():
                    copy(way, z, piece, theirs).wait_recv()
                    total[part, :] += theirs[...].astype(f32)

        for distance in range(1, nz):
            for piece in range(len(pieces)):
                for way in range(2):
                    target = nz - distance if way == 0 else distance - 1

                    @pl.when(z < target if way == 0 else z > target)
                    def _():
                        copy(way, target, piece, part_of(parts, target, piece)).wait_send()

    steps = [functools.partial(step, distance, piece) for distance in range(1, nz) for piece in range(len(pieces))]
    return steps, end


class SumItem:
    def __init__(self, here, index, place, buffers, x_first):
        self.here, self.index, self.place, self.x_first = here, index, place, x_first
        self.own, self.sib, self.second, self.first = buffers

    moved = PlaneItem.moved

    def slot(self, a, b):
        return 2 * a + b

    def begin(self, load, send, recv):
        for a in range(2):
            for b in range(2):
                n = self.slot(a, b)
                self.sib_copy(a, b, send, recv).start()
                pltpu.make_async_copy(self.place(*self.moved(a, b, 0)[1:]), self.own.at[n], load.at[self.index, n]).start()

    def sib_copy(self, a, b, send, recv):
        n = self.slot(a, b)
        src = self.place(*self.moved(a, b, 1)[1:])
        return remote(src, self.sib.at[n], send.at[self.index, n], recv.at[self.index, n], self.moved(0, 0, 1))

    def second_copy(self, a, send, recv):
        n = 4 + a
        src = self.sib.at[self.slot(a, 1)]
        return remote(src, self.second.at[a], send.at[self.index, n], recv.at[self.index, n], self.moved(0, 1, 0))

    def first_copy(self, send, recv):
        src = self.second.at[1]
        return remote(src, self.first, send.at[self.index, 6], recv.at[self.index, 6], self.moved(1, 0, 0))

    def after_core(self, load, send, recv):
        for b in (1, 0):
            for a in range(2):
                n = self.slot(a, b)
                pltpu.make_async_copy(self.own.at[n], self.own.at[n], load.at[self.index, n]).wait()
                self.sib_copy(a, b, send, recv).wait_recv()
                add_to(self.sib.at[n], self.own.at[n])
                if b == 1:
                    self.second_copy(a, send, recv).start()

    def after_second(self, send, recv):
        for a in (1, 0):
            self.second_copy(a, send, recv).wait_recv()
            add_to(self.second.at[a], self.sib.at[self.slot(a, 0)])
            if a == 1:
                self.first_copy(send, recv).start()

    def after_first(self, send, recv, total=None):
        self.first_copy(send, recv).wait_recv()
        if total is None:
            add_to(self.first, self.second.at[0])
        else:
            total[...] = self.first[...].astype(f32) + self.second[0].astype(f32)

    def end(self, send, recv):
        for a in range(2):
            for b in range(2):
                self.sib_copy(a, b, send, recv).wait_send()
            self.second_copy(a, send, recv).wait_send()
        self.first_copy(send, recv).wait_send()


def add_to(total, term):
    rows, columns = total.shape
    if rows % 16 == 0:

        @pl.loop(0, rows // 16)
        def _(i):
            part = pl.ds(pl.multiple_of(i * 16, 16), 16)
            total[part, :] = (total[part, :].astype(f32) + term[part, :].astype(f32)).astype(bf16)
    else:
        wide = max(w for w in (128, 256, 384, 512, 640) if columns % w == 0)

        @pl.loop(0, columns // wide)
        def _(i):
            part = pl.ds(pl.multiple_of(i * wide, 128), wide)
            total[:, part] = (total[:, part].astype(f32) + term[:, part].astype(f32)).astype(bf16)


SUM_LAG = 3


def unit_owner(number, batches, heads, here_units):
    per_batch = heads // here_units
    return number // per_batch, lax.rem(number, per_batch) * here_units


def exchange(me, n_dp, copy):
    ny = 2

    def device(number):
        return (number // ny, lax.rem(number, ny))

    far = [lax.rem(me + d, n_dp) for d in range(1, n_dp)]
    near = [lax.rem(me + n_dp - d, n_dp) for d in range(1, n_dp)]

    def start():
        for number in far:
            copy(number, me, device(number)).start()

    def arrive():
        for number in near:
            copy(me, number, device(number)).wait_recv()

    def end():
        for number in far:
            copy(number, me, device(number)).wait_send()

    return start, arrive, end


def tile_spans(length):
    tile = 256 if length % 512 == 0 else length // 2
    for start in range(0, length, tile):
        if start < length // 2:
            yield start, tile, 0, length // 2
        else:
            yield start, tile, start, start + tile


def masked(values, start, tile, mask_from, keys, length, fill):
    key = mask_from + lax.broadcasted_iota(jnp.int32, (keys - mask_from, tile), 0)
    query = start + lax.broadcasted_iota(jnp.int32, (keys - mask_from, tile), 1)
    allowed = (key <= query) | ((key < length) & (query < length))
    tail = jnp.where(allowed, values[mask_from:], fill)
    return tail if mask_from == 0 else jnp.concatenate([values[:mask_from], tail], axis=0)


X_FIRST = {
    "egu": lambda k: k == 1,
    "sgu": lambda k: k % 2 == 1,
    "sd": lambda k: False,
    "ed": lambda k: k == 1,
}


def plane_items(here, arrays, outs, start=0):
    items = []

    def add(place, own, x_first):
        items.append(PlaneItem(here, start + len(items), place, own, x_first))

    if "ed" in arrays:
        source, ed = arrays["ed"], outs["ed"]
        half = source.shape[0] // 2
        for h in range(2):
            rows = pl.ds(h * half, half)
            add(lambda py, px, pc, rows=rows: ed.at[px * 2 + pc, py, rows], source.at[rows], X_FIRST["ed"](h))
    if "sd" in arrays:
        sd = outs["sd"]
        add(lambda py, px, pc: sd.at[(py * 2 + px) * 2 + pc], arrays["sd"], X_FIRST["sd"](0))
    if "egu" in arrays:
        source, egu = arrays["egu"], outs["egu"]
        for zs in range(source.shape[0]):
            add(lambda py, px, pc, zs=zs: egu.at[px * 2 + pc, zs * 2 + py], source.at[zs], X_FIRST["egu"](zs))
    if "sgu" in arrays:
        source, sgu = arrays["sgu"], outs["sgu"]
        for zs in range(source.shape[0]):
            place = lambda py, px, pc, zs=zs: sgu.at[((zs * 2 + py) * 2 + px) * 2 + pc]
            add(place, source.at[zs], X_FIRST["sgu"](zs))
    return items


def attend_kernel(nz, batches, *refs):
    prefix, qkv, egu_in, sgu_in, cot_in, ids_in = refs[:6]
    context, units, lse, egu, sgu, cot = refs[6:12]
    result, cot_own, egu_own, sgu_own, local, loads, send, recv = refs[12:20]
    csend, crecv, psend, precv, lsend, lrecv = refs[20:]
    here = position()
    z, y, x, c = here
    n_dp = nz * 2
    me = z * 2 + y
    kinds, width, all_rows = qkv.shape
    rows = all_rows // batches
    heads = width // HEAD_DIM
    count = units.shape[1] // HEAD_DIM
    span = count * HEAD_DIM
    length = units.shape[2]
    greet(
        [(lax.rem(me + d, n_dp) // 2, lax.rem(me + d, 2), x, c) for d in range(1, n_dp)]
        + [(z, y, 1 - x, c), (z, y, x, 1 - c)]
    )

    def columns(number):
        return pl.ds(pl.multiple_of(number * rows, rows), rows)

    def qkv_block(number):
        batch, head = unit_owner(number, batches, heads, count)
        return qkv.at[:, pl.ds(pl.multiple_of(head * HEAD_DIM, HEAD_DIM), span), columns(batch)]

    def qkv_copy(number, source, device):
        return remote(
            qkv_block(number), units.at[:, :, columns(source)], send.at[number], recv.at[source], (*device, x, c)
        )

    start, arrive, end = exchange(me, n_dp, qkv_copy)
    start()
    keep = pltpu.make_async_copy(qkv_block(me), units.at[:, :, columns(me)], local.at[0])
    keep.start()
    items = plane_items(here, {"egu": egu_in, "sgu": sgu_in}, {"egu": egu, "sgu": sgu})
    for item in items:
        for number in (0, 1, 3):
            item.copy(number, psend, precv).start()
    fills = [(cot_in.at[b, 0], cot_own.at[pl.ds(b * rows, rows)]) for b in range(batches)]
    fills += [(ids_in, cot_own.at[pl.ds(all_rows, EXTRA)])]
    fills += [(egu_in, egu_own), (sgu_in, sgu_own)]
    fills = [pltpu.make_async_copy(src, dst, loads.at[i]) for i, (src, dst) in enumerate(fills)]
    for copy in fills:
        copy.start()
    owns = [(cot_own, cot.at[z])]
    owns += [(egu_own.at[zs], egu.at[x * 2 + c, zs * 2 + y]) for zs in range(nz)]
    owns += [(sgu_own.at[zs], sgu.at[((zs * 2 + y) * 2 + x) * 2 + c]) for zs in range(nz)]
    keeps = [pltpu.make_async_copy(src, dst, local.at[1 + i]) for i, (src, dst) in enumerate(owns)]
    for copy in fills:
        copy.wait()
    for copy in keeps:
        copy.start()

    def have_first(item):
        item.arrival(0, psend, precv).wait_recv()
        item.copy(2, psend, precv).start()
        item.copy(4, psend, precv).start()

    def have_second(item):
        item.arrival(1, psend, precv).wait_recv()
        item.copy(5, psend, precv).start()
        item.arrival(2, psend, precv).wait_recv()
        item.copy(6, psend, precv).start()

    early = 0
    for item in items[:early]:
        have_first(item)
    line_start, line_steps, line_end = line_gather_steps(
        z, nz, cot_own, cot, lsend, lrecv, line_partners(here, nz), row_pieces(cot.shape[1])
    )
    line_start()
    arrive()
    keep.wait()

    my_batch, my_head = unit_owner(me, batches, heads, count)
    limit = prefix[my_batch, 0]

    def context_copy(head):
        def copy(number, source, device):
            _, first_head = unit_owner(source, batches, heads, count)
            batch, _ = unit_owner(source, batches, heads, count)
            part = pl.ds(pl.multiple_of((first_head + head) * HEAD_DIM, HEAD_DIM), HEAD_DIM)
            return remote(
                result.at[pl.ds(head * HEAD_DIM, HEAD_DIM), columns(number)],
                context.at[part, columns(batch)],
                csend.at[head, number],
                crecv.at[head, source],
                (*device, x, c),
            )

        return copy

    def attend(head):
        part = pl.ds(head * HEAD_DIM, HEAD_DIM)
        for first, tile, mask_from, keys in tile_spans(length):
            queries = units[0, part, pl.ds(first, tile)] * bf16(1.0 / math.sqrt(HEAD_DIM))
            scores = dot(units[1, part, pl.ds(0, keys)], queries, ((0,), (0,)))
            scores = masked(scores, first, tile, mask_from, keys, limit, neg_fill)
            top = jnp.max(scores, axis=0, keepdims=True)
            weights = jnp.exp(scores - top)
            total = jnp.sum(weights, axis=0, keepdims=True)
            lse[head, :, pl.ds(first, tile)] = top + jnp.log(total)
            mean = dot(units[2, part, pl.ds(0, keys)], weights.astype(bf16), ((1,), (0,))) / total
            result[part, pl.ds(first, tile)] = mean.astype(bf16)

    exchanges = [exchange(me, n_dp, context_copy(head)) for head in range(count)]
    own_part = [pl.ds(pl.multiple_of((my_head + head) * HEAD_DIM, HEAD_DIM), HEAD_DIM) for head in range(count)]
    own_copies = [
        pltpu.make_async_copy(
            result.at[pl.ds(head * HEAD_DIM, HEAD_DIM), columns(me)],
            context.at[own_part[head], columns(my_batch)],
            local.at[1 + len(owns) + head],
        )
        for head in range(count)
    ]
    later = [functools.partial(have_first, item) for item in items[early:]]
    later += [functools.partial(have_second, item) for item in items]
    line_steps = list(line_steps)
    for head in range(count):
        attend(head)
        exchanges[head][0]()
        own_copies[head].start()
    share = -(-len(later) // max(1, len(line_steps)))
    while later or line_steps:
        for step in later[:share]:
            step()
        later = later[share:]
        if line_steps:
            line_steps.pop(0)()
    for item in items:
        for number in range(3, 7):
            item.arrival(number, psend, precv).wait_recv()
    for head in range(count):
        exchanges[head][1]()
        own_copies[head].wait()
    for item in items:
        for number in range(7):
            item.copy(number, psend, precv).wait_send()
    end()
    line_end()
    for head in range(count):
        exchanges[head][2]()
    for copy in keeps:
        copy.wait()


def attend_fast(prefix, qkv, egu, sgu, cot, ids):
    nz = lax.axis_size("z")
    n_dp = nz * 2
    kinds, width, all_rows = qkv.shape
    batches = cot.shape[0]
    heads = width // HEAD_DIM
    count = batches * heads // n_dp
    length = n_dp * all_rows // batches
    any_space, vmem = pl.BlockSpec(memory_space=pl.ANY), pl.BlockSpec(memory_space=pltpu.VMEM)
    shapes = [
        ((width, all_rows), bf16),
        ((kinds, count * HEAD_DIM, length), bf16),
        ((count, 1, length), f32),
        ((4, nz * 2, *egu.shape[1:]), bf16),
        ((nz * 8, *sgu.shape[1:]), bf16),
        ((nz, all_rows + EXTRA, width), bf16),
    ]
    dma = pltpu.SemaphoreType.DMA
    items = 2 * nz
    line = dma((2, nz, LINE_PIECES))
    context, units, lse, egu, sgu, cot = pl.pallas_call(
        functools.partial(attend_kernel, nz, batches),
        out_shape=[jax.ShapeDtypeStruct(*shape) for shape in shapes],
        in_specs=[pl.BlockSpec(memory_space=pltpu.SMEM)] + [any_space] * 5,
        out_specs=[any_space, vmem, vmem] + [any_space] * 3,
        scratch_shapes=[
            pltpu.VMEM((count * HEAD_DIM, length), bf16),
            pltpu.VMEM((all_rows + EXTRA, width), bf16),
            *[pltpu.VMEM(a.shape, bf16) for a in (egu, sgu)],
            dma((2 + 2 * nz + count,)),
            dma((batches + 3,)),
            dma((n_dp,)),
            dma((n_dp,)),
            dma((count, n_dp)),
            dma((count, n_dp)),
            dma((items, 7)),
            dma((items, 7)),
            line,
            line,
        ],
        compiler_params=params(4, 58 << 20),
        name="attend",
    )(prefix, qkv, egu, sgu, cot, ids)
    return context, (units, lse), egu.reshape(4, -1, egu.shape[-1]), sgu.reshape(-1, sgu.shape[-1]), cot


def first_kernel(nz, *refs):
    attn_in, halves_in, (ed_in, sd_in) = refs[:5], refs[5:9], refs[9:11]
    attn, egu, sgu, ed, sd, attn_own, egu_own, sgu_own, ed_own, sd_own = refs[11:21]
    local, stores, zsend, zrecv, psend, precv = refs[21:]
    here = position()
    z, y, x, c = here
    line = [lax.rem(z + d, nz) for d in range(nz)]
    ff = egu.shape[-1] // 2

    def flat(zs, py, px, pc):
        return ((zs * 2 + py) * 2 + px) * 2 + pc

    mine = flat(z, y, x, c)
    gathered, start = [], 0
    for i, ref in enumerate(attn_in):
        gathered.append(
            pltpu.make_async_copy(ref, attn_own.at[:, pl.ds(start, ref.shape[1])], local.at[i])
        )
        start += ref.shape[1]
    for kind in range(4):
        src = halves_in[kind].at[:, pl.ds(pl.multiple_of(z * ff, ff), ff)]
        dst = (egu_own if kind < 2 else sgu_own).at[:, pl.ds(kind % 2 * ff, ff)]
        gathered.append(pltpu.make_async_copy(src, dst, local.at[5 + kind]))
    gathered.append(pltpu.make_async_copy(ed_in, ed_own, local.at[9]))
    gathered.append(pltpu.make_async_copy(sd_in, sd_own, local.at[10]))
    for copy in gathered:
        copy.start()
    greet([(line[d], y, x, c) for d in range(1, nz)] + [(z, 1 - y, x, c), (z, y, 1 - x, c), (z, y, x, 1 - c)])

    def half_block(kind, to, at):
        src = halves_in[kind].at[:, pl.ds(pl.multiple_of(to * ff, ff), ff)]
        return src, (egu if kind < 2 else sgu).at[at, :, pl.ds(kind % 2 * ff, ff)]

    def half_copy(kind, d, arriving=False):
        to, frm = line[d], line[(nz - d) % nz]
        src, dst = half_block(kind, to, frm if arriving else z)
        return remote(src, dst, zsend.at[1 + kind, d], zrecv.at[1 + kind, d], (to, y, x, c))

    def attn_copy(d, arriving=False):
        to, frm = line[d], line[(nz - d) % nz]
        ref = attn.at[flat(frm if arriving else z, y, x, c)]
        return remote(ref if arriving else attn_own, ref, zsend.at[0, d], zrecv.at[0, d], (to, y, x, c))

    items = []
    for d in range(nz):
        place = lambda py, px, pc, frm=line[(nz - d) % nz]: attn.at[flat(frm, py, px, pc)]
        items.append(PlaneItem(here, d, place, place(y, x, c) if d else attn_own, d % 2 == 1))

    def have_own(item):
        for number in (0, 1, 3):
            item.copy(number, psend, precv).start()

    far_first = sorted(range(1, nz), key=lambda d: abs(d - nz / 2))
    for copy in gathered:
        copy.wait()
    for d in far_first:
        attn_copy(d).start()
    have_own(items[0])
    for d in far_first:
        for kind in range(4):
            half_copy(kind, d).start()
    more = plane_items(here, {"ed": ed_own, "sd": sd_own}, {"ed": ed, "sd": sd}, nz)
    for item in more:
        have_own(item)
    keeps = [(attn_own, attn.at[mine]), (egu_own, egu.at[z]), (sgu_own, sgu.at[z])]
    keeps += [(ed_own, ed.at[x * 2 + c, y]), (sd_own, sd.at[(y * 2 + x) * 2 + c])]
    keeps = [pltpu.make_async_copy(src, dst, stores.at[i]) for i, (src, dst) in enumerate(keeps)]
    for copy in keeps:
        copy.start()
    for d in range(1, nz):
        attn_copy(d, True).wait_recv()
        have_own(items[d])
    items += more
    for item in items:
        item.arrival(0, psend, precv).wait_recv()
        item.copy(2, psend, precv).start()
        item.copy(4, psend, precv).start()
    for item in items:
        item.arrival(1, psend, precv).wait_recv()
        item.copy(5, psend, precv).start()
    for item in items:
        item.arrival(2, psend, precv).wait_recv()
        item.copy(6, psend, precv).start()
    for item in items:
        for number in range(3, 7):
            item.arrival(number, psend, precv).wait_recv()
    for d in range(1, nz):
        for kind in range(4):
            half_copy(kind, d, True).wait_recv()
    for item in items:
        for number in range(7):
            item.copy(number, psend, precv).wait_send()
    for d in range(1, nz):
        attn_copy(d).wait_send()
        for kind in range(4):
            half_copy(kind, d).wait_send()
    for copy in keeps:
        copy.wait()


def first_fast(attn, halves, ed, sd):
    nz = lax.axis_size("z")
    dma = pltpu.SemaphoreType.DMA
    rows = attn[0].shape[0]
    shapes = [(nz * 8, rows, sum(a.shape[1] for a in attn))]
    shapes += [(nz, half.shape[0], 2 * half.shape[1] // nz) for half in halves[::2]]
    own = [pltpu.VMEM(shape[1:], bf16) for shape in shapes] + [pltpu.VMEM(a.shape, bf16) for a in (ed, sd)]
    shapes += [(4, 2, *ed.shape), (8, *sd.shape)]
    attn, egu, sgu, ed, sd = pl.pallas_call(
        functools.partial(first_kernel, nz),
        out_shape=[jax.ShapeDtypeStruct(shape, bf16) for shape in shapes],
        in_specs=any_specs(11),
        out_specs=any_specs(5),
        scratch_shapes=own
        + [dma((11,)), dma((5,)), dma((5, nz)), dma((5, nz)), dma((nz + 3, 7)), dma((nz + 3, 7))],
        compiler_params=params(0, 58 << 20),
        name="first",
    )(*attn, *halves, ed, sd)
    return attn.reshape(-1, attn.shape[-1]), (egu, sgu), ed.reshape(4, -1, ed.shape[-1]), sd.reshape(-1, sd.shape[-1])


def backward_kernel(nz, batches, kinds, *refs):
    refs = list(refs)
    take = lambda n: [refs.pop(0) for _ in range(n)]
    prefix, cosine, sine, grad_in, units, lse = take(6)
    inputs = dict(zip(kinds, take(len(kinds))))
    (rows_in,) = take(1)
    (grads,) = take(1)
    outputs = dict(zip(kinds, take(len(kinds))))
    (rows_total,) = take(1)
    grad, dkey, dvalue, result = take(4)
    buffers = {kind: take(4) for kind in kinds}
    local, send, recv, csend, crecv, load, psend, precv, store = take(9)
    rows_parts, up, down, lload, lsend, lrecv = take(6)
    here = position()
    z, y, x, c = here
    n_dp = nz * 2
    me = z * 2 + y
    width, all_rows = grad_in.shape
    rows = all_rows // batches
    heads = width // HEAD_DIM
    span, length = grad.shape
    count = span // HEAD_DIM
    row_load = pltpu.make_async_copy(rows_in, rows_parts, lload)
    row_load.start()
    greet(
        [(lax.rem(me + d, n_dp) // 2, lax.rem(me + d, 2), x, c) for d in range(1, n_dp)]
        + [(z, y, 1 - x, c), (z, y, x, 1 - c)]
    )

    def columns(number):
        return pl.ds(pl.multiple_of(number * rows, rows), rows)

    def grad_block(number):
        batch, head = unit_owner(number, batches, heads, count)
        return grad_in.at[pl.ds(pl.multiple_of(head * HEAD_DIM, HEAD_DIM), span), columns(batch)]

    def grad_copy(number, source, device):
        return remote(
            grad_block(number), grad.at[:, columns(source)], send.at[number], recv.at[source], (*device, x, c)
        )

    start, arrive, end = exchange(me, n_dp, grad_copy)
    start()
    keep = pltpu.make_async_copy(grad_block(me), grad.at[:, columns(me)], local.at[0])
    keep.start()

    places = {
        "egu": lambda zs: lambda py, px, pc: inputs["egu"].at[px * 2 + pc, zs * 2 + py],
        "sgu": lambda zs: lambda py, px, pc: inputs["sgu"].at[((zs * 2 + py) * 2 + px) * 2 + pc],
    }
    items, finals = [], []
    for kind in kinds:
        for k in range(nz):
            parts = tuple(buffer.at[k] for buffer in buffers[kind])
            item = SumItem(here, len(items), places[kind](k), parts, X_FIRST[kind](k))
            finals.append(pltpu.make_async_copy(item.first, outputs[kind].at[k], store.at[item.index]))
            items.append(item)
    for item in items:
        item.begin(load, psend, precv)
    row_load.wait()
    row_steps, row_end = line_sum_steps(
        z, nz, rows_parts, rows_total, up, down, lsend, lrecv, line_partners(here, nz), row_pieces(rows_parts.shape[1])
    )

    def stage(t):
        if t < len(items):
            items[t].after_core(load, psend, precv)
        if 0 <= t - SUM_LAG < len(items):
            items[t - SUM_LAG].after_second(psend, precv)
        if 0 <= t - 2 * SUM_LAG < len(items):
            items[t - 2 * SUM_LAG].after_first(psend, precv)
            finals[t - 2 * SUM_LAG].start()

    steps = [functools.partial(stage, t) for t in range(len(items) + 2 * SUM_LAG)]
    for step in steps[:2] + row_steps[:2] + steps[2:2]:
        step()
    steps, row_steps = steps[2:], row_steps[2:]
    arrive()
    keep.wait()

    my_batch, my_head = unit_owner(me, batches, heads, count)
    limit = prefix[my_batch, 0]
    inv = 1.0 / math.sqrt(HEAD_DIM)

    def head_rows(source, head):
        _, first_head = unit_owner(source, batches, heads, count)
        return pl.ds(pl.multiple_of((first_head + head) * HEAD_DIM, HEAD_DIM), HEAD_DIM)

    def grads_copy(head):
        def copy(number, source, device):
            batch, _ = unit_owner(source, batches, heads, count)
            return remote(
                result.at[:, pl.ds(head * HEAD_DIM, HEAD_DIM), columns(number)],
                grads.at[:, head_rows(source, head), columns(batch)],
                csend.at[head, number],
                crecv.at[head, source],
                (*device, x, c),
            )

        return copy

    def unrotate(values, place):
        first, second = values[: HEAD_DIM // 2], values[HEAD_DIM // 2 :]
        cos, sin = cosine[:, place], sine[:, place]
        return jnp.concatenate([first * cos + second * sin, second * cos - first * sin], axis=0).astype(bf16)

    def attend(head):
        part = pl.ds(head * HEAD_DIM, HEAD_DIM)
        dkey[...] = jnp.zeros_like(dkey)
        dvalue[...] = jnp.zeros_like(dvalue)
        for first, tile, mask_from, keys in tile_spans(length):
            here_q, upto = pl.ds(first, tile), pl.ds(0, keys)
            queries = units[0, part, here_q] * bf16(inv)
            key, value, out_grad = units[1, part, upto], units[2, part, upto], grad[part, here_q]
            scores = dot(key, queries, ((0,), (0,)))
            probs = jnp.exp(scores - lse[head, :, here_q])
            probs = masked(probs, first, tile, mask_from, keys, limit, 0.0)
            prob_grad = dot(value, out_grad, ((0,), (0,)))
            delta = jnp.sum(probs * prob_grad, axis=0, keepdims=True)
            score_grad = (probs * (prob_grad - delta)).astype(bf16)
            query_grad = dot(key, score_grad, ((1,), (0,))) * inv
            result[0, part, here_q] = unrotate(query_grad, here_q)
            dkey[:, upto] += dot(queries, score_grad, ((1,), (1,)))
            dvalue[:, upto] += dot(out_grad, probs.astype(bf16), ((1,), (1,)))
        result[1, part, :] = unrotate(dkey[...], slice(None))
        result[2, part, :] = dvalue[...].astype(bf16)

    exchanges = [exchange(me, n_dp, grads_copy(head)) for head in range(count)]
    own_copies = [
        pltpu.make_async_copy(
            result.at[:, pl.ds(head * HEAD_DIM, HEAD_DIM), columns(me)],
            grads.at[:, head_rows(me, head), columns(my_batch)],
            local.at[1 + head],
        )
        for head in range(count)
    ]
    for head in range(count):
        attend(head)
        exchanges[head][0]()
        own_copies[head].start()
        for step in steps[:2]:
            step()
        steps = steps[2:]
        for step in row_steps[:LINE_PIECES]:
            step()
        row_steps = row_steps[LINE_PIECES:]
    for step in steps + row_steps:
        step()
    row_end()
    for head in range(count):
        exchanges[head][1]()
        own_copies[head].wait()
    for item in items:
        item.end(psend, precv)
    for final in finals:
        final.wait()
    end()
    for head in range(count):
        exchanges[head][2]()


def backward_fast(prefix, tables, grad, saved, egu, sgu, rows):
    nz = lax.axis_size("z")
    n_dp = nz * 2
    units, lse = saved
    batches = prefix.shape[0]
    span, length = units.shape[1:]
    count = span // HEAD_DIM
    wide = egu.shape[-1]
    arrays = {
        "egu": egu.reshape(4, nz * 2, -1, wide),
        "sgu": sgu.reshape(nz * 8, -1, wide),
    }
    kinds = tuple(arrays)
    rows = rows.reshape(nz, -1, rows.shape[-1])
    any_space, vmem = pl.BlockSpec(memory_space=pl.ANY), pl.BlockSpec(memory_space=pltpu.VMEM)
    block = {kind: arrays[kind].shape[-2:] for kind in kinds}
    results = [((3, *grad.shape), bf16)] + [((nz, *block[kind]), bf16) for kind in kinds]
    results += [(rows.shape[1:], f32)]
    scratch = [
        pltpu.VMEM((span, length), bf16),
        pltpu.VMEM((HEAD_DIM, length), f32),
        pltpu.VMEM((HEAD_DIM, length), f32),
        pltpu.VMEM((3, span, length), bf16),
    ]
    n, items = nz, 2 * nz
    for kind in kinds:
        scratch += [pltpu.VMEM((n, 4, *block[kind]), bf16), pltpu.VMEM((n, 4, *block[kind]), bf16)]
        scratch += [pltpu.VMEM((n, 2, *block[kind]), bf16), pltpu.VMEM((n, *block[kind]), bf16)]
    dma = pltpu.SemaphoreType.DMA
    scratch += [dma((1 + count,)), dma((n_dp,)), dma((n_dp,)), dma((count, n_dp)), dma((count, n_dp))]
    scratch += [dma((items, 4)), dma((items, 7)), dma((items, 7)), dma((items,))]
    line = dma((2, nz, LINE_PIECES))
    scratch += [pltpu.VMEM(rows.shape, bf16)] * 3 + [dma, line, line]
    outs = pl.pallas_call(
        functools.partial(backward_kernel, nz, batches, kinds),
        out_shape=[jax.ShapeDtypeStruct(*result) for result in results],
        in_specs=[pl.BlockSpec(memory_space=pltpu.SMEM), vmem, vmem, any_space, vmem, vmem] + [any_space] * 3,
        out_specs=[any_space] * 3 + [vmem],
        scratch_shapes=scratch,
        compiler_params=params(5, 58 << 20),
        name="attend_backward",
    )(prefix, *tables, grad, units, lse, *arrays.values(), rows)
    grads, egu, sgu, total = outs
    return grads, (egu, sgu), total


class WideSumItem(SumItem):
    def __init__(self, here, index, place, buffers, x_first, starts):
        super().__init__(here, index, place, buffers, x_first)
        self.starts = starts

    def loads(self, a, b, load):
        n = self.slot(a, b)
        for i, (start, src) in enumerate(zip(self.starts, self.place(*self.moved(a, b, 0)[1:]))):
            part = pl.ds(start, src.shape[1])
            yield pltpu.make_async_copy(src, self.own.at[n, :, part], load.at[self.index, n, i])

    def sib_copies(self, a, b, send, recv):
        n = self.slot(a, b)
        for i, (start, src) in enumerate(zip(self.starts, self.place(*self.moved(a, b, 1)[1:]))):
            part = pl.ds(start, src.shape[1])
            sems = send.at[self.index, n, i], recv.at[self.index, n, i]
            yield remote(src, self.sib.at[n, :, part], *sems, self.moved(0, 0, 1))

    def begin(self, load, send, recv):
        for b in (1, 0):
            for a in range(2):
                for copy in (*self.sib_copies(a, b, send, recv), *self.loads(a, b, load)):
                    copy.start()

    def after_core(self, load, wide_send, wide_recv, send, recv):
        for b in (1, 0):
            for a in range(2):
                n = self.slot(a, b)
                for copy in self.loads(a, b, load):
                    copy.wait()
                for copy in self.sib_copies(a, b, wide_send, wide_recv):
                    copy.wait_recv()
                add_to(self.sib.at[n], self.own.at[n])
                if b == 1:
                    self.second_copy(a, send, recv).start()

    def end(self, wide_send, wide_recv, send, recv):
        for a in range(2):
            for b in range(2):
                for copy in self.sib_copies(a, b, wide_send, wide_recv):
                    copy.wait_send()
            self.second_copy(a, send, recv).wait_send()
        self.first_copy(send, recv).wait_send()


def last_kernel(nz, count, *refs):
    refs = list(refs)
    take = lambda n: [refs.pop(0) for _ in range(n)]
    attn_in, (egu_in, sgu_in, ed_in, sd_in) = take(count), take(4)
    attn_out, egu, sgu, ed_out, sd_out = take(5)
    own, sib, second, first, zbuf = take(5)
    ed_parts, sd_parts = take(4), take(4)
    local, load, zsend, zrecv, wsend, wrecv, psend, precv, store, more_load = take(10)
    here = position()
    z, y, x, c = here
    line = [lax.rem(z + d, nz) for d in range(nz)]
    greet([(line[d], y, x, c) for d in range(1, nz)] + [(z, 1 - y, x, c), (z, y, 1 - x, c), (z, y, x, 1 - c)])
    starts, start = [], 0
    for ref in attn_in:
        starts.append(start)
        start += ref.shape[2]
    far_first = sorted(range(nz), key=lambda d: abs(d - nz / 2))
    items = []
    for d in far_first:
        place = lambda py, px, pc, zs=line[d]: [ref.at[((zs * 2 + py) * 2 + px) * 2 + pc] for ref in attn_in]
        parts = (own.at[d], sib.at[d], second.at[d], first.at[d])
        items.append((d, WideSumItem(here, d, place, parts, d % 2 == 1, starts)))
    half = ed_in.shape[2] // 2
    more = []
    for h in range(2):
        rows = pl.ds(h * half, half)
        place = lambda py, px, pc, rows=rows: ed_in.at[px * 2 + pc, py, rows]
        more.append(SumItem(here, nz + h, place, tuple(p.at[h] for p in ed_parts), X_FIRST["ed"](h)))
        more[-1].total = ed_out.at[rows]
    place = lambda py, px, pc: sd_in.at[(py * 2 + px) * 2 + pc]
    more.append(SumItem(here, nz + 2, place, tuple(p.at[0] for p in sd_parts), X_FIRST["sd"](0)))
    more[-1].total = sd_out
    for _, item in items:
        item.begin(load, wsend, wrecv)
    for item in more:
        item.begin(more_load, psend, precv)

    def line_copy(kind, d, arriving=False):
        to, frm = line[d], line[(nz - d) % nz]
        at = frm if arriving else z
        dst = (zbuf, egu, sgu)[kind].at[at]
        src = dst if arriving else (first.at[d], egu_in.at[to], sgu_in.at[to])[kind]
        return remote(src, dst, zsend.at[kind, d], zrecv.at[kind, d], (to, y, x, c))

    for kind in (1, 2):
        for d in far_first[:-1]:
            line_copy(kind, d).start()
    pairs = ((egu_in, egu), (sgu_in, sgu))
    keeps = [pltpu.make_async_copy(src.at[z], dst.at[z], local.at[i]) for i, (src, dst) in enumerate(pairs)]
    for copy in keeps:
        copy.start()
    mine = pltpu.make_async_copy(first.at[0], zbuf.at[z], store)
    both = items + [(None, item) for item in more]
    for t in range(len(both) + 2 * SUM_LAG):
        if t < len(items):
            items[t][1].after_core(load, wsend, wrecv, psend, precv)
        elif t < len(both):
            both[t][1].after_core(more_load, psend, precv)
        if 0 <= t - SUM_LAG < len(both):
            both[t - SUM_LAG][1].after_second(psend, precv)
        if 0 <= t - 2 * SUM_LAG:
            d, item = both[t - 2 * SUM_LAG]
            item.after_first(psend, precv, None if d is not None else item.total)
            if d == 0:
                mine.start()
            elif d is not None:
                line_copy(0, d).start()
    for copy in keeps:
        copy.wait()
    for kind in (1, 2):
        for d in range(1, nz):
            line_copy(kind, d, True).wait_recv()
    mine.wait()
    for d in range(1, nz):
        line_copy(0, d, True).wait_recv()
    attn_out[...] = sum(zbuf[k].astype(f32) for k in range(nz))
    for _, item in items:
        item.end(wsend, wrecv, psend, precv)
    for item in more:
        item.end(psend, precv)
    for kind in range(3):
        for d in range(1, nz):
            line_copy(kind, d).wait_send()


def last_fast(attn, egu, sgu, ed, sd):
    nz = lax.axis_size("z")
    dma = pltpu.SemaphoreType.DMA
    attn = [part.reshape(nz * 8, -1, part.shape[-1]) for part in attn]
    rows, columns = attn[0].shape[1], sum(part.shape[2] for part in attn)
    width = attn[0].shape[0] * rows
    block = (rows, columns)
    vmem = pl.BlockSpec(memory_space=pltpu.VMEM)
    shapes = [block, egu.shape, sgu.shape]
    ed, sd = ed.reshape(4, 2, -1, width), sd.reshape(8, -1, width)
    shapes += [ed.shape[2:], sd.shape[1:]]
    half = (ed.shape[2] // 2, width)
    count = len(attn)
    types = (f32, bf16, bf16, f32, f32)
    return pl.pallas_call(
        functools.partial(last_kernel, nz, count),
        out_shape=[jax.ShapeDtypeStruct(*both) for both in zip(shapes, types)],
        in_specs=any_specs(count + 4),
        out_specs=[vmem] * 5,
        scratch_shapes=[
            pltpu.VMEM((nz, 4, *block), bf16),
            pltpu.VMEM((nz, 4, *block), bf16),
            pltpu.VMEM((nz, 2, *block), bf16),
            pltpu.VMEM((nz, *block), bf16),
            pltpu.VMEM((nz, *block), bf16),
            *[pltpu.VMEM((2, *n, *half), bf16) for n in ((4,), (4,), (2,), ())],
            *[pltpu.VMEM((1, *n, *shapes[-1]), bf16) for n in ((4,), (4,), (2,), ())],
            dma((2,)),
            dma((nz, 4, count)),
            dma((3, nz)),
            dma((3, nz)),
            dma((nz, 4, count)),
            dma((nz, 4, count)),
            dma((nz + 3, 7)),
            dma((nz + 3, 7)),
            dma,
            dma((nz + 3, 4)),
        ],
        compiler_params=params(3, 58 << 20),
        name="last",
    )(*attn, egu, sgu, ed, sd)


def finish_kernel(*refs):
    attn, egu, sgu, ed, sd, attended, out_sum = refs[:7]
    squares, (sgate, sup, sdown, egate, eup, edown, block_out) = refs[7:11], refs[11:]
    width = attended.shape[1]
    for i, ref in enumerate(squares):
        ref[...] = attn[:, pl.ds(i * width, width)]
    for source, outs in ((egu, (egate, eup)), (sgu, (sgate, sup))):
        planes, ff = source.shape[0], source.shape[2] // 2
        for k in range(planes):
            for j in range(2):
                outs[j][:, pl.ds(k * ff, ff)] = source[k, :, pl.ds(j * ff, ff)].astype(f32)
    edown[...] = ed[...]
    sdown[...] = sd[...]
    block_out[...] = (attended[...] + out_sum[...]).astype(bf16)


def finish_fast(sums, attended, out_sum):
    attn, egu, sgu, ed, sd = sums
    width = attended.shape[1]
    shapes = [(attn.shape[0], width)] * 4
    shapes += [(sgu.shape[1], sgu.shape[0] * sgu.shape[2] // 2)] * 2 + [sd.shape]
    shapes += [(egu.shape[1], egu.shape[0] * egu.shape[2] // 2)] * 2 + [ed.shape]
    return pl.pallas_call(
        finish_kernel,
        out_shape=[jax.ShapeDtypeStruct(shape, f32) for shape in shapes]
        + [jax.ShapeDtypeStruct(attended.shape, bf16)],
        compiler_params=pltpu.CompilerParams(vmem_limit_bytes=60 << 20),
        name="finish",
    )(attn, egu, sgu, ed, sd, attended, out_sum)


ORDER = ((0, 1, 2, 3), (1, 0, 2, 3), (2, 3, 1, 0), (3, 2, 1, 0))
EXTRA = 16


def by_distance(z, index):
    code = jnp.int32(0)
    for plane, order in enumerate(ORDER):
        code = jnp.where(z == plane, sum(p * 4**i for i, p in enumerate(order)), code)
    for _ in range(3):
        code = jnp.where(index > 0, code // 4, code)
        index = index - 1
    return lax.rem(code, 4)


def ffn_kernel(capacity, *refs):
    refs = list(refs)
    take = lambda n: [refs.pop(0) for _ in range(n)]
    mixed_in, cot_in, router_in, *weights_in = take(7)
    out_part, total, *grads = take(6)
    weights = take(4)
    egu, sgu, ed, sd = weights
    mixed, cot, router, arrived, pair_grad, expert_hidden, act_grad, s_hidden, s_grad = take(9)
    slot_out, slot_grad, hots, gate_dot, outs, parts, up, down, wide_stage, deep_stage = take(10)
    local, loads, gsend, grecv, ssend, srecv, stores = take(7)
    here = position()
    z, y, x, c = here
    nz = 4
    neighbour = line_partners(here, nz)
    experts = egu.shape[0]
    rows, width = mixed_in.shape
    group = 128
    groups = rows // group
    slots = groups * capacity
    ff = ed.shape[1]

    loading = [pltpu.make_async_copy(router_in, router, local.at[0])]
    loading += [pltpu.make_async_copy(mixed_in, mixed.at[z], local.at[1])]
    loading += [pltpu.make_async_copy(cot_in, cot, local.at[2])]
    shared_loads = [
        pltpu.make_async_copy(weights_in[1], sgu, local.at[3]),
        pltpu.make_async_copy(weights_in[3], sd, local.at[4]),
    ]
    for copy in loading:
        copy.start()

    def expert_loads(e):
        return [
            pltpu.make_async_copy(weights_in[0].at[e], egu.at[e], loads.at[0, e]),
            pltpu.make_async_copy(weights_in[2].at[e], ed.at[e], loads.at[1, e]),
        ]

    for e in range(experts):
        for copy in expert_loads(e):
            copy.start()
    for copy in shared_loads:
        copy.start()
    greet_line(here, nz)

    def may_send(way):
        return z < nz - 1 if way == 0 else z > 0

    def chunk_copy(way, source, src=None):
        dst = mixed.at[source]
        return remote(dst if src is None else src, dst, gsend.at[way, source], grecv.at[way, source], neighbour(1 - 2 * way))

    for way in range(2):
        pl.when(may_send(way))(lambda: chunk_copy(way, z, mixed_in).start())

    def receive(source):
        for way in range(2):

            @pl.when(source < z if way == 0 else source > z)
            def _():
                chunk_copy(way, source).wait_recv()
                pl.when(may_send(way))(lambda: chunk_copy(way, source).start())

    piece_rows = (pl.ds(0, group), pl.ds(group, parts.shape[1] - group))
    came = (up, down)

    def part_copy(way, target, piece):
        part = piece_rows[piece]
        return remote(
            parts.at[target, part],
            came[way].at[target, part],
            ssend.at[way, target, piece],
            srecv.at[way, target, piece],
            neighbour(1 - 2 * way),
        )

    def relay(target, piece):
        part = piece_rows[piece]
        for way in range(2):
            ahead = z < target if way == 0 else z > target
            inner = z > 0 if way == 0 else z < nz - 1

            @pl.when(ahead & inner)
            def _():
                part_copy(way, target, piece).wait_recv()
                mine, theirs = parts.at[target, part], came[way].at[target, part]
                mine[...] = (mine[...].astype(f32) + theirs[...].astype(f32)).astype(bf16)

            pl.when(ahead)(lambda: part_copy(way, target, piece).start())

    for copy in loading:
        copy.wait()

    sub = lax.broadcasted_iota(jnp.int32, (8, group), 0).astype(f32)
    before = lax.broadcasted_iota(jnp.int32, (group, group), 0) < lax.broadcasted_iota(jnp.int32, (group, group), 1)
    before = jnp.where(before, 1.0, 0.0).astype(bf16)
    slot_iota = lax.broadcasted_iota(jnp.int32, (capacity, group), 0).astype(f32)

    def chunk(index, source):
        tokens = mixed.at[source]
        named, ranks, probs = [], [], []
        for g in range(groups):
            lanes = pl.ds(g * group, group)
            ids = cot[source, pl.ds(rows, EXTRA), lanes].astype(f32)
            hot = jnp.where((sub == ids[0:1]) | (sub == ids[1:2]), 1.0, 0.0)
            logits = dot(router[...], mixed[source, lanes, :], ((1,), (1,)))[:8]
            top = jnp.max(jnp.where(hot > 0, logits, neg_fill), axis=0, keepdims=True)
            powers = jnp.where(hot > 0, jnp.exp(logits - top), 0.0)
            probs.append(powers / jnp.sum(powers, axis=0, keepdims=True))
            rank = dot(jnp.concatenate([hot, hot], axis=0).astype(bf16), before, ((1,), (0,)))[:8]
            ranks.append(jnp.where(hot > 0, rank, float(group * TOP_K)))
        gate_dot[...] = jnp.zeros_like(gate_dot)

        def row_of(table, e):
            return jnp.sum(jnp.where(sub == e.astype(f32), table, 0.0), axis=0, keepdims=True)

        @pl.loop(0, experts)
        def _(e):
            @pl.when(index == 0)
            def _():
                for copy in expert_loads(e):
                    copy.wait()

            here_slots = pl.ds(pl.multiple_of(source * slots, 16), slots)
            hot_of, prob_of, cot_of = [], [], []
            for g in range(groups):
                lanes = pl.ds(g * group, group)
                hot = jnp.where(slot_iota == row_of(ranks[g], e), 1.0, 0.0)
                prob_of.append(jnp.sum(hot * row_of(probs[g], e), axis=1, keepdims=True))
                low_hot = hot.astype(bf16)
                hots[g, pl.ds(pl.multiple_of(e * capacity, 16), capacity), :] = low_hot
                hot_of.append(hot)
                mine = pl.ds(pl.multiple_of(source * slots + g * capacity, 16), capacity)
                arrived[e, mine, :] = dot(low_hot, mixed[source, lanes, :], ((1,), (0,))).astype(bf16)
                picked = dot(low_hot, cot[source, lanes, :], ((1,), (0,)))
                cot_of.append(picked)
                pair_grad[e, mine, :] = (picked * prob_of[g]).astype(bf16)
            act = dot(arrived[e, here_slots, :], egu[e], ((1,), (0,)))
            hidden_grad = dot(pair_grad[e, here_slots, :], ed[e], ((1,), (1,)))
            gate_act, up_act = act[:, :ff], act[:, ff:]
            sig = jax.nn.sigmoid(gate_act)
            silu = gate_act * sig
            hidden = (silu * up_act).astype(bf16)
            expert_hidden[e, here_slots, :] = hidden
            gate_grad = (hidden_grad * up_act * (sig * (1.0 + gate_act * (1.0 - sig)))).astype(bf16)
            up_grad = (hidden_grad * silu).astype(bf16)
            act_grad[e, here_slots, pl.ds(0, ff)] = gate_grad
            act_grad[e, here_slots, pl.ds(ff, ff)] = up_grad
            out = dot(hidden, ed[e], ((1,), (0,)))
            back = dot(act_grad[e, here_slots, :], egu[e], ((1,), (1,)))
            for g in range(groups):
                mine, stack = slice(g * capacity, (g + 1) * capacity), pl.ds(pl.multiple_of(e * capacity, 16), capacity)
                lanes = pl.ds(g * group, group)
                slot_out[g, stack, :] = (out[mine] * prob_of[g]).astype(bf16)
                slot_grad[g, stack, :] = back[mine].astype(bf16)
                dots = jnp.sum(out[mine] * cot_of[g], axis=1, keepdims=True)
                dots = jnp.sum(hot_of[g] * dots, axis=0, keepdims=True)
                gate_dot[:, lanes] += jnp.where(sub == e.astype(f32), dots, 0.0)

        @pl.when(index == 0)
        def _():
            for copy in shared_loads:
                copy.wait()

        act = dot(tokens[...], sgu[...], ((1,), (0,)))
        hidden_grad = dot(cot[source, pl.ds(0, rows), :], sd[...], ((1,), (1,)))
        gate_act, up_act = act[:, :ff], act[:, ff:]
        sig = jax.nn.sigmoid(gate_act)
        silu = gate_act * sig
        hidden = (silu * up_act).astype(bf16)
        mine = pl.ds(pl.multiple_of(source * rows, 16), rows)
        s_hidden[mine, :] = hidden
        s_grad[mine, pl.ds(0, ff)] = (hidden_grad * up_act * (sig * (1.0 + gate_act * (1.0 - sig)))).astype(bf16)
        s_grad[mine, pl.ds(ff, ff)] = (hidden_grad * silu).astype(bf16)
        out = dot(hidden, sd[...], ((1,), (0,)))
        back = dot(s_grad[mine, :], sgu[...], ((1,), (1,)))
        for g in range(groups):
            lanes = pl.ds(g * group, group)
            span = slice(g * group, (g + 1) * group)
            outs[source, lanes, :] = (out[span] + dot(hots[g], slot_out[g], ((0,), (0,)))).astype(bf16)
            parts[source, lanes, :] = (back[span] + dot(hots[g], slot_grad[g], ((0,), (0,)))).astype(bf16)
        dots = jnp.concatenate([gate_dot[...], jnp.zeros((EXTRA - 8, rows), f32)], axis=0)
        parts[source, pl.ds(rows, EXTRA), :] = jnp.concatenate(
            [dots, jnp.zeros((EXTRA, width - rows), f32)], axis=1
        ).astype(bf16)

    inner = (z > 0) & (z < nz - 1)

    @pl.loop(0, nz)
    def _(index):
        source = by_distance(z, index)
        pl.when((index == 1) | (index == 3) | ((index == 2) & jnp.logical_not(inner)))(lambda: receive(source))
        pl.when((index == 1) & inner)(lambda: receive(by_distance(z, jnp.int32(2))))
        chunk(index, source)

        @pl.when(jnp.logical_not(inner) & (index > 0))
        def _():
            for piece in range(2):
                relay(source, piece)

        @pl.when(inner & (index == 3))
        def _():
            for piece in range(2):
                relay(by_distance(z, jnp.int32(2)), piece)

    out_copy = pltpu.make_async_copy(outs, out_part, local.at[5])
    out_copy.start()
    far, near = by_distance(z, jnp.int32(3)), by_distance(z, jnp.int32(1))

    def stage_copies(e, slot):
        return [
            pltpu.make_async_copy(wide_stage.at[slot], grads[0].at[e], stores.at[0, slot]),
            pltpu.make_async_copy(deep_stage.at[slot], grads[2].at[e], stores.at[1, slot]),
        ]

    def weight_grads(slot, rows_in, wide, hidden, deep):
        for k in range(0, wide.shape[1], 512):
            span = pl.ds(k, 512)
            wide_stage[slot, :, span] = dot(rows_in[...], wide[:, span], ((0,), (0,))).astype(bf16)
        deep_stage[slot] = dot(hidden[...], deep[...], ((0,), (0,))).astype(bf16)

    @pl.loop(0, experts)
    def _(e):
        slot = lax.rem(e, 2)

        @pl.when(e >= 2)
        def _():
            for copy in stage_copies(e - 2, slot):
                copy.wait()

        weight_grads(slot, arrived.at[e], act_grad.at[e], expert_hidden.at[e], pair_grad.at[e])
        for copy in stage_copies(e, slot):
            copy.start()
        pl.when(inner & (e == 1))(lambda: relay(far, 0))
        pl.when(inner & (e == 2))(lambda: relay(far, 1))
        pl.when(inner & (e == 3))(lambda: relay(near, 0))

    for copy in stage_copies(experts - 2, 0):
        copy.wait()
    tokens = mixed.reshape(nz * rows, width)
    for k in range(0, 2 * ff, 512):
        span = pl.ds(k, 512)
        wide_stage[0, :, span] = dot(tokens[...], s_grad[:, span], ((0,), (0,))).astype(bf16)
    cots = jnp.concatenate([cot[k, pl.ds(0, rows), :] for k in range(nz)], axis=0)
    deep_stage[0] = dot(s_hidden[...], cots, ((0,), (0,))).astype(bf16)
    shared_stores = [
        pltpu.make_async_copy(wide_stage.at[0], grads[1], stores.at[0, 0]),
        pltpu.make_async_copy(deep_stage.at[0], grads[3], stores.at[1, 0]),
    ]
    for copy in shared_stores:
        copy.start()
    pl.when(inner)(lambda: relay(near, 1))
    total[...] = parts[z].astype(f32)
    for way in range(2):

        @pl.when(z > 0 if way == 0 else z < nz - 1)
        def _():
            for piece in range(2):
                part_copy(way, z, piece).wait_recv()
            total[...] += came[way][z].astype(f32)

    for copy in stage_copies(experts - 1, 1) + shared_stores + [out_copy]:
        copy.wait()
    for way in range(2):
        for plane in range(nz):
            sent = (plane <= z if way == 0 else plane >= z) & may_send(way)
            pl.when(sent)(lambda: chunk_copy(way, plane).wait_send())

            @pl.when(z < plane if way == 0 else z > plane)
            def _():
                for piece in range(2):
                    part_copy(way, plane, piece).wait_send()


def ffn_fast(mixed, cot, router, weights, capacity):
    nz = lax.axis_size("z")
    egu, sgu, ed, sd = weights
    rows, width = mixed.shape
    experts, ff = ed.shape[:2]
    cot = cot.reshape(nz, -1, width)
    slots = nz * rows // 128 * capacity
    groups = rows // 128
    vmem, dma = pltpu.VMEM, pltpu.SemaphoreType.DMA
    low = lambda *shape: vmem(shape, bf16)
    scratch = [low(*w.shape) for w in weights]
    scratch += [low(nz, rows, width), low(*cot.shape), low(*router.shape)]
    scratch += [low(experts, slots, width), low(experts, slots, width)]
    scratch += [low(experts, slots, ff), low(experts, slots, 2 * ff), low(nz * rows, ff), low(nz * rows, 2 * ff)]
    stack = experts * capacity
    scratch += [low(groups, stack, width), low(groups, stack, width), low(groups, stack, 128), vmem((8, rows), f32)]
    scratch += [low(nz, rows, width)] + [low(*cot.shape)] * 3
    scratch += [low(2, width, 2 * ff), low(2, ff, width)]
    scratch += [dma((6,)), dma((2, experts)), dma((2, nz)), dma((2, nz)), dma((2, nz, 2)), dma((2, nz, 2)), dma((2, 2))]
    any_space = pl.BlockSpec(memory_space=pl.ANY)
    out_part, total, *grads = pl.pallas_call(
        functools.partial(ffn_kernel, capacity),
        out_shape=[
            jax.ShapeDtypeStruct((nz, rows, width), bf16),
            jax.ShapeDtypeStruct((rows + EXTRA, width), f32),
        ]
        + [jax.ShapeDtypeStruct(w.shape, bf16) for w in weights],
        in_specs=any_specs(7),
        out_specs=[any_space, pl.BlockSpec(memory_space=pltpu.VMEM)] + [any_space] * 4,
        scratch_shapes=scratch,
        compiler_params=params(1, 60 << 20),
        name="feed_forward",
    )(mixed, cot, router, *weights)
    return out_part, total, grads


def visible_units(prefix, heads, here, length):
    unit = lax.axis_index(DP) * here + jnp.arange(here)
    lengths = prefix[jnp.minimum(unit // heads, prefix.shape[0] - 1), 0]
    pos = jnp.arange(length, dtype=jnp.int32)
    low = pos[None, :] < lengths[:, None]
    return (pos[None, None, :] <= pos[None, :, None]) | (low[:, :, None] & low[:, None, :])


def attention_forward(qkv, batches, heads, prefix):
    units = to_units(qkv)
    q, k, v = units[:, 0], units[:, 1], units[:, 2]
    allowed = visible_units(prefix, heads, q.shape[0], q.shape[-1])
    scores = dot(q, k, ((1,), (1,)), ((0,), (0,))) * (1.0 / math.sqrt(HEAD_DIM))
    scores = jnp.where(allowed, scores, neg_fill)
    top = jnp.max(scores, axis=-1, keepdims=True)
    weights = jnp.exp(scores - top)
    total = jnp.sum(weights, axis=-1, keepdims=True)
    lse = top + jnp.log(total)
    probs = (weights / total).astype(bf16)
    context = dot(v, probs, ((2,), (2,)), ((0,), (0,))).astype(bf16)
    return from_units(context[:, None], batches, heads)[0], (q, k, v, lse)


def attention_backward(context_grad, saved, batches, heads, prefix):
    q, k, v, lse = saved
    grad = to_units(context_grad[None])[:, 0]
    allowed = visible_units(prefix, heads, q.shape[0], q.shape[-1])
    inv = 1.0 / math.sqrt(HEAD_DIM)
    scores = dot(q, k, ((1,), (1,)), ((0,), (0,))) * inv
    probs = jnp.where(allowed, jnp.exp(scores - lse), 0.0)
    prob_grad = dot(grad, v, ((1,), (1,)), ((0,), (0,)))
    delta = jnp.sum(probs * prob_grad, axis=-1, keepdims=True)
    score_grad = (probs * (prob_grad - delta)).astype(bf16)
    dq = dot(k, score_grad, ((2,), (2,)), ((0,), (0,))) * inv
    dk = dot(q, score_grad, ((2,), (1,)), ((0,), (0,))) * inv
    dv = dot(grad, probs.astype(bf16), ((2,), (1,)), ((0,), (0,)))
    return from_units(jnp.stack([dq, dk, dv], axis=1).astype(bf16), batches, heads)


def by_batch(tensor, batches):
    kinds, width, count = tensor.shape
    return jnp.transpose(tensor.reshape(kinds, width, batches, count // batches), (0, 2, 1, 3))


def gates(mixed_rows, pair_ids, router_w):
    hot = (pair_ids[..., None] == jnp.arange(router_w.shape[1], dtype=jnp.int32)).astype(f32)
    logits = dot(mixed_rows, router_w, ((1,), (0,)))
    return hot, jax.nn.softmax(jnp.sum(hot * logits[:, None, :], axis=-1), axis=-1)


def ffn_plain(mixed, cot_line, router_w, weights, capacity, rows):
    nz, (count, width), experts = lax.axis_size("z"), mixed.shape, router_w.shape[1]
    egu, sgu, ed, sd = weights
    slice_ff = sd.shape[0]
    cot_line = cot_line.reshape(nz, -1, width)
    mixed_line = gather_line(mixed)
    cot_rows = cot_line[:, :count].reshape(nz * count, width)
    ids = jnp.transpose(cot_line[:, count : count + TOP_K, :count], (0, 2, 1)).reshape(-1, TOP_K).astype(jnp.int32)
    lines = mixed_line.shape[0]
    groups = lines // rows

    hot, probs = gates(mixed_line, ids, router_w)
    hot_int = hot.astype(jnp.int32).reshape(groups, rows * TOP_K, experts)
    earlier = jnp.cumsum(hot_int, axis=1) - hot_int
    rank = jnp.sum(earlier * hot_int, axis=-1).reshape(groups, rows, TOP_K)
    group_ids = ids.reshape(groups, rows, TOP_K)
    slot = jnp.where(rank < capacity, group_ids * capacity + rank, experts * capacity)
    slot_hot = (slot[..., None] == jnp.arange(experts * capacity, dtype=jnp.int32)).astype(bf16)
    token_hot = jnp.sum(slot_hot, axis=2)
    slot_probs = jnp.sum(slot_hot.astype(f32) * probs.reshape(groups, rows, TOP_K, 1), axis=(1, 2))

    def dispatch(values):
        per_group = dot(token_hot, values.reshape(groups, rows, width), ((1,), (1,)), ((0,), (0,)))
        per_group = per_group.reshape(groups, experts, capacity, width)
        return jnp.transpose(per_group, (1, 0, 2, 3)).reshape(experts, groups * capacity, width)

    def per_slot(values):
        return jnp.transpose(values.reshape(groups, experts, capacity), (1, 0, 2)).reshape(experts, -1, 1)

    def combine(slots):
        per_group = jnp.transpose(slots.reshape(experts, groups, capacity, width), (1, 0, 2, 3))
        per_group = per_group.reshape(groups, experts * capacity, width)
        return dot(token_hot, per_group, ((2,), (1,)), ((0,), (0,))).reshape(lines, width)

    slot_p = per_slot(slot_probs)
    arrived = dispatch(mixed_line).astype(bf16)
    cot_slots = dispatch(cot_rows)
    pair_grad = (cot_slots * slot_p).astype(bf16)
    batch = ((0,), (0,))
    act = dot(arrived, egu, ((2,), (1,)), batch)
    gate_act, up_act = act[..., :slice_ff], act[..., slice_ff:]
    sig = jax.nn.sigmoid(gate_act)
    silu_act = gate_act * sig
    expert_hidden = (silu_act * up_act).astype(bf16)
    expert_out = dot(expert_hidden, ed, ((2,), (1,)), batch)
    hidden_grad = dot(pair_grad, ed, ((2,), (2,)), batch)
    gate_up_grad = jnp.concatenate(
        [hidden_grad * up_act * sig * (1.0 + gate_act * (1.0 - sig)), hidden_grad * silu_act], axis=-1
    ).astype(bf16)
    grad_egu = dot(arrived, gate_up_grad, ((1,), (1,)), batch).astype(bf16)
    grad_ed = dot(expert_hidden, pair_grad, ((1,), (1,)), batch).astype(bf16)
    slot_grad = dot(gate_up_grad, egu, ((2,), (2,)), batch).astype(bf16)
    gate_dot = jnp.sum(cot_slots * expert_out, axis=-1)
    gate_dot = jnp.transpose(gate_dot.reshape(experts, groups, capacity), (1, 0, 2)).reshape(groups, 1, 1, -1)
    pair_dot = jnp.sum(slot_hot.astype(f32) * gate_dot, axis=-1).reshape(lines, TOP_K)
    expert_sum = combine((expert_out * slot_p).astype(bf16))

    s_act = dot(mixed_line, sgu, ((1,), (0,)))
    s_in, s_lift = s_act[:, :slice_ff], s_act[:, slice_ff:]
    s_sig = jax.nn.sigmoid(s_in)
    s_silu = s_in * s_sig
    s_hidden = (s_silu * s_lift).astype(bf16)
    s_hidden_grad = dot(cot_rows, sd, ((1,), (1,)))
    s_grad = jnp.concatenate(
        [s_hidden_grad * s_lift * s_sig * (1.0 + s_in * (1.0 - s_sig)), s_hidden_grad * s_silu], axis=-1
    ).astype(bf16)
    grad_sgu = dot(mixed_line, s_grad, ((0,), (0,))).astype(bf16)
    grad_sd = dot(s_hidden, cot_rows, ((0,), (0,))).astype(bf16)
    out_part = (dot(s_hidden, sd, ((1,), (0,))) + expert_sum).astype(bf16)
    mixed_part = combine(slot_grad) + dot(s_grad, sgu, ((1,), (1,)))
    pair_dot = jnp.sum(hot * pair_dot[..., None], axis=1).reshape(nz, count, experts)
    pair_dot = jnp.pad(jnp.transpose(pair_dot, (0, 2, 1)), ((0, 0), (0, EXTRA - experts), (0, width - count)))
    mixed_part = jnp.concatenate([mixed_part.reshape(nz, count, width), pair_dot], axis=1).astype(bf16)
    mixed_sum = sum_line(mixed_part.reshape(-1, width)).astype(f32)
    return out_part, mixed_sum, (grad_egu, grad_sgu, grad_ed, grad_sd)


def shards(
    hidden,
    routes,
    prefix,
    cotangent,
    attn_gain,
    w_query,
    w_key,
    w_value,
    w_output,
    ffn_gain,
    router,
    shared_gate,
    shared_up,
    shared_down,
    expert_gate,
    expert_up,
    expert_down,
):
    nz = lax.axis_size("z")
    batches, _, rows, width = hidden.shape
    count = batches * rows
    heads = width // HEAD_DIM
    experts = router.shape[1]
    own = router.shape[0]
    capacity = (5 * rows * TOP_K + 4 * experts - 1) // (4 * experts)
    slice_ff = shared_gate.shape[1] // nz

    misc = jnp.concatenate(
        [router, attn_gain[:, None], ffn_gain[:, None], jnp.zeros((own, MISC - experts - 2), bf16)], axis=1
    )
    attn_shard = (w_query, w_key, w_value, w_output, misc)
    cot = cotangent.reshape(count, width)
    pair_ids = routes.reshape(count, TOP_K)
    ids_rows = jnp.pad(pair_ids.T.astype(bf16), ((0, EXTRA - TOP_K), (0, width - count)))
    halves = (expert_gate[0], expert_up[0], shared_gate, shared_up)

    def slices(gate, up):
        both = jnp.stack([gate.reshape(-1, nz, slice_ff), up.reshape(-1, nz, slice_ff)], axis=2)
        return jnp.transpose(both.reshape(-1, nz, 2 * slice_ff), (1, 0, 2))

    fast = paired(batches, heads)
    if fast:
        attn_full, lined, ed, sd = first_fast(attn_shard, halves, expert_down[0], shared_down)
    else:
        attn_full = gather_all(jnp.concatenate(attn_shard, axis=1))

    w_qkv = attn_full[:, : 3 * width]
    w_out = attn_full[:, 3 * width : 4 * width]
    misc_full = attn_full[:, 4 * width :]
    router_w = misc_full[:, :experts]
    gain_attn = misc_full[:, experts].astype(f32)
    gain_ffn = misc_full[:, experts + 1].astype(f32)

    x_in = hidden.reshape(count, width).astype(f32)
    attn_scale = rms_scale(x_in)
    attn_norm = x_in * attn_scale
    normed = (attn_norm * gain_attn).astype(bf16)
    positions = lax.axis_index(DP) * rows + jnp.arange(rows, dtype=jnp.int32)
    cosine, sine = rotary_tables(jnp.tile(positions, batches))
    projected = dot(w_qkv, normed, ((0,), (1,)))
    turned = rotate_t(projected[: 2 * width], cosine, sine, 1.0)
    qkv = jnp.concatenate([turned, projected[2 * width :]], axis=0).astype(bf16).reshape(3, width, count)
    if fast:
        context, saved, egu, sgu, cot_line = attend_fast(prefix, qkv, *lined, cotangent, ids_rows)
        ffn = egu, sgu, ed, sd
    else:
        context, saved = attention_forward(by_batch(qkv, batches), batches, heads, prefix)
        context = jnp.transpose(context, (1, 0, 2)).reshape(width, count)
        ffn = gather_weights(slices(*halves[:2]), slices(*halves[2:]), expert_down[0], shared_down)
        cot_line = gather_line(jnp.concatenate([cot, ids_rows], axis=0))
    attended = x_in + dot(context, w_out, ((0,), (0,)))
    ffn_scale = rms_scale(attended)
    ffn_norm = attended * ffn_scale
    mixed = (ffn_norm * gain_ffn).astype(bf16)

    if fast:
        router_rows = jnp.pad(router_w.T, ((0, 16 - experts), (0, 0)))
        out_part, mixed_sum, ffn_grads = ffn_fast(mixed, cot_line, router_rows, ffn, capacity)
    else:
        out_part, mixed_sum, ffn_grads = ffn_plain(mixed, cot_line, router_w, ffn, capacity, rows)

    hot, probs = gates(mixed, pair_ids, router_w)
    gate_grads = jnp.sum(hot * mixed_sum[count : count + experts, :count].T[:, None, :], axis=-1)
    picked = probs * (gate_grads - jnp.sum(probs * gate_grads, axis=-1, keepdims=True))
    logit_grad = jnp.sum(hot * picked[..., None], axis=1)
    grad_router = jnp.dot(mixed.astype(f32).T, logit_grad, precision=highest)
    mixed_grad = mixed_sum[:count] + jnp.dot(logit_grad, router_w.astype(f32).T, precision=highest)
    cot_wide = cot.astype(f32)
    inner = mixed_grad * gain_ffn
    grad_gffn = jnp.sum(mixed_grad * ffn_norm, axis=0)
    attended_grad = cot_wide + ffn_scale * (inner - ffn_norm * jnp.mean(inner * ffn_norm, axis=-1, keepdims=True))
    out_grad = attended_grad.astype(bf16)
    grad_wout = dot(context, out_grad, ((1,), (0,)))
    context_grad = dot(w_out, out_grad, ((1,), (1,))).astype(bf16)

    if fast:
        tables = rotary_tables(jnp.arange(rows * lax.axis_size(DP), dtype=jnp.int32))
        qkv_grad, lined, out_sum = backward_fast(prefix, tables, context_grad, saved, *ffn_grads[:2], out_part)
        qkv_grad = qkv_grad.reshape(3 * width, count)
    else:
        context_grad = by_batch(context_grad[None], batches)[0]
        rot_grad = attention_backward(context_grad, saved, batches, heads, prefix)
        rot_grad = jnp.transpose(rot_grad, (0, 2, 1, 3)).reshape(3 * width, count).astype(f32)
        turned = rotate_t(rot_grad[: 2 * width], cosine, sine, -1.0)
        qkv_grad = jnp.concatenate([turned, rot_grad[2 * width :]], axis=0).astype(bf16)
        egu_sum, sgu_sum, ed_sum, sd_sum = sum_weights(*ffn_grads)
        out_sum = sum_line(out_part)
    grad_wqkv = dot(normed, qkv_grad, ((0,), (1,)))
    normed_grad = dot(qkv_grad, w_qkv, ((0,), (1,)))
    grad_gattn = jnp.sum(normed_grad * attn_norm, axis=0)
    inner = normed_grad * gain_attn
    input_grad = (
        attended_grad + attn_scale * (inner - attn_norm * jnp.mean(inner * attn_norm, axis=-1, keepdims=True))
    ).astype(bf16)

    grad_misc = jnp.concatenate(
        [grad_router, grad_gattn[:, None], grad_gffn[:, None], jnp.zeros((width, MISC - experts - 2), f32)], axis=1
    )
    attn_parts = [part.astype(bf16) for part in (grad_wqkv, grad_wout, grad_misc)]

    def joined(blocks):
        both = jnp.transpose(blocks.reshape(nz, -1, 2, slice_ff), (2, 1, 0, 3)).astype(f32)
        return both.reshape(2, -1, nz * slice_ff)

    if fast:
        sums = last_fast(attn_parts, *lined, *ffn_grads[2:])
        *weight_sums, block_rows = finish_fast(sums, attended, out_sum)
        misc_sums = sums[0][:, 4 * width :]
    else:
        attn_sums = sum_all(jnp.concatenate(attn_parts, axis=1)).astype(f32)
        *attn_sums, misc_sums = jnp.split(attn_sums, [width, 2 * width, 3 * width, 4 * width], axis=1)
        downs = [down.astype(f32) for down in (sd_sum, ed_sum)]
        weight_sums = (*attn_sums, *joined(sgu_sum), downs[0], *joined(egu_sum), downs[1])
        block_rows = (attended + out_sum.astype(f32)).astype(bf16)
    return (
        block_rows.reshape(batches, 1, rows, width),
        input_grad.reshape(batches, 1, rows, width),
        misc_sums[:, experts],
        *weight_sums[:4],
        misc_sums[:, experts + 1],
        misc_sums[:, :experts],
        *weight_sums[4:7],
        *[total[None] for total in weight_sums[7:]],
    )


def solution(mesh):
    n_dp, n_expert = mesh.shape["dp"], mesh.shape["expert"]
    nz = 4 if n_dp % 4 == 0 else 1
    grid = Mesh(mesh.devices.reshape(nz, n_dp // nz, n_expert // 2, 2), ALL)
    rows = P(None, EXPERT, DP, None)
    line = P(ALL)
    dense = P(ALL, None)
    expert = P(EXPERT, DP, None)
    return jax.shard_map(
        shards,
        mesh=grid,
        in_specs=(rows, rows, P(None, EXPERT), rows, line)
        + (dense,) * 4
        + (line,)
        + (dense,) * 4
        + (expert,) * 3,
        out_specs=(rows, rows, line) + (dense,) * 4 + (line,) + (dense,) * 4 + (expert,) * 3,
        check_vma=False,
    )
```
